32 devices in a mesh: expert: 2 (over x), fsdp: 16 (over z, y, core).
Axes of the slice: x: 2, y: 2, z: 4, core: 2. Of those that a mesh axis runs over, the one named last changes fastest.
Arguments:
- inputs: bfloat16 [31360, 512], P(('expert', 'fsdp')), may hold values from -6 to 6
- cotangent: bfloat16 [31360, 512], P(('expert', 'fsdp')), may hold values from -6 to 6
- routes: int32 [31360, 2], P(('expert', 'fsdp')), may hold values from 0 to 7, as said below
- slots: int32 [31360, 2], P(('expert', 'fsdp')), may hold values from -1 to 257, as said below
- qkv_weight: bfloat16 [512, 1536], P('fsdp'), may hold values from -0.25 to 0.25
- out_weight: bfloat16 [512, 512], P('fsdp'), may hold values from -0.75 to 0.75
- router_weight: bfloat16 [512, 8], P('fsdp'), may hold values from -0.1875 to 0.1875
- norm1_gain: bfloat16 [512], P('fsdp'), may hold values from 0.5 to 1.5
- norm1_shift: bfloat16 [512], P('fsdp'), may hold values from -1 to 1
- norm2_gain: bfloat16 [512], P('fsdp'), may hold values from 0.5 to 1.5
- norm2_shift: bfloat16 [512], P('fsdp'), may hold values from -1 to 1
- expert_up: bfloat16 [8, 512, 2048], P('expert', 'fsdp'), may hold values from -0.25 to 0.25
- expert_down: bfloat16 [8, 2048, 512], P('expert', 'fsdp'), may hold values from -0.875 to 0.875
Outputs:
- output: bfloat16 [31360, 512], P(('expert', 'fsdp'))
- input_grad: float32 [31360, 512], P(('expert', 'fsdp'))
- qkv_grad: float32 [512, 1536], P('fsdp')
- out_grad: float32 [512, 512], P('fsdp')
- router_grad: float32 [512, 8], P('fsdp')
- norm1_gain_grad: float32 [512], P('fsdp')
- norm1_shift_grad: float32 [512], P('fsdp')
- norm2_gain_grad: float32 [512], P('fsdp')
- norm2_shift_grad: float32 [512], P('fsdp')
- up_grad: float32 [8, 512, 2048], P('expert', 'fsdp')
- down_grad: float32 [8, 2048, 512], P('expert', 'fsdp')
The draws below stay inside these ranges and needn't reach their ends.
Inputs may be any that keep to these rules, and one draw needn't show every extreme that they name: `routes`: each row names two different experts. Within the 980 rows of one device and for each expert, the kept routes hold slots 0, 1, 2, ... once each without gaps, all first routes (column 0) before second ones, each column in one order of priority over the device's patches; a route with slot -1 is dropped and so is every later route to that expert. In every device's rows some expert fills all 258 slots.
All inputs are finite; a program needn't handle non-finite values.
Results may differ from the reference program's by a relative error of at most 0.024.
Values may be sent and summed in bfloat16 or wider, within the bound.
A program may use at most 192 MiB of HBM per device.

```python
import jax
import jax.numpy as jnp
from jax import lax

D = 512
HEADS = 8
HEAD_DIM = 64
FF = 2048
PATCHES = 49
IMG_DEV = 20
TOK_DEV = 980
TOKENS = 31360
EXPERTS = 8
CAP = 258


def route_tables(key):
    groups = TOKENS // TOK_DEV
    keys_list = jax.random.split(key, 5)
    heavy = jax.random.randint(keys_list[0], (), 0, EXPERTS)
    first = jax.random.randint(keys_list[1], (groups, TOK_DEV), 0, EXPERTS)
    position = jnp.arange(TOK_DEV, dtype=jnp.int32)[None, :]
    lottery = jax.random.randint(keys_list[2], (groups, TOK_DEV), 0, 1 << 19) * TOK_DEV + position
    forced = jnp.argsort(jnp.argsort(lottery, axis=1), axis=1) < CAP + 3
    first = jnp.where(forced, heavy, first)
    second = (first + jax.random.randint(keys_list[3], (groups, TOK_DEV), 1, EXPERTS)) % EXPERTS
    ranking = jax.random.randint(keys_list[4], (groups, TOK_DEV), 0, 1 << 19) * TOK_DEV + position
    ordering = jnp.argsort(ranking, axis=1)
    inverse = jnp.argsort(ordering, axis=1)
    labels = jnp.arange(EXPERTS, dtype=jnp.int32)

    def counts_of(picked_ids):
        ordered_ids = jnp.take_along_axis(picked_ids, ordering, axis=1)
        onehot = (ordered_ids[:, :, None] == labels).astype(jnp.int32)
        before = jnp.cumsum(onehot, axis=1) - onehot
        earlier = jnp.sum(before * onehot, axis=2)
        return (jnp.take_along_axis(earlier, inverse, axis=1), jnp.sum(onehot, axis=1))
    count_first, totals_first = counts_of(first)
    count_second, unused_totals = counts_of(second)
    count_second = count_second + jnp.take_along_axis(totals_first, second, axis=1)
    counts = jnp.stack([count_first, count_second], axis=-1)
    slot_table = jnp.where(counts < CAP, counts, -1)
    route_table = jnp.stack([first, second], axis=-1)
    return (route_table.reshape(TOKENS, 2).astype(jnp.int32), slot_table.reshape(TOKENS, 2).astype(jnp.int32))


def draw_routes(key, part):
    return route_tables(key)[0]


def draw_slots(key, part):
    return route_tables(key)[1]


def steps_of(own_key, dims, pieces, low, high):
    def one(dim, blocks):
        draws = jax.random.uniform(jax.random.fold_in(jax.random.fold_in(own_key, 6), dim), (blocks,), jnp.float32, low / len(pieces), high / len(pieces))
        return jnp.repeat(jnp.exp(draws), dims[dim] // blocks).reshape((-1,) + (1,) * (len(dims) - dim - 1))

    level = one(*pieces[0])
    for cut in pieces[1:]:
        level = level * one(*cut)
    return level


def scatter_about(rng, shape, scale, limit, cuts=(), kind=jnp.bfloat16):
    values = jax.random.normal(rng, shape, jnp.float32) * scale
    if len(cuts) > 0:
        values = steps_of(rng, shape, cuts, -0.22, 0.18) * values
    return jnp.clip(values, min=-limit, max=limit).astype(kind)


def setup_inputs(seed: int = 0) -> dict:
    streams_of = jax.random.split(jax.random.key(seed), 14)
    inputs = scatter_about(streams_of[0], (TOKENS, D), 1.0, 6.0, ((0, 32),))
    cotangent = scatter_about(streams_of[1], (TOKENS, D), 1.0, 6.0, ((0, 32),))
    routes = draw_routes(jax.random.fold_in(streams_of[13], 71), 0)
    slots = draw_slots(jax.random.fold_in(streams_of[13], 71), 0)
    qkv_weight = scatter_about(streams_of[4], (D, 3 * D), D ** -0.5, 0.25, ((0, 16),))
    out_weight = scatter_about(streams_of[5], (D, D), (D // 7) ** -0.5, 0.75, ((0, 16),))
    router_weight = scatter_about(streams_of[6], (D, EXPERTS), (2 * D) ** -0.5, 0.1875, ((0, 16),))
    norm1_gain = jnp.clip(1.0 + 0.1 * jax.random.normal(streams_of[7], (D,), jnp.float32), 0.5, 1.5).astype(jnp.bfloat16)
    norm1_shift = scatter_about(streams_of[8], (D,), 0.2, 1.0, ((0, 16),))
    norm2_gain = jnp.clip(1.0 + 0.1 * jax.random.normal(streams_of[9], (D,), jnp.float32), 0.5, 1.5).astype(jnp.bfloat16)
    norm2_shift = scatter_about(streams_of[10], (D,), 0.2, 1.0, ((0, 16),))
    expert_up = scatter_about(streams_of[11], (EXPERTS, D, FF), D ** -0.5, 0.25, ((0, 2), (1, 16)))
    expert_down = scatter_about(streams_of[12], (EXPERTS, FF, D), (max(1, (3 * FF) // (2 * EXPERTS * EXPERTS))) ** -0.5, 0.875, ((0, 2), (1, 16)))
    return {"inputs": inputs, "cotangent": cotangent, "routes": routes, "slots": slots, "qkv_weight": qkv_weight, "out_weight": out_weight, "router_weight": router_weight, "norm1_gain": norm1_gain, "norm1_shift": norm1_shift, "norm2_gain": norm2_gain, "norm2_shift": norm2_shift, "expert_up": expert_up, "expert_down": expert_down}


EPS = 1e-06
HIGHEST = lax.Precision.HIGHEST

@jax.custom_vjp
def low(v):
    return lax.optimization_barrier(v.astype(jnp.bfloat16)).astype(jnp.float32)

@jax.custom_vjp
def low_back(v):
    return v

def low_keep(v):
    return (low(v), None)

def low_pass(kept, grad):
    return (grad,)

def back_keep(v):
    return (v, None)

def back_low(kept, grad):
    return (low(grad),)
low.defvjp(low_keep, low_pass)
low_back.defvjp(back_keep, back_low)

def layer_norm(values, gain, shift):
    center = lax.optimization_barrier(jnp.mean(values, axis=-1, keepdims=True))
    offset = values - center
    spread = lax.optimization_barrier(jnp.mean(offset * offset, axis=-1, keepdims=True))
    return offset * lax.rsqrt(spread + EPS) * gain + shift

def attention_group(normed, qkv_weight, out_weight):
    triple = low(low_back(jnp.dot(normed, qkv_weight, precision=HIGHEST)))
    triple = triple.reshape(IMG_DEV, PATCHES, 3, HEADS, HEAD_DIM)
    queries = triple[:, :, 0]
    keys_all = triple[:, :, 1]
    values = triple[:, :, 2]
    scores = low_back(jnp.einsum('iqhd,ikhd->ihqk', queries, keys_all, precision=HIGHEST) * HEAD_DIM ** (-0.5))
    weights = low(jax.nn.softmax(scores, axis=-1))
    attended = jnp.einsum('ihqk,ikhd->iqhd', weights, values, precision=HIGHEST).reshape(TOK_DEV, D)
    attended = low(low_back(attended))
    return low_back(jnp.dot(attended, out_weight, precision=HIGHEST))

def expert_layer(operands):
    expert_rows, up_matrix, down_matrix = operands
    hidden = low_back(jnp.dot(expert_rows, up_matrix, precision=HIGHEST))
    active = low(jax.nn.gelu(hidden, approximate=False))
    return low(low_back(jnp.dot(active, down_matrix, precision=HIGHEST)))

def place_rows(index_row, value_rows):
    return jnp.zeros((EXPERTS * CAP + 1, D), jnp.float32).at[index_row].add(value_rows)

def pick_rows(table, index_row):
    return table[index_row]

def forward(inputs, qkv_weight, out_weight, router_weight, norm1_gain, norm1_shift, norm2_gain, norm2_shift, expert_up, expert_down, routes, slots):
    groups = TOKENS // TOK_DEV
    first_normed = low(layer_norm(inputs, norm1_gain, norm1_shift))

    def attend(block_rows):
        return attention_group(block_rows, qkv_weight, out_weight)
    branch = lax.map(jax.checkpoint(attend), first_normed.reshape(groups, TOK_DEV, D))
    middle = inputs + branch.reshape(TOKENS, D)
    second_normed = low(layer_norm(middle, norm2_gain, norm2_shift))
    logits = low_back(jnp.dot(second_normed, router_weight, precision=HIGHEST))
    router_probs = jax.nn.softmax(logits, axis=-1)
    gate_values = jnp.take_along_axis(router_probs, routes, axis=1)
    targets = jnp.where(slots >= 0, routes * CAP + slots, EXPERTS * CAP).astype(jnp.int32)
    targets = targets.reshape(groups, TOK_DEV * 2)
    copies = jnp.repeat(second_normed.reshape(groups, TOK_DEV, D), 2, axis=1)
    buffers = jax.vmap(place_rows)(targets, copies)[:, :EXPERTS * CAP]
    buffers = low_back(buffers).reshape(groups, EXPERTS, CAP, D).transpose(1, 0, 2, 3)
    buffers = buffers.reshape(EXPERTS, groups * CAP, D)
    produced = lax.map(jax.checkpoint(expert_layer), (buffers, expert_up, expert_down))
    produced = produced.reshape(EXPERTS, groups, CAP, D).transpose(1, 0, 2, 3).reshape(groups, EXPERTS * CAP, D)
    padded = jnp.concatenate([produced, jnp.zeros((groups, 1, D), jnp.float32)], axis=1)
    selected = low_back(jax.vmap(pick_rows)(padded, targets)).reshape(TOKENS, 2, D)
    return middle + lax.optimization_barrier(jnp.sum(gate_values[:, :, None] * selected, axis=1))

def reference(inputs, cotangent, routes, slots, qkv_weight, out_weight, router_weight, norm1_gain, norm1_shift, norm2_gain, norm2_shift, expert_up, expert_down):
    floats = tuple((member.astype(jnp.float32) for member in (inputs, qkv_weight, out_weight, router_weight, norm1_gain, norm1_shift, norm2_gain, norm2_shift, expert_up, expert_down)))

    def closed(*params):
        return forward(*params, routes, slots)
    result, pullback = jax.vjp(closed, *floats)
    gradients = pullback(cotangent.astype(jnp.float32))
    return (result.astype(jnp.bfloat16), gradients[0], gradients[1], gradients[2], gradients[3], gradients[4], gradients[5], gradients[6], gradients[7], gradients[8], gradients[9])
```

```python
import functools

import jax
import jax.numpy as jnp
from jax import lax
from jax.experimental import pallas as pl
from jax.experimental.pallas import tpu as pltpu
from jax.sharding import PartitionSpec as P

HEADS = 8
HEAD_DIM = 64
PATCHES = 49
EPS = 1e-06
ROOT_HALF = 0.7071067811865476
DENSITY_SCALE = 0.3989422804014327

BLOCK = 256
GROUP_IMAGES = BLOCK // PATCHES
GROUP_ROWS = GROUP_IMAGES * PATCHES
LANES = 128
NORM_LANE = 64
FF_CHUNK = 512
VMEM_LIMIT = 60 * 1024 * 1024

F32 = jnp.float32
BF16 = jnp.bfloat16


def dot(left, right):
    return lax.dot_general(left, right, (((1,), (0,)), ((), ())), preferred_element_type=F32)


def dot_rows(left, right):
    return lax.dot_general(left, right, (((0,), (0,)), ((), ())), preferred_element_type=F32)


def dot_against(left, right):
    return lax.dot_general(left, right, (((1,), (1,)), ((), ())), preferred_element_type=F32)


def iota(shape, dim):
    return lax.broadcasted_iota(jnp.int32, shape, dim)


def normalize(values):
    center = jnp.mean(values, axis=-1, keepdims=True)
    offset = values - center
    spread = jnp.mean(offset * offset, axis=-1, keepdims=True)
    inverse = lax.rsqrt(spread + EPS)
    return offset * inverse, inverse


def denormalize(upstream, normed, inverse, gain):
    scaled = upstream * gain
    return inverse * (
        scaled
        - jnp.mean(scaled, axis=-1, keepdims=True)
        - normed * jnp.mean(scaled * normed, axis=-1, keepdims=True)
    )


def to_row(column):
    n = column.shape[0]
    parts = []
    for at in range(0, n, LANES):
        eye = iota((LANES, LANES), 0) == iota((LANES, LANES), 1)
        parts.append(jnp.sum(jnp.where(eye, column[at : at + LANES], 0.0), axis=0, keepdims=True))
    return parts[0] if len(parts) == 1 else jnp.concatenate(parts, axis=1)


def rows_of(g):
    return pl.ds(pl.multiple_of(g * BLOCK, BLOCK), BLOCK)


def gates_of(probs, meta):
    lane = iota(probs.shape, 1)
    first = jnp.sum(jnp.where(lane == meta[:, 2:3], probs, 0.0), axis=1, keepdims=True)
    second = jnp.sum(jnp.where(lane == meta[:, 3:4], probs, 0.0), axis=1, keepdims=True)
    return first, second


def forward_kernel(
    experts,
    x_ref, cot_ref, meta_ref, meta_row_ref, params_ref,
    act_one_ref, triple_ref, weights_ref, attended_ref, mid_ref, act_two_ref, probs_ref,
    sent_ref, grad_sent_ref, cot_sent_ref,
    bias_ref, gate_rows_ref,
):
    width = x_ref.shape[1]
    groups = x_ref.shape[0] // BLOCK
    small = params_ref[:, 4 * width :]
    small_rows = jnp.transpose(small.astype(F32))
    image_row = iota((BLOCK, BLOCK), 0) // PATCHES
    image_col = iota((BLOCK, BLOCK), 1) // PATCHES
    bias_ref[...] = jnp.where(image_row == image_col, 0.0, -1e30)

    @pl.loop(0, groups)
    def _(g):
        rows = rows_of(g)
        x = x_ref[rows, :].astype(F32)
        normed, _ = normalize(x)
        act = (normed * small_rows[NORM_LANE : NORM_LANE + 1] + small_rows[NORM_LANE + 1 : NORM_LANE + 2]).astype(BF16)
        act_one_ref[rows, :] = act
        triple_ref[rows, :] = dot(act, params_ref[:, : 3 * width]).astype(BF16)
        low = iota((BLOCK, LANES), 1) < HEAD_DIM
        for pair in range(HEADS // 2):
            at = pair * LANES
            q = triple_ref[rows, at : at + LANES] * HEAD_DIM ** (-0.5)
            k = triple_ref[rows, width + at : width + at + LANES]
            v = triple_ref[rows, 2 * width + at : 2 * width + at + LANES]
            total = None
            for half in range(2):
                mask = low if half == 0 else jnp.logical_not(low)
                scores = dot_against(jnp.where(mask, q, 0.0).astype(BF16), k) + bias_ref[...]
                top = jnp.max(scores, axis=-1, keepdims=True)
                raised = jnp.exp(scores - top)
                probs = raised / jnp.sum(raised, axis=-1, keepdims=True)
                probs = probs.astype(BF16)
                weights_ref[g, 2 * pair + half] = probs
                part = dot(probs, jnp.where(mask, v, 0.0).astype(BF16))
                total = part if total is None else total + part
            attended_ref[rows, at : at + LANES] = total.astype(BF16)
        mid = x + dot(attended_ref[rows, :], params_ref[:, 3 * width : 4 * width])
        mid_ref[rows, :] = mid
        normed, _ = normalize(mid)
        act = (normed * small_rows[NORM_LANE + 2 : NORM_LANE + 3] + small_rows[NORM_LANE + 3 : NORM_LANE + 4]).astype(BF16)
        act_two_ref[rows, :] = act
        logits = jnp.where(iota((BLOCK, LANES), 1) < experts, dot(act, small), -1e30)
        raised = jnp.exp(logits - jnp.max(logits, axis=-1, keepdims=True))
        probs = raised / jnp.sum(raised, axis=-1, keepdims=True)
        probs_ref[rows, :] = probs
        first, second = gates_of(probs, meta_ref[rows, :])
        gate_rows_ref[0:1, rows] = to_row(first)
        gate_rows_ref[1:2, rows] = to_row(second)

    capacity = sent_ref.shape[1]

    @pl.loop(0, experts)
    def _(e):
        slot = iota((capacity, x_ref.shape[0]), 0) + e * capacity
        in_first = slot == meta_row_ref[0:1, :]
        in_second = slot == meta_row_ref[1:2, :]
        picks = jnp.where(jnp.logical_or(in_first, in_second), 1.0, 0.0).astype(BF16)
        gate = jnp.sum(
            jnp.where(in_first, gate_rows_ref[0:1, :], jnp.where(in_second, gate_rows_ref[1:2, :], 0.0)),
            axis=1, keepdims=True,
        )
        sent_ref[e] = dot(picks, act_two_ref[...]).astype(BF16)
        cot_slots = dot(picks, cot_ref[...])
        cot_sent_ref[e] = cot_slots.astype(BF16)
        grad_sent_ref[e] = (gate * cot_slots).astype(BF16)


def expert_kernel(rows_ref, grad_ref, up_ref, down_ref, back_ref, grad_rows_ref, up_part_ref, down_part_ref, back_sum, grad_sum):
    hidden_width = up_ref.shape[2]
    chunks = hidden_width // FF_CHUNK
    back_sum[...] = jnp.zeros_like(back_sum)
    grad_sum[...] = jnp.zeros_like(grad_sum)

    @pl.loop(0, chunks)
    def _(f):
        at = pl.ds(pl.multiple_of(f * FF_CHUNK, FF_CHUNK), FF_CHUNK)
        rows, grads = rows_ref[0], grad_ref[0]
        up, down = up_ref[0, :, at], down_ref[0, at, :]
        hidden = dot(rows, up)
        spread = 0.5 * (1.0 + lax.erf(hidden * ROOT_HALF))
        active = (hidden * spread).astype(BF16)
        slope = spread + hidden * (DENSITY_SCALE * jnp.exp(-0.5 * hidden * hidden))
        back_sum[...] += dot(active, down)
        grad_hidden = (dot_against(grads, down) * slope).astype(BF16)
        grad_sum[...] += dot_against(grad_hidden, up)
        up_part_ref[0, :, at] = dot_rows(rows, grad_hidden).astype(BF16)
        down_part_ref[0, at, :] = dot_rows(active, grads).astype(BF16)

    back_ref[0] = back_sum[...].astype(BF16)
    grad_rows_ref[0] = grad_sum[...].astype(BF16)


def backward_kernel(
    experts,
    x_ref, cot_ref, meta_ref, params_ref, act_one_ref, triple_ref, weights_ref, attended_ref, mid_ref, act_two_ref,
    probs_ref, back_ref, grad_slots_ref, cot_slots_ref,
    out_ref, input_grad_ref, params_grad_ref,
    dot_row_ref, place_ref, gated_ref, branch_ref, grad_triple_ref, logit_grad_ref, sums_ref,
):
    width = x_ref.shape[1]
    groups = x_ref.shape[0] // BLOCK
    places = back_ref.shape[0]
    small = params_ref[:, 4 * width :]
    small_rows = jnp.transpose(small.astype(F32))
    gain_one = small_rows[NORM_LANE : NORM_LANE + 1]
    gain_two = small_rows[NORM_LANE + 2 : NORM_LANE + 3]
    sums_ref[...] = jnp.zeros_like(sums_ref)

    @pl.loop(0, places // LANES)
    def _(c):
        at = pl.ds(pl.multiple_of(c * LANES, LANES), LANES)
        column = jnp.sum(back_ref[at, :].astype(F32) * cot_slots_ref[at, :].astype(F32), axis=1, keepdims=True)
        dot_row_ref[0:1, at] = to_row(column)

    @pl.loop(0, groups)
    def _(g):
        rows = rows_of(g)
        meta = meta_ref[rows, :]
        probs = probs_ref[rows, :]
        gate_first, gate_second = gates_of(probs, meta)
        lane = iota((BLOCK, LANES), 1)
        grad_first = jnp.zeros((BLOCK, LANES), F32)
        grad_second = jnp.zeros((BLOCK, LANES), F32)
        for c in range(places // LANES):
            at = c * LANES
            in_first = lane == meta[:, 0:1] - at
            in_second = lane == meta[:, 1:2] - at
            place_ref[:, at : at + LANES] = jnp.where(jnp.logical_or(in_first, in_second), 1.0, 0.0).astype(BF16)
            gated_ref[:, at : at + LANES] = jnp.where(in_first, gate_first, jnp.where(in_second, gate_second, 0.0)).astype(BF16)
            dots = dot_row_ref[0:1, at : at + LANES]
            grad_first += jnp.where(in_first, dots, 0.0)
            grad_second += jnp.where(in_second, dots, 0.0)
        grad_first = jnp.sum(grad_first, axis=1, keepdims=True)
        grad_second = jnp.sum(grad_second, axis=1, keepdims=True)
        mid = mid_ref[rows, :]
        out_ref[rows, :] = (mid + dot(gated_ref[...], back_ref[...])).astype(BF16)
        grad_probs = jnp.where(lane == meta[:, 2:3], grad_first, 0.0) + jnp.where(lane == meta[:, 3:4], grad_second, 0.0)
        grad_logits = (probs * (grad_probs - jnp.sum(grad_probs * probs, axis=-1, keepdims=True))).astype(BF16)
        logit_grad_ref[rows, :] = grad_logits
        grad_act = dot(place_ref[...], grad_slots_ref[...]) + dot_against(grad_logits, small)
        normed, inverse = normalize(mid)
        sums_ref[NORM_LANE + 2 : NORM_LANE + 3, :] += jnp.sum(grad_act * normed, axis=0, keepdims=True)
        sums_ref[NORM_LANE + 3 : NORM_LANE + 4, :] += jnp.sum(grad_act, axis=0, keepdims=True)
        grad_mid = cot_ref[rows, :].astype(F32) + denormalize(grad_act, normed, inverse, gain_two)
        input_grad_ref[rows, :] = grad_mid
        branch = grad_mid.astype(BF16)
        branch_ref[rows, :] = branch
        grad_attended = dot_against(branch, params_ref[:, 3 * width : 4 * width]).astype(BF16)
        low = lane < HEAD_DIM
        for pair in range(HEADS // 2):
            at = pair * LANES
            q = triple_ref[rows, at : at + LANES] * HEAD_DIM ** (-0.5)
            k = triple_ref[rows, width + at : width + at + LANES]
            v = triple_ref[rows, 2 * width + at : 2 * width + at + LANES]
            upstream = grad_attended[:, at : at + LANES]
            grad_q = grad_k = grad_v = jnp.zeros((BLOCK, LANES), F32)
            for half in range(2):
                mask = low if half == 0 else jnp.logical_not(low)
                upstream_half = jnp.where(mask, upstream, 0.0).astype(BF16)
                weights = weights_ref[g, 2 * pair + half]
                kept = weights.astype(F32)
                grad_weights = dot_against(upstream_half, v)
                inner = jnp.sum(grad_weights * kept, axis=-1, keepdims=True)
                grad_scores = (kept * (grad_weights - inner)).astype(BF16)
                grad_q += dot(grad_scores, jnp.where(mask, k, 0.0).astype(BF16))
                grad_k += dot_rows(grad_scores, jnp.where(mask, q, 0.0).astype(BF16))
                grad_v += dot_rows(weights, upstream_half)
            grad_triple_ref[rows, at : at + LANES] = (grad_q * HEAD_DIM ** (-0.5)).astype(BF16)
            grad_triple_ref[rows, width + at : width + at + LANES] = grad_k.astype(BF16)
            grad_triple_ref[rows, 2 * width + at : 2 * width + at + LANES] = grad_v.astype(BF16)
        grad_act = dot_against(grad_triple_ref[rows, :], params_ref[:, : 3 * width])
        normed, inverse = normalize(x_ref[rows, :].astype(F32))
        sums_ref[NORM_LANE : NORM_LANE + 1, :] += jnp.sum(grad_act * normed, axis=0, keepdims=True)
        sums_ref[NORM_LANE + 1 : NORM_LANE + 2, :] += jnp.sum(grad_act, axis=0, keepdims=True)
        input_grad_ref[rows, :] += denormalize(grad_act, normed, inverse, gain_one)

    params_grad_ref[:, : 3 * width] = dot_rows(act_one_ref[...], grad_triple_ref[...]).astype(BF16)
    params_grad_ref[:, 3 * width : 4 * width] = dot_rows(attended_ref[...], branch_ref[...]).astype(BF16)
    router_part = dot_rows(act_two_ref[...], logit_grad_ref[...])
    norm_part = jnp.transpose(sums_ref[...])
    params_grad_ref[:, 4 * width :] = (router_part + norm_part).astype(BF16)


def on_device(
    inputs, cotangent, routes, slots, qkv_weight, out_weight, router_weight,
    norm1_gain, norm1_shift, norm2_gain, norm2_shift, expert_up, expert_down,
):
    rows_dev, width = inputs.shape
    groups = rows_dev // GROUP_ROWS
    rows_pad = groups * BLOCK
    fsdp = lax.axis_size("fsdp")
    peers = lax.axis_size("expert")
    held = expert_up.shape[0]
    experts = held * peers
    capacity = (42 * rows_dev + 20 * experts - 1) // (20 * experts)
    capacity = -(-capacity // 16) * 16
    places = -(-experts * capacity // LANES) * LANES

    def pad_rows(array, value=0):
        array = array.reshape(groups, GROUP_ROWS, array.shape[1])
        array = jnp.pad(array, ((0, 0), (0, BLOCK - GROUP_ROWS), (0, 0)), constant_values=value)
        return array.reshape(rows_pad, array.shape[2])

    def cut_rows(array):
        return array.reshape(groups, BLOCK, width)[:, :GROUP_ROWS].reshape(rows_dev, width)

    norms = jnp.stack([norm1_gain, norm1_shift, norm2_gain, norm2_shift], axis=1)
    shard = jnp.concatenate(
        [
            qkv_weight,
            out_weight,
            jnp.pad(router_weight, ((0, 0), (0, NORM_LANE - experts))),
            jnp.pad(norms, ((0, 0), (0, LANES - NORM_LANE - 4))),
        ],
        axis=1,
    )
    params = lax.all_gather(shard, "fsdp", axis=0, tiled=True)
    up_full = lax.all_gather(expert_up, "fsdp", axis=1, tiled=True)
    down_full = lax.all_gather(expert_down, "fsdp", axis=1, tiled=True)

    x = pad_rows(inputs)
    cot = pad_rows(cotangent)
    targets = jnp.where(slots >= 0, routes * capacity + slots, -1)
    meta = pad_rows(jnp.concatenate([targets, routes], axis=1), -1)
    meta_row = jnp.transpose(meta)

    vmem = pl.BlockSpec(memory_space=pltpu.VMEM)
    shape = jax.ShapeDtypeStruct
    params_spec = pltpu.CompilerParams(vmem_limit_bytes=VMEM_LIMIT)
    saved = pl.pallas_call(
        functools.partial(forward_kernel, experts),
        out_shape=(
            shape((rows_pad, width), BF16),
            shape((rows_pad, 3 * width), BF16),
            shape((groups, HEADS, BLOCK, BLOCK), BF16),
            shape((rows_pad, width), BF16),
            shape((rows_pad, width), F32),
            shape((rows_pad, width), BF16),
            shape((rows_pad, LANES), F32),
            shape((experts, capacity, width), BF16),
            shape((experts, capacity, width), BF16),
            shape((experts, capacity, width), BF16),
        ),
        in_specs=[vmem] * 5,
        out_specs=[vmem] * 10,
        scratch_shapes=[pltpu.VMEM((BLOCK, BLOCK), F32), pltpu.VMEM((8, rows_pad), F32)],
        compiler_params=params_spec,
        name="attention_forward",
    )(x, cot, meta, meta_row, params)
    act_one, triple, weights, attended, mid, act_two, probs, sent, grad_sent, cot_slots = saved

    arrived = lax.all_to_all(sent, "expert", split_axis=0, concat_axis=1, tiled=True)
    grad_arrived = lax.all_to_all(grad_sent, "expert", split_axis=0, concat_axis=1, tiled=True)
    expert_rows = peers * capacity
    hidden_width = up_full.shape[2]

    def block(*dims):
        return pl.BlockSpec((1, *dims), lambda e: (e, 0, 0))

    back, grad_rows, up_part, down_part = pl.pallas_call(
        expert_kernel,
        grid=(held,),
        out_shape=(
            shape((held, expert_rows, width), BF16),
            shape((held, expert_rows, width), BF16),
            shape((held, width, hidden_width), BF16),
            shape((held, hidden_width, width), BF16),
        ),
        in_specs=[block(expert_rows, width)] * 2 + [block(width, hidden_width), block(hidden_width, width)],
        out_specs=[block(expert_rows, width)] * 2 + [block(width, hidden_width), block(hidden_width, width)],
        scratch_shapes=[pltpu.VMEM((expert_rows, width), F32)] * 2,
        compiler_params=params_spec,
        name="experts",
    )(arrived, grad_arrived, up_full, down_full)

    returned = lax.all_to_all(back, "expert", split_axis=1, concat_axis=0, tiled=True)
    grad_returned = lax.all_to_all(grad_rows, "expert", split_axis=1, concat_axis=0, tiled=True)
    up_grad = lax.psum_scatter(up_part, "fsdp", scatter_dimension=1, tiled=True).astype(F32)
    down_grad = lax.psum_scatter(down_part, "fsdp", scatter_dimension=1, tiled=True).astype(F32)

    def flat(array):
        array = array.reshape(experts * capacity, width)
        return jnp.pad(array, ((0, places - experts * capacity), (0, 0)))

    out, input_grad, params_grad = pl.pallas_call(
        functools.partial(backward_kernel, experts),
        out_shape=(
            shape((rows_pad, width), BF16),
            shape((rows_pad, width), F32),
            shape((width, 4 * width + LANES), BF16),
        ),
        in_specs=[vmem] * 14,
        out_specs=[vmem] * 3,
        scratch_shapes=[
            pltpu.VMEM((8, places), F32),
            pltpu.VMEM((BLOCK, places), BF16),
            pltpu.VMEM((BLOCK, places), BF16),
            pltpu.VMEM((rows_pad, width), BF16),
            pltpu.VMEM((rows_pad, 3 * width), BF16),
            pltpu.VMEM((rows_pad, LANES), BF16),
            pltpu.VMEM((LANES, width), F32),
        ],
        compiler_params=params_spec,
        name="attention_backward",
    )(
        x, cot, meta, params, act_one, triple, weights, attended, mid, act_two, probs,
        flat(returned), flat(grad_returned), flat(cot_slots),
    )
    share = lax.psum_scatter(params_grad, "fsdp", scatter_dimension=0, tiled=True)
    share = lax.psum(share, "expert").astype(F32)
    norm_share = share[:, 4 * width + NORM_LANE : 4 * width + NORM_LANE + 4]
    return (
        cut_rows(out),
        cut_rows(input_grad),
        share[:, : 3 * width],
        share[:, 3 * width : 4 * width],
        share[:, 4 * width : 4 * width + experts],
        norm_share[:, 0],
        norm_share[:, 1],
        norm_share[:, 2],
        norm_share[:, 3],
        up_grad,
        down_grad,
    )


def solution(mesh):
    tokens = P(("expert", "fsdp"), None)
    rows, vector, expert = P("fsdp", None), P("fsdp"), P("expert", "fsdp", None)
    return jax.shard_map(
        on_device,
        mesh=mesh,
        in_specs=(tokens,) * 4 + (rows,) * 3 + (vector,) * 4 + (expert,) * 2,
        out_specs=(tokens,) * 2 + (rows,) * 3 + (vector,) * 4 + (expert,) * 2,
        check_vma=False,
    )
```

```python
import functools

import jax
import jax.numpy as jnp
from jax import lax
from jax.experimental import pallas as pl
from jax.experimental.pallas import tpu as pltpu
from jax.sharding import PartitionSpec as P

HEADS = 8
HEAD_DIM = 64
PATCHES = 49
EPS = 1e-06
ROOT_HALF = 0.7071067811865476
DENSITY_SCALE = 0.3989422804014327

BLOCK = 256
GROUP_IMAGES = BLOCK // PATCHES
GROUP_ROWS = GROUP_IMAGES * PATCHES
LANES = 128
NORM_LANE = 64
FF_CHUNK = 512
VMEM_LIMIT = 60 * 1024 * 1024

MESH = pl.DeviceIdType.MESH
F32 = jnp.float32
BF16 = jnp.bfloat16


def dot(left, right):
    return lax.dot_general(left, right, (((1,), (0,)), ((), ())), preferred_element_type=F32)


def dot_rows(left, right):
    return lax.dot_general(left, right, (((0,), (0,)), ((), ())), preferred_element_type=F32)


def dot_against(left, right):
    return lax.dot_general(left, right, (((1,), (1,)), ((), ())), preferred_element_type=F32)


def iota(shape, dim):
    return lax.broadcasted_iota(jnp.int32, shape, dim)


def normalize(values):
    center = jnp.mean(values, axis=-1, keepdims=True)
    offset = values - center
    spread = jnp.mean(offset * offset, axis=-1, keepdims=True)
    inverse = lax.rsqrt(spread + EPS)
    return offset * inverse, inverse


def denormalize(upstream, normed, inverse, gain):
    scaled = upstream * gain
    return inverse * (
        scaled
        - jnp.mean(scaled, axis=-1, keepdims=True)
        - normed * jnp.mean(scaled * normed, axis=-1, keepdims=True)
    )


def to_row(column):
    n = column.shape[0]
    parts = []
    for at in range(0, n, LANES):
        eye = iota((LANES, LANES), 0) == iota((LANES, LANES), 1)
        parts.append(jnp.sum(jnp.where(eye, column[at : at + LANES], 0.0), axis=0, keepdims=True))
    return parts[0] if len(parts) == 1 else jnp.concatenate(parts, axis=1)


def rows_of(g):
    return pl.ds(pl.multiple_of(g * BLOCK, BLOCK), BLOCK)


def gates_of(probs, meta):
    lane = iota(probs.shape, 1)
    first = jnp.sum(jnp.where(lane == meta[:, 2:3], probs, 0.0), axis=1, keepdims=True)
    second = jnp.sum(jnp.where(lane == meta[:, 3:4], probs, 0.0), axis=1, keepdims=True)
    return first, second


class Place:
    def __init__(self, fsdp):
        self.count = fsdp
        self.A, self.B = 4, fsdp // 8
        self.x = lax.axis_index("expert")
        self.me = lax.axis_index("fsdp")
        self.c = lax.rem(self.me, 2)
        line = lax.div(self.me, 2)
        self.b = lax.rem(line, self.B)
        self.a = lax.div(line, self.B)

    def index(self, a, b, c):
        return (a * self.B + b) * 2 + c

    def other_b(self, j):
        return lax.rem(self.b + 1 + j, self.B)

    def at(self, a, b, c):
        return (self.x, self.index(a, b, c))


def greet(place, peers, line_only):
    barrier = pltpu.get_barrier_semaphore()

    def signal(device):
        pl.semaphore_signal(barrier, inc=1, device_id=device, device_id_type=MESH)

    if line_only:
        pl.when(place.a > 0)(lambda: signal(place.at(place.a - 1, place.b, place.c)))
        pl.when(place.a < place.A - 1)(lambda: signal(place.at(place.a + 1, place.b, place.c)))
        line = jnp.where(place.a > 0, 1, 0) + jnp.where(place.a < place.A - 1, 1, 0)
    else:
        for k in range(1, place.A):
            signal(place.at(lax.rem(place.a + k, place.A), place.b, place.c))
        line = place.A - 1
    for j in range(place.B - 1):
        signal(place.at(place.a, place.other_b(j), place.c))
    signal(place.at(place.a, place.b, 1 - place.c))
    for k in range(1, peers):
        signal((lax.rem(place.x + k, peers), place.me))
    pl.semaphore_wait(barrier, line + place.B - 1 + 1 + peers - 1)


class Gather:
    RIGHT, LEFT, CORE, ACROSS = 0, 1, 2, 3

    def __init__(self, place, own, full, block, send_sem, recv_sem, local_sem):
        self.place, self.own, self.full, self.block = place, own, full, block
        self.send_sem, self.recv_sem, self.local_sem = send_sem, recv_sem, local_sem

    def copy(self, shard, route, source, a, b, c):
        return pltpu.make_async_remote_copy(
            src_ref=source, dst_ref=self.block(self.full, shard),
            send_sem=self.send_sem.at[shard, route], recv_sem=self.recv_sem.at[shard],
            device_id=self.place.at(a, b, c), device_id_type=MESH,
        )

    def onward(self, shard, source, right, left, across, act):
        p = self.place
        if right is not None:
            pl.when(right)(lambda: act(self.copy(shard, self.RIGHT, source, p.a + 1, p.b, p.c)))
        if left is not None:
            pl.when(left)(lambda: act(self.copy(shard, self.LEFT, source, p.a - 1, p.b, p.c)))
        if across:
            for j in range(p.B - 1):
                act(self.copy(shard, self.ACROSS + j, source, p.a, p.other_b(j), p.c))
        act(self.copy(shard, self.CORE, source, p.a, p.b, 1 - p.c))

    def local(self):
        return pltpu.make_async_copy(self.own, self.block(self.full, self.place.me), self.local_sem)

    def start(self):
        p = self.place
        self.local().start()
        self.onward(p.me, self.own, p.a < p.A - 1, p.a > 0, True, lambda copy: copy.start())

    def arrived(self, shard):
        p = self.place
        self.copy(shard, self.CORE, self.block(self.full, shard), p.a, p.b, 1 - p.c).wait_recv()

    def line_step(self, k):
        p = self.place

        def from_left():
            shard = p.index(p.a - k, p.b, p.c)
            self.arrived(shard)
            self.onward(shard, self.block(self.full, shard), p.a < p.A - 1, None, True, lambda copy: copy.start())

        def from_right():
            shard = p.index(p.a + k, p.b, p.c)
            self.arrived(shard)
            self.onward(shard, self.block(self.full, shard), None, p.a > 0, True, lambda copy: copy.start())

        pl.when(p.a - k >= 0)(from_left)
        pl.when(p.a + k < p.A)(from_right)

    def across_step(self, k):
        p = self.place

        def row(a):
            for j in range(p.B - 1):
                shard = p.index(a, p.other_b(j), p.c)
                self.arrived(shard)
                self.onward(shard, self.block(self.full, shard), None, None, False, lambda copy: copy.start())

        if k == 0:
            row(p.a)
        else:
            pl.when(p.a - k >= 0)(lambda: row(p.a - k))
            pl.when(p.a + k < p.A)(lambda: row(p.a + k))

    def finish_recv(self):
        p = self.place
        self.local().wait()
        for a in range(p.A):
            for b in range(p.B):
                self.arrived(p.index(a, b, 1 - p.c))

    def finish_send(self):
        p = self.place
        wait = lambda copy: copy.wait_send()
        self.onward(p.me, self.own, p.a < p.A - 1, p.a > 0, True, wait)
        for k in range(1, p.A):

            def from_left(k=k):
                shard = p.index(p.a - k, p.b, p.c)
                self.onward(shard, self.block(self.full, shard), p.a < p.A - 1, None, True, wait)

            def from_right(k=k):
                shard = p.index(p.a + k, p.b, p.c)
                self.onward(shard, self.block(self.full, shard), None, p.a > 0, True, wait)

            pl.when(p.a - k >= 0)(from_left)
            pl.when(p.a + k < p.A)(from_right)
        for a in range(p.A):
            for j in range(p.B - 1):
                shard = p.index(a, p.other_b(j), p.c)
                self.onward(shard, self.block(self.full, shard), None, None, False, wait)


def forward_kernel(
    experts, fsdp, peers,
    x_ref, cot_ref, meta_ref, meta_row_ref, shard_ref, up_ref, down_ref,
    act_one_out, triple_out, weights_out, attended_out, mid_out, act_two_out, probs_out,
    arrived_out, grad_arrived_out, cot_sent_out, params_out, up_full, down_full,
    params_ref, act_one_ref, triple_ref, weights_ref, attended_ref, mid_ref, act_two_ref, probs_ref,
    sent_ref, grad_sent_ref, cot_sent_ref, bias_ref, gate_rows_ref,
    send_sem, recv_sem, local_sem, save_sem, swap_send, swap_recv, swap_local, tail_sem,
):
    width = x_ref.shape[1]
    groups = x_ref.shape[0] // BLOCK
    held = experts // peers
    place = Place(fsdp)
    greet(place, peers, True)

    def rows_block(ref, shard):
        size = shard_ref.shape[0]
        return ref.at[pl.ds(pl.multiple_of(shard * size, size), size), :]

    def middle_block(size):
        return lambda ref, shard: ref.at[:, pl.ds(pl.multiple_of(shard * size, size), size), :]

    gathers = [
        Gather(place, own, full, block, send_sem.at[i], recv_sem.at[i], local_sem.at[i])
        for i, (own, full, block) in enumerate(
            (
                (shard_ref, params_ref, rows_block),
                (up_ref, up_full, middle_block(up_ref.shape[1])),
                (down_ref, down_full, middle_block(down_ref.shape[1])),
            )
        )
    ]
    params, up, down = gathers
    params.start()
    image_row = iota((BLOCK, BLOCK), 0) // PATCHES
    image_col = iota((BLOCK, BLOCK), 1) // PATCHES
    bias_ref[...] = jnp.where(image_row == image_col, 0.0, -1e30)
    for k in range(1, place.A):
        params.line_step(k)
        params.across_step(k - 1)
    up.start()
    down.start()
    params.across_step(place.A - 1)
    params.finish_recv()
    params_copy = pltpu.make_async_copy(params_ref, params_out, tail_sem.at[0])
    params_copy.start()

    events = []
    for k in range(1, place.A):
        for gather in (up, down):
            events.append(functools.partial(gather.line_step, k))
            events.append(functools.partial(gather.across_step, k - 1))
    for gather in (up, down):
        events.append(functools.partial(gather.across_step, place.A - 1))

    small = params_ref[:, 4 * width :]
    small_rows = jnp.transpose(small.astype(F32))

    def saves(g):
        rows = rows_of(g)
        pairs = (
            (act_one_ref, act_one_out), (triple_ref, triple_out), (weights_ref, weights_out), (attended_ref, attended_out),
            (mid_ref, mid_out), (act_two_ref, act_two_out), (probs_ref, probs_out),
        )
        return [
            pltpu.make_async_copy(here.at[rows, :], there.at[rows, :], save_sem.at[i, g])
            for i, (here, there) in enumerate(pairs)
        ]

    @pl.loop(0, groups)
    def _(g):
        rows = rows_of(g)
        x = x_ref[rows, :].astype(F32)
        normed, _ = normalize(x)
        act = (normed * small_rows[NORM_LANE : NORM_LANE + 1] + small_rows[NORM_LANE + 1 : NORM_LANE + 2]).astype(BF16)
        act_one_ref[rows, :] = act
        triple_ref[rows, :] = dot(act, params_ref[:, : 3 * width]).astype(BF16)
        low = iota((BLOCK, LANES), 1) < HEAD_DIM
        for pair in range(HEADS // 2):
            at = pair * LANES
            q = triple_ref[rows, at : at + LANES] * HEAD_DIM ** (-0.5)
            k = triple_ref[rows, width + at : width + at + LANES]
            v = triple_ref[rows, 2 * width + at : 2 * width + at + LANES]
            total = None
            for half in range(2):
                mask = low if half == 0 else jnp.logical_not(low)
                scores = dot_against(jnp.where(mask, q, 0.0).astype(BF16), k) + bias_ref[...]
                top = jnp.max(scores, axis=-1, keepdims=True)
                raised = jnp.exp(scores - top)
                probs = raised / jnp.sum(raised, axis=-1, keepdims=True)
                probs = probs.astype(BF16)
                head = (2 * pair + half) * BLOCK
                weights_ref[rows, head : head + BLOCK] = probs
                part = dot(probs, jnp.where(mask, v, 0.0).astype(BF16))
                total = part if total is None else total + part
            attended_ref[rows, at : at + LANES] = total.astype(BF16)
        mid = x + dot(attended_ref[rows, :], params_ref[:, 3 * width : 4 * width])
        mid_ref[rows, :] = mid
        normed, _ = normalize(mid)
        act = (normed * small_rows[NORM_LANE + 2 : NORM_LANE + 3] + small_rows[NORM_LANE + 3 : NORM_LANE + 4]).astype(BF16)
        act_two_ref[rows, :] = act
        logits = jnp.where(iota((BLOCK, LANES), 1) < experts, dot(act, small), -1e30)
        raised = jnp.exp(logits - jnp.max(logits, axis=-1, keepdims=True))
        probs = raised / jnp.sum(raised, axis=-1, keepdims=True)
        probs_ref[rows, :] = probs
        first, second = gates_of(probs, meta_ref[rows, :])
        gate_rows_ref[0:1, rows] = to_row(first)
        gate_rows_ref[1:2, rows] = to_row(second)
        for copy in saves(g):
            copy.start()
        for i in range(2):
            pl.when(g == 2 * i + 1)(events[2 * i])
            pl.when(g == 2 * i + 1)(events[2 * i + 1])

    capacity = sent_ref.shape[1]

    def swaps(e):
        owner, slot = lax.div(e, held), lax.rem(e, held)
        out = []
        for i, (here, there) in enumerate(((sent_ref, arrived_out), (grad_sent_ref, grad_arrived_out))):
            far = pltpu.make_async_remote_copy(
                src_ref=here.at[e], dst_ref=there.at[slot, place.x],
                send_sem=swap_send.at[i, e], recv_sem=swap_recv.at[i, slot, place.x],
                device_id=(owner, place.me), device_id_type=MESH,
            )
            near = pltpu.make_async_copy(here.at[e], there.at[slot, place.x], swap_local.at[i, slot])
            out.append((far, near))
        return owner != place.x, out

    @pl.loop(0, experts)
    def _(i):
        e = lax.rem((place.x + 1) * held + i, experts)
        slot = iota((capacity, x_ref.shape[0]), 0) + e * capacity
        in_first = slot == meta_row_ref[0:1, :]
        in_second = slot == meta_row_ref[1:2, :]
        picks = jnp.where(jnp.logical_or(in_first, in_second), 1.0, 0.0).astype(BF16)
        gate = jnp.sum(
            jnp.where(in_first, gate_rows_ref[0:1, :], jnp.where(in_second, gate_rows_ref[1:2, :], 0.0)),
            axis=1, keepdims=True,
        )
        sent_ref[e] = dot(picks, act_two_ref[...]).astype(BF16)
        cot_slots = dot(picks, cot_ref[...])
        cot_sent_ref[e] = cot_slots.astype(BF16)
        grad_sent_ref[e] = (gate * cot_slots).astype(BF16)
        away, copies = swaps(e)
        for far, near in copies:
            pl.when(away)(far.start)
            pl.when(jnp.logical_not(away))(near.start)

    cot_copy = pltpu.make_async_copy(cot_sent_ref, cot_sent_out, tail_sem.at[1])
    cot_copy.start()
    for event in events[4:]:
        event()
    for gather in (up, down):
        gather.finish_recv()

    @pl.loop(0, groups)
    def _(g):
        for copy in saves(g):
            copy.wait()

    params_copy.wait()
    cot_copy.wait()

    @pl.loop(0, experts)
    def _(e):
        away, copies = swaps(e)
        for far, near in copies:
            pl.when(away)(far.wait_send)
            pl.when(jnp.logical_not(away))(near.wait)

    for i, there in enumerate((arrived_out, grad_arrived_out)):
        for slot in range(held):
            for k in range(1, peers):
                other = lax.rem(place.x + k, peers)
                pltpu.make_async_remote_copy(
                    src_ref=there.at[slot, other], dst_ref=there.at[slot, other],
                    send_sem=swap_send.at[i, 0], recv_sem=swap_recv.at[i, slot, other],
                    device_id=(other, place.me), device_id_type=MESH,
                ).wait_recv()
    for gather in gathers:
        gather.finish_send()


def expert_kernel(rows_ref, grad_ref, up_ref, down_ref, back_ref, grad_rows_ref, up_part_ref, down_part_ref, back_sum, grad_sum):
    hidden_width = up_ref.shape[2]
    chunks = hidden_width // FF_CHUNK
    back_sum[...] = jnp.zeros_like(back_sum)
    grad_sum[...] = jnp.zeros_like(grad_sum)

    @pl.loop(0, chunks)
    def _(f):
        at = pl.ds(pl.multiple_of(f * FF_CHUNK, FF_CHUNK), FF_CHUNK)
        rows, grads = rows_ref[0], grad_ref[0]
        up, down = up_ref[0, :, at], down_ref[0, at, :]
        hidden = dot(rows, up)
        spread = 0.5 * (1.0 + lax.erf(hidden * ROOT_HALF))
        active = (hidden * spread).astype(BF16)
        slope = spread + hidden * (DENSITY_SCALE * jnp.exp(-0.5 * hidden * hidden))
        back_sum[...] += dot(active, down)
        grad_hidden = (dot_against(grads, down) * slope).astype(BF16)
        grad_sum[...] += dot_against(grad_hidden, up)
        up_part_ref[0, :, at] = dot_rows(rows, grad_hidden).astype(BF16)
        down_part_ref[0, at, :] = dot_rows(active, grads).astype(BF16)

    back_ref[0] = back_sum[...].astype(BF16)
    grad_rows_ref[0] = grad_sum[...].astype(BF16)


def backward_kernel(
    experts,
    x_ref, cot_ref, meta_ref, params_ref, act_one_ref, triple_ref, weights_ref, attended_ref, mid_ref, act_two_ref,
    probs_ref, back_ref, grad_slots_ref, cot_slots_ref,
    out_ref, input_grad_ref, params_grad_ref,
    dot_row_ref, place_ref, gated_ref, branch_ref, grad_triple_ref, logit_grad_ref, sums_ref,
):
    width = x_ref.shape[1]
    groups = x_ref.shape[0] // BLOCK
    places = back_ref.shape[0]
    small = params_ref[:, 4 * width :]
    small_rows = jnp.transpose(small.astype(F32))
    gain_one = small_rows[NORM_LANE : NORM_LANE + 1]
    gain_two = small_rows[NORM_LANE + 2 : NORM_LANE + 3]
    sums_ref[...] = jnp.zeros_like(sums_ref)

    @pl.loop(0, places // LANES)
    def _(c):
        at = pl.ds(pl.multiple_of(c * LANES, LANES), LANES)
        column = jnp.sum(back_ref[at, :].astype(F32) * cot_slots_ref[at, :].astype(F32), axis=1, keepdims=True)
        dot_row_ref[0:1, at] = to_row(column)

    @pl.loop(0, groups)
    def _(g):
        rows = rows_of(g)
        meta = meta_ref[rows, :]
        probs = probs_ref[rows, :]
        gate_first, gate_second = gates_of(probs, meta)
        lane = iota((BLOCK, LANES), 1)
        grad_first = jnp.zeros((BLOCK, LANES), F32)
        grad_second = jnp.zeros((BLOCK, LANES), F32)
        for c in range(places // LANES):
            at = c * LANES
            in_first = lane == meta[:, 0:1] - at
            in_second = lane == meta[:, 1:2] - at
            place_ref[:, at : at + LANES] = jnp.where(jnp.logical_or(in_first, in_second), 1.0, 0.0).astype(BF16)
            gated_ref[:, at : at + LANES] = jnp.where(in_first, gate_first, jnp.where(in_second, gate_second, 0.0)).astype(BF16)
            dots = dot_row_ref[0:1, at : at + LANES]
            grad_first += jnp.where(in_first, dots, 0.0)
            grad_second += jnp.where(in_second, dots, 0.0)
        grad_first = jnp.sum(grad_first, axis=1, keepdims=True)
        grad_second = jnp.sum(grad_second, axis=1, keepdims=True)
        mid = mid_ref[rows, :]
        out_ref[rows, :] = (mid + dot(gated_ref[...], back_ref[...])).astype(BF16)
        grad_probs = jnp.where(lane == meta[:, 2:3], grad_first, 0.0) + jnp.where(lane == meta[:, 3:4], grad_second, 0.0)
        grad_logits = (probs * (grad_probs - jnp.sum(grad_probs * probs, axis=-1, keepdims=True))).astype(BF16)
        logit_grad_ref[rows, :] = grad_logits
        grad_act = dot(place_ref[...], grad_slots_ref[...]) + dot_against(grad_logits, small)
        normed, inverse = normalize(mid)
        sums_ref[NORM_LANE + 2 : NORM_LANE + 3, :] += jnp.sum(grad_act * normed, axis=0, keepdims=True)
        sums_ref[NORM_LANE + 3 : NORM_LANE + 4, :] += jnp.sum(grad_act, axis=0, keepdims=True)
        grad_mid = cot_ref[rows, :].astype(F32) + denormalize(grad_act, normed, inverse, gain_two)
        input_grad_ref[rows, :] = grad_mid
        branch = grad_mid.astype(BF16)
        branch_ref[rows, :] = branch
        grad_attended = dot_against(branch, params_ref[:, 3 * width : 4 * width]).astype(BF16)
        low = lane < HEAD_DIM
        for pair in range(HEADS // 2):
            at = pair * LANES
            q = triple_ref[rows, at : at + LANES] * HEAD_DIM ** (-0.5)
            k = triple_ref[rows, width + at : width + at + LANES]
            v = triple_ref[rows, 2 * width + at : 2 * width + at + LANES]
            upstream = grad_attended[:, at : at + LANES]
            grad_q = grad_k = grad_v = jnp.zeros((BLOCK, LANES), F32)
            for half in range(2):
                mask = low if half == 0 else jnp.logical_not(low)
                upstream_half = jnp.where(mask, upstream, 0.0).astype(BF16)
                head = (2 * pair + half) * BLOCK
                weights = weights_ref[rows, head : head + BLOCK]
                kept = weights.astype(F32)
                grad_weights = dot_against(upstream_half, v)
                inner = jnp.sum(grad_weights * kept, axis=-1, keepdims=True)
                grad_scores = (kept * (grad_weights - inner)).astype(BF16)
                grad_q += dot(grad_scores, jnp.where(mask, k, 0.0).astype(BF16))
                grad_k += dot_rows(grad_scores, jnp.where(mask, q, 0.0).astype(BF16))
                grad_v += dot_rows(weights, upstream_half)
            grad_triple_ref[rows, at : at + LANES] = (grad_q * HEAD_DIM ** (-0.5)).astype(BF16)
            grad_triple_ref[rows, width + at : width + at + LANES] = grad_k.astype(BF16)
            grad_triple_ref[rows, 2 * width + at : 2 * width + at + LANES] = grad_v.astype(BF16)
        grad_act = dot_against(grad_triple_ref[rows, :], params_ref[:, : 3 * width])
        normed, inverse = normalize(x_ref[rows, :].astype(F32))
        sums_ref[NORM_LANE : NORM_LANE + 1, :] += jnp.sum(grad_act * normed, axis=0, keepdims=True)
        sums_ref[NORM_LANE + 1 : NORM_LANE + 2, :] += jnp.sum(grad_act, axis=0, keepdims=True)
        input_grad_ref[rows, :] += denormalize(grad_act, normed, inverse, gain_one)

    params_grad_ref[:, : 3 * width] = dot_rows(act_one_ref[...], grad_triple_ref[...]).astype(BF16)
    params_grad_ref[:, 3 * width : 4 * width] = dot_rows(attended_ref[...], branch_ref[...]).astype(BF16)
    router_part = dot_rows(act_two_ref[...], logit_grad_ref[...])
    norm_part = jnp.transpose(sums_ref[...])
    params_grad_ref[:, 4 * width :] = (router_part + norm_part).astype(BF16)


def on_device(
    inputs, cotangent, routes, slots, qkv_weight, out_weight, router_weight,
    norm1_gain, norm1_shift, norm2_gain, norm2_shift, expert_up, expert_down,
):
    rows_dev, width = inputs.shape
    groups = rows_dev // GROUP_ROWS
    rows_pad = groups * BLOCK
    fsdp = lax.axis_size("fsdp")
    peers = lax.axis_size("expert")
    held = expert_up.shape[0]
    experts = held * peers
    capacity = (42 * rows_dev + 20 * experts - 1) // (20 * experts)
    capacity = -(-capacity // 16) * 16
    places = -(-experts * capacity // LANES) * LANES

    def pad_rows(array, value=0):
        array = array.reshape(groups, GROUP_ROWS, array.shape[1])
        array = jnp.pad(array, ((0, 0), (0, BLOCK - GROUP_ROWS), (0, 0)), constant_values=value)
        return array.reshape(rows_pad, array.shape[2])

    def cut_rows(array):
        return array.reshape(groups, BLOCK, width)[:, :GROUP_ROWS].reshape(rows_dev, width)

    norms = jnp.stack([norm1_gain, norm1_shift, norm2_gain, norm2_shift], axis=1)
    shard = jnp.concatenate(
        [
            qkv_weight,
            out_weight,
            jnp.pad(router_weight, ((0, 0), (0, NORM_LANE - experts))),
            jnp.pad(norms, ((0, 0), (0, LANES - NORM_LANE - 4))),
        ],
        axis=1,
    )
    x = pad_rows(inputs)
    cot = pad_rows(cotangent)
    targets = jnp.where(slots >= 0, routes * capacity + slots, -1)
    meta = pad_rows(jnp.concatenate([targets, routes], axis=1), -1)
    meta_row = jnp.transpose(meta)

    vmem = pl.BlockSpec(memory_space=pltpu.VMEM)
    hbm = pl.BlockSpec(memory_space=pl.ANY)
    shape = jax.ShapeDtypeStruct
    params_spec = pltpu.CompilerParams(vmem_limit_bytes=VMEM_LIMIT)
    kept = (
        shape((rows_pad, width), BF16),
        shape((rows_pad, 3 * width), BF16),
        shape((rows_pad, HEADS * BLOCK), BF16),
        shape((rows_pad, width), BF16),
        shape((rows_pad, width), F32),
        shape((rows_pad, width), BF16),
        shape((rows_pad, LANES), F32),
    )
    slots_shape = shape((experts, capacity, width), BF16)
    arrived_shape = shape((held, peers, capacity, width), BF16)
    packed = (fsdp * shard.shape[0], shard.shape[1])
    scratch = lambda s: pltpu.VMEM(s.shape, s.dtype)
    dma = pltpu.SemaphoreType.DMA
    saved = pl.pallas_call(
        functools.partial(forward_kernel, experts, fsdp, peers),
        out_shape=(
            *kept, arrived_shape, arrived_shape, slots_shape, shape(packed, BF16),
            shape((held, fsdp * expert_up.shape[1], expert_up.shape[2]), BF16),
            shape((held, fsdp * expert_down.shape[1], expert_down.shape[2]), BF16),
        ),
        in_specs=[vmem] * 5 + [hbm] * 2,
        out_specs=[hbm] * 13,
        scratch_shapes=[
            pltpu.VMEM(packed, BF16), *map(scratch, kept), *[scratch(slots_shape)] * 3,
            pltpu.VMEM((BLOCK, BLOCK), F32), pltpu.VMEM((8, rows_pad), F32),
            dma((3, fsdp, 3 + fsdp // 8 - 1)), dma((3, fsdp)), dma((3,)), dma((len(kept), groups)),
            dma((2, experts)), dma((2, held, peers)), dma((2, held)), dma((2,)),
        ],
        compiler_params=pltpu.CompilerParams(vmem_limit_bytes=VMEM_LIMIT, collective_id=0, has_side_effects=True),
        name="attention_forward",
    )(x, cot, meta, meta_row, shard, expert_up, expert_down)
    act_one, triple, weights, attended, mid, act_two, probs, arrived, grad_arrived, cot_slots, params, up_full, down_full = saved

    expert_rows = peers * capacity
    arrived = arrived.reshape(held, expert_rows, width)
    grad_arrived = grad_arrived.reshape(held, expert_rows, width)
    hidden_width = up_full.shape[2]

    def block(*dims):
        return pl.BlockSpec((1, *dims), lambda e: (e, 0, 0))

    back, grad_rows, up_part, down_part = pl.pallas_call(
        expert_kernel,
        grid=(held,),
        out_shape=(
            shape((held, expert_rows, width), BF16),
            shape((held, expert_rows, width), BF16),
            shape((held, width, hidden_width), BF16),
            shape((held, hidden_width, width), BF16),
        ),
        in_specs=[block(expert_rows, width)] * 2 + [block(width, hidden_width), block(hidden_width, width)],
        out_specs=[block(expert_rows, width)] * 2 + [block(width, hidden_width), block(hidden_width, width)],
        scratch_shapes=[pltpu.VMEM((expert_rows, width), F32)] * 2,
        compiler_params=params_spec,
        name="experts",
    )(arrived, grad_arrived, up_full, down_full)

    returned = lax.all_to_all(back, "expert", split_axis=1, concat_axis=0, tiled=True)
    grad_returned = lax.all_to_all(grad_rows, "expert", split_axis=1, concat_axis=0, tiled=True)
    up_grad = lax.psum_scatter(up_part, "fsdp", scatter_dimension=1, tiled=True).astype(F32)
    down_grad = lax.psum_scatter(down_part, "fsdp", scatter_dimension=1, tiled=True).astype(F32)

    def flat(array):
        array = array.reshape(experts * capacity, width)
        return jnp.pad(array, ((0, places - experts * capacity), (0, 0)))

    out, input_grad, params_grad = pl.pallas_call(
        functools.partial(backward_kernel, experts),
        out_shape=(
            shape((rows_pad, width), BF16),
            shape((rows_pad, width), F32),
            shape((width, 4 * width + LANES), BF16),
        ),
        in_specs=[vmem] * 14,
        out_specs=[vmem] * 3,
        scratch_shapes=[
            pltpu.VMEM((8, places), F32),
            pltpu.VMEM((BLOCK, places), BF16),
            pltpu.VMEM((BLOCK, places), BF16),
            pltpu.VMEM((rows_pad, width), BF16),
            pltpu.VMEM((rows_pad, 3 * width), BF16),
            pltpu.VMEM((rows_pad, LANES), BF16),
            pltpu.VMEM((LANES, width), F32),
        ],
        compiler_params=params_spec,
        name="attention_backward",
    )(
        x, cot, meta, params, act_one, triple, weights, attended, mid, act_two, probs,
        flat(returned), flat(grad_returned), flat(cot_slots),
    )
    share = lax.psum_scatter(params_grad, "fsdp", scatter_dimension=0, tiled=True)
    share = lax.psum(share, "expert").astype(F32)
    norm_share = share[:, 4 * width + NORM_LANE : 4 * width + NORM_LANE + 4]
    return (
        cut_rows(out),
        cut_rows(input_grad),
        share[:, : 3 * width],
        share[:, 3 * width : 4 * width],
        share[:, 4 * width : 4 * width + experts],
        norm_share[:, 0],
        norm_share[:, 1],
        norm_share[:, 2],
        norm_share[:, 3],
        up_grad,
        down_grad,
    )


def solution(mesh):
    tokens = P(("expert", "fsdp"), None)
    rows, vector, expert = P("fsdp", None), P("fsdp"), P("expert", "fsdp", None)
    return jax.shard_map(
        on_device,
        mesh=mesh,
        in_specs=(tokens,) * 4 + (rows,) * 3 + (vector,) * 4 + (expert,) * 2,
        out_specs=(tokens,) * 2 + (rows,) * 3 + (vector,) * 4 + (expert,) * 2,
        check_vma=False,
    )
```

```python
import functools

import jax
import jax.numpy as jnp
from jax import lax
from jax.experimental import pallas as pl
from jax.experimental.pallas import tpu as pltpu
from jax.sharding import PartitionSpec as P

HEADS = 8
HEAD_DIM = 64
PATCHES = 49
EPS = 1e-06
ROOT_HALF = 0.7071067811865476
DENSITY_SCALE = 0.3989422804014327

BLOCK = 256
GROUP_IMAGES = BLOCK // PATCHES
GROUP_ROWS = GROUP_IMAGES * PATCHES
LANES = 128
NORM_LANE = 64
FF_CHUNK = 512
VMEM_LIMIT = 62 * 1024 * 1024

MESH = pl.DeviceIdType.MESH
F32 = jnp.float32
BF16 = jnp.bfloat16


def dot(left, right):
    return lax.dot_general(left, right, (((1,), (0,)), ((), ())), preferred_element_type=F32)


def dot_rows(left, right):
    return lax.dot_general(left, right, (((0,), (0,)), ((), ())), preferred_element_type=F32)


def dot_against(left, right):
    return lax.dot_general(left, right, (((1,), (1,)), ((), ())), preferred_element_type=F32)


def iota(shape, dim):
    return lax.broadcasted_iota(jnp.int32, shape, dim)


def normalize(values):
    center = jnp.mean(values, axis=-1, keepdims=True)
    offset = values - center
    spread = jnp.mean(offset * offset, axis=-1, keepdims=True)
    inverse = lax.rsqrt(spread + EPS)
    return offset * inverse, inverse


def denormalize(upstream, normed, inverse, gain):
    scaled = upstream * gain
    return inverse * (
        scaled
        - jnp.mean(scaled, axis=-1, keepdims=True)
        - normed * jnp.mean(scaled * normed, axis=-1, keepdims=True)
    )


def to_row(column):
    n = column.shape[0]
    parts = []
    for at in range(0, n, LANES):
        eye = iota((LANES, LANES), 0) == iota((LANES, LANES), 1)
        parts.append(jnp.sum(jnp.where(eye, column[at : at + LANES], 0.0), axis=0, keepdims=True))
    return parts[0] if len(parts) == 1 else jnp.concatenate(parts, axis=1)


def rows_of(g):
    return pl.ds(pl.multiple_of(g * BLOCK, BLOCK), BLOCK)


def gates_of(probs, meta):
    lane = iota(probs.shape, 1)
    first = jnp.sum(jnp.where(lane == meta[:, 2:3], probs, 0.0), axis=1, keepdims=True)
    second = jnp.sum(jnp.where(lane == meta[:, 3:4], probs, 0.0), axis=1, keepdims=True)
    return first, second


class Place:
    def __init__(self, fsdp):
        self.count = fsdp
        self.A, self.B = 4, fsdp // 8
        self.x = lax.axis_index("expert")
        self.me = lax.axis_index("fsdp")
        self.c = lax.rem(self.me, 2)
        line = lax.div(self.me, 2)
        self.b = lax.rem(line, self.B)
        self.a = lax.div(line, self.B)

    def index(self, a, b, c):
        return (a * self.B + b) * 2 + c

    def other_b(self, j):
        return lax.rem(self.b + 1 + j, self.B)

    def at(self, a, b, c):
        return (self.x, self.index(a, b, c))


def greet(place, peers, line_only):
    barrier = pltpu.get_barrier_semaphore()

    def signal(device):
        pl.semaphore_signal(barrier, inc=1, device_id=device, device_id_type=MESH)

    if line_only:
        pl.when(place.a > 0)(lambda: signal(place.at(place.a - 1, place.b, place.c)))
        pl.when(place.a < place.A - 1)(lambda: signal(place.at(place.a + 1, place.b, place.c)))
        line = jnp.where(place.a > 0, 1, 0) + jnp.where(place.a < place.A - 1, 1, 0)
    else:
        for k in range(1, place.A):
            signal(place.at(lax.rem(place.a + k, place.A), place.b, place.c))
        line = place.A - 1
    for j in range(place.B - 1):
        signal(place.at(place.a, place.other_b(j), place.c))
    signal(place.at(place.a, place.b, 1 - place.c))
    for k in range(1, peers):
        signal((lax.rem(place.x + k, peers), place.me))
    pl.semaphore_wait(barrier, line + place.B - 1 + 1 + peers - 1)


class Gather:
    RIGHT, LEFT, CORE, ACROSS = 0, 1, 2, 3

    def __init__(self, place, own, full, block, send_sem, recv_sem, local_sem):
        self.place, self.own, self.full, self.block = place, own, full, block
        self.send_sem, self.recv_sem, self.local_sem = send_sem, recv_sem, local_sem

    def copy(self, shard, route, source, a, b, c):
        return pltpu.make_async_remote_copy(
            src_ref=source, dst_ref=self.block(self.full, shard),
            send_sem=self.send_sem.at[shard, route], recv_sem=self.recv_sem.at[shard],
            device_id=self.place.at(a, b, c), device_id_type=MESH,
        )

    def onward(self, shard, source, right, left, across, act):
        p = self.place
        if right is not None:
            pl.when(right)(lambda: act(self.copy(shard, self.RIGHT, source, p.a + 1, p.b, p.c)))
        if left is not None:
            pl.when(left)(lambda: act(self.copy(shard, self.LEFT, source, p.a - 1, p.b, p.c)))
        if across:
            for j in range(p.B - 1):
                act(self.copy(shard, self.ACROSS + j, source, p.a, p.other_b(j), p.c))
        act(self.copy(shard, self.CORE, source, p.a, p.b, 1 - p.c))

    def local(self):
        return pltpu.make_async_copy(self.own, self.block(self.full, self.place.me), self.local_sem)

    def start(self):
        p = self.place
        self.local().start()
        self.onward(p.me, self.own, p.a < p.A - 1, p.a > 0, True, lambda copy: copy.start())

    def arrived(self, shard):
        p = self.place
        self.copy(shard, self.CORE, self.block(self.full, shard), p.a, p.b, 1 - p.c).wait_recv()

    def line_step(self, k):
        p = self.place

        def from_left():
            shard = p.index(p.a - k, p.b, p.c)
            self.arrived(shard)
            self.onward(shard, self.block(self.full, shard), p.a < p.A - 1, None, True, lambda copy: copy.start())

        def from_right():
            shard = p.index(p.a + k, p.b, p.c)
            self.arrived(shard)
            self.onward(shard, self.block(self.full, shard), None, p.a > 0, True, lambda copy: copy.start())

        pl.when(p.a - k >= 0)(from_left)
        pl.when(p.a + k < p.A)(from_right)

    def across_step(self, k):
        p = self.place

        def row(a):
            for j in range(p.B - 1):
                shard = p.index(a, p.other_b(j), p.c)
                self.arrived(shard)
                self.onward(shard, self.block(self.full, shard), None, None, False, lambda copy: copy.start())

        if k == 0:
            row(p.a)
        else:
            pl.when(p.a - k >= 0)(lambda: row(p.a - k))
            pl.when(p.a + k < p.A)(lambda: row(p.a + k))

    def finish_recv(self):
        p = self.place
        self.local().wait()
        for a in range(p.A):
            for b in range(p.B):
                self.arrived(p.index(a, b, 1 - p.c))

    def finish_send(self):
        p = self.place
        wait = lambda copy: copy.wait_send()
        self.onward(p.me, self.own, p.a < p.A - 1, p.a > 0, True, wait)
        for k in range(1, p.A):

            def from_left(k=k):
                shard = p.index(p.a - k, p.b, p.c)
                self.onward(shard, self.block(self.full, shard), p.a < p.A - 1, None, True, wait)

            def from_right(k=k):
                shard = p.index(p.a + k, p.b, p.c)
                self.onward(shard, self.block(self.full, shard), None, p.a > 0, True, wait)

            pl.when(p.a - k >= 0)(from_left)
            pl.when(p.a + k < p.A)(from_right)
        for a in range(p.A):
            for j in range(p.B - 1):
                shard = p.index(a, p.other_b(j), p.c)
                self.onward(shard, self.block(self.full, shard), None, None, False, wait)


def forward_kernel(
    experts, fsdp, peers,
    x_ref, cot_ref, meta_ref, meta_row_ref, shard_ref, up_ref, down_ref,
    act_one_out, triple_out, weights_out, attended_out, mid_out, act_two_out, probs_out,
    arrived_out, grad_arrived_out, cot_sent_out, params_out, up_full, down_full,
    params_ref, act_one_ref, triple_ref, weights_ref, attended_ref, mid_ref, act_two_ref, probs_ref,
    sent_ref, grad_sent_ref, cot_sent_ref, bias_ref, gate_rows_ref,
    send_sem, recv_sem, local_sem, save_sem, swap_send, swap_recv, swap_local, tail_sem,
):
    width = x_ref.shape[1]
    groups = x_ref.shape[0] // BLOCK
    held = experts // peers
    place = Place(fsdp)
    greet(place, peers, True)

    def rows_block(ref, shard):
        size = shard_ref.shape[0]
        return ref.at[pl.ds(pl.multiple_of(shard * size, size), size), :]

    def middle_block(size):
        return lambda ref, shard: ref.at[:, pl.ds(pl.multiple_of(shard * size, size), size), :]

    gathers = [
        Gather(place, own, full, block, send_sem.at[i], recv_sem.at[i], local_sem.at[i])
        for i, (own, full, block) in enumerate(
            (
                (shard_ref, params_ref, rows_block),
                (up_ref, up_full, middle_block(up_ref.shape[1])),
                (down_ref, down_full, middle_block(down_ref.shape[1])),
            )
        )
    ]
    params, up, down = gathers
    params.start()
    image_row = iota((BLOCK, BLOCK), 0) // PATCHES
    image_col = iota((BLOCK, BLOCK), 1) // PATCHES
    bias_ref[...] = jnp.where(image_row == image_col, 0.0, -1e30)
    for k in range(1, place.A):
        params.line_step(k)
        params.across_step(k - 1)
    up.start()
    down.start()
    params.across_step(place.A - 1)
    params.finish_recv()
    params_copy = pltpu.make_async_copy(params_ref, params_out, tail_sem.at[0])
    params_copy.start()

    events = []
    for k in range(1, place.A):
        for gather in (up, down):
            events.append(functools.partial(gather.line_step, k))
            events.append(functools.partial(gather.across_step, k - 1))
    for gather in (up, down):
        events.append(functools.partial(gather.across_step, place.A - 1))

    small = params_ref[:, 4 * width :]
    small_rows = jnp.transpose(small.astype(F32))

    def saves(g):
        rows = rows_of(g)
        pairs = (
            (act_one_ref, act_one_out), (triple_ref, triple_out), (weights_ref, weights_out), (attended_ref, attended_out),
            (mid_ref, mid_out), (act_two_ref, act_two_out), (probs_ref, probs_out),
        )
        return [
            pltpu.make_async_copy(here.at[rows, :], there.at[rows, :], save_sem.at[i, g])
            for i, (here, there) in enumerate(pairs)
        ]

    @pl.loop(0, groups)
    def _(g):
        rows = rows_of(g)
        x = x_ref[rows, :].astype(F32)
        normed, _ = normalize(x)
        act = (normed * small_rows[NORM_LANE : NORM_LANE + 1] + small_rows[NORM_LANE + 1 : NORM_LANE + 2]).astype(BF16)
        act_one_ref[rows, :] = act
        triple_ref[rows, :] = dot(act, params_ref[:, : 3 * width]).astype(BF16)
        low = iota((BLOCK, LANES), 1) < HEAD_DIM
        for pair in range(HEADS // 2):
            at = pair * LANES
            q = triple_ref[rows, at : at + LANES] * HEAD_DIM ** (-0.5)
            k = triple_ref[rows, width + at : width + at + LANES]
            v = triple_ref[rows, 2 * width + at : 2 * width + at + LANES]
            total = None
            for half in range(2):
                mask = low if half == 0 else jnp.logical_not(low)
                scores = dot_against(jnp.where(mask, q, 0.0).astype(BF16), k) + bias_ref[...]
                top = jnp.max(scores, axis=-1, keepdims=True)
                raised = jnp.exp(scores - top)
                probs = raised / jnp.sum(raised, axis=-1, keepdims=True)
                probs = probs.astype(BF16)
                head = (2 * pair + half) * BLOCK
                weights_ref[rows, head : head + BLOCK] = probs
                part = dot(probs, jnp.where(mask, v, 0.0).astype(BF16))
                total = part if total is None else total + part
            attended_ref[rows, at : at + LANES] = total.astype(BF16)
        mid = x + dot(attended_ref[rows, :], params_ref[:, 3 * width : 4 * width])
        mid_ref[rows, :] = mid
        normed, _ = normalize(mid)
        act = (normed * small_rows[NORM_LANE + 2 : NORM_LANE + 3] + small_rows[NORM_LANE + 3 : NORM_LANE + 4]).astype(BF16)
        act_two_ref[rows, :] = act
        logits = jnp.where(iota((BLOCK, LANES), 1) < experts, dot(act, small), -1e30)
        raised = jnp.exp(logits - jnp.max(logits, axis=-1, keepdims=True))
        probs = raised / jnp.sum(raised, axis=-1, keepdims=True)
        probs_ref[rows, :] = probs
        first, second = gates_of(probs, meta_ref[rows, :])
        gate_rows_ref[0:1, rows] = to_row(first)
        gate_rows_ref[1:2, rows] = to_row(second)
        for copy in saves(g):
            copy.start()
        for i in range(2):
            pl.when(g == 2 * i + 1)(events[2 * i])
            pl.when(g == 2 * i + 1)(events[2 * i + 1])

    capacity = sent_ref.shape[1]

    def swaps(e):
        owner, slot = lax.div(e, held), lax.rem(e, held)
        out = []
        for i, (here, there) in enumerate(((sent_ref, arrived_out), (grad_sent_ref, grad_arrived_out))):
            far = pltpu.make_async_remote_copy(
                src_ref=here.at[e], dst_ref=there.at[slot, place.x],
                send_sem=swap_send.at[i, e], recv_sem=swap_recv.at[i, slot, place.x],
                device_id=(owner, place.me), device_id_type=MESH,
            )
            near = pltpu.make_async_copy(here.at[e], there.at[slot, place.x], swap_local.at[i, slot])
            out.append((far, near))
        return owner != place.x, out

    @pl.loop(0, experts)
    def _(i):
        e = lax.rem((place.x + 1) * held + i, experts)
        slot = iota((capacity, x_ref.shape[0]), 0) + e * capacity
        in_first = slot == meta_row_ref[0:1, :]
        in_second = slot == meta_row_ref[1:2, :]
        picks = jnp.where(jnp.logical_or(in_first, in_second), 1.0, 0.0).astype(BF16)
        gate = jnp.sum(
            jnp.where(in_first, gate_rows_ref[0:1, :], jnp.where(in_second, gate_rows_ref[1:2, :], 0.0)),
            axis=1, keepdims=True,
        )
        sent_ref[e] = dot(picks, act_two_ref[...]).astype(BF16)
        cot_slots = dot(picks, cot_ref[...])
        cot_sent_ref[e] = cot_slots.astype(BF16)
        grad_sent_ref[e] = (gate * cot_slots).astype(BF16)
        away, copies = swaps(e)
        for far, near in copies:
            pl.when(away)(far.start)
            pl.when(jnp.logical_not(away))(near.start)

    cot_copy = pltpu.make_async_copy(cot_sent_ref, cot_sent_out, tail_sem.at[1])
    cot_copy.start()
    for event in events[4:]:
        event()
    for gather in (up, down):
        gather.finish_recv()

    @pl.loop(0, groups)
    def _(g):
        for copy in saves(g):
            copy.wait()

    params_copy.wait()
    cot_copy.wait()

    @pl.loop(0, experts)
    def _(e):
        away, copies = swaps(e)
        for far, near in copies:
            pl.when(away)(far.wait_send)
            pl.when(jnp.logical_not(away))(near.wait)

    for i, there in enumerate((arrived_out, grad_arrived_out)):
        for slot in range(held):
            for k in range(1, peers):
                other = lax.rem(place.x + k, peers)
                pltpu.make_async_remote_copy(
                    src_ref=there.at[slot, other], dst_ref=there.at[slot, other],
                    send_sem=swap_send.at[i, 0], recv_sem=swap_recv.at[i, slot, other],
                    device_id=(other, place.me), device_id_type=MESH,
                ).wait_recv()
    for gather in gathers:
        gather.finish_send()


class Scatter:
    def __init__(self, place, part, sums, across, line, send, recv):
        self.place, self.part, self.sums, self.across, self.line = place, part, sums, across, line
        self.send, self.recv = send, recv

    def remote(self, source, target, item, route, a, b, c):
        return pltpu.make_async_remote_copy(
            src_ref=source, dst_ref=target, send_sem=self.send.at[item, route], recv_sem=self.recv.at[item, route],
            device_id=self.place.at(a, b, c), device_id_type=MESH,
        )

    def core_copy(self, item):
        p = self.place
        return self.remote(self.part(item).at[:, :, 1 - p.c], self.sums.at[item], item, 0, p.a, p.b, 1 - p.c)

    def across_copies(self, item):
        p = self.place
        out = []
        for j in range(p.B - 1):
            to, back = p.other_b(j), p.B - 2 - j
            copy = self.remote(self.sums.at[item, :, to], self.across.at[item, back], item, 1 + back, p.a, to, p.c)
            out.append(copy)
        return out

    def line_copies(self, item):
        p = self.place
        out = []
        for k in range(1, p.A):
            to, back = lax.rem(p.a + k, p.A), p.A - 1 - k
            copy = self.remote(self.sums.at[item, to, p.b], self.line.at[item, back], item, p.B + back, to, p.b, p.c)
            out.append(copy)
        return out

    def start(self, item):
        self.core_copy(item).start()

    def core_step(self, item):
        p = self.place
        self.core_copy(item).wait()
        part = self.part(item)

        @pl.loop(0, p.A * p.B)
        def _(i):
            a, b = lax.div(i, p.B), lax.rem(i, p.B)
            total = self.sums[item, a, b].astype(F32) + part[a, b, p.c].astype(F32)
            self.sums[item, a, b] = total.astype(BF16)

        for copy in self.across_copies(item):
            copy.start()

    def across_step(self, item):
        p = self.place
        for copy in self.across_copies(item):
            copy.wait_recv()

        @pl.loop(0, p.A)
        def _(a):
            total = self.sums[item, a, p.b].astype(F32)
            for j in range(p.B - 1):
                total += self.across[item, j, a].astype(F32)
            self.sums[item, a, p.b] = total.astype(BF16)

        for copy in self.line_copies(item):
            copy.start()

    def line_step(self, item):
        p = self.place
        for copy in self.line_copies(item):
            copy.wait_recv()
        total = self.sums[item, p.a, p.b].astype(F32)
        for k in range(p.A - 1):
            total += self.line[item, k].astype(F32)
        return total

    def finish(self, item):
        for copy in self.across_copies(item) + self.line_copies(item):
            copy.wait_send()


def backward_kernel(
    experts, fsdp, peers,
    x_in, cot_in, meta_ref, params_in, act_one_in, triple_in, weights_in, attended_in, mid_in, act_two_in, probs_in,
    arrived_in, grad_arrived_in, cot_slots_in, up_full, down_full,
    out_out, input_grad_out, share_out, up_grad_out, down_grad_out,
    x_ref, params_ref, triple_ref, probs_ref,
    rows_ref, grad_ref, up_ref, down_ref, back_ref, grad_slots_ref, float_ref,
    part_up, part_down, sums_up, sums_down, sums_par, across_up, across_down, across_par, line_up, line_down, line_par,
    stage_up, stage_down, swap_ref,
    dot_row_ref, place_ref, gated_ref, logit_grad_ref, column_ref,
    load_sem, expert_sem, late_sem, save_sem, return_send, return_recv, swap_send, swap_recv,
    up_send, up_recv, down_send, down_recv, par_send, par_recv, stage_sem,
):
    width = x_ref.shape[1]
    rows_pad = x_ref.shape[0]
    groups = rows_pad // BLOCK
    places = back_ref.shape[0]
    capacity = places // experts
    held = up_full.shape[0]
    expert_rows = places // held
    hidden_width = up_ref.shape[2]
    chunks = hidden_width // FF_CHUNK
    place = Place(fsdp)
    copy_in = pltpu.make_async_copy
    loads = [
        copy_in(there, here, load_sem.at[i])
        for i, (there, here) in enumerate(
            ((params_in, params_ref), (triple_in, triple_ref), (probs_in, probs_ref),
             (x_in, x_ref))
        )
    ]

    def held_rows(e):
        return pl.ds(pl.multiple_of(e * expert_rows, 16), expert_rows)

    def expert_loads(e):
        slot = lax.rem(e, 2)
        return [
            copy_in(arrived_in.at[e], rows_ref.at[held_rows(e), :], expert_sem.at[0, slot]),
            copy_in(grad_arrived_in.at[e], grad_ref.at[held_rows(e), :], expert_sem.at[1, slot]),
            copy_in(up_full.at[e], up_ref.at[slot], expert_sem.at[2, slot]),
            copy_in(down_full.at[e], down_ref.at[slot], expert_sem.at[3, slot]),
        ]

    for copy in expert_loads(0) + loads:
        copy.start()
    greet(place, peers, False)

    A, B = place.A, place.B
    up = Scatter(
        place, lambda e: part_up.at[lax.rem(e, 2), :, :, :, :, pl.ds(0, hidden_width)],
        sums_up, across_up, line_up, up_send, up_recv,
    )
    down = Scatter(place, lambda e: part_down.at[lax.rem(e, 2)], sums_down, across_down, line_down, down_send, down_recv)
    par = Scatter(place, lambda e: part_up.at[0], sums_par, across_par, line_par, par_send, par_recv)

    def slot_rows(e, x):
        return pl.ds(pl.multiple_of((x * held + e) * capacity, 16), capacity)

    def returns(e):
        out = []
        for i, (here, there) in enumerate(((rows_ref, back_ref), (grad_ref, grad_slots_ref))):
            for k in range(1, peers):
                to, back = lax.rem(place.x + k, peers), peers - 1 - k
                out.append(
                    pltpu.make_async_remote_copy(
                        src_ref=here.at[pl.ds(pl.multiple_of(e * expert_rows + to * capacity, 16), capacity), :],
                        dst_ref=there.at[slot_rows(e, place.x), :],
                        send_sem=return_send.at[i, e, back], recv_sem=return_recv.at[i, e, back],
                        device_id=(to, place.me), device_id_type=MESH,
                    )
                )
        return out

    @pl.loop(0, held)
    def _(e):
        slot = lax.rem(e, 2)

        @pl.when(e + 1 < held)
        def _():
            for copy in expert_loads(e + 1):
                copy.start()

        for copy in expert_loads(e):
            copy.wait()
        float_ref[...] = jnp.zeros_like(float_ref)

        @pl.loop(0, chunks)
        def _(f):
            at = pl.ds(pl.multiple_of(f * FF_CHUNK, FF_CHUNK), FF_CHUNK)
            rows, grads = rows_ref[held_rows(e), :], grad_ref[held_rows(e), :]
            up_part, down_part = up_ref[slot, :, at], down_ref[slot, at, :]
            hidden = dot(rows, up_part)
            spread = 0.5 * (1.0 + lax.erf(hidden * ROOT_HALF))
            active = (hidden * spread).astype(BF16)
            slope = spread + hidden * (DENSITY_SCALE * jnp.exp(-0.5 * hidden * hidden))
            float_ref[:expert_rows, :] += dot(active, down_part)
            grad_hidden = (dot_against(grads, down_part) * slope).astype(BF16)
            float_ref[expert_rows : 2 * expert_rows, :] += dot_against(grad_hidden, up_part)
            size = part_up.shape[4]
            part_up[slot, :, :, :, :, at] = dot_rows(rows, grad_hidden).astype(BF16).reshape(A, B, 2, size, FF_CHUNK)
            size = part_down.shape[4]
            blocks = FF_CHUNK // size // 2
            value = dot_rows(active, grads).astype(BF16).reshape(blocks, 2, size, width)
            for i in range(blocks):
                line = f * blocks + i
                part_down[slot, lax.div(line, B), lax.rem(line, B)] = value[i]

            @pl.when(jnp.logical_and(f == 0, e >= 1))
            def _():
                up.core_step(e - 1)
                down.core_step(e - 1)

        rows_ref[held_rows(e), :] = float_ref[:expert_rows, :].astype(BF16)
        grad_ref[held_rows(e), :] = float_ref[expert_rows : 2 * expert_rows, :].astype(BF16)
        for copy in returns(e):
            copy.start()
        own = pl.ds(pl.multiple_of(e * expert_rows + place.x * capacity, 16), capacity)
        back_ref[slot_rows(e, place.x), :] = rows_ref[own, :]
        grad_slots_ref[slot_rows(e, place.x), :] = grad_ref[own, :]
        up.start(e)
        down.start(e)

    def late_loads():
        out = []
        for g in range(groups):
            half = groups // 2
            rows = pl.ds((g % half) * BLOCK, BLOCK)
            out.append(copy_in(weights_in.at[pl.ds(g * BLOCK, BLOCK), :], up_ref.at[g // half, rows, :], late_sem.at[4 + g]))
        for i, array in enumerate((act_one_in, attended_in, act_two_in, cot_in)):
            rows = pl.ds((i % 2) * rows_pad, rows_pad)
            out.append(copy_in(array, down_ref.at[i // 2, rows, :], late_sem.at[i]))
        out.append(copy_in(mid_in, float_ref.at[pl.ds(0, rows_pad), :], late_sem.at[4 + groups]))
        return out

    for copy in late_loads():
        copy.start()
    act_one = down_ref.at[0, pl.ds(0, rows_pad), :]
    attended = down_ref.at[0, pl.ds(rows_pad, rows_pad), :]
    act_two = down_ref.at[1, pl.ds(0, rows_pad), :]
    cot_ref = down_ref.at[1, pl.ds(rows_pad, rows_pad), :]
    input_grad_ref = float_ref

    def stage_copies(e):
        slot = lax.rem(e, 2)
        return (
            copy_in(stage_up.at[slot], up_grad_out.at[e], stage_sem.at[0, slot]),
            copy_in(stage_down.at[slot], down_grad_out.at[e], stage_sem.at[1, slot]),
        )

    def expert_line(e):
        if e >= 2:
            for copy in stage_copies(e - 2):
                copy.wait()
        stage_up[e % 2] = up.line_step(e)
        stage_down[e % 2] = down.line_step(e)
        for copy in stage_copies(e):
            copy.start()

    def expert_across(e):
        up.across_step(e)
        down.across_step(e)

    up.core_step(held - 1)
    down.core_step(held - 1)
    expert_across(0)

    for copy in loads + late_loads():
        copy.wait()
    slot_loads = [
        copy_in(cot_slots_in.at[held_rows(e), :], rows_ref.at[held_rows(e), :], load_sem.at[4 + e]) for e in range(held)
    ]
    for e in range(held):
        for copy in returns(e):
            copy.wait()
        slot_loads[e].start()
    for copy in slot_loads:
        copy.wait()

    small = params_ref[:, 4 * width :]
    small_rows = jnp.transpose(small.astype(F32))
    gain_one = small_rows[NORM_LANE : NORM_LANE + 1]
    gain_two = small_rows[NORM_LANE + 2 : NORM_LANE + 3]
    column_ref[...] = jnp.zeros_like(column_ref)

    @pl.loop(0, places // LANES)
    def _(c):
        at = pl.ds(pl.multiple_of(c * LANES, LANES), LANES)
        column = jnp.sum(back_ref[at, :].astype(F32) * rows_ref[at, :].astype(F32), axis=1, keepdims=True)
        dot_row_ref[0:1, at] = to_row(column)

    def saves(g):
        rows = rows_of(g)
        return (
            copy_in(cot_ref.at[rows, :], out_out.at[rows, :], save_sem.at[0, g]),
            copy_in(input_grad_ref.at[rows, :], input_grad_out.at[rows, :], save_sem.at[1, g]),
        )

    @pl.loop(0, groups)
    def _(g):
        rows = rows_of(g)
        half_groups = groups // 2
        weight_rows = rows_of(lax.rem(g, half_groups))
        meta = meta_ref[rows, :]
        probs = probs_ref[rows, :]
        gate_first, gate_second = gates_of(probs, meta)
        lane = iota((BLOCK, LANES), 1)
        grad_first = jnp.zeros((BLOCK, LANES), F32)
        grad_second = jnp.zeros((BLOCK, LANES), F32)
        for c in range(places // LANES):
            at = c * LANES
            in_first = lane == meta[:, 0:1] - at
            in_second = lane == meta[:, 1:2] - at
            place_ref[:, at : at + LANES] = jnp.where(jnp.logical_or(in_first, in_second), 1.0, 0.0).astype(BF16)
            gated_ref[:, at : at + LANES] = jnp.where(in_first, gate_first, jnp.where(in_second, gate_second, 0.0)).astype(BF16)
            dots = dot_row_ref[0:1, at : at + LANES]
            grad_first += jnp.where(in_first, dots, 0.0)
            grad_second += jnp.where(in_second, dots, 0.0)
        grad_first = jnp.sum(grad_first, axis=1, keepdims=True)
        grad_second = jnp.sum(grad_second, axis=1, keepdims=True)
        mid = input_grad_ref[rows, :]
        grad_probs = jnp.where(lane == meta[:, 2:3], grad_first, 0.0) + jnp.where(lane == meta[:, 3:4], grad_second, 0.0)
        grad_logits = (probs * (grad_probs - jnp.sum(grad_probs * probs, axis=-1, keepdims=True))).astype(BF16)
        logit_grad_ref[rows, :] = grad_logits
        grad_act = dot(place_ref[...], grad_slots_ref[...]) + dot_against(grad_logits, small)
        normed, inverse = normalize(mid)
        column_ref[NORM_LANE + 2 : NORM_LANE + 3, :] += jnp.sum(grad_act * normed, axis=0, keepdims=True)
        column_ref[NORM_LANE + 3 : NORM_LANE + 4, :] += jnp.sum(grad_act, axis=0, keepdims=True)
        grad_mid = cot_ref[rows, :].astype(F32) + denormalize(grad_act, normed, inverse, gain_two)
        cot_ref[rows, :] = (mid + dot(gated_ref[...], back_ref[...])).astype(BF16)
        input_grad_ref[rows, :] = grad_mid
        grad_attended = dot_against(grad_mid.astype(BF16), params_ref[:, 3 * width : 4 * width]).astype(BF16)
        low = lane < HEAD_DIM
        for pair in range(HEADS // 2):
            at = pair * LANES
            q = triple_ref[rows, at : at + LANES] * HEAD_DIM ** (-0.5)
            k = triple_ref[rows, width + at : width + at + LANES]
            v = triple_ref[rows, 2 * width + at : 2 * width + at + LANES]
            upstream = grad_attended[:, at : at + LANES]
            grad_q = grad_k = grad_v = jnp.zeros((BLOCK, LANES), F32)
            for half in range(2):
                mask = low if half == 0 else jnp.logical_not(low)
                upstream_half = jnp.where(mask, upstream, 0.0).astype(BF16)
                head = (2 * pair + half) * BLOCK
                weights = up_ref[lax.div(g, half_groups), weight_rows, head : head + BLOCK]
                kept = weights.astype(F32)
                grad_weights = dot_against(upstream_half, v)
                inner = jnp.sum(grad_weights * kept, axis=-1, keepdims=True)
                grad_scores = (kept * (grad_weights - inner)).astype(BF16)
                grad_q += dot(grad_scores, jnp.where(mask, k, 0.0).astype(BF16))
                grad_k += dot_rows(grad_scores, jnp.where(mask, q, 0.0).astype(BF16))
                grad_v += dot_rows(weights, upstream_half)
            triple_ref[rows, at : at + LANES] = (grad_q * HEAD_DIM ** (-0.5)).astype(BF16)
            triple_ref[rows, width + at : width + at + LANES] = grad_k.astype(BF16)
            triple_ref[rows, 2 * width + at : 2 * width + at + LANES] = grad_v.astype(BF16)
        grad_act = dot_against(triple_ref[rows, :], params_ref[:, : 3 * width])
        normed, inverse = normalize(x_ref[rows, :].astype(F32))
        column_ref[NORM_LANE : NORM_LANE + 1, :] += jnp.sum(grad_act * normed, axis=0, keepdims=True)
        column_ref[NORM_LANE + 1 : NORM_LANE + 2, :] += jnp.sum(grad_act, axis=0, keepdims=True)
        grad_mid = input_grad_ref[rows, :]
        x_ref[rows, :] = grad_mid.astype(BF16)
        input_grad_ref[rows, :] = grad_mid + denormalize(grad_act, normed, inverse, gain_one)
        for copy in saves(g):
            copy.start()
        pl.when(g == 0)(lambda: expert_across(1))
        pl.when(g == 2)(lambda: expert_line(0))
        pl.when(g == 2)(lambda: expert_across(2))

    size = part_up.shape[4]
    split = (A, B, 2, size)
    part_up[0, :, :, :, :, : 3 * width] = dot_rows(act_one[...], triple_ref[...]).astype(BF16).reshape(*split, 3 * width)
    part_up[0, :, :, :, :, 3 * width : 4 * width] = dot_rows(attended[...], x_ref[...]).astype(BF16).reshape(*split, width)
    small_part = dot_rows(act_two[...], logit_grad_ref[...]) + jnp.transpose(column_ref[...])
    part_up[0, :, :, :, :, 4 * width :] = small_part.astype(BF16).reshape(*split, LANES)
    par.start(0)
    expert_line(1)
    par.core_step(0)
    expert_across(3)
    expert_line(2)
    par.across_step(0)
    expert_line(3)
    swap_ref[place.x] = par.line_step(0).astype(BF16)

    def swaps():
        out = []
        for k in range(1, peers):
            to, back = lax.rem(place.x + k, peers), peers - 1 - k
            out.append(
                pltpu.make_async_remote_copy(
                    src_ref=swap_ref.at[place.x], dst_ref=swap_ref.at[place.x],
                    send_sem=swap_send.at[back], recv_sem=swap_recv.at[back],
                    device_id=(to, place.me), device_id_type=MESH,
                )
            )
        return out

    for copy in swaps():
        copy.start()

    @pl.loop(0, groups)
    def _(g):
        for copy in saves(g):
            copy.wait()

    for e in range(held - 2, held):
        for copy in stage_copies(e):
            copy.wait()
    for e in range(held):
        up.finish(e)
        down.finish(e)
    par.finish(0)
    for copy in swaps():
        copy.wait()
    total = swap_ref[0].astype(F32)
    for i in range(1, peers):
        total += swap_ref[i].astype(F32)
    share_out[...] = total


def on_device(
    inputs, cotangent, routes, slots, qkv_weight, out_weight, router_weight,
    norm1_gain, norm1_shift, norm2_gain, norm2_shift, expert_up, expert_down,
):
    rows_dev, width = inputs.shape
    groups = rows_dev // GROUP_ROWS
    rows_pad = groups * BLOCK
    fsdp = lax.axis_size("fsdp")
    peers = lax.axis_size("expert")
    held = expert_up.shape[0]
    experts = held * peers
    capacity = (42 * rows_dev + 20 * experts - 1) // (20 * experts)
    capacity = -(-capacity // 16) * 16
    places = experts * capacity

    def pad_rows(array, value=0):
        array = array.reshape(groups, GROUP_ROWS, array.shape[1])
        array = jnp.pad(array, ((0, 0), (0, BLOCK - GROUP_ROWS), (0, 0)), constant_values=value)
        return array.reshape(rows_pad, array.shape[2])

    def cut_rows(array):
        return array.reshape(groups, BLOCK, width)[:, :GROUP_ROWS].reshape(rows_dev, width)

    norms = jnp.stack([norm1_gain, norm1_shift, norm2_gain, norm2_shift], axis=1)
    shard = jnp.concatenate(
        [
            qkv_weight,
            out_weight,
            jnp.pad(router_weight, ((0, 0), (0, NORM_LANE - experts))),
            jnp.pad(norms, ((0, 0), (0, LANES - NORM_LANE - 4))),
        ],
        axis=1,
    )
    x = pad_rows(inputs)
    cot = pad_rows(cotangent)
    targets = jnp.where(slots >= 0, routes * capacity + slots, -1)
    meta = pad_rows(jnp.concatenate([targets, routes], axis=1), -1)
    meta_row = jnp.transpose(meta)

    vmem = pl.BlockSpec(memory_space=pltpu.VMEM)
    hbm = pl.BlockSpec(memory_space=pl.ANY)
    shape = jax.ShapeDtypeStruct
    params_spec = pltpu.CompilerParams(vmem_limit_bytes=VMEM_LIMIT)
    kept = (
        shape((rows_pad, width), BF16),
        shape((rows_pad, 3 * width), BF16),
        shape((rows_pad, HEADS * BLOCK), BF16),
        shape((rows_pad, width), BF16),
        shape((rows_pad, width), F32),
        shape((rows_pad, width), BF16),
        shape((rows_pad, LANES), F32),
    )
    slots_shape = shape((experts, capacity, width), BF16)
    arrived_shape = shape((held, peers, capacity, width), BF16)
    packed = (fsdp * shard.shape[0], shard.shape[1])
    scratch = lambda s: pltpu.VMEM(s.shape, s.dtype)
    dma = pltpu.SemaphoreType.DMA
    saved = pl.pallas_call(
        functools.partial(forward_kernel, experts, fsdp, peers),
        out_shape=(
            *kept, arrived_shape, arrived_shape, slots_shape, shape(packed, BF16),
            shape((held, fsdp * expert_up.shape[1], expert_up.shape[2]), BF16),
            shape((held, fsdp * expert_down.shape[1], expert_down.shape[2]), BF16),
        ),
        in_specs=[vmem] * 5 + [hbm] * 2,
        out_specs=[hbm] * 13,
        scratch_shapes=[
            pltpu.VMEM(packed, BF16), *map(scratch, kept), *[scratch(slots_shape)] * 3,
            pltpu.VMEM((BLOCK, BLOCK), F32), pltpu.VMEM((8, rows_pad), F32),
            dma((3, fsdp, 3 + fsdp // 8 - 1)), dma((3, fsdp)), dma((3,)), dma((len(kept), groups)),
            dma((2, experts)), dma((2, held, peers)), dma((2, held)), dma((2,)),
        ],
        compiler_params=pltpu.CompilerParams(vmem_limit_bytes=VMEM_LIMIT, collective_id=0, has_side_effects=True),
        name="attention_forward",
    )(x, cot, meta, meta_row, shard, expert_up, expert_down)
    act_one, triple, weights, attended, mid, act_two, probs, arrived, grad_arrived, cot_slots, params, up_full, down_full = saved

    expert_rows = peers * capacity
    arrived = arrived.reshape(held, expert_rows, width)
    grad_arrived = grad_arrived.reshape(held, expert_rows, width)
    hidden_width = up_full.shape[2]
    up_rows, down_rows = expert_up.shape[1], expert_down.shape[1]
    A, B = 4, fsdp // 8
    packed_width = shard.shape[1]

    def buffer(*dims, dtype=BF16):
        return pltpu.VMEM(dims, dtype)

    out, input_grad, share, up_grad, down_grad = pl.pallas_call(
        functools.partial(backward_kernel, experts, fsdp, peers),
        out_shape=(
            shape((rows_pad, width), BF16),
            shape((rows_pad, width), F32),
            shape((up_rows, packed_width), F32),
            shape(expert_up.shape, F32),
            shape(expert_down.shape, F32),
        ),
        in_specs=[hbm] * 2 + [vmem] + [hbm] * 13,
        out_specs=[hbm] * 2 + [vmem] + [hbm] * 2,
        scratch_shapes=[
            buffer(rows_pad, width), buffer(*packed), buffer(rows_pad, 3 * width),
            buffer(rows_pad, LANES, dtype=F32),
            buffer(places, width), buffer(places, width),
            buffer(2, width, hidden_width), buffer(2, hidden_width, width),
            buffer(places, width), buffer(places, width),
            buffer(max(2 * expert_rows, rows_pad), width, dtype=F32),
            buffer(2, A, B, 2, up_rows, packed_width), buffer(2, A, B, 2, down_rows, width),
            buffer(held, A, B, up_rows, hidden_width), buffer(held, A, B, down_rows, width), buffer(1, A, B, up_rows, packed_width),
            buffer(held, B - 1, A, up_rows, hidden_width), buffer(held, B - 1, A, down_rows, width),
            buffer(1, B - 1, A, up_rows, packed_width),
            buffer(held, A - 1, up_rows, hidden_width), buffer(held, A - 1, down_rows, width),
            buffer(1, A - 1, up_rows, packed_width),
            buffer(2, up_rows, hidden_width, dtype=F32), buffer(2, down_rows, width, dtype=F32),
            buffer(peers, up_rows, packed_width),
            buffer(8, places, dtype=F32), buffer(BLOCK, places), buffer(BLOCK, places),
            buffer(rows_pad, LANES), buffer(LANES, width, dtype=F32),
            dma((4 + held,)), dma((4, 2)), dma((5 + groups,)), dma((2, groups)),
            dma((2, held, peers - 1)), dma((2, held, peers - 1)), dma((peers - 1,)), dma((peers - 1,)),
            dma((held, A + B - 1)), dma((held, A + B - 1)), dma((held, A + B - 1)), dma((held, A + B - 1)),
            dma((1, A + B - 1)), dma((1, A + B - 1)), dma((2, 2)),
        ],
        compiler_params=pltpu.CompilerParams(vmem_limit_bytes=VMEM_LIMIT, collective_id=1, has_side_effects=True),
        name="experts_and_backward",
    )(
        x, cot, meta, params, act_one, triple, weights, attended, mid, act_two, probs,
        arrived, grad_arrived, cot_slots.reshape(experts * capacity, width), up_full, down_full,
    )
    norm_share = share[:, 4 * width + NORM_LANE : 4 * width + NORM_LANE + 4]
    return (
        cut_rows(out),
        cut_rows(input_grad),
        share[:, : 3 * width],
        share[:, 3 * width : 4 * width],
        share[:, 4 * width : 4 * width + experts],
        norm_share[:, 0],
        norm_share[:, 1],
        norm_share[:, 2],
        norm_share[:, 3],
        up_grad,
        down_grad,
    )


def solution(mesh):
    tokens = P(("expert", "fsdp"), None)
    rows, vector, expert = P("fsdp", None), P("fsdp"), P("expert", "fsdp", None)
    return jax.shard_map(
        on_device,
        mesh=mesh,
        in_specs=(tokens,) * 4 + (rows,) * 3 + (vector,) * 4 + (expert,) * 2,
        out_specs=(tokens,) * 2 + (rows,) * 3 + (vector,) * 4 + (expert,) * 2,
        check_vma=False,
    )
```

```python
import functools

import jax
import jax.numpy as jnp
from jax import lax
from jax.experimental import pallas as pl
from jax.experimental.pallas import tpu as pltpu
from jax.sharding import PartitionSpec as P

HEADS = 8
HEAD_DIM = 64
PATCHES = 49
EPS = 1e-06
ROOT_HALF = 0.7071067811865476
DENSITY_SCALE = 0.3989422804014327

BLOCK = 256
GROUP_IMAGES = BLOCK // PATCHES
GROUP_ROWS = GROUP_IMAGES * PATCHES
LANES = 128
NORM_LANE = 64
FF_CHUNK = 256
MAX_ROWS = 1088
VMEM_LIMIT = 62 * 1024 * 1024

MESH = pl.DeviceIdType.MESH
F32 = jnp.float32
BF16 = jnp.bfloat16


def dot(left, right):
    return lax.dot_general(left, right, (((1,), (0,)), ((), ())), preferred_element_type=F32)


def dot_rows(left, right):
    return lax.dot_general(left, right, (((0,), (0,)), ((), ())), preferred_element_type=F32)


def dot_against(left, right):
    return lax.dot_general(left, right, (((1,), (1,)), ((), ())), preferred_element_type=F32)


def iota(shape, dim):
    return lax.broadcasted_iota(jnp.int32, shape, dim)


def normalize(values):
    center = jnp.mean(values, axis=-1, keepdims=True)
    offset = values - center
    spread = jnp.mean(offset * offset, axis=-1, keepdims=True)
    inverse = lax.rsqrt(spread + EPS)
    return offset * inverse, inverse


def denormalize(upstream, normed, inverse, gain):
    scaled = upstream * gain
    return inverse * (
        scaled
        - jnp.mean(scaled, axis=-1, keepdims=True)
        - normed * jnp.mean(scaled * normed, axis=-1, keepdims=True)
    )


def to_row(column):
    n = column.shape[0]
    parts = []
    for at in range(0, n, LANES):
        eye = iota((LANES, LANES), 0) == iota((LANES, LANES), 1)
        parts.append(jnp.sum(jnp.where(eye, column[at : at + LANES], 0.0), axis=0, keepdims=True))
    return parts[0] if len(parts) == 1 else jnp.concatenate(parts, axis=1)


def rows_of(g):
    return pl.ds(pl.multiple_of(g * BLOCK, BLOCK), BLOCK)


def gates_of(probs, meta):
    lane = iota(probs.shape, 1)
    first = jnp.sum(jnp.where(lane == meta[:, 2:3], probs, 0.0), axis=1, keepdims=True)
    second = jnp.sum(jnp.where(lane == meta[:, 3:4], probs, 0.0), axis=1, keepdims=True)
    return first, second


class Place:
    def __init__(self, fsdp, xs):
        self.A, self.B = 4, fsdp // 8
        self.x = lax.axis_index("expert")
        self.me = lax.axis_index("fsdp")
        self.c = lax.rem(self.me, 2)
        line = lax.div(self.me, 2)
        self.b = lax.rem(line, self.B)
        self.a = lax.div(line, self.B)
        self.peers = xs * self.B
        self.peer = self.x * self.B + self.b

    def index(self, a, b, c):
        return (a * self.B + b) * 2 + c

    def other_b(self, j):
        return lax.rem(self.b + 1 + j, self.B)

    def at(self, a, b, c):
        return (self.x, self.index(a, b, c))

    def at_peer(self, peer):
        return (lax.div(peer, self.B), self.index(self.a, lax.rem(peer, self.B), self.c))

    def other_peer(self, k):
        return lax.rem(self.peer + k, self.peers)


def greet(place):
    barrier = pltpu.get_barrier_semaphore()

    def signal(device):
        pl.semaphore_signal(barrier, inc=1, device_id=device, device_id_type=MESH)

    for k in range(1, place.A):
        signal(place.at(lax.rem(place.a + k, place.A), place.b, place.c))
    for k in range(1, place.peers):
        signal(place.at_peer(place.other_peer(k)))
    signal(place.at(place.a, place.b, 1 - place.c))
    pl.semaphore_wait(barrier, place.A - 1 + place.peers - 1 + 1)


class Gather:
    RIGHT, LEFT, CORE, ACROSS = 0, 1, 2, 3

    def __init__(self, place, own, full, block, send_sem, recv_sem, local_sem):
        self.place, self.own, self.full, self.block = place, own, full, block
        self.send_sem, self.recv_sem, self.local_sem = send_sem, recv_sem, local_sem

    def copy(self, shard, route, source, a, b, c):
        return pltpu.make_async_remote_copy(
            src_ref=source, dst_ref=self.block(self.full, shard),
            send_sem=self.send_sem.at[shard, route], recv_sem=self.recv_sem.at[shard],
            device_id=self.place.at(a, b, c), device_id_type=MESH,
        )

    def onward(self, shard, source, right, left, across, act):
        p = self.place
        if right is not None:
            pl.when(right)(lambda: act(self.copy(shard, self.RIGHT, source, p.a + 1, p.b, p.c)))
        if left is not None:
            pl.when(left)(lambda: act(self.copy(shard, self.LEFT, source, p.a - 1, p.b, p.c)))
        if across:
            for j in range(p.B - 1):
                act(self.copy(shard, self.ACROSS + j, source, p.a, p.other_b(j), p.c))
        act(self.copy(shard, self.CORE, source, p.a, p.b, 1 - p.c))

    def local(self):
        return pltpu.make_async_copy(self.own, self.block(self.full, self.place.me), self.local_sem)

    def start(self):
        p = self.place
        self.local().start()
        self.onward(p.me, self.own, p.a < p.A - 1, p.a > 0, True, lambda copy: copy.start())

    def arrived(self, shard):
        p = self.place
        self.copy(shard, self.CORE, self.block(self.full, shard), p.a, p.b, 1 - p.c).wait_recv()

    def line_step(self, k):
        p = self.place

        def from_left():
            shard = p.index(p.a - k, p.b, p.c)
            self.arrived(shard)
            self.onward(shard, self.block(self.full, shard), p.a < p.A - 1, None, True, lambda copy: copy.start())

        def from_right():
            shard = p.index(p.a + k, p.b, p.c)
            self.arrived(shard)
            self.onward(shard, self.block(self.full, shard), None, p.a > 0, True, lambda copy: copy.start())

        pl.when(p.a - k >= 0)(from_left)
        pl.when(p.a + k < p.A)(from_right)

    def across_step(self, k):
        p = self.place

        def row(a):
            for j in range(p.B - 1):
                shard = p.index(a, p.other_b(j), p.c)
                self.arrived(shard)
                self.onward(shard, self.block(self.full, shard), None, None, False, lambda copy: copy.start())

        if k == 0:
            row(p.a)
        else:
            pl.when(p.a - k >= 0)(lambda: row(p.a - k))
            pl.when(p.a + k < p.A)(lambda: row(p.a + k))

    def finish_recv(self):
        p = self.place
        self.local().wait()
        for a in range(p.A):
            for b in range(p.B):
                self.arrived(p.index(a, b, 1 - p.c))

    def finish_send(self):
        p = self.place
        wait = lambda copy: copy.wait_send()
        self.onward(p.me, self.own, p.a < p.A - 1, p.a > 0, True, wait)
        for k in range(1, p.A):

            def from_left(k=k):
                shard = p.index(p.a - k, p.b, p.c)
                self.onward(shard, self.block(self.full, shard), p.a < p.A - 1, None, True, wait)

            def from_right(k=k):
                shard = p.index(p.a + k, p.b, p.c)
                self.onward(shard, self.block(self.full, shard), None, p.a > 0, True, wait)

            pl.when(p.a - k >= 0)(from_left)
            pl.when(p.a + k < p.A)(from_right)
        for a in range(p.A):
            for j in range(p.B - 1):
                shard = p.index(a, p.other_b(j), p.c)
                self.onward(shard, self.block(self.full, shard), None, None, False, wait)


class ExpertGather:
    RIGHT, LEFT, CORE, ACROSS = 0, 1, 2, 3

    def __init__(self, place, own, full, count, send_sem, recv_sem, local_sem):
        self.place, self.own, self.full, self.count = place, own, full, count
        self.send_sem, self.recv_sem, self.local_sem = send_sem, recv_sem, local_sem
        self.size = own.shape[1]
        self.depth = self.size * place.A * place.B * 2

    def block(self, el, shard):
        return self.full.at[pl.ds(pl.multiple_of(el * self.depth + shard * self.size, self.size), self.size), :]

    def mine(self, el):
        return self.own.at[self.place.b * self.count + el]

    def copy(self, el, shard, route, source, a, b, c):
        return pltpu.make_async_remote_copy(
            src_ref=source, dst_ref=self.block(el, shard),
            send_sem=self.send_sem.at[el, shard, route], recv_sem=self.recv_sem.at[el, shard],
            device_id=self.place.at(a, b, c), device_id_type=MESH,
        )

    def across(self, el):
        p = self.place
        out = []
        for j in range(p.B - 1):
            to = p.other_b(j)
            out.append(self.copy(el, p.me, self.ACROSS + j, self.own.at[to * self.count + el], p.a, to, p.c))
        return out

    def local(self, el):
        return pltpu.make_async_copy(self.mine(el), self.block(el, self.place.me), self.local_sem.at[el])

    def onward(self, el, shard, source, right, left, act):
        p = self.place
        if right:
            pl.when(p.a < p.A - 1)(lambda: act(self.copy(el, shard, self.RIGHT, source, p.a + 1, p.b, p.c)))
        if left:
            pl.when(p.a > 0)(lambda: act(self.copy(el, shard, self.LEFT, source, p.a - 1, p.b, p.c)))
        act(self.copy(el, shard, self.CORE, source, p.a, p.b, 1 - p.c))

    def arrived(self, el, shard):
        p = self.place
        self.copy(el, shard, self.CORE, self.block(el, shard), p.a, p.b, 1 - p.c).wait_recv()

    def start_across(self, el):
        for copy in self.across(el):
            copy.start()

    def start_own(self, el):
        self.local(el).start()
        self.onward(el, self.place.me, self.mine(el), True, True, lambda copy: copy.start())

    def across_step(self, el):
        p = self.place
        for j in range(p.B - 1):
            shard = p.index(p.a, p.other_b(j), p.c)
            self.arrived(el, shard)
            self.onward(el, shard, self.block(el, shard), True, True, lambda copy: copy.start())

    def line_step(self, el, k):
        p = self.place

        def row(a, right, left):
            for b in range(p.B):
                shard = p.index(a, b, p.c)
                self.arrived(el, shard)
                self.onward(el, shard, self.block(el, shard), right, left, lambda copy: copy.start())

        pl.when(p.a - k >= 0)(lambda: row(p.a - k, True, False))
        pl.when(p.a + k < p.A)(lambda: row(p.a + k, False, True))

    def core_wait(self, el):
        p = self.place
        self.local(el).wait()
        for a in range(p.A):
            for b in range(p.B):
                self.arrived(el, p.index(a, b, 1 - p.c))

    def finish(self, el):
        p = self.place
        wait = lambda copy: copy.wait_send()
        for copy in self.across(el):
            wait(copy)
        self.onward(el, p.me, self.mine(el), True, True, wait)
        for j in range(p.B - 1):
            shard = p.index(p.a, p.other_b(j), p.c)
            self.onward(el, shard, self.block(el, shard), True, True, wait)

        def row(a, right, left):
            for b in range(p.B):
                shard = p.index(a, b, p.c)
                self.onward(el, shard, self.block(el, shard), right, left, wait)

        for k in range(1, p.A):
            pl.when(p.a - k >= 0)(functools.partial(row, p.a - k, True, False))
            pl.when(p.a + k < p.A)(functools.partial(row, p.a + k, False, True))


class ExpertScatter:
    def __init__(self, place, part, sums, line, out, count, send, recv, local_sem):
        self.place, self.part, self.sums, self.line, self.out, self.count = place, part, sums, line, out, count
        self.send, self.recv, self.local_sem = send, recv, local_sem

    def remote(self, source, target, el, route, a, b, c):
        return pltpu.make_async_remote_copy(
            src_ref=source, dst_ref=target, send_sem=self.send.at[el, route], recv_sem=self.recv.at[el, route],
            device_id=self.place.at(a, b, c), device_id_type=MESH,
        )

    def core_copy(self, el):
        p = self.place
        return self.remote(self.part(el).at[:, :, 1 - p.c], self.sums.at[el], el, 0, p.a, p.b, 1 - p.c)

    def line_copies(self, el):
        p = self.place
        out = []
        for k in range(1, p.A):
            to, back = lax.rem(p.a + k, p.A), p.A - 1 - k
            out.append(self.remote(self.sums.at[el, to], self.line.at[el, back], el, 1 + back, to, p.b, p.c))
        return out

    def last_copies(self, el):
        p = self.place
        out = []
        for j in range(p.B - 1):
            to, back = p.other_b(j), p.B - 2 - j
            target = self.out.at[p.b * self.count + el]
            out.append(self.remote(self.sums.at[el, p.a, to], target, el, p.A + back, p.a, to, p.c))
        return out

    def local(self, el):
        p = self.place
        return pltpu.make_async_copy(self.sums.at[el, p.a, p.b], self.out.at[p.b * self.count + el], self.local_sem.at[el])

    def start(self, el):
        self.core_copy(el).start()

    def core_step(self, el):
        p = self.place
        self.core_copy(el).wait()
        part = self.part(el)

        @pl.loop(0, p.A * p.B)
        def _(i):
            a, b = lax.div(i, p.B), lax.rem(i, p.B)
            total = self.sums[el, a, b].astype(F32) + part[a, b, p.c].astype(F32)
            self.sums[el, a, b] = total.astype(BF16)

        for copy in self.line_copies(el):
            copy.start()

    def line_step(self, el):
        p = self.place
        for copy in self.line_copies(el):
            copy.wait_recv()

        @pl.loop(0, p.B)
        def _(b):
            total = self.sums[el, p.a, b].astype(F32)
            for k in range(p.A - 1):
                total += self.line[el, k, b].astype(F32)
            self.sums[el, p.a, b] = total.astype(BF16)

        for copy in self.last_copies(el) + [self.local(el)]:
            copy.start()

    def finish(self, el):
        for copy in self.line_copies(el):
            copy.wait_send()
        for copy in self.last_copies(el) + [self.local(el)]:
            copy.wait()


class Scatter:
    def __init__(self, place, part, sums, across, line, send, recv):
        self.place, self.part, self.sums, self.across, self.line = place, part, sums, across, line
        self.send, self.recv = send, recv

    def remote(self, source, target, item, route, a, b, c):
        return pltpu.make_async_remote_copy(
            src_ref=source, dst_ref=target, send_sem=self.send.at[item, route], recv_sem=self.recv.at[item, route],
            device_id=self.place.at(a, b, c), device_id_type=MESH,
        )

    def core_copy(self, item):
        p = self.place
        return self.remote(self.part(item).at[:, :, 1 - p.c], self.sums.at[item], item, 0, p.a, p.b, 1 - p.c)

    def across_copies(self, item):
        p = self.place
        out = []
        for j in range(p.B - 1):
            to, back = p.other_b(j), p.B - 2 - j
            copy = self.remote(self.sums.at[item, :, to], self.across.at[item, back], item, 1 + back, p.a, to, p.c)
            out.append(copy)
        return out

    def line_copies(self, item):
        p = self.place
        out = []
        for k in range(1, p.A):
            to, back = lax.rem(p.a + k, p.A), p.A - 1 - k
            copy = self.remote(self.sums.at[item, to, p.b], self.line.at[item, back], item, p.B + back, to, p.b, p.c)
            out.append(copy)
        return out

    def start(self, item):
        self.core_copy(item).start()

    def core_step(self, item):
        p = self.place
        self.core_copy(item).wait()
        part = self.part(item)

        @pl.loop(0, p.A * p.B)
        def _(i):
            a, b = lax.div(i, p.B), lax.rem(i, p.B)
            total = self.sums[item, a, b].astype(F32) + part[a, b, p.c].astype(F32)
            self.sums[item, a, b] = total.astype(BF16)

        for copy in self.across_copies(item):
            copy.start()

    def across_step(self, item):
        p = self.place
        for copy in self.across_copies(item):
            copy.wait_recv()

        @pl.loop(0, p.A)
        def _(a):
            total = self.sums[item, a, p.b].astype(F32)
            for j in range(p.B - 1):
                total += self.across[item, j, a].astype(F32)
            self.sums[item, a, p.b] = total.astype(BF16)

        for copy in self.line_copies(item):
            copy.start()

    def line_step(self, item):
        p = self.place
        for copy in self.line_copies(item):
            copy.wait_recv()
        total = self.sums[item, p.a, p.b].astype(F32)
        for k in range(p.A - 1):
            total += self.line[item, k].astype(F32)
        return total

    def finish(self, item):
        for copy in self.across_copies(item) + self.line_copies(item):
            copy.wait_send()


def block_kernel(
    experts, fsdp, xs, count,
    x_in, cot_in, meta_ref, meta_row_ref, shard_ref, up_in, down_in,
    out_out, input_grad_out, share_out, up_grad_out, down_grad_out,
    act_one_save, weights_save, attended_save, mid_save, act_two_save,
    x_ref, params_ref, triple_ref, probs_ref,
    sent_ref, cot_sent_ref, gate_sent_ref, rows_ref, grad_ref, gate_ref, back_ref, grad_slots_ref,
    up_ref, down_ref, part_up_ref, part_down_ref, float_ref,
    sums_up, sums_down, line_up, line_down, sums_par, across_par, line_par, swap_ref,
    bias_ref, gate_rows_ref, dot_row_ref, place_ref, gated_ref, logit_grad_ref, column_ref,
    load_sem, save_sem, late_sem, store_sem, par_gather_send, par_gather_recv, par_gather_local,
    gather_send, gather_recv, gather_local, swap_send, swap_recv, return_send, return_recv,
    scatter_send, scatter_recv, scatter_local, par_send, par_recv, share_send, share_recv,
):
    rows_pad, width = x_ref.shape
    groups = rows_pad // BLOCK
    places = sent_ref.shape[0]
    capacity = places // experts
    hidden_width = up_ref.shape[1]
    chunks = hidden_width // FF_CHUNK
    held = up_in.shape[0]
    place = Place(fsdp, xs)
    A, B, sources = place.A, place.B, place.peers
    expert_rows = sources * capacity
    row_block = float_ref.shape[0] // 2
    copy_in = pltpu.make_async_copy

    weights_ref = part_up_ref
    act_one, attended, act_two, cot_ref = (part_down_ref.at[pl.ds(i * rows_pad, rows_pad), :] for i in range(4))
    mid_ref = float_ref

    loads = [copy_in(x_in, x_ref, load_sem.at[0]), copy_in(cot_in, cot_ref, load_sem.at[1])]
    for copy in loads:
        copy.start()
    greet(place)

    def rows_block(ref, shard):
        size = shard_ref.shape[0]
        return ref.at[pl.ds(pl.multiple_of(shard * size, size), size), :]

    params = Gather(place, shard_ref, params_ref, rows_block, par_gather_send, par_gather_recv, par_gather_local)
    weights_in = [
        ExpertGather(place, own, full, count, gather_send.at[i], gather_recv.at[i], gather_local.at[i])
        for i, (own, full) in enumerate(((up_in, up_ref), (down_in, down_ref)))
    ]

    def each(step, el, *more):
        if el < count:
            for gather in weights_in:
                getattr(gather, step)(el, *more)

    params.start()
    for el in range(count):
        each("start_across", el)
    image_row = iota((BLOCK, BLOCK), 0) // PATCHES
    image_col = iota((BLOCK, BLOCK), 1) // PATCHES
    bias_ref[...] = jnp.where(image_row == image_col, 0.0, -1e30)

    def slot_rows(e):
        return pl.ds(pl.multiple_of(e * capacity, 16), capacity)

    def source_rows(el, source):
        return pl.ds(pl.multiple_of(el * expert_rows + source * capacity, 16), capacity)

    def find(e):
        slot = iota((capacity, rows_pad), 0) + e * capacity
        in_first = slot == meta_row_ref[0:1, :]
        in_second = slot == meta_row_ref[1:2, :]
        return in_first, in_second, jnp.where(jnp.logical_or(in_first, in_second), 1.0, 0.0).astype(BF16)

    def swap(kind, here, there, el, peer):
        return pltpu.make_async_remote_copy(
            src_ref=here.at[slot_rows(peer * count + el), :], dst_ref=there.at[source_rows(el, place.peer), :],
            send_sem=swap_send.at[kind, peer * count + el], recv_sem=swap_recv.at[kind, el, place.peer],
            device_id=place.at_peer(peer), device_id_type=MESH,
        )

    def swap_wait(kind, there, el):
        @pl.loop(1, sources)
        def _(k):
            source = place.other_peer(k)
            pltpu.make_async_remote_copy(
                src_ref=there.at[source_rows(el, source), :], dst_ref=there.at[source_rows(el, source), :],
                send_sem=swap_send.at[kind, 0], recv_sem=swap_recv.at[kind, el, source],
                device_id=place.at_peer(source), device_id_type=MESH,
            ).wait_recv()

    for copy in loads:
        copy.wait()
    for k in range(1, A):
        params.line_step(k)
        params.across_step(k - 1)

        @pl.loop((k - 1) * experts // (A - 1), k * experts // (A - 1))
        def _(e):
            _, _, picks = find(e)
            cot_sent_ref[slot_rows(e), :] = dot(picks, cot_ref[...]).astype(BF16)

    params.across_step(A - 1)
    each("start_own", 0)
    params.finish_recv()
    for el in range(count):

        @pl.loop(1, sources)
        def _(k):
            swap(2, cot_sent_ref, grad_ref, el, place.other_peer(k)).start()

        grad_ref[source_rows(el, place.peer), :] = cot_sent_ref[slot_rows(place.peer * count + el), :]

    small = params_ref[:, 4 * width :]
    small_rows = jnp.transpose(small.astype(F32))

    def saves(g):
        rows = rows_of(g)
        pairs = (
            (act_one, act_one_save), (weights_ref.at[:, pl.ds(0, HEADS * BLOCK)], weights_save), (attended, attended_save),
            (mid_ref, mid_save), (act_two, act_two_save),
        )
        return [
            copy_in(here.at[rows, :], there.at[rows, :], save_sem.at[i, g]) for i, (here, there) in enumerate(pairs)
        ]

    @pl.loop(0, groups)
    def _(g):
        rows = rows_of(g)
        x = x_ref[rows, :].astype(F32)
        normed, _ = normalize(x)
        act = (normed * small_rows[NORM_LANE : NORM_LANE + 1] + small_rows[NORM_LANE + 1 : NORM_LANE + 2]).astype(BF16)
        act_one[rows, :] = act
        triple_ref[rows, :] = dot(act, params_ref[:, : 3 * width]).astype(BF16)
        low = iota((BLOCK, LANES), 1) < HEAD_DIM
        for pair in range(HEADS // 2):
            at = pair * LANES
            q = triple_ref[rows, at : at + LANES] * HEAD_DIM ** (-0.5)
            k = triple_ref[rows, width + at : width + at + LANES]
            v = triple_ref[rows, 2 * width + at : 2 * width + at + LANES]
            total = None
            for half in range(2):
                mask = low if half == 0 else jnp.logical_not(low)
                scores = dot_against(jnp.where(mask, q, 0.0).astype(BF16), k) + bias_ref[...]
                top = jnp.max(scores, axis=-1, keepdims=True)
                raised = jnp.exp(scores - top)
                probs = raised / jnp.sum(raised, axis=-1, keepdims=True)
                probs = probs.astype(BF16)
                head = (2 * pair + half) * BLOCK
                weights_ref[rows, head : head + BLOCK] = probs
                part = dot(probs, jnp.where(mask, v, 0.0).astype(BF16))
                total = part if total is None else total + part
            attended[rows, at : at + LANES] = total.astype(BF16)

        @pl.when(g == 0)
        def _():
            each("across_step", 0)

        mid = x + dot(attended[rows, :], params_ref[:, 3 * width : 4 * width])
        mid_ref[rows, :] = mid
        normed, _ = normalize(mid)
        act = (normed * small_rows[NORM_LANE + 2 : NORM_LANE + 3] + small_rows[NORM_LANE + 3 : NORM_LANE + 4]).astype(BF16)
        act_two[rows, :] = act
        logits = jnp.where(iota((BLOCK, LANES), 1) < experts, dot(act, small), -1e30)
        raised = jnp.exp(logits - jnp.max(logits, axis=-1, keepdims=True))
        probs = raised / jnp.sum(raised, axis=-1, keepdims=True)
        probs_ref[rows, :] = probs
        first, second = gates_of(probs, meta_ref[rows, :])
        gate_rows_ref[0:1, rows] = to_row(first)
        gate_rows_ref[1:2, rows] = to_row(second)
        for copy in saves(g):
            copy.start()

        @pl.when(g == 1)
        def _():
            each("line_step", 0, 1)
            each("start_own", 1)
            each("across_step", 1)

        @pl.when(g == groups - 1)
        def _():
            each("line_step", 0, 2)

    @pl.loop(0, experts)
    def _(i):
        el, peer = lax.div(i, sources), place.other_peer(lax.rem(i, sources) + 1)
        e = peer * count + el
        in_first, in_second, picks = find(e)
        gate = jnp.sum(
            jnp.where(in_first, gate_rows_ref[0:1, :], jnp.where(in_second, gate_rows_ref[1:2, :], 0.0)),
            axis=1, keepdims=True,
        )
        sent_ref[slot_rows(e), :] = dot(picks, act_two[...]).astype(BF16)
        gate_sent_ref[slot_rows(e), :] = jnp.broadcast_to(gate, (capacity, LANES))

        @pl.when(peer != place.peer)
        def _():
            swap(0, sent_ref, rows_ref, el, peer).start()
            swap(1, gate_sent_ref, gate_ref, el, peer).start()

        @pl.when(peer == place.peer)
        def _():
            rows_ref[source_rows(el, peer), :] = sent_ref[slot_rows(e), :]
            gate_ref[source_rows(el, peer), :] = gate_sent_ref[slot_rows(e), :]

        @pl.when(i == experts // 2)
        def _():
            each("line_step", 1, 1)

    each("line_step", 0, 3)

    @pl.loop(0, groups)
    def _(g):
        for copy in saves(g):
            copy.wait()

    part_up = part_up_ref.at[pl.ds(0, count * width), :].reshape(count, A, B, 2, up_in.shape[1], part_up_ref.shape[1])
    part_down = part_down_ref.at[pl.ds(0, count * hidden_width), :].reshape(count, A, B, 2, down_in.shape[1], width)
    scatters = [
        ExpertScatter(place, part, sums, line, out, count, scatter_send.at[i], scatter_recv.at[i], scatter_local.at[i])
        for i, (part, sums, line, out) in enumerate(
            (
                (lambda el: part_up.at[el, :, :, :, :, pl.ds(0, hidden_width)], sums_up, line_up, up_grad_out),
                (lambda el: part_down.at[el], sums_down, line_down, down_grad_out),
            )
        )
    ]

    def all_scatters(step, el):
        for scatter in scatters:
            getattr(scatter, step)(el)

    par = Scatter(place, lambda e: part_up.at[0], sums_par, across_par, line_par, par_send, par_recv)

    def returned(kind, here, there, el, peer):
        return pltpu.make_async_remote_copy(
            src_ref=here.at[source_rows(el, peer), :], dst_ref=there.at[slot_rows(place.peer * count + el), :],
            send_sem=return_send.at[kind, el, peer], recv_sem=return_recv.at[kind, el, place.peer],
            device_id=place.at_peer(peer), device_id_type=MESH,
        )

    def return_wait(kind, there, el):
        @pl.loop(1, sources)
        def _(k):
            source = place.other_peer(k)
            target = there.at[slot_rows(source * count + el), :]
            pltpu.make_async_remote_copy(
                src_ref=target, dst_ref=target,
                send_sem=return_send.at[kind, 0, 0], recv_sem=return_recv.at[kind, el, source],
                device_id=place.at_peer(source), device_id_type=MESH,
            ).wait_recv()

    def expert(el):
        each("core_wait", el)
        for kind, there in enumerate((rows_ref, gate_ref, grad_ref)):
            swap_wait(kind, there, el)

        @pl.loop(0, sources)
        def _(source):
            at = source_rows(el, source)
            grad_ref[at, :] = (gate_ref[at, 0:1] * grad_ref[at, :].astype(F32)).astype(BF16)

        for begin in range(0, expert_rows, row_block):
            here = pl.ds(el * expert_rows + begin, row_block)
            float_ref[...] = jnp.zeros_like(float_ref)

            @pl.loop(0, chunks)
            def _(f):
                at = pl.ds(pl.multiple_of(f * FF_CHUNK, FF_CHUNK), FF_CHUNK)
                down_at = pl.ds(pl.multiple_of(el * hidden_width + f * FF_CHUNK, FF_CHUNK), FF_CHUNK)
                rows, grads = rows_ref[here, :], grad_ref[here, :]
                up_part, down_part = up_ref[el * width : (el + 1) * width, at], down_ref[down_at, :]
                hidden = dot(rows, up_part)
                spread = 0.5 * (1.0 + lax.erf(hidden * ROOT_HALF))
                active = (hidden * spread).astype(BF16)
                slope = spread + hidden * (DENSITY_SCALE * jnp.exp(-0.5 * hidden * hidden))
                float_ref[:row_block, :] += dot(active, down_part)
                grad_hidden = (dot_against(grads, down_part) * slope).astype(BF16)
                float_ref[row_block:, :] += dot_against(grad_hidden, up_part)
                size = up_in.shape[1]
                up_sum = dot_rows(rows, grad_hidden).reshape(A, B, 2, size, FF_CHUNK)
                if begin > 0:
                    up_sum += part_up[el, :, :, :, :, at].astype(F32)
                part_up[el, :, :, :, :, at] = up_sum.astype(BF16)
                down_sum = dot_rows(active, grads)
                at = pl.ds(pl.multiple_of(el * hidden_width + f * FF_CHUNK, FF_CHUNK), FF_CHUNK)
                if begin > 0:
                    down_sum += part_down_ref[at, :].astype(F32)
                part_down_ref[at, :] = down_sum.astype(BF16)
                if begin == 0 and el == 0:
                    pl.when(f == 1)(lambda: each("line_step", 1, 2))
                    pl.when(f == chunks // 2)(lambda: each("line_step", 1, 3))
                if begin == 0 and el > 0:
                    pl.when(f == 0)(lambda: all_scatters("core_step", el - 1))

            rows_ref[here, :] = float_ref[:row_block, :].astype(BF16)
            grad_ref[here, :] = float_ref[row_block:, :].astype(BF16)

        all_scatters("start", el)

        @pl.loop(1, sources)
        def _(k):
            peer = place.other_peer(k)
            returned(0, rows_ref, back_ref, el, peer).start()
            returned(1, grad_ref, grad_slots_ref, el, peer).start()

        own, target = source_rows(el, place.peer), slot_rows(place.peer * count + el)
        back_ref[target, :] = rows_ref[own, :]
        grad_slots_ref[target, :] = grad_ref[own, :]

    for el in range(count):
        expert(el)

    def late_loads():
        out = [copy_in(weights_save, up_ref.at[pl.ds(0, rows_pad), :], late_sem.at[0])]
        for i, array in enumerate((act_one_save, attended_save, act_two_save, cot_in)):
            out.append(copy_in(array, down_ref.at[pl.ds(i * rows_pad, rows_pad), :], late_sem.at[1 + i]))
        out.append(copy_in(mid_save, float_ref.at[pl.ds(0, rows_pad), :], late_sem.at[5]))
        return out

    for el in range(count):
        each("finish", el)
    for copy in late_loads():
        copy.start()
    act_one, attended, act_two, cot_ref = (down_ref.at[pl.ds(i * rows_pad, rows_pad), :] for i in range(4))
    weights_ref = up_ref
    input_grad_ref = float_ref
    all_scatters("core_step", count - 1)
    for copy in late_loads():
        copy.wait()
    for el in range(count):
        return_wait(0, back_ref, el)
    gain_one = small_rows[NORM_LANE : NORM_LANE + 1]
    gain_two = small_rows[NORM_LANE + 2 : NORM_LANE + 3]
    column_ref[...] = jnp.zeros_like(column_ref)

    @pl.loop(0, places // LANES)
    def _(c):
        at = pl.ds(pl.multiple_of(c * LANES, LANES), LANES)
        column = jnp.sum(back_ref[at, :].astype(F32) * cot_sent_ref[at, :].astype(F32), axis=1, keepdims=True)
        dot_row_ref[0:1, at] = to_row(column)

    for el in range(count):
        return_wait(1, grad_slots_ref, el)

    def stores(g):
        rows = rows_of(g)
        return (
            copy_in(cot_ref.at[rows, :], out_out.at[rows, :], store_sem.at[0, g]),
            copy_in(input_grad_ref.at[rows, :], input_grad_out.at[rows, :], store_sem.at[1, g]),
        )

    @pl.loop(0, groups)
    def _(g):
        rows = rows_of(g)
        meta = meta_ref[rows, :]
        probs = probs_ref[rows, :]
        gate_first, gate_second = gates_of(probs, meta)
        lane = iota((BLOCK, LANES), 1)
        grad_first = jnp.zeros((BLOCK, LANES), F32)
        grad_second = jnp.zeros((BLOCK, LANES), F32)
        for c in range(places // LANES):
            at = c * LANES
            in_first = lane == meta[:, 0:1] - at
            in_second = lane == meta[:, 1:2] - at
            place_ref[:, at : at + LANES] = jnp.where(jnp.logical_or(in_first, in_second), 1.0, 0.0).astype(BF16)
            gated_ref[:, at : at + LANES] = jnp.where(in_first, gate_first, jnp.where(in_second, gate_second, 0.0)).astype(BF16)
            dots = dot_row_ref[0:1, at : at + LANES]
            grad_first += jnp.where(in_first, dots, 0.0)
            grad_second += jnp.where(in_second, dots, 0.0)
        grad_first = jnp.sum(grad_first, axis=1, keepdims=True)
        grad_second = jnp.sum(grad_second, axis=1, keepdims=True)
        mid = input_grad_ref[rows, :]
        grad_probs = jnp.where(lane == meta[:, 2:3], grad_first, 0.0) + jnp.where(lane == meta[:, 3:4], grad_second, 0.0)
        grad_logits = (probs * (grad_probs - jnp.sum(grad_probs * probs, axis=-1, keepdims=True))).astype(BF16)
        logit_grad_ref[rows, :] = grad_logits
        grad_act = dot(place_ref[...], grad_slots_ref[...]) + dot_against(grad_logits, small)
        normed, inverse = normalize(mid)
        column_ref[NORM_LANE + 2 : NORM_LANE + 3, :] += jnp.sum(grad_act * normed, axis=0, keepdims=True)
        column_ref[NORM_LANE + 3 : NORM_LANE + 4, :] += jnp.sum(grad_act, axis=0, keepdims=True)
        grad_mid = cot_ref[rows, :].astype(F32) + denormalize(grad_act, normed, inverse, gain_two)
        cot_ref[rows, :] = (mid + dot(gated_ref[...], back_ref[...])).astype(BF16)
        input_grad_ref[rows, :] = grad_mid
        grad_attended = dot_against(grad_mid.astype(BF16), params_ref[:, 3 * width : 4 * width]).astype(BF16)
        low = lane < HEAD_DIM
        for pair in range(HEADS // 2):
            at = pair * LANES
            q = triple_ref[rows, at : at + LANES] * HEAD_DIM ** (-0.5)
            k = triple_ref[rows, width + at : width + at + LANES]
            v = triple_ref[rows, 2 * width + at : 2 * width + at + LANES]
            upstream = grad_attended[:, at : at + LANES]
            grad_q = grad_k = grad_v = jnp.zeros((BLOCK, LANES), F32)
            for half in range(2):
                mask = low if half == 0 else jnp.logical_not(low)
                upstream_half = jnp.where(mask, upstream, 0.0).astype(BF16)
                head = (2 * pair + half) * BLOCK
                weights = weights_ref[rows, head : head + BLOCK]
                kept = weights.astype(F32)
                grad_weights = dot_against(upstream_half, v)
                inner = jnp.sum(grad_weights * kept, axis=-1, keepdims=True)
                grad_scores = (kept * (grad_weights - inner)).astype(BF16)
                grad_q += dot(grad_scores, jnp.where(mask, k, 0.0).astype(BF16))
                grad_k += dot_rows(grad_scores, jnp.where(mask, q, 0.0).astype(BF16))
                grad_v += dot_rows(weights, upstream_half)
            triple_ref[rows, at : at + LANES] = (grad_q * HEAD_DIM ** (-0.5)).astype(BF16)
            triple_ref[rows, width + at : width + at + LANES] = grad_k.astype(BF16)
            triple_ref[rows, 2 * width + at : 2 * width + at + LANES] = grad_v.astype(BF16)
        grad_act = dot_against(triple_ref[rows, :], params_ref[:, : 3 * width])
        normed, inverse = normalize(x_ref[rows, :].astype(F32))
        column_ref[NORM_LANE : NORM_LANE + 1, :] += jnp.sum(grad_act * normed, axis=0, keepdims=True)
        column_ref[NORM_LANE + 1 : NORM_LANE + 2, :] += jnp.sum(grad_act, axis=0, keepdims=True)
        grad_mid = input_grad_ref[rows, :]
        x_ref[rows, :] = grad_mid.astype(BF16)
        input_grad_ref[rows, :] = grad_mid + denormalize(grad_act, normed, inverse, gain_one)
        for copy in stores(g):
            copy.start()
        pl.when(g == 1)(lambda: all_scatters("line_step", 0))

    size = up_in.shape[1]
    split = (A, B, 2, size)
    part_up[0, :, :, :, :, : 3 * width] = dot_rows(act_one[...], triple_ref[...]).astype(BF16).reshape(*split, 3 * width)
    part_up[0, :, :, :, :, 3 * width : 4 * width] = dot_rows(attended[...], x_ref[...]).astype(BF16).reshape(*split, width)
    small_part = dot_rows(act_two[...], logit_grad_ref[...]) + jnp.transpose(column_ref[...])
    part_up[0, :, :, :, :, 4 * width :] = small_part.astype(BF16).reshape(*split, LANES)
    par.start(0)
    par.core_step(0)
    par.across_step(0)
    for el in range(1, count):
        all_scatters("line_step", el)
    swap_ref[place.x] = par.line_step(0).astype(BF16)

    def shares():
        out = []
        for k in range(1, xs):
            to, back = lax.rem(place.x + k, xs), xs - 1 - k
            out.append(
                pltpu.make_async_remote_copy(
                    src_ref=swap_ref.at[place.x], dst_ref=swap_ref.at[place.x],
                    send_sem=share_send.at[back], recv_sem=share_recv.at[back],
                    device_id=(to, place.me), device_id_type=MESH,
                )
            )
        return out

    for copy in shares():
        copy.start()

    @pl.loop(0, groups)
    def _(g):
        for copy in stores(g):
            copy.wait()

    params.finish_send()
    for el in range(count):

        @pl.loop(1, sources)
        def _(k):
            peer = place.other_peer(k)
            swap(0, sent_ref, rows_ref, el, peer).wait_send()
            swap(1, gate_sent_ref, gate_ref, el, peer).wait_send()
            swap(2, cot_sent_ref, grad_ref, el, peer).wait_send()
            returned(0, rows_ref, back_ref, el, peer).wait_send()
            returned(1, grad_ref, grad_slots_ref, el, peer).wait_send()

        all_scatters("finish", el)
    par.finish(0)
    for copy in shares():
        copy.wait()
    total = swap_ref[0].astype(F32)
    for i in range(1, xs):
        total += swap_ref[i].astype(F32)
    share_out[...] = total


def on_device(
    inputs, cotangent, routes, slots, qkv_weight, out_weight, router_weight,
    norm1_gain, norm1_shift, norm2_gain, norm2_shift, expert_up, expert_down,
):
    rows_dev, width = inputs.shape
    groups = rows_dev // GROUP_ROWS
    rows_pad = groups * BLOCK
    fsdp = lax.axis_size("fsdp")
    peers = lax.axis_size("expert")
    held = expert_up.shape[0]
    experts = held * peers
    capacity = (42 * rows_dev + 20 * experts - 1) // (20 * experts)
    capacity = -(-capacity // 16) * 16
    places = experts * capacity

    def pad_rows(array, value=0):
        array = array.reshape(groups, GROUP_ROWS, array.shape[1])
        array = jnp.pad(array, ((0, 0), (0, BLOCK - GROUP_ROWS), (0, 0)), constant_values=value)
        return array.reshape(rows_pad, array.shape[2])

    def cut_rows(array):
        return array.reshape(groups, BLOCK, width)[:, :GROUP_ROWS].reshape(rows_dev, width)

    norms = jnp.stack([norm1_gain, norm1_shift, norm2_gain, norm2_shift], axis=1)
    shard = jnp.concatenate(
        [
            qkv_weight,
            out_weight,
            jnp.pad(router_weight, ((0, 0), (0, NORM_LANE - experts))),
            jnp.pad(norms, ((0, 0), (0, LANES - NORM_LANE - 4))),
        ],
        axis=1,
    )
    x = pad_rows(inputs)
    cot = pad_rows(cotangent)
    targets = jnp.where(slots >= 0, routes * capacity + slots, -1)
    meta = pad_rows(jnp.concatenate([targets, routes], axis=1), -1)
    meta_row = jnp.transpose(meta)

    vmem = pl.BlockSpec(memory_space=pltpu.VMEM)
    hbm = pl.BlockSpec(memory_space=pl.ANY)
    shape = jax.ShapeDtypeStruct
    dma = pltpu.SemaphoreType.DMA
    A, B = 4, fsdp // 8
    count = held // B
    sources = peers * B
    up_rows, down_rows = expert_up.shape[1], expert_down.shape[1]
    hidden_width = expert_up.shape[2]
    packed_width = shard.shape[1]
    expert_rows = sources * capacity
    row_block = max(n for n in range(16, MAX_ROWS + 1, 16) if expert_rows % n == 0)
    routes_of = 3 + B - 1

    def buffer(*dims, dtype=BF16):
        return pltpu.VMEM(dims, dtype)

    out, input_grad, share, up_grad, down_grad, *_ = pl.pallas_call(
        functools.partial(block_kernel, experts, fsdp, peers, count),
        out_shape=(
            shape((rows_pad, width), BF16),
            shape((rows_pad, width), F32),
            shape((up_rows, packed_width), F32),
            shape(expert_up.shape, BF16),
            shape(expert_down.shape, BF16),
            shape((rows_pad, width), BF16),
            shape((rows_pad, HEADS * BLOCK), BF16),
            shape((rows_pad, width), BF16),
            shape((rows_pad, width), F32),
            shape((rows_pad, width), BF16),
        ),
        in_specs=[hbm] * 2 + [vmem] * 3 + [hbm] * 2,
        out_specs=[hbm] * 2 + [vmem] + [hbm] * 7,
        scratch_shapes=[
            buffer(rows_pad, width), buffer(fsdp * up_rows, packed_width), buffer(rows_pad, 3 * width),
            buffer(rows_pad, LANES, dtype=F32),
            buffer(places, width), buffer(places, width), buffer(places, LANES, dtype=F32),
            buffer(places, width), buffer(places, width), buffer(places, LANES, dtype=F32),
            buffer(places, width), buffer(places, width),
            buffer(max(count * width, rows_pad), hidden_width), buffer(max(count * hidden_width, 4 * rows_pad), width),
            buffer(max(count * width, rows_pad), packed_width), buffer(max(count * hidden_width, 4 * rows_pad), width),
            buffer(max(2 * row_block, rows_pad), width, dtype=F32),
            buffer(count, A, B, up_rows, hidden_width), buffer(count, A, B, down_rows, width),
            buffer(count, A - 1, B, up_rows, hidden_width), buffer(count, A - 1, B, down_rows, width),
            buffer(1, A, B, up_rows, packed_width), buffer(1, B - 1, A, up_rows, packed_width),
            buffer(1, A - 1, up_rows, packed_width), buffer(peers, up_rows, packed_width),
            buffer(BLOCK, BLOCK, dtype=F32), buffer(8, rows_pad, dtype=F32), buffer(8, places, dtype=F32),
            buffer(BLOCK, places), buffer(BLOCK, places), buffer(rows_pad, LANES), buffer(LANES, width, dtype=F32),
            dma((2,)), dma((5, groups)), dma((6,)), dma((2, groups)),
            dma((fsdp, routes_of)), dma((fsdp,)), dma,
            dma((2, count, fsdp, routes_of)), dma((2, count, fsdp)), dma((2, count)),
            dma((3, experts)), dma((3, count, sources)), dma((2, count, sources)), dma((2, count, sources)),
            dma((2, count, A + B - 1)), dma((2, count, A + B - 1)), dma((2, count)),
            dma((1, A + B - 1)), dma((1, A + B - 1)), dma((peers - 1,)), dma((peers - 1,)),
        ],
        compiler_params=pltpu.CompilerParams(vmem_limit_bytes=VMEM_LIMIT, collective_id=0, has_side_effects=True),
        name="encoder_block",
    )(x, cot, meta, meta_row, shard, expert_up, expert_down)
    norm_share = share[:, 4 * width + NORM_LANE : 4 * width + NORM_LANE + 4]
    return (
        cut_rows(out),
        cut_rows(input_grad),
        share[:, : 3 * width],
        share[:, 3 * width : 4 * width],
        share[:, 4 * width : 4 * width + experts],
        norm_share[:, 0],
        norm_share[:, 1],
        norm_share[:, 2],
        norm_share[:, 3],
        up_grad.astype(F32),
        down_grad.astype(F32),
    )


def solution(mesh):
    tokens = P(("expert", "fsdp"), None)
    rows, vector, expert = P("fsdp", None), P("fsdp"), P("expert", "fsdp", None)
    return jax.shard_map(
        on_device,
        mesh=mesh,
        in_specs=(tokens,) * 4 + (rows,) * 3 + (vector,) * 4 + (expert,) * 2,
        out_specs=(tokens,) * 2 + (rows,) * 3 + (vector,) * 4 + (expert,) * 2,
        check_vma=False,
    )
```

```python
import functools

import jax
import jax.numpy as jnp
from jax import lax
from jax.experimental import pallas as pl
from jax.experimental.pallas import tpu as pltpu
from jax.sharding import PartitionSpec as P

HEADS = 8
HEAD_DIM = 64
PATCHES = 49
EPS = 1e-06
ROOT_HALF = 0.7071067811865476
DENSITY_SCALE = 0.3989422804014327

BLOCK = 256
GROUP_IMAGES = BLOCK // PATCHES
GROUP_ROWS = GROUP_IMAGES * PATCHES
LANES = 128
NORM_LANE = 64
FF_CHUNK = 512
MAX_ROWS = 640
VMEM_LIMIT = 62 * 1024 * 1024

MESH = pl.DeviceIdType.MESH
PLAN = {
    ("start", 0): [("across", 0)],
    ("start", 1): [("own", 0)],
    ("start", 3): [("passed", 0)],
    ("begin", 0): [("relay", 0, 1, True), ("cots", 0)],
    ("middle", 1): [("relay", 0, 1, False), ("relay", 0, 2, True)],
    ("end", 1): [("across", 1)],
    ("end", 2): [("own", 1)],
    ("middle", 3): [("relay", 0, 2, False), ("relay", 0, 3, True)],
    ("end", 3): [("passed", 1)],
    ("dispatch", 7): [("relay", 0, 3, False), ("relay", 1, 1, True)],
    ("before", 0, 0): [("rows", 1)],
    ("expert", 0, 0): [("relay", 1, 1, False)],
    ("expert", 0, 1): [("cots", 1), ("relay", 1, 2, True)],
    ("expert", 0, 3): [("relay", 1, 2, False)],
    ("expert", 0, 6): [("relay", 1, 3, True)],
    ("expert", 0, 7): [("relay", 1, 3, False)],
    ("expert", 1, 0): [("sums", 0), ("sum_relay", 0, 0)],
    ("expert", 1, 4): [("outputs", 0)],
    ("expert", 1, 5): [("sum_relay", 0, 1)],
}
F32 = jnp.float32
BF16 = jnp.bfloat16


def dot(left, right):
    return lax.dot_general(left, right, (((1,), (0,)), ((), ())), preferred_element_type=F32)


def dot_rows(left, right):
    return lax.dot_general(left, right, (((0,), (0,)), ((), ())), preferred_element_type=F32)


def dot_against(left, right):
    return lax.dot_general(left, right, (((1,), (1,)), ((), ())), preferred_element_type=F32)


def iota(shape, dim):
    return lax.broadcasted_iota(jnp.int32, shape, dim)


def normalize(values):
    center = jnp.mean(values, axis=-1, keepdims=True)
    offset = values - center
    spread = jnp.mean(offset * offset, axis=-1, keepdims=True)
    inverse = lax.rsqrt(spread + EPS)
    return offset * inverse, inverse


def denormalize(upstream, normed, inverse, gain):
    scaled = upstream * gain
    return inverse * (
        scaled
        - jnp.mean(scaled, axis=-1, keepdims=True)
        - normed * jnp.mean(scaled * normed, axis=-1, keepdims=True)
    )


def to_row(column):
    n = column.shape[0]
    parts = []
    for at in range(0, n, LANES):
        size = min(LANES, n - at)
        eye = iota((size, LANES), 0) == iota((size, LANES), 1)
        parts.append(jnp.sum(jnp.where(eye, column[at : at + size], 0.0), axis=0, keepdims=True))
    return parts[0] if len(parts) == 1 else jnp.concatenate(parts, axis=1)


def to_column(row, n):
    eye = iota((n, row.shape[1]), 0) == iota((n, row.shape[1]), 1)
    return jnp.sum(jnp.where(eye, row, 0.0), axis=1, keepdims=True)


def rows_of(g):
    return pl.ds(pl.multiple_of(g * BLOCK, BLOCK), BLOCK)


def gates_of(probs, meta):
    lane = iota(probs.shape, 1)
    first = jnp.sum(jnp.where(lane == meta[:, 2:3], probs, 0.0), axis=1, keepdims=True)
    second = jnp.sum(jnp.where(lane == meta[:, 3:4], probs, 0.0), axis=1, keepdims=True)
    return first, second


class Place:
    def __init__(self, fsdp, xs):
        self.A, self.B = 4, fsdp // 8
        self.x = lax.axis_index("expert")
        self.me = lax.axis_index("fsdp")
        self.c = lax.rem(self.me, 2)
        line = lax.div(self.me, 2)
        self.b = lax.rem(line, self.B)
        self.a = lax.div(line, self.B)
        self.xs, self.peers = xs, xs * self.B
        self.peer = self.x * self.B + self.b

    def index(self, a, b, c):
        return (a * self.B + b) * 2 + c

    def other_b(self, j):
        return lax.rem(self.b + 1 + j, self.B)

    def at(self, a, b, c):
        return (self.x, self.index(a, b, c))

    def at_peer(self, peer):
        return (lax.div(peer, self.B), self.index(self.a, lax.rem(peer, self.B), self.c))

    def other_peer(self, k):
        x, b = lax.rem(self.x + lax.rem(k, self.xs), self.xs), lax.rem(self.b + lax.div(k, self.xs), self.B)
        return x * self.B + b

    def seen_from(self, k):
        x, b = lax.rem(self.xs - lax.rem(k, self.xs), self.xs), lax.rem(self.B - lax.div(k, self.xs), self.B)
        return b * self.xs + x


def greet(place, meanwhile):
    barrier = pltpu.get_barrier_semaphore()

    def signal(device):
        pl.semaphore_signal(barrier, inc=1, device_id=device, device_id_type=MESH)

    for k in range(1, place.A):
        signal(place.at(lax.rem(place.a + k, place.A), place.b, place.c))
    for k in range(1, place.peers):
        signal(place.at_peer(place.other_peer(k)))
    signal(place.at(place.a, place.b, 1 - place.c))
    meanwhile()
    pl.semaphore_wait(barrier, place.A - 1 + place.peers - 1 + 1)


class Gather:
    RIGHT, LEFT, CORE, ACROSS = 0, 1, 2, 3

    def __init__(self, place, own, full, block, send_sem, recv_sem, local_sem):
        self.place, self.own, self.full, self.block = place, own, full, block
        self.send_sem, self.recv_sem, self.local_sem = send_sem, recv_sem, local_sem

    def copy(self, shard, route, source, a, b, c):
        return pltpu.make_async_remote_copy(
            src_ref=source, dst_ref=self.block(self.full, shard),
            send_sem=self.send_sem.at[shard, route], recv_sem=self.recv_sem.at[shard],
            device_id=self.place.at(a, b, c), device_id_type=MESH,
        )

    def onward(self, shard, source, right, left, across, act):
        p = self.place
        if right is not None:
            pl.when(right)(lambda: act(self.copy(shard, self.RIGHT, source, p.a + 1, p.b, p.c)))
        if left is not None:
            pl.when(left)(lambda: act(self.copy(shard, self.LEFT, source, p.a - 1, p.b, p.c)))
        if across:
            for j in range(p.B - 1):
                act(self.copy(shard, self.ACROSS + j, source, p.a, p.other_b(j), p.c))
        act(self.copy(shard, self.CORE, source, p.a, p.b, 1 - p.c))

    def local(self):
        return pltpu.make_async_copy(self.own, self.block(self.full, self.place.me), self.local_sem)

    def start(self):
        p = self.place
        self.local().start()
        self.onward(p.me, self.own, p.a < p.A - 1, p.a > 0, True, lambda copy: copy.start())

    def arrived(self, shard):
        p = self.place
        self.copy(shard, self.CORE, self.block(self.full, shard), p.a, p.b, 1 - p.c).wait_recv()

    def line_step(self, k):
        p = self.place

        def from_left():
            shard = p.index(p.a - k, p.b, p.c)
            self.arrived(shard)
            self.onward(shard, self.block(self.full, shard), p.a < p.A - 1, None, True, lambda copy: copy.start())

        def from_right():
            shard = p.index(p.a + k, p.b, p.c)
            self.arrived(shard)
            self.onward(shard, self.block(self.full, shard), None, p.a > 0, True, lambda copy: copy.start())

        pl.when(p.a - k >= 0)(from_left)
        pl.when(p.a + k < p.A)(from_right)

    def across_step(self, k):
        p = self.place

        def row(a):
            for j in range(p.B - 1):
                shard = p.index(a, p.other_b(j), p.c)
                self.arrived(shard)
                self.onward(shard, self.block(self.full, shard), None, None, False, lambda copy: copy.start())

        if k == 0:
            row(p.a)
        else:
            pl.when(p.a - k >= 0)(lambda: row(p.a - k))
            pl.when(p.a + k < p.A)(lambda: row(p.a + k))

    def finish_recv(self):
        p = self.place
        self.local().wait()
        for a in range(p.A):
            for b in range(p.B):
                self.arrived(p.index(a, b, 1 - p.c))

    def finish_send(self):
        p = self.place
        wait = lambda copy: copy.wait_send()
        self.onward(p.me, self.own, p.a < p.A - 1, p.a > 0, True, wait)
        for k in range(1, p.A):

            def from_left(k=k):
                shard = p.index(p.a - k, p.b, p.c)
                self.onward(shard, self.block(self.full, shard), p.a < p.A - 1, None, True, wait)

            def from_right(k=k):
                shard = p.index(p.a + k, p.b, p.c)
                self.onward(shard, self.block(self.full, shard), None, p.a > 0, True, wait)

            pl.when(p.a - k >= 0)(from_left)
            pl.when(p.a + k < p.A)(from_right)
        for a in range(p.A):
            for j in range(p.B - 1):
                shard = p.index(a, p.other_b(j), p.c)
                self.onward(shard, self.block(self.full, shard), None, None, False, wait)


class ExpertGather:
    RIGHT, LEFT, CORE, ACROSS = 0, 1, 2, 3

    def __init__(self, place, own, full, count, send_sem, recv_sem, local_sem):
        self.place, self.own, self.full, self.count = place, own, full, count
        self.send_sem, self.recv_sem, self.local_sem = send_sem, recv_sem, local_sem
        self.size = own.shape[1]
        self.depth = self.size * place.A * place.B * 2

    def block(self, el, shard):
        return self.full.at[pl.ds(pl.multiple_of(el * self.depth + shard * self.size, self.size), self.size), :]

    def mine(self, el):
        return self.own.at[self.place.b * self.count + el]

    def copy(self, el, shard, route, source, a, b, c):
        return pltpu.make_async_remote_copy(
            src_ref=source, dst_ref=self.block(el, shard),
            send_sem=self.send_sem.at[el, shard, route], recv_sem=self.recv_sem.at[el, shard],
            device_id=self.place.at(a, b, c), device_id_type=MESH,
        )

    def across(self, el):
        p = self.place
        out = []
        for j in range(p.B - 1):
            to = p.other_b(j)
            out.append(self.copy(el, p.me, self.ACROSS + j, self.own.at[to * self.count + el], p.a, to, p.c))
        return out

    def local(self, el):
        return pltpu.make_async_copy(self.mine(el), self.block(el, self.place.me), self.local_sem.at[el])

    def onward(self, el, shard, source, right, left, act):
        p = self.place
        if right:
            pl.when(p.a < p.A - 1)(lambda: act(self.copy(el, shard, self.RIGHT, source, p.a + 1, p.b, p.c)))
        if left:
            pl.when(p.a > 0)(lambda: act(self.copy(el, shard, self.LEFT, source, p.a - 1, p.b, p.c)))
        act(self.copy(el, shard, self.CORE, source, p.a, p.b, 1 - p.c))

    def arrived(self, el, shard):
        p = self.place
        self.copy(el, shard, self.CORE, self.block(el, shard), p.a, p.b, 1 - p.c).wait_recv()

    def start_across(self, el):
        for copy in self.across(el):
            copy.start()

    def start_own(self, el):
        self.local(el).start()
        self.onward(el, self.place.me, self.mine(el), True, True, lambda copy: copy.start())

    def across_step(self, el):
        p = self.place
        for j in range(p.B - 1):
            shard = p.index(p.a, p.other_b(j), p.c)
            self.arrived(el, shard)
            self.onward(el, shard, self.block(el, shard), True, True, lambda copy: copy.start())

    def line_step(self, el, k, own):
        p = self.place

        def row(a, right, left):
            for b in [p.b] if own else [p.other_b(j) for j in range(p.B - 1)]:
                shard = p.index(a, b, p.c)
                self.arrived(el, shard)
                self.onward(el, shard, self.block(el, shard), right, left, lambda copy: copy.start())

        pl.when(p.a - k >= 0)(lambda: row(p.a - k, True, False))
        pl.when(p.a + k < p.A)(lambda: row(p.a + k, False, True))

    def core_wait(self, el):
        p = self.place
        self.local(el).wait()
        for a in range(p.A):
            for b in range(p.B):
                self.arrived(el, p.index(a, b, 1 - p.c))

    def finish(self, el):
        p = self.place
        wait = lambda copy: copy.wait_send()
        for copy in self.across(el):
            wait(copy)
        self.onward(el, p.me, self.mine(el), True, True, wait)
        for j in range(p.B - 1):
            shard = p.index(p.a, p.other_b(j), p.c)
            self.onward(el, shard, self.block(el, shard), True, True, wait)

        def row(a, right, left):
            for b in range(p.B):
                shard = p.index(a, b, p.c)
                self.onward(el, shard, self.block(el, shard), right, left, wait)

        for k in range(1, p.A):
            pl.when(p.a - k >= 0)(functools.partial(row, p.a - k, True, False))
            pl.when(p.a + k < p.A)(functools.partial(row, p.a + k, False, True))


class ExpertScatter:
    def __init__(self, place, part, sums, line, out, count, send, recv, local_sem):
        self.place, self.part, self.sums, self.line, self.out, self.count = place, part, sums, line, out, count
        self.send, self.recv, self.local_sem = send, recv, local_sem

    def remote(self, source, target, el, route, a, b, c):
        return pltpu.make_async_remote_copy(
            src_ref=source, dst_ref=target, send_sem=self.send.at[el, route], recv_sem=self.recv.at[el, route],
            device_id=self.place.at(a, b, c), device_id_type=MESH,
        )

    def core_copy(self, el):
        p = self.place
        return self.remote(self.part(el).at[:, :, 1 - p.c], self.sums.at[el], el, 0, p.a, p.b, 1 - p.c)

    def right_copy(self, el, target):
        p = self.place
        return self.remote(self.sums.at[el, target], self.line.at[el, 0, target - 1], el, target, p.a + 1, p.b, p.c)

    def left_copy(self, el, target):
        p = self.place
        return self.remote(self.sums.at[el, target], self.line.at[el, 1, target], el, p.A + target, p.a - 1, p.b, p.c)

    def add(self, el, target, way, slot):
        @pl.loop(0, self.place.B)
        def _(b):
            total = self.sums[el, target, b].astype(F32) + self.line[el, way, slot, b].astype(F32)
            self.sums[el, target, b] = total.astype(BF16)

    def relay_step(self, el, step):
        p = self.place

        @pl.when(p.a <= step)
        def _():
            target = p.a + p.A - 1 - step

            @pl.when(p.a > 0)
            def _():
                self.right_copy(el, target).wait_recv()
                self.add(el, target, 0, target - 1)

            self.right_copy(el, target).start()

        @pl.when(p.a >= p.A - 1 - step)
        def _():
            target = p.a - (p.A - 1 - step)

            @pl.when(p.a < p.A - 1)
            def _():
                self.left_copy(el, target).wait_recv()
                self.add(el, target, 1, target)

            self.left_copy(el, target).start()

    def last_copies(self, el):
        p = self.place
        out = []
        for j in range(p.B - 1):
            to, back = p.other_b(j), p.B - 2 - j
            target = self.out.at[p.b * self.count + el]
            out.append(self.remote(self.sums.at[el, p.a, to], target, el, 2 * p.A - 1 + back, p.a, to, p.c))
        return out

    def local(self, el):
        p = self.place
        return pltpu.make_async_copy(self.sums.at[el, p.a, p.b], self.out.at[p.b * self.count + el], self.local_sem.at[el])

    def start(self, el):
        self.core_copy(el).start()

    def core_step(self, el):
        p = self.place
        self.core_copy(el).wait()
        part = self.part(el)

        @pl.loop(0, p.A * p.B)
        def _(i):
            a, b = lax.div(i, p.B), lax.rem(i, p.B)
            total = self.sums[el, a, b].astype(F32) + part[a, b, p.c].astype(F32)
            self.sums[el, a, b] = total.astype(BF16)

    def line_step(self, el):
        p = self.place

        @pl.when(p.a > 0)
        def _():
            self.right_copy(el, p.a).wait_recv()
            self.add(el, p.a, 0, p.a - 1)

        @pl.when(p.a < p.A - 1)
        def _():
            self.left_copy(el, p.a).wait_recv()
            self.add(el, p.a, 1, p.a)

        for copy in self.last_copies(el) + [self.local(el)]:
            copy.start()

    def finish(self, el):
        p = self.place
        for target in range(1, p.A):
            pl.when(p.a < target)(self.right_copy(el, target).wait_send)
        for target in range(p.A - 1):
            pl.when(p.a > target)(self.left_copy(el, target).wait_send)
        for copy in self.last_copies(el) + [self.local(el)]:
            copy.wait()


class Scatter:
    def __init__(self, place, part, sums, across, line, send, recv):
        self.place, self.part, self.sums, self.across, self.line = place, part, sums, across, line
        self.send, self.recv = send, recv

    def remote(self, source, target, item, route, a, b, c):
        return pltpu.make_async_remote_copy(
            src_ref=source, dst_ref=target, send_sem=self.send.at[item, route], recv_sem=self.recv.at[item, route],
            device_id=self.place.at(a, b, c), device_id_type=MESH,
        )

    def core_copy(self, item):
        p = self.place
        return self.remote(self.part(item).at[:, :, 1 - p.c], self.sums.at[item], item, 0, p.a, p.b, 1 - p.c)

    def across_copies(self, item):
        p = self.place
        out = []
        for j in range(p.B - 1):
            to, back = p.other_b(j), p.B - 2 - j
            copy = self.remote(self.sums.at[item, :, to], self.across.at[item, back], item, 1 + back, p.a, to, p.c)
            out.append(copy)
        return out

    def line_copies(self, item):
        p = self.place
        out = []
        for k in range(1, p.A):
            to, back = lax.rem(p.a + k, p.A), p.A - 1 - k
            copy = self.remote(self.sums.at[item, to, p.b], self.line.at[item, back], item, p.B + back, to, p.b, p.c)
            out.append(copy)
        return out

    def start(self, item):
        self.core_copy(item).start()

    def core_step(self, item):
        p = self.place
        self.core_copy(item).wait()
        part = self.part(item)

        @pl.loop(0, p.A * p.B)
        def _(i):
            a, b = lax.div(i, p.B), lax.rem(i, p.B)
            total = self.sums[item, a, b].astype(F32) + part[a, b, p.c].astype(F32)
            self.sums[item, a, b] = total.astype(BF16)

        for copy in self.across_copies(item):
            copy.start()

    def across_step(self, item):
        p = self.place
        for copy in self.across_copies(item):
            copy.wait_recv()

        @pl.loop(0, p.A)
        def _(a):
            total = self.sums[item, a, p.b].astype(F32)
            for j in range(p.B - 1):
                total += self.across[item, j, a].astype(F32)
            self.sums[item, a, p.b] = total.astype(BF16)

        for copy in self.line_copies(item):
            copy.start()

    def line_step(self, item):
        p = self.place
        for copy in self.line_copies(item):
            copy.wait_recv()
        total = self.sums[item, p.a, p.b].astype(F32)
        for k in range(p.A - 1):
            total += self.line[item, k].astype(F32)
        return total

    def finish(self, item):
        for copy in self.across_copies(item) + self.line_copies(item):
            copy.wait_send()


def block_kernel(
    experts, fsdp, xs, count,
    x_in, cot_in, routes_ref, slots_ref, qkv_ref, out_ref, router_ref, gain_one_ref, shift_one_ref, gain_two_ref, shift_two_ref,
    up_in, down_in,
    out_out, input_grad_out, share_out, up_grad_out, down_grad_out,
    act_one_save, weights_save, attended_save, mid_save, act_two_save,
    x_raw, cot_raw, shard_ref, meta_row_ref, meta_ref, x_ref, params_ref, triple_ref, probs_ref,
    sent_ref, cot_sent_ref, gate_sent_ref, rows_ref, grad_ref, gate_ref, back_ref, grad_slots_ref, dots_sent_ref, dots_ref,
    up_ref, down_ref, part_up_ref, part_down_ref, float_ref,
    sums_up, sums_down, line_up, line_down, sums_par, across_par, line_par, swap_ref,
    bias_ref, gate_rows_ref, dot_row_ref, place_ref, gated_ref, logit_grad_ref, column_ref,
    load_sem, save_sem, late_sem, store_sem, par_gather_send, par_gather_recv, par_gather_local,
    gather_send, gather_recv, gather_local, swap_send, swap_recv, return_send, return_recv,
    scatter_send, scatter_recv, scatter_local, par_send, par_recv, share_send, share_recv,
):
    rows_pad, width = x_ref.shape
    groups = rows_pad // BLOCK
    places = sent_ref.shape[0]
    capacity = places // experts
    hidden_width = up_ref.shape[1]
    chunks = hidden_width // FF_CHUNK
    held = up_in.shape[0]
    place = Place(fsdp, xs)
    A, B, sources = place.A, place.B, place.peers
    expert_rows = sources * capacity
    row_block = gated_ref.shape[0]
    copy_in = pltpu.make_async_copy

    weights_ref = part_up_ref
    act_one, attended, act_two, cot_ref = (part_down_ref.at[pl.ds(i * rows_pad, rows_pad), :] for i in range(4))
    mid_ref = float_ref

    loads = [copy_in(x_in, x_raw, load_sem.at[0]), copy_in(cot_in, cot_raw, load_sem.at[1])]
    for copy in loads:
        copy.start()

    def spread(raw, there):
        for g in range(groups):
            there[g * BLOCK : g * BLOCK + GROUP_ROWS, :] = raw[g * GROUP_ROWS : (g + 1) * GROUP_ROWS, :]
            there[g * BLOCK + GROUP_ROWS : (g + 1) * BLOCK, :] = jnp.zeros((BLOCK - GROUP_ROWS, width), BF16)

    def prepare():
        shard_ref[:, : 3 * width] = qkv_ref[...]
        shard_ref[:, 3 * width : 4 * width] = out_ref[...]
        size = shard_ref.shape[0]
        eye = iota((size, size), 0) == iota((size, size), 1)
        lane = iota((size, LANES), 1)
        small = jnp.zeros((size, LANES), F32)
        for i, norm_ref in enumerate((gain_one_ref, shift_one_ref, gain_two_ref, shift_two_ref)):
            row = norm_ref[...].astype(F32).reshape(1, size)
            column = jnp.sum(jnp.where(eye, row, 0.0), axis=1, keepdims=True)
            small = jnp.where(lane == NORM_LANE + i, column, small)
        shard_ref[:, 4 * width :] = small.astype(BF16)
        shard_ref[:, 4 * width : 4 * width + experts] = jnp.transpose(router_ref[...].astype(F32)).astype(BF16)

    greet(place, prepare)

    def rows_block(ref, shard):
        size = shard_ref.shape[0]
        return ref.at[pl.ds(pl.multiple_of(shard * size, size), size), :]

    params = Gather(place, shard_ref, params_ref, rows_block, par_gather_send, par_gather_recv, par_gather_local)
    weights_in = [
        ExpertGather(place, own, full, count, gather_send.at[i], gather_recv.at[i], gather_local.at[i])
        for i, (own, full) in enumerate(((up_in, up_ref), (down_in, down_ref)))
    ]

    def each(step, el, *more):
        if el < count:
            for gather in weights_in:
                getattr(gather, step)(el, *more)

    def do(*point):
        for name, el, *more in PLAN.get(point, ()):
            if el < count:
                with jax.named_scope("_".join(map(str, (name, el, *more)))):
                    actions[name](el, *more)

    actions = {
        "across": lambda el: each("start_across", el),
        "own": lambda el: each("start_own", el),
        "passed": lambda el: each("across_step", el),
        "relay": lambda *more: each("line_step", *more),
        "cots": lambda el: cot_swaps(el),
        "rows": lambda el: row_swaps(el),
        "sums": lambda el: all_scatters("core_step", el),
        "sum_relay": lambda el, step: all_scatters("relay_step", el, step),
        "outputs": lambda el: give_back(2, el),
    }
    params.start()
    do("start", 0)
    targets = jnp.where(slots_ref[...] >= 0, routes_ref[...] * capacity + slots_ref[...], -1)
    meta_row_ref[...] = jnp.full(meta_row_ref.shape, -1, jnp.int32)
    for g in range(groups):
        at = slice(g * BLOCK, g * BLOCK + GROUP_ROWS)
        meta_row_ref[0:2, at] = targets[:, g * GROUP_ROWS : (g + 1) * GROUP_ROWS]
        meta_row_ref[2:4, at] = routes_ref[:, g * GROUP_ROWS : (g + 1) * GROUP_ROWS]
    image_row = iota((BLOCK, BLOCK), 0) // PATCHES
    image_col = iota((BLOCK, BLOCK), 1) // PATCHES
    bias_ref[...] = jnp.where(image_row == image_col, 0.0, -1e30)

    def slot_rows(e):
        return pl.ds(pl.multiple_of(e * capacity, 16), capacity)

    def source_rows(el, source):
        return pl.ds(pl.multiple_of(el * expert_rows + source * capacity, 16), capacity)

    def find(e):
        slot = iota((capacity, rows_pad), 0) + e * capacity
        in_first = slot == meta_row_ref[0:1, :]
        in_second = slot == meta_row_ref[1:2, :]
        return in_first, in_second, jnp.where(jnp.logical_or(in_first, in_second), 1.0, 0.0).astype(BF16)

    def swap(kind, el, k):
        peer, back = place.other_peer(k), place.seen_from(k)
        e = peer * count + el
        if kind == 1:
            source, target = gate_sent_ref.at[e], gate_ref.at[el * sources + back]
        else:
            here, there = (sent_ref, rows_ref) if kind == 0 else (cot_sent_ref, grad_ref)
            source, target = here.at[slot_rows(e), :], there.at[source_rows(el, back), :]
        return pltpu.make_async_remote_copy(
            src_ref=source, dst_ref=target, send_sem=swap_send.at[kind, el, k], recv_sem=swap_recv.at[kind, el, back],
            device_id=place.at_peer(peer), device_id_type=MESH,
        )

    def swap_wait(kind, el, k):
        if kind == 1:
            target = gate_ref.at[el * sources + k]
        else:
            target = (rows_ref if kind == 0 else grad_ref).at[source_rows(el, k), :]
        pltpu.make_async_remote_copy(
            src_ref=target, dst_ref=target, send_sem=swap_send.at[kind, el, k], recv_sem=swap_recv.at[kind, el, k],
            device_id=place.at_peer(place.other_peer(k)), device_id_type=MESH,
        ).wait_recv()

    def cot_swaps(el):
        @pl.loop(1, sources)
        def _(k):
            swap(2, el, k).start()

        grad_ref[source_rows(el, 0), :] = cot_sent_ref[slot_rows(place.peer * count + el), :]

    def row_swaps(el):
        @pl.loop(1, sources)
        def _(k):
            swap(0, el, k).start()
            swap(1, el, k).start()

    for copy in loads:
        copy.wait()
    spread(cot_raw, cot_ref)
    for k in range(1, A):
        params.line_step(k)
        do("start", k)
        params.across_step(k - 1)

        @pl.loop((k - 1) * experts // (A - 1), k * experts // (A - 1))
        def _(e):
            _, _, picks = find(e)
            cot_sent_ref[slot_rows(e), :] = dot(picks, cot_ref[...]).astype(BF16)

        if k == 1:
            spread(x_raw, x_ref)
            meta_ref[...] = jnp.transpose(meta_row_ref[...])

    params.across_step(A - 1)
    params.finish_recv()
    do("begin", 0)

    small = params_ref[:, 4 * width :]
    small_rows = jnp.transpose(small.astype(F32))

    def saves(g):
        rows = rows_of(g)
        pairs = (
            (act_one, act_one_save), (weights_ref.at[:, pl.ds(0, HEADS * BLOCK)], weights_save), (attended, attended_save),
            (mid_ref, mid_save), (act_two, act_two_save),
        )
        return [
            copy_in(here.at[rows, :], there.at[rows, :], save_sem.at[i, g]) for i, (here, there) in enumerate(pairs)
        ]

    @pl.loop(0, groups)
    def _(g):
        rows = rows_of(g)
        x = x_ref[rows, :].astype(F32)
        normed, _ = normalize(x)
        act = (normed * small_rows[NORM_LANE : NORM_LANE + 1] + small_rows[NORM_LANE + 1 : NORM_LANE + 2]).astype(BF16)
        act_one[rows, :] = act
        triple_ref[rows, :] = dot(act, params_ref[:, : 3 * width]).astype(BF16)
        low = iota((BLOCK, LANES), 1) < HEAD_DIM
        for pair in range(HEADS // 2):
            at = pair * LANES
            q = triple_ref[rows, at : at + LANES] * HEAD_DIM ** (-0.5)
            k = triple_ref[rows, width + at : width + at + LANES]
            v = triple_ref[rows, 2 * width + at : 2 * width + at + LANES]
            total = None
            for half in range(2):
                mask = low if half == 0 else jnp.logical_not(low)
                scores = dot_against(jnp.where(mask, q, 0.0).astype(BF16), k) + bias_ref[...]
                top = jnp.max(scores, axis=-1, keepdims=True)
                raised = jnp.exp(scores - top)
                probs = raised / jnp.sum(raised, axis=-1, keepdims=True)
                probs = probs.astype(BF16)
                head = (2 * pair + half) * BLOCK
                weights_ref[rows, head : head + BLOCK] = probs
                part = dot(probs, jnp.where(mask, v, 0.0).astype(BF16))
                total = part if total is None else total + part
            attended[rows, at : at + LANES] = total.astype(BF16)

        for i in range(groups):
            pl.when(g == i)(functools.partial(do, "middle", i))

        mid = x + dot(attended[rows, :], params_ref[:, 3 * width : 4 * width])
        mid_ref[rows, :] = mid
        normed, _ = normalize(mid)
        act = (normed * small_rows[NORM_LANE + 2 : NORM_LANE + 3] + small_rows[NORM_LANE + 3 : NORM_LANE + 4]).astype(BF16)
        act_two[rows, :] = act
        logits = jnp.where(iota((BLOCK, LANES), 1) < experts, dot(act, small), -1e30)
        raised = jnp.exp(logits - jnp.max(logits, axis=-1, keepdims=True))
        probs = raised / jnp.sum(raised, axis=-1, keepdims=True)
        probs_ref[rows, :] = probs
        first, second = gates_of(probs, meta_ref[rows, :])
        gate_rows_ref[0:1, rows] = to_row(first)
        gate_rows_ref[1:2, rows] = to_row(second)
        for copy in saves(g):
            copy.start()

        for i in range(groups):
            pl.when(g == i)(functools.partial(do, "end", i))

    @pl.loop(0, experts)
    def _(i):
        el, k = lax.div(i, sources), lax.rem(lax.rem(i, sources) + 1, sources)
        e = place.other_peer(k) * count + el
        in_first, in_second, picks = find(e)
        gate = jnp.sum(
            jnp.where(in_first, gate_rows_ref[0:1, :], jnp.where(in_second, gate_rows_ref[1:2, :], 0.0)),
            axis=1, keepdims=True,
        )
        sent_ref[slot_rows(e), :] = dot(picks, act_two[...]).astype(BF16)
        gate_sent_ref[e, 0:1, :] = to_row(gate)

        @pl.when(jnp.logical_and(el == 0, k > 0))
        def _():
            swap(0, el, k).start()
            swap(1, el, k).start()

        @pl.when(k == 0)
        def _():
            rows_ref[source_rows(el, 0), :] = sent_ref[slot_rows(e), :]
            gate_ref[el * sources] = gate_sent_ref[e]

        for at in range(8):
            pl.when(i == at)(functools.partial(do, "dispatch", at))

    @pl.loop(0, groups)
    def _(g):
        for copy in saves(g):
            copy.wait()

    part_up = part_up_ref.at[pl.ds(0, count * width), :].reshape(count, A, B, 2, up_in.shape[1], part_up_ref.shape[1])
    part_down = part_down_ref.at[pl.ds(0, count * hidden_width), :].reshape(count, A, B, 2, down_in.shape[1], width)
    scatters = [
        ExpertScatter(place, part, sums, line, out, count, scatter_send.at[i], scatter_recv.at[i], scatter_local.at[i])
        for i, (part, sums, line, out) in enumerate(
            (
                (lambda el: part_up.at[el, :, :, :, :, pl.ds(0, hidden_width)], sums_up, line_up, up_grad_out),
                (lambda el: part_down.at[el], sums_down, line_down, down_grad_out),
            )
        )
    ]

    def all_scatters(step, el, *more):
        for scatter in scatters:
            getattr(scatter, step)(el, *more)

    par = Scatter(place, lambda e: part_up.at[0], sums_par, across_par, line_par, par_send, par_recv)

    def returned(kind, el, k):
        e = place.peer * count + el
        if kind == 1:
            source, target = dots_sent_ref.at[el * sources + k], dots_ref.at[e]
        else:
            here, there = (grad_ref, grad_slots_ref) if kind == 0 else (rows_ref, back_ref)
            source, target = here.at[source_rows(el, k), :], there.at[slot_rows(e), :]
        return pltpu.make_async_remote_copy(
            src_ref=source, dst_ref=target,
            send_sem=return_send.at[kind, el, k], recv_sem=return_recv.at[kind, el, place.seen_from(k)],
            device_id=place.at_peer(place.other_peer(k)), device_id_type=MESH,
        )

    def give_back(kind, el, first=1, stop=sources):
        @pl.loop(first, stop)
        def _(k):
            returned(kind, el, k).start()

    def return_wait(kind, el):
        @pl.loop(1, sources)
        def _(k):
            e = place.other_peer(k) * count + el
            target = dots_ref.at[e] if kind == 1 else (grad_slots_ref if kind == 0 else back_ref).at[slot_rows(e), :]
            pltpu.make_async_remote_copy(
                src_ref=target, dst_ref=target, send_sem=return_send.at[kind, el, k], recv_sem=return_recv.at[kind, el, k],
                device_id=place.at_peer(place.other_peer(k)), device_id_type=MESH,
            ).wait_recv()

    def expert(el):
        blocks = expert_rows // row_block
        block_sources = row_block // capacity
        order = list(range(blocks))
        if el > 0 and el == count - 1:
            order.reverse()
        each("core_wait", el)
        for turn, block in enumerate(order):
            first, stop = block * block_sources, (block + 1) * block_sources
            for kind in range(3):
                pl.loop(max(first, 1), stop)(functools.partial(swap_wait, kind, el))
            do("before", el, turn)
            here = pl.ds(el * expert_rows + block * row_block, row_block)
            float_ref[: 2 * row_block, :] = jnp.zeros((2 * row_block, width), F32)

            @pl.loop(first, stop)
            def _(k):
                gate = to_column(gate_ref[el * sources + k, 0:1, :], capacity)
                cots = grad_ref[source_rows(el, k), :].astype(F32)
                local = pl.ds(pl.multiple_of((k - first) * capacity, 16), capacity)
                gated_ref[local, :] = (gate * cots).astype(BF16)

            @pl.loop(0, chunks)
            def _(f):
                at = pl.ds(pl.multiple_of(f * FF_CHUNK, FF_CHUNK), FF_CHUNK)
                down_at = pl.ds(pl.multiple_of(el * hidden_width + f * FF_CHUNK, FF_CHUNK), FF_CHUNK)
                rows, grads = rows_ref[here, :], gated_ref[...]
                up_part, down_part = up_ref[el * width : (el + 1) * width, at], down_ref[down_at, :]
                hidden = dot(rows, up_part)
                spread = 0.5 * (1.0 + lax.erf(hidden * ROOT_HALF))
                active = (hidden * spread).astype(BF16)
                slope = spread + hidden * (DENSITY_SCALE * jnp.exp(-0.5 * hidden * hidden))
                float_ref[:row_block, :] += dot(active, down_part)
                grad_hidden = (dot_against(grads, down_part) * slope).astype(BF16)
                float_ref[row_block : 2 * row_block, :] += dot_against(grad_hidden, up_part)
                size = up_in.shape[1]
                up_sum = dot_rows(rows, grad_hidden).reshape(A, B, 2, size, FF_CHUNK)
                down_sum = dot_rows(active, grads)
                if turn > 0:
                    up_sum += part_up[el, :, :, :, :, at].astype(F32)
                    down_sum += part_down_ref[down_at, :].astype(F32)
                part_up[el, :, :, :, :, at] = up_sum.astype(BF16)
                part_down_ref[down_at, :] = down_sum.astype(BF16)
                for i in range(chunks):
                    pl.when(f == i)(functools.partial(do, "expert", el, turn * chunks + i))

            @pl.loop(first, stop)
            def _(k):
                at = source_rows(el, k)
                local = pl.ds(pl.multiple_of((k - first) * capacity, 16), capacity)
                back = float_ref[local, :].astype(BF16)
                rows_ref[at, :] = back
                dots = jnp.sum(back.astype(F32) * grad_ref[at, :].astype(F32), axis=1, keepdims=True)
                dots_sent_ref[el * sources + k, 0:1, :] = to_row(dots)
                local = pl.ds(pl.multiple_of(row_block + (k - first) * capacity, 16), capacity)
                grad_ref[at, :] = float_ref[local, :].astype(BF16)

            give_back(0, el, max(first, 1), stop)
            give_back(1, el, max(first, 1), stop)

        all_scatters("start", el)
        own, e = source_rows(el, 0), place.peer * count + el
        back_ref[slot_rows(e), :] = rows_ref[own, :]
        grad_slots_ref[slot_rows(e), :] = grad_ref[own, :]
        dots_ref[e] = dots_sent_ref[el * sources]

    for el in range(count):
        expert(el)

    def late_loads():
        out = [copy_in(weights_save, up_ref.at[pl.ds(0, rows_pad), :], late_sem.at[0])]
        for i, array in enumerate((act_one_save, attended_save, act_two_save)):
            out.append(copy_in(array, down_ref.at[pl.ds(i * rows_pad, rows_pad), :], late_sem.at[1 + i]))
        for i in range(2):
            out.append(copy_in(mid_save, float_ref.at[pl.ds(i * rows_pad, rows_pad), :], late_sem.at[4 + i]))
        return out

    for el in range(count):
        each("finish", el)
    for copy in late_loads():
        copy.start()
    spread(cot_raw, down_ref.at[pl.ds(3 * rows_pad, rows_pad), :])
    act_one, attended, act_two, cot_ref = (down_ref.at[pl.ds(i * rows_pad, rows_pad), :] for i in range(4))
    weights_ref = up_ref
    input_grad_ref = float_ref
    all_scatters("core_step", count - 1)
    if count > 1:
        all_scatters("relay_step", count - 2, 2)
    for copy in late_loads():
        copy.wait()
    for kind in range(2):
        for el in range(count):
            return_wait(kind, el)
    give_back(2, count - 1)
    all_scatters("relay_step", count - 1, 0)
    gain_one = small_rows[NORM_LANE : NORM_LANE + 1]
    gain_two = small_rows[NORM_LANE + 2 : NORM_LANE + 3]
    column_ref[...] = jnp.zeros_like(column_ref)
    flat = jnp.zeros((8, places), F32)
    for e in range(experts):
        row = dots_ref[e]
        row = jnp.concatenate([row, jnp.zeros((8, places - row.shape[1]), F32)], axis=1)
        flat += pltpu.roll(row, e * capacity, 1) if e else row
    dot_row_ref[...] = flat

    def last_sums(g):
        with jax.named_scope("last_sums_%d" % g):
            if g == 0 and count > 1:
                all_scatters("line_step", count - 2)
            if g == 1:
                all_scatters("relay_step", count - 1, 1)
            if g == 3:
                all_scatters("relay_step", count - 1, 2)

    def store(i, g):
        rows = rows_of(g)
        here, there = ((cot_ref, out_out), (input_grad_ref, input_grad_out))[i]
        return copy_in(here.at[rows, :], there.at[rows, :], store_sem.at[i, g])

    @pl.loop(0, groups)
    def _(g):
        rows = rows_of(g)
        meta = meta_ref[rows, :]
        probs = probs_ref[rows, :]
        lane = iota((BLOCK, LANES), 1)
        grad_first = jnp.zeros((BLOCK, LANES), F32)
        grad_second = jnp.zeros((BLOCK, LANES), F32)
        for c in range(places // LANES):
            at = c * LANES
            in_first = lane == meta[:, 0:1] - at
            in_second = lane == meta[:, 1:2] - at
            place_ref[:, at : at + LANES] = jnp.where(jnp.logical_or(in_first, in_second), 1.0, 0.0).astype(BF16)
            dots = dot_row_ref[0:1, at : at + LANES]
            grad_first += jnp.where(in_first, dots, 0.0)
            grad_second += jnp.where(in_second, dots, 0.0)
        grad_first = jnp.sum(grad_first, axis=1, keepdims=True)
        grad_second = jnp.sum(grad_second, axis=1, keepdims=True)
        mid = input_grad_ref[rows, :]
        grad_probs = jnp.where(lane == meta[:, 2:3], grad_first, 0.0) + jnp.where(lane == meta[:, 3:4], grad_second, 0.0)
        grad_logits = (probs * (grad_probs - jnp.sum(grad_probs * probs, axis=-1, keepdims=True))).astype(BF16)
        logit_grad_ref[rows, :] = grad_logits
        grad_act = dot(place_ref[...], grad_slots_ref[...]) + dot_against(grad_logits, small)
        normed, inverse = normalize(mid)
        column_ref[NORM_LANE + 2 : NORM_LANE + 3, :] += jnp.sum(grad_act * normed, axis=0, keepdims=True)
        column_ref[NORM_LANE + 3 : NORM_LANE + 4, :] += jnp.sum(grad_act, axis=0, keepdims=True)
        grad_mid = cot_ref[rows, :].astype(F32) + denormalize(grad_act, normed, inverse, gain_two)
        input_grad_ref[rows, :] = grad_mid
        grad_attended = dot_against(grad_mid.astype(BF16), params_ref[:, 3 * width : 4 * width]).astype(BF16)
        low = lane < HEAD_DIM
        for pair in range(HEADS // 2):
            at = pair * LANES
            q = triple_ref[rows, at : at + LANES] * HEAD_DIM ** (-0.5)
            k = triple_ref[rows, width + at : width + at + LANES]
            v = triple_ref[rows, 2 * width + at : 2 * width + at + LANES]
            upstream = grad_attended[:, at : at + LANES]
            grad_q = grad_k = grad_v = jnp.zeros((BLOCK, LANES), F32)
            for half in range(2):
                mask = low if half == 0 else jnp.logical_not(low)
                upstream_half = jnp.where(mask, upstream, 0.0).astype(BF16)
                head = (2 * pair + half) * BLOCK
                weights = weights_ref[rows, head : head + BLOCK]
                kept = weights.astype(F32)
                grad_weights = dot_against(upstream_half, v)
                inner = jnp.sum(grad_weights * kept, axis=-1, keepdims=True)
                grad_scores = (kept * (grad_weights - inner)).astype(BF16)
                grad_q += dot(grad_scores, jnp.where(mask, k, 0.0).astype(BF16))
                grad_k += dot_rows(grad_scores, jnp.where(mask, q, 0.0).astype(BF16))
                grad_v += dot_rows(weights, upstream_half)
            triple_ref[rows, at : at + LANES] = (grad_q * HEAD_DIM ** (-0.5)).astype(BF16)
            triple_ref[rows, width + at : width + at + LANES] = grad_k.astype(BF16)
            triple_ref[rows, 2 * width + at : 2 * width + at + LANES] = grad_v.astype(BF16)
        grad_act = dot_against(triple_ref[rows, :], params_ref[:, : 3 * width])
        normed, inverse = normalize(x_ref[rows, :].astype(F32))
        column_ref[NORM_LANE : NORM_LANE + 1, :] += jnp.sum(grad_act * normed, axis=0, keepdims=True)
        column_ref[NORM_LANE + 1 : NORM_LANE + 2, :] += jnp.sum(grad_act, axis=0, keepdims=True)
        grad_mid = input_grad_ref[rows, :]
        x_ref[rows, :] = grad_mid.astype(BF16)
        input_grad_ref[rows, :] = grad_mid + denormalize(grad_act, normed, inverse, gain_one)
        store(1, g).start()
        for i in range(groups):
            pl.when(g == i)(functools.partial(last_sums, i))

    size = up_in.shape[1]
    split = (A, B, 2, size)
    part_up[0, :, :, :, :, : 3 * width] = dot_rows(act_one[...], triple_ref[...]).astype(BF16).reshape(*split, 3 * width)
    part_up[0, :, :, :, :, 3 * width : 4 * width] = dot_rows(attended[...], x_ref[...]).astype(BF16).reshape(*split, width)
    small_part = dot_rows(act_two[...], logit_grad_ref[...]) + jnp.transpose(column_ref[...])
    part_up[0, :, :, :, :, 4 * width :] = small_part.astype(BF16).reshape(*split, LANES)
    par.start(0)
    for el in range(count):
        return_wait(2, el)

    def combine(g):
        rows = rows_of(g)
        meta = meta_ref[rows, :]
        gate_first, gate_second = gates_of(probs_ref[rows, :], meta)
        lane = iota((BLOCK, LANES), 1)
        for c in range(places // LANES):
            at = c * LANES
            in_first = lane == meta[:, 0:1] - at
            in_second = lane == meta[:, 1:2] - at
            place_ref[:, at : at + LANES] = jnp.where(in_first, gate_first, jnp.where(in_second, gate_second, 0.0)).astype(BF16)
        mid = float_ref[pl.ds(pl.multiple_of(rows_pad + g * BLOCK, BLOCK), BLOCK), :]
        cot_ref[rows, :] = (mid + dot(place_ref[...], back_ref[...])).astype(BF16)
        store(0, g).start()

    pl.loop(0, groups // 2)(combine)
    par.core_step(0)
    pl.loop(groups // 2, groups)(combine)
    par.across_step(0)
    all_scatters("line_step", count - 1)
    swap_ref[place.x] = par.line_step(0).astype(BF16)

    def shares():
        out = []
        for k in range(1, xs):
            to, back = lax.rem(place.x + k, xs), xs - 1 - k
            out.append(
                pltpu.make_async_remote_copy(
                    src_ref=swap_ref.at[place.x], dst_ref=swap_ref.at[place.x],
                    send_sem=share_send.at[back], recv_sem=share_recv.at[back],
                    device_id=(to, place.me), device_id_type=MESH,
                )
            )
        return out

    for copy in shares():
        copy.start()

    @pl.loop(0, groups)
    def _(g):
        for i in range(2):
            store(i, g).wait()

    params.finish_send()
    for el in range(count):

        @pl.loop(1, sources)
        def _(k):
            for kind in range(3):
                swap(kind, el, k).wait_send()
                returned(kind, el, k).wait_send()

        all_scatters("finish", el)
    par.finish(0)
    for copy in shares():
        copy.wait()
    total = swap_ref[0].astype(F32)
    for i in range(1, xs):
        total += swap_ref[i].astype(F32)
    share_out[...] = total


def finish_kernel(
    experts, out_pad, input_grad_pad, share, up_half, down_half,
    out, input_grad, qkv, out_weight, router, gain_one, shift_one, gain_two, shift_two, up, down,
):
    width = out.shape[1]
    for g in range(out_pad.shape[0] // BLOCK):
        here, there = slice(g * BLOCK, g * BLOCK + GROUP_ROWS), slice(g * GROUP_ROWS, (g + 1) * GROUP_ROWS)
        out[there, :] = out_pad[here, :]
        input_grad[there, :] = input_grad_pad[here, :]
    qkv[...] = share[:, : 3 * width]
    out_weight[...] = share[:, 3 * width : 4 * width]
    small = jnp.transpose(share[:, 4 * width :])
    router[...] = small[:experts, :]
    for i, vector in enumerate((gain_one, shift_one, gain_two, shift_two)):
        vector[...] = small[NORM_LANE + i : NORM_LANE + i + 1, :].reshape(vector.shape)
    up[...] = up_half[...].astype(F32)
    down[...] = down_half[...].astype(F32)


def on_device(
    inputs, cotangent, routes, slots, qkv_weight, out_weight, router_weight,
    norm1_gain, norm1_shift, norm2_gain, norm2_shift, expert_up, expert_down,
):
    rows_dev, width = inputs.shape
    groups = rows_dev // GROUP_ROWS
    rows_pad = groups * BLOCK
    fsdp = lax.axis_size("fsdp")
    peers = lax.axis_size("expert")
    held = expert_up.shape[0]
    experts = held * peers
    capacity = (42 * rows_dev + 20 * experts - 1) // (20 * experts)
    capacity = -(-capacity // 16) * 16
    places = experts * capacity

    vmem = pl.BlockSpec(memory_space=pltpu.VMEM)
    hbm = pl.BlockSpec(memory_space=pl.ANY)
    shape = jax.ShapeDtypeStruct
    dma = pltpu.SemaphoreType.DMA
    A, B = 4, fsdp // 8
    count = held // B
    sources = peers * B
    up_rows, down_rows = expert_up.shape[1], expert_down.shape[1]
    hidden_width = expert_up.shape[2]
    packed_width = 4 * width + LANES
    expert_rows = sources * capacity
    row_block = max(n for n in range(capacity, MAX_ROWS + 1, capacity) if expert_rows % n == 0)
    routes_of = 3 + B - 1
    lanes_of = -(-capacity // LANES) * LANES

    def buffer(*dims, dtype=BF16):
        return pltpu.VMEM(dims, dtype)

    out, input_grad, share, up_grad, down_grad, *_ = pl.pallas_call(
        functools.partial(block_kernel, experts, fsdp, peers, count),
        out_shape=(
            shape((rows_pad, width), BF16),
            shape((rows_pad, width), F32),
            shape((up_rows, packed_width), F32),
            shape(expert_up.shape, BF16),
            shape(expert_down.shape, BF16),
            shape((rows_pad, width), BF16),
            shape((rows_pad, HEADS * BLOCK), BF16),
            shape((rows_pad, width), BF16),
            shape((rows_pad, width), F32),
            shape((rows_pad, width), BF16),
        ),
        in_specs=[hbm] * 2 + [vmem] * 9 + [hbm] * 2,
        out_specs=[hbm] * 2 + [vmem] + [hbm] * 7,
        scratch_shapes=[
            buffer(rows_dev, width), buffer(rows_dev, width), buffer(up_rows, packed_width),
            buffer(8, rows_pad, dtype=jnp.int32), buffer(rows_pad, 8, dtype=jnp.int32),
            buffer(rows_pad, width), buffer(fsdp * up_rows, packed_width), buffer(rows_pad, 3 * width),
            buffer(rows_pad, LANES, dtype=F32),
            buffer(places, width), buffer(places, width), buffer(experts, 8, lanes_of, dtype=F32),
            buffer(places, width), buffer(places, width), buffer(experts, 8, lanes_of, dtype=F32),
            buffer(places, width), buffer(places, width),
            buffer(experts, 8, lanes_of, dtype=F32), buffer(experts, 8, lanes_of, dtype=F32),
            buffer(max(count * width, rows_pad), hidden_width), buffer(max(count * hidden_width, 4 * rows_pad), width),
            buffer(max(count * width, rows_pad), packed_width), buffer(max(count * hidden_width, 4 * rows_pad), width),
            buffer(max(2 * row_block, 2 * rows_pad), width, dtype=F32),
            buffer(count, A, B, up_rows, hidden_width), buffer(count, A, B, down_rows, width),
            buffer(count, 2, A - 1, B, up_rows, hidden_width), buffer(count, 2, A - 1, B, down_rows, width),
            buffer(1, A, B, up_rows, packed_width), buffer(1, B - 1, A, up_rows, packed_width),
            buffer(1, A - 1, up_rows, packed_width), buffer(peers, up_rows, packed_width),
            buffer(BLOCK, BLOCK, dtype=F32), buffer(8, rows_pad, dtype=F32), buffer(8, places, dtype=F32),
            buffer(BLOCK, places), buffer(row_block, width), buffer(rows_pad, LANES), buffer(LANES, width, dtype=F32),
            dma((2,)), dma((5, groups)), dma((6,)), dma((2, groups)),
            dma((fsdp, routes_of)), dma((fsdp,)), dma,
            dma((2, count, fsdp, routes_of)), dma((2, count, fsdp)), dma((2, count)),
            dma((3, count, sources)), dma((3, count, sources)), dma((3, count, sources)), dma((3, count, sources)),
            dma((2, count, 2 * A + B - 2)), dma((2, count, 2 * A + B - 2)), dma((2, count)),
            dma((1, A + B - 1)), dma((1, A + B - 1)), dma((peers - 1,)), dma((peers - 1,)),
        ],
        compiler_params=pltpu.CompilerParams(vmem_limit_bytes=VMEM_LIMIT, collective_id=0, has_side_effects=True),
        name="encoder_block",
    )(
        inputs, cotangent, routes.T, slots.T, qkv_weight, out_weight, router_weight.T,
        norm1_gain, norm1_shift, norm2_gain, norm2_shift, expert_up, expert_down,
    )
    vector = shape((up_rows,), F32)
    results = pl.pallas_call(
        functools.partial(finish_kernel, experts),
        out_shape=(
            shape((rows_dev, width), BF16),
            shape((rows_dev, width), F32),
            shape((up_rows, 3 * width), F32),
            shape((up_rows, width), F32),
            shape((experts, up_rows), F32),
            *[vector] * 4,
            shape(expert_up.shape, F32),
            shape(expert_down.shape, F32),
        ),
        in_specs=[vmem] * 5,
        out_specs=[vmem] * 11,
        compiler_params=pltpu.CompilerParams(vmem_limit_bytes=VMEM_LIMIT),
        name="results",
    )(out, input_grad, share, up_grad, down_grad)
    return (*results[:4], results[4].T, *results[5:])


def solution(mesh):
    tokens = P(("expert", "fsdp"), None)
    rows, vector, expert = P("fsdp", None), P("fsdp"), P("expert", "fsdp", None)
    return jax.shard_map(
        on_device,
        mesh=mesh,
        in_specs=(tokens,) * 4 + (rows,) * 3 + (vector,) * 4 + (expert,) * 2,
        out_specs=(tokens,) * 2 + (rows,) * 3 + (vector,) * 4 + (expert,) * 2,
        check_vma=False,
    )
```

```python
import functools

import jax
import jax.numpy as jnp
from jax import lax
from jax.experimental import pallas as pl
from jax.experimental.pallas import tpu as pltpu
from jax.sharding import PartitionSpec as P

HEADS = 8
HEAD_DIM = 64
PATCHES = 49
EPS = 1e-06
ROOT_HALF = 0.7071067811865476
DENSITY_SCALE = 0.3989422804014327

BLOCK = 256
GROUP_IMAGES = BLOCK // PATCHES
GROUP_ROWS = GROUP_IMAGES * PATCHES
LANES = 128
NORM_LANE = 64
FF_CHUNK = 512
MAX_ROWS = 640
VMEM_LIMIT = 63 * 1024 * 1024

MESH = pl.DeviceIdType.MESH
PLAN = {
    ("start", 0): [("across", 0)],
    ("start", 1): [("own", 0)],
    ("start", 3): [("passed", 0)],
    ("after", 3): [("relay", 0, 1, True)],
    ("begin", 0): [("cots", 0)],
    ("end", 0): [("relay", 0, 1, False)],
    ("middle", 1): [("relay", 0, 2, True)],
    ("end", 1): [("across", 1)],
    ("end", 2): [("relay", 0, 2, False), ("cots_across", 1)],
    ("dispatch", 7): [("own", 1), ("passed", 1), ("ends", 0)],
    ("expert", 0, 0): [("relay", 1, 1, True)],
    ("expert", 0, 1): [("rows", 1), ("relay", 1, 1, False)],
    ("expert", 0, 3): [("cots_along", 1), ("relay", 1, 2, True)],
    ("expert", 0, 4): [("relay", 1, 2, False)],
    ("expert", 0, 7): [("ends", 1)],
    ("expert", 1, 0): [("sums", 0), ("sum_relay", 0, 0)],
    ("expert", 1, 4): [("sum_relay", 0, 1)],
    ("after_expert", 1): [("outputs_across", 0)],
    ("returned", 0): [("outputs_along", 0)],
    ("returned", 1): [("outputs", 1)],
}
F32 = jnp.float32
BF16 = jnp.bfloat16


def dot(left, right):
    return lax.dot_general(left, right, (((1,), (0,)), ((), ())), preferred_element_type=F32)


def dot_rows(left, right):
    return lax.dot_general(left, right, (((0,), (0,)), ((), ())), preferred_element_type=F32)


def dot_against(left, right):
    return lax.dot_general(left, right, (((1,), (1,)), ((), ())), preferred_element_type=F32)


def iota(shape, dim):
    return lax.broadcasted_iota(jnp.int32, shape, dim)


def normalize(values):
    center = jnp.mean(values, axis=-1, keepdims=True)
    offset = values - center
    spread = jnp.mean(offset * offset, axis=-1, keepdims=True)
    inverse = lax.rsqrt(spread + EPS)
    return offset * inverse, inverse


def denormalize(upstream, normed, inverse, gain):
    scaled = upstream * gain
    return inverse * (
        scaled
        - jnp.mean(scaled, axis=-1, keepdims=True)
        - normed * jnp.mean(scaled * normed, axis=-1, keepdims=True)
    )


def to_row(column):
    n = column.shape[0]
    parts = []
    for at in range(0, n, LANES):
        size = min(LANES, n - at)
        eye = iota((size, LANES), 0) == iota((size, LANES), 1)
        parts.append(jnp.sum(jnp.where(eye, column[at : at + size], 0.0), axis=0, keepdims=True))
    return parts[0] if len(parts) == 1 else jnp.concatenate(parts, axis=1)


def to_column(row, n):
    eye = iota((n, row.shape[1]), 0) == iota((n, row.shape[1]), 1)
    return jnp.sum(jnp.where(eye, row, 0.0), axis=1, keepdims=True)


def rows_of(g):
    return pl.ds(pl.multiple_of(g * BLOCK, BLOCK), BLOCK)


def gates_of(probs, meta):
    lane = iota(probs.shape, 1)
    first = jnp.sum(jnp.where(lane == meta[:, 2:3], probs, 0.0), axis=1, keepdims=True)
    second = jnp.sum(jnp.where(lane == meta[:, 3:4], probs, 0.0), axis=1, keepdims=True)
    return first, second


class Place:
    def __init__(self, fsdp, xs):
        self.A, self.B = 4, fsdp // 8
        self.x = lax.axis_index("expert")
        self.me = lax.axis_index("fsdp")
        self.c = lax.rem(self.me, 2)
        line = lax.div(self.me, 2)
        self.b = lax.rem(line, self.B)
        self.a = lax.div(line, self.B)
        self.xs, self.peers = xs, xs * self.B
        self.peer = self.x * self.B + self.b

    def index(self, a, b, c):
        return (a * self.B + b) * 2 + c

    def other_b(self, j):
        return lax.rem(self.b + 1 + j, self.B)

    def at(self, a, b, c):
        return (self.x, self.index(a, b, c))

    def at_peer(self, peer):
        return (lax.div(peer, self.B), self.index(self.a, lax.rem(peer, self.B), self.c))

    def other_peer(self, k):
        x, b = lax.rem(self.x + lax.rem(k, self.xs), self.xs), lax.rem(self.b + lax.div(k, self.xs), self.B)
        return x * self.B + b

    def seen_from(self, k):
        x, b = lax.rem(self.xs - lax.rem(k, self.xs), self.xs), lax.rem(self.B - lax.div(k, self.xs), self.B)
        return b * self.xs + x


def greet(place, meanwhile):
    barrier = pltpu.get_barrier_semaphore()

    def signal(device):
        pl.semaphore_signal(barrier, inc=1, device_id=device, device_id_type=MESH)

    for k in range(1, place.A):
        signal(place.at(lax.rem(place.a + k, place.A), place.b, place.c))
    for k in range(1, place.peers):
        signal(place.at_peer(place.other_peer(k)))
    signal(place.at(place.a, place.b, 1 - place.c))
    meanwhile()
    pl.semaphore_wait(barrier, place.A - 1 + place.peers - 1 + 1)


class Gather:
    RIGHT, LEFT, CORE, ACROSS = 0, 1, 2, 3

    def __init__(self, place, own, full, block, send_sem, recv_sem, local_sem):
        self.place, self.own, self.full, self.block = place, own, full, block
        self.send_sem, self.recv_sem, self.local_sem = send_sem, recv_sem, local_sem

    def copy(self, shard, route, source, a, b, c):
        return pltpu.make_async_remote_copy(
            src_ref=source, dst_ref=self.block(self.full, shard),
            send_sem=self.send_sem.at[route], recv_sem=self.recv_sem.at[self.arrival(shard, route)],
            device_id=self.place.at(a, b, c), device_id_type=MESH,
        )

    def arrival(self, shard, route):
        return self.place.A * self.place.B if route == self.CORE else lax.div(shard, 2)

    def some(self, route, blocks):
        size = self.own.shape[0]
        ref = self.full.at[pl.ds(0, blocks * size), :]
        p = self.place
        return pltpu.make_async_remote_copy(
            src_ref=ref, dst_ref=ref, send_sem=self.send_sem.at[route], recv_sem=self.recv_sem.at[p.A * p.B],
            device_id=p.at(p.a, p.b, 1 - p.c), device_id_type=MESH,
        )

    def onward(self, shard, source, right, left, across, act):
        p = self.place
        if right is not None:
            pl.when(right)(lambda: act(self.copy(shard, self.RIGHT, source, p.a + 1, p.b, p.c)))
        if left is not None:
            pl.when(left)(lambda: act(self.copy(shard, self.LEFT, source, p.a - 1, p.b, p.c)))
        if across:
            for j in range(p.B - 1):
                act(self.copy(shard, self.ACROSS + j, source, p.a, p.other_b(j), p.c))
        act(self.copy(shard, self.CORE, source, p.a, p.b, 1 - p.c))

    def local(self):
        return pltpu.make_async_copy(self.own, self.block(self.full, self.place.me), self.local_sem)

    def start(self):
        p = self.place
        self.local().start()
        self.onward(p.me, self.own, p.a < p.A - 1, p.a > 0, True, lambda copy: copy.start())

    def arrived(self, shard):
        p = self.place
        self.copy(shard, self.RIGHT, self.block(self.full, shard), p.a, p.b, 1 - p.c).wait_recv()

    def line_step(self, k):
        p = self.place

        def from_left():
            shard = p.index(p.a - k, p.b, p.c)
            self.arrived(shard)
            self.onward(shard, self.block(self.full, shard), p.a < p.A - 1, None, True, lambda copy: copy.start())

        def from_right():
            shard = p.index(p.a + k, p.b, p.c)
            self.arrived(shard)
            self.onward(shard, self.block(self.full, shard), None, p.a > 0, True, lambda copy: copy.start())

        pl.when(p.a - k >= 0)(from_left)
        pl.when(p.a + k < p.A)(from_right)

    def across_step(self, k):
        p = self.place

        def row(a):
            for j in range(p.B - 1):
                shard = p.index(a, p.other_b(j), p.c)
                self.arrived(shard)
                self.onward(shard, self.block(self.full, shard), None, None, False, lambda copy: copy.start())

        if k == 0:
            row(p.a)
        else:
            pl.when(p.a - k >= 0)(lambda: row(p.a - k))
            pl.when(p.a + k < p.A)(lambda: row(p.a + k))

    def finish_recv(self):
        p = self.place
        self.local().wait()
        self.some(self.CORE, p.A * p.B).wait_recv()

    def finish_send(self):
        p = self.place
        for a in range(p.A - 1):
            pl.when(p.a == a)(self.some(self.RIGHT, a + 1).wait_send)
            pl.when(p.a == a + 1)(self.some(self.LEFT, p.A - 1 - a).wait_send)
        for j in range(p.B - 1):
            self.some(self.ACROSS + j, p.A).wait_send()
        self.some(self.CORE, p.A * p.B).wait_send()


class ExpertGather:
    RIGHT, LEFT, CORE, ACROSS = 0, 1, 2, 3

    def __init__(self, place, own, full, count, send_sem, recv_sem, local_sem):
        self.place, self.own, self.full, self.count = place, own, full, count
        self.send_sem, self.recv_sem, self.local_sem = send_sem, recv_sem, local_sem
        self.size = own.shape[1]
        self.depth = self.size * place.A * place.B * 2

    def block(self, el, shard):
        return self.full.at[pl.ds(pl.multiple_of(el * self.depth + shard * self.size, self.size), self.size), :]

    def mine(self, el):
        return self.own.at[self.place.b * self.count + el]

    def copy(self, el, shard, route, source, a, b, c):
        return pltpu.make_async_remote_copy(
            src_ref=source, dst_ref=self.block(el, shard),
            send_sem=self.send_sem.at[el, route], recv_sem=self.recv_sem.at[el, self.arrival(shard, route)],
            device_id=self.place.at(a, b, c), device_id_type=MESH,
        )

    def arrival(self, shard, route):
        return self.place.A * self.place.B if route == self.CORE else lax.div(shard, 2)

    def some(self, el, route, blocks):
        ref = self.full.at[pl.ds(el * self.depth, blocks * self.size), :]
        p = self.place
        return pltpu.make_async_remote_copy(
            src_ref=ref, dst_ref=ref, send_sem=self.send_sem.at[el, route], recv_sem=self.recv_sem.at[el, p.A * p.B],
            device_id=p.at(p.a, p.b, 1 - p.c), device_id_type=MESH,
        )

    def across(self, el):
        p = self.place
        out = []
        for j in range(p.B - 1):
            to = p.other_b(j)
            out.append(self.copy(el, p.me, self.ACROSS + j, self.own.at[to * self.count + el], p.a, to, p.c))
        return out

    def local(self, el):
        return pltpu.make_async_copy(self.mine(el), self.block(el, self.place.me), self.local_sem.at[el])

    def onward(self, el, shard, source, right, left, act):
        p = self.place
        if right:
            pl.when(p.a < p.A - 1)(lambda: act(self.copy(el, shard, self.RIGHT, source, p.a + 1, p.b, p.c)))
        if left:
            pl.when(p.a > 0)(lambda: act(self.copy(el, shard, self.LEFT, source, p.a - 1, p.b, p.c)))
        act(self.copy(el, shard, self.CORE, source, p.a, p.b, 1 - p.c))

    def arrived(self, el, shard):
        p = self.place
        self.copy(el, shard, self.RIGHT, self.block(el, shard), p.a, p.b, 1 - p.c).wait_recv()

    def start_across(self, el):
        for copy in self.across(el):
            copy.start()

    def start_own(self, el):
        self.local(el).start()
        self.onward(el, self.place.me, self.mine(el), True, True, lambda copy: copy.start())

    def across_step(self, el):
        p = self.place
        for j in range(p.B - 1):
            shard = p.index(p.a, p.other_b(j), p.c)
            self.arrived(el, shard)
            self.onward(el, shard, self.block(el, shard), True, True, lambda copy: copy.start())

    def line_step(self, el, k, own):
        p = self.place

        def row(a, right, left):
            for b in [p.b] if own else [p.other_b(j) for j in range(p.B - 1)]:
                shard = p.index(a, b, p.c)
                self.arrived(el, shard)
                self.onward(el, shard, self.block(el, shard), right, left, lambda copy: copy.start())

        pl.when(p.a - k >= 0)(lambda: row(p.a - k, True, False))
        pl.when(p.a + k < p.A)(lambda: row(p.a + k, False, True))

    def core_wait(self, el):
        p = self.place
        self.local(el).wait()
        self.some(el, self.CORE, p.A * p.B).wait_recv()

    def finish(self, el):
        p = self.place
        for copy in self.across(el):
            copy.wait_send()
        for a in range(p.A - 1):
            pl.when(p.a == a)(self.some(el, self.RIGHT, (a + 1) * p.B).wait_send)
            pl.when(p.a == a + 1)(self.some(el, self.LEFT, (p.A - 1 - a) * p.B).wait_send)
        self.some(el, self.CORE, p.A * p.B).wait_send()


class ExpertScatter:
    def __init__(self, place, part, sums, line, out, count, send, recv, local_sem):
        self.place, self.part, self.sums, self.line, self.out, self.count = place, part, sums, line, out, count
        self.send, self.recv, self.local_sem = send, recv, local_sem

    CORE, RIGHT, LEFT, LAST = 0, 1, 2, 3

    def remote(self, source, target, el, route, arrival, a, b, c):
        return pltpu.make_async_remote_copy(
            src_ref=source, dst_ref=target, send_sem=self.send.at[el, route], recv_sem=self.recv.at[el, arrival],
            device_id=self.place.at(a, b, c), device_id_type=MESH,
        )

    def core_copy(self, el):
        p = self.place
        return self.remote(self.part(el).at[:, :, 1 - p.c], self.sums.at[el], el, self.CORE, 0, p.a, p.b, 1 - p.c)

    def right_copy(self, el, target):
        p = self.place
        return self.remote(
            self.sums.at[el, target], self.line.at[el, 0, target - 1], el, self.RIGHT, target, p.a + 1, p.b, p.c
        )

    def left_copy(self, el, target):
        p = self.place
        return self.remote(
            self.sums.at[el, target], self.line.at[el, 1, target], el, self.LEFT, p.A + target, p.a - 1, p.b, p.c
        )

    def add(self, el, target, way, slot):
        @pl.loop(0, self.place.B)
        def _(b):
            total = self.sums[el, target, b].astype(F32) + self.line[el, way, slot, b].astype(F32)
            self.sums[el, target, b] = total.astype(BF16)

    def relay_step(self, el, step):
        p = self.place

        @pl.when(p.a <= step)
        def _():
            target = p.a + p.A - 1 - step

            @pl.when(p.a > 0)
            def _():
                self.right_copy(el, target).wait_recv()
                self.add(el, target, 0, target - 1)

            self.right_copy(el, target).start()

        @pl.when(p.a >= p.A - 1 - step)
        def _():
            target = p.a - (p.A - 1 - step)

            @pl.when(p.a < p.A - 1)
            def _():
                self.left_copy(el, target).wait_recv()
                self.add(el, target, 1, target)

            self.left_copy(el, target).start()

    def last_copies(self, el):
        p = self.place
        out = []
        for j in range(p.B - 1):
            to, back = p.other_b(j), p.B - 2 - j
            target = self.out.at[p.b * self.count + el]
            out.append(self.remote(self.sums.at[el, p.a, to], target, el, self.LAST + j, 2 * p.A - 1 + back, p.a, to, p.c))
        return out

    def local(self, el):
        p = self.place
        return pltpu.make_async_copy(self.sums.at[el, p.a, p.b], self.out.at[p.b * self.count + el], self.local_sem.at[el])

    def start(self, el):
        self.core_copy(el).start()

    def core_step(self, el):
        p = self.place
        self.core_copy(el).wait()
        part = self.part(el)

        @pl.loop(0, p.A * p.B)
        def _(i):
            a, b = lax.div(i, p.B), lax.rem(i, p.B)
            total = self.sums[el, a, b].astype(F32) + part[a, b, p.c].astype(F32)
            self.sums[el, a, b] = total.astype(BF16)

    def line_step(self, el):
        p = self.place

        @pl.when(p.a > 0)
        def _():
            self.right_copy(el, p.a).wait_recv()
            self.add(el, p.a, 0, p.a - 1)

        @pl.when(p.a < p.A - 1)
        def _():
            self.left_copy(el, p.a).wait_recv()
            self.add(el, p.a, 1, p.a)

        for copy in self.last_copies(el) + [self.local(el)]:
            copy.start()

    def finish(self, el):
        p = self.place
        for a in range(p.A - 1):
            for route, at, count in ((self.RIGHT, a, p.A - 1 - a), (self.LEFT, a + 1, a + 1)):
                some = self.sums.at[el, pl.ds(0, count)]
                pl.when(p.a == at)(self.remote(some, some, el, route, 0, p.a, p.b, 1 - p.c).wait_send)
        for copy in self.last_copies(el) + [self.local(el)]:
            copy.wait()


class Scatter:
    def __init__(self, place, part, sums, across, line, columns, send, recv):
        self.place, self.part, self.sums, self.across, self.line = place, part, sums, across, line
        self.columns, self.send, self.recv = columns, send, recv

    CORE, ACROSS, LINE = 0, 1, 2

    def remote(self, source, target, item, route, a, b, c):
        return pltpu.make_async_remote_copy(
            src_ref=source, dst_ref=target,
            send_sem=self.send.at[item, min(route, 1)], recv_sem=self.recv.at[item, route],
            device_id=self.place.at(a, b, c), device_id_type=MESH,
        )

    def all_of(self, ref, item, route):
        p = self.place
        return self.remote(ref, ref, item, route, p.a, p.b, 1 - p.c)

    def core_copy(self, item):
        p, at = self.place, self.columns[item]
        return self.remote(self.part.at[:, :, 1 - p.c, :, at], self.sums.at[:, :, :, at], item, self.CORE, p.a, p.b, 1 - p.c)

    def across_copies(self, item):
        p, at = self.place, self.columns[item]
        out = []
        for j in range(p.B - 1):
            to, back = p.other_b(j), p.B - 2 - j
            copy = self.remote(self.sums.at[:, to, :, at], self.across.at[back, :, :, at], item, self.ACROSS, p.a, to, p.c)
            out.append(copy)
        return out

    def line_copies(self, item):
        p, at = self.place, self.columns[item]
        out = []
        for k in range(1, p.A):
            to, back = lax.rem(p.a + k, p.A), p.A - 1 - k
            copy = self.remote(self.sums.at[to, p.b, :, at], self.line.at[back, :, at], item, self.LINE, to, p.b, p.c)
            out.append(copy)
        return out

    def start(self, item):
        self.core_copy(item).start()

    def core_step(self, item):
        p, at = self.place, self.columns[item]
        self.core_copy(item).wait()

        @pl.loop(0, p.A * p.B)
        def _(i):
            a, b = lax.div(i, p.B), lax.rem(i, p.B)
            total = self.sums[a, b, :, at].astype(F32) + self.part[a, b, p.c, :, at].astype(F32)
            self.sums[a, b, :, at] = total.astype(BF16)

        for copy in self.across_copies(item):
            copy.start()

    def across_step(self, item):
        p, at = self.place, self.columns[item]
        self.all_of(self.across.at[:, :, :, at], item, self.ACROSS).wait_recv()

        @pl.loop(0, p.A)
        def _(a):
            total = self.sums[a, p.b, :, at].astype(F32)
            for j in range(p.B - 1):
                total += self.across[j, a, :, at].astype(F32)
            self.sums[a, p.b, :, at] = total.astype(BF16)

        for copy in self.line_copies(item):
            copy.start()

    def line_step(self, item):
        p, at = self.place, self.columns[item]
        self.all_of(self.line.at[:, :, at], item, self.LINE).wait_recv()
        total = self.sums[p.a, p.b, :, at].astype(F32)
        for k in range(p.A - 1):
            total += self.line[k, :, at].astype(F32)
        return total

    def finish(self, item):
        p, at = self.place, self.columns[item]
        blocks = self.sums.reshape(p.A * p.B, *self.sums.shape[2:])
        self.all_of(blocks.at[pl.ds(0, (p.B - 1) * p.A + p.A - 1), :, at], item, self.LINE).wait_send()


def block_kernel(
    experts, fsdp, xs, count,
    x_in, cot_in, routes_ref, slots_ref, qkv_ref, out_ref, router_ref, gain_one_ref, shift_one_ref, gain_two_ref, shift_two_ref,
    up_in, down_in,
    out_out, input_grad_out, share_out, up_grad_out, down_grad_out,
    act_one_save, weights_save, attended_save, mid_save, act_two_save,
    x_raw, cot_raw, shard_ref, meta_row_ref, meta_ref, x_ref, params_ref, triple_ref, probs_ref,
    sent_ref, cot_sent_ref, gate_sent_ref, rows_ref, grad_ref, gate_ref, back_ref, grad_slots_ref, dots_sent_ref, dots_ref,
    up_ref, down_ref, part_up_ref, part_down_ref, float_ref,
    sums_up, sums_down, line_up, line_down, sums_par, across_par, line_par, swap_ref,
    bias_ref, gate_rows_ref, dot_row_ref, place_ref, gated_ref, logit_grad_ref, column_ref,
    load_sem, save_sem, late_sem, store_sem, par_gather_send, par_gather_recv, par_gather_local,
    gather_send, gather_recv, gather_local, swap_send, swap_recv, return_send, return_recv,
    scatter_send, scatter_recv, scatter_local, par_send, par_recv, share_send, share_recv,
):
    rows_pad, width = x_ref.shape
    groups = rows_pad // BLOCK
    places = sent_ref.shape[0]
    capacity = places // experts
    hidden_width = up_ref.shape[1]
    chunks = hidden_width // FF_CHUNK
    held = up_in.shape[0]
    place = Place(fsdp, xs)
    A, B, sources = place.A, place.B, place.peers
    expert_rows = sources * capacity
    row_block = gated_ref.shape[0]
    copy_in = pltpu.make_async_copy

    weights_ref = part_up_ref
    act_one, attended, act_two, cot_ref = (part_down_ref.at[pl.ds(i * rows_pad, rows_pad), :] for i in range(4))
    mid_ref = float_ref

    loads = [copy_in(x_in, x_raw, load_sem.at[0]), copy_in(cot_in, cot_raw, load_sem.at[1])]
    for copy in loads:
        copy.start()

    def spread(raw, there):
        for g in range(groups):
            there[g * BLOCK : g * BLOCK + GROUP_ROWS, :] = raw[g * GROUP_ROWS : (g + 1) * GROUP_ROWS, :]
            there[g * BLOCK + GROUP_ROWS : (g + 1) * BLOCK, :] = jnp.zeros((BLOCK - GROUP_ROWS, width), BF16)

    def prepare():
        shard_ref[:, : 3 * width] = qkv_ref[...]
        shard_ref[:, 3 * width : 4 * width] = out_ref[...]
        size = shard_ref.shape[0]
        eye = iota((size, size), 0) == iota((size, size), 1)
        lane = iota((size, LANES), 1)
        small = jnp.zeros((size, LANES), F32)
        for i, norm_ref in enumerate((gain_one_ref, shift_one_ref, gain_two_ref, shift_two_ref)):
            row = norm_ref[...].astype(F32).reshape(1, size)
            column = jnp.sum(jnp.where(eye, row, 0.0), axis=1, keepdims=True)
            small = jnp.where(lane == NORM_LANE + i, column, small)
        shard_ref[:, 4 * width :] = small.astype(BF16)
        shard_ref[:, 4 * width : 4 * width + experts] = jnp.transpose(router_ref[...].astype(F32)).astype(BF16)

    greet(place, prepare)

    def rows_block(ref, shard):
        size = shard_ref.shape[0]
        return ref.at[pl.ds(pl.multiple_of(shard * size, size), size), :]

    params = Gather(place, shard_ref, params_ref, rows_block, par_gather_send, par_gather_recv, par_gather_local)
    weights_in = [
        ExpertGather(place, own, full, count, gather_send.at[i], gather_recv.at[i], gather_local.at[i])
        for i, (own, full) in enumerate(((up_in, up_ref), (down_in, down_ref)))
    ]

    def each(step, el, *more):
        if el < count:
            for gather in weights_in:
                getattr(gather, step)(el, *more)

    def do(*point):
        for name, el, *more in PLAN.get(point, ()):
            if el < count:
                with jax.named_scope("_".join(map(str, (name, el, *more)))):
                    actions[name](el, *more)

    inner = jnp.logical_and(place.a > 0, place.a < A - 1)

    def ends(el):
        for k in range(1, A):
            for own in (True, False):
                each("line_step", el, k, own)

    actions = {
        "across": lambda el: each("start_across", el),
        "own": lambda el: each("start_own", el),
        "passed": lambda el: each("across_step", el),
        "relay": lambda el, k, own: pl.when(inner)(lambda: each("line_step", el, k, own)),
        "ends": lambda el: pl.when(jnp.logical_not(inner))(lambda: ends(el)),
        "cots": lambda el: cot_swaps(el, True, True),
        "cots_across": lambda el: cot_swaps(el, True, False),
        "cots_along": lambda el: cot_swaps(el, False, True),
        "rows": lambda el: row_swaps(el),
        "sums": lambda el: all_scatters("core_step", el),
        "outputs": lambda el: outputs(el, True, True),
        "outputs_across": lambda el: outputs(el, True, False),
        "outputs_along": lambda el: outputs(el, False, True),
        "sum_relay": lambda el, step: all_scatters("relay_step", el, step),
    }
    params.start()
    do("start", 0)
    targets = jnp.where(slots_ref[...] >= 0, routes_ref[...] * capacity + slots_ref[...], -1)
    meta_row_ref[...] = jnp.full(meta_row_ref.shape, -1, jnp.int32)
    for g in range(groups):
        at = slice(g * BLOCK, g * BLOCK + GROUP_ROWS)
        meta_row_ref[0:2, at] = targets[:, g * GROUP_ROWS : (g + 1) * GROUP_ROWS]
        meta_row_ref[2:4, at] = routes_ref[:, g * GROUP_ROWS : (g + 1) * GROUP_ROWS]
    image_row = iota((BLOCK, BLOCK), 0) // PATCHES
    image_col = iota((BLOCK, BLOCK), 1) // PATCHES
    bias_ref[...] = jnp.where(image_row == image_col, 0.0, -1e30)

    def slot_rows(e):
        return pl.ds(pl.multiple_of(e * capacity, 16), capacity)

    def source_rows(el, source):
        return pl.ds(pl.multiple_of(el * expert_rows + source * capacity, 16), capacity)

    def find(e):
        slot = iota((capacity, rows_pad), 0) + e * capacity
        in_first = slot == meta_row_ref[0:1, :]
        in_second = slot == meta_row_ref[1:2, :]
        return in_first, in_second, jnp.where(jnp.logical_or(in_first, in_second), 1.0, 0.0).astype(BF16)

    def swap(kind, el, k):
        peer, back = place.other_peer(k), place.seen_from(k)
        e = peer * count + el
        if kind == 1:
            source, target = gate_sent_ref.at[e], gate_ref.at[el * sources + back]
        else:
            here, there = (sent_ref, rows_ref) if kind == 0 else (cot_sent_ref, grad_ref)
            source, target = here.at[slot_rows(e), :], there.at[source_rows(el, back), :]
        return pltpu.make_async_remote_copy(
            src_ref=source, dst_ref=target, send_sem=swap_send.at[kind, el], recv_sem=swap_recv.at[kind, el, back],
            device_id=place.at_peer(peer), device_id_type=MESH,
        )

    def swap_wait(kind, el, k):
        if kind == 1:
            target = gate_ref.at[el * sources + k]
        else:
            target = (rows_ref if kind == 0 else grad_ref).at[source_rows(el, k), :]
        pltpu.make_async_remote_copy(
            src_ref=target, dst_ref=target, send_sem=swap_send.at[kind, el], recv_sem=swap_recv.at[kind, el, k],
            device_id=place.at_peer(place.other_peer(k)), device_id_type=MESH,
        ).wait_recv()

    def all_of(kind, send, recv):
        some = gate_ref.at[pl.ds(0, sources - 1)] if kind == 1 else rows_ref.at[pl.ds(0, (sources - 1) * capacity), :]
        return pltpu.make_async_remote_copy(
            src_ref=some, dst_ref=some, send_sem=send, recv_sem=recv,
            device_id=place.at(place.a, place.b, 1 - place.c), device_id_type=MESH,
        )

    def cot_swaps(el, across, along):
        @pl.loop(1, sources)
        def _(k):
            if across and along:
                swap(2, el, k).start()
            else:
                pl.when((lax.rem(k, xs) == 0) == across)(swap(2, el, k).start)

        if not along:
            return
        grad_ref[source_rows(el, 0), :] = cot_sent_ref[slot_rows(place.peer * count + el), :]

    def row_swaps(el):
        @pl.loop(1, sources)
        def _(k):
            swap(0, el, k).start()
            swap(1, el, k).start()

    for copy in loads:
        copy.wait()
    spread(cot_raw, cot_ref)
    for k in range(1, A):
        params.line_step(k)
        do("start", k)

        @pl.loop((k - 1) * experts // (A - 1), k * experts // (A - 1))
        def _(e):
            _, _, picks = find(e)
            cot_sent_ref[slot_rows(e), :] = dot(picks, cot_ref[...]).astype(BF16)

        if k == 1:
            spread(x_raw, x_ref)
            meta_ref[...] = jnp.transpose(meta_row_ref[...])
        do("after", k)
        params.across_step(k - 1)

    params.across_step(A - 1)
    params.finish_recv()
    do("begin", 0)

    small = params_ref[:, 4 * width :]
    small_rows = jnp.transpose(small.astype(F32))

    def saves(rows):
        pairs = (
            (act_one, act_one_save), (weights_ref.at[:, pl.ds(0, HEADS * BLOCK)], weights_save), (attended, attended_save),
            (mid_ref, mid_save), (act_two, act_two_save),
        )
        return [copy_in(here.at[rows, :], there.at[rows, :], save_sem.at[i]) for i, (here, there) in enumerate(pairs)]

    @pl.loop(0, groups)
    def _(g):
        rows = rows_of(g)
        x = x_ref[rows, :].astype(F32)
        normed, _ = normalize(x)
        act = (normed * small_rows[NORM_LANE : NORM_LANE + 1] + small_rows[NORM_LANE + 1 : NORM_LANE + 2]).astype(BF16)
        act_one[rows, :] = act
        triple_ref[rows, :] = dot(act, params_ref[:, : 3 * width]).astype(BF16)
        low = iota((BLOCK, LANES), 1) < HEAD_DIM
        for pair in range(HEADS // 2):
            at = pair * LANES
            q = triple_ref[rows, at : at + LANES] * HEAD_DIM ** (-0.5)
            k = triple_ref[rows, width + at : width + at + LANES]
            v = triple_ref[rows, 2 * width + at : 2 * width + at + LANES]
            total = None
            for half in range(2):
                mask = low if half == 0 else jnp.logical_not(low)
                scores = dot_against(jnp.where(mask, q, 0.0).astype(BF16), k) + bias_ref[...]
                top = jnp.max(scores, axis=-1, keepdims=True)
                raised = jnp.exp(scores - top)
                probs = raised / jnp.sum(raised, axis=-1, keepdims=True)
                probs = probs.astype(BF16)
                head = (2 * pair + half) * BLOCK
                weights_ref[rows, head : head + BLOCK] = probs
                part = dot(probs, jnp.where(mask, v, 0.0).astype(BF16))
                total = part if total is None else total + part
            attended[rows, at : at + LANES] = total.astype(BF16)

        for i in range(groups):
            pl.when(g == i)(functools.partial(do, "middle", i))

        mid = x + dot(attended[rows, :], params_ref[:, 3 * width : 4 * width])
        mid_ref[rows, :] = mid
        normed, _ = normalize(mid)
        act = (normed * small_rows[NORM_LANE + 2 : NORM_LANE + 3] + small_rows[NORM_LANE + 3 : NORM_LANE + 4]).astype(BF16)
        act_two[rows, :] = act
        logits = jnp.where(iota((BLOCK, LANES), 1) < experts, dot(act, small), -1e30)
        raised = jnp.exp(logits - jnp.max(logits, axis=-1, keepdims=True))
        probs = raised / jnp.sum(raised, axis=-1, keepdims=True)
        probs_ref[rows, :] = probs
        first, second = gates_of(probs, meta_ref[rows, :])
        gate_rows_ref[0:1, rows] = to_row(first)
        gate_rows_ref[1:2, rows] = to_row(second)
        for copy in saves(rows):
            copy.start()

        for i in range(groups):
            pl.when(g == i)(functools.partial(do, "end", i))

    @pl.loop(0, experts)
    def _(i):
        el, k = lax.div(i, sources), lax.rem(lax.rem(i, sources) + 1, sources)
        e = place.other_peer(k) * count + el
        in_first, in_second, picks = find(e)
        gate = jnp.sum(
            jnp.where(in_first, gate_rows_ref[0:1, :], jnp.where(in_second, gate_rows_ref[1:2, :], 0.0)),
            axis=1, keepdims=True,
        )
        sent_ref[slot_rows(e), :] = dot(picks, act_two[...]).astype(BF16)
        gate_sent_ref[e, 0:1, :] = to_row(gate)

        @pl.when(jnp.logical_and(el == 0, k > 0))
        def _():
            swap(0, el, k).start()
            swap(1, el, k).start()

        @pl.when(k == 0)
        def _():
            rows_ref[source_rows(el, 0), :] = sent_ref[slot_rows(e), :]
            gate_ref[el * sources] = gate_sent_ref[e]

        for at in range(8):
            pl.when(i == at)(functools.partial(do, "dispatch", at))

    for copy in saves(pl.ds(0, rows_pad)):
        copy.wait()

    part_up = part_up_ref.at[pl.ds(0, count * width), :].reshape(count, A, B, 2, up_in.shape[1], part_up_ref.shape[1])
    part_down = part_down_ref.at[pl.ds(0, count * hidden_width), :].reshape(count, A, B, 2, down_in.shape[1], width)
    scatters = [
        ExpertScatter(place, part, sums, line, out, count, scatter_send.at[i], scatter_recv.at[i], scatter_local.at[i])
        for i, (part, sums, line, out) in enumerate(
            (
                (lambda el: part_up.at[el, :, :, :, :, pl.ds(0, hidden_width)], sums_up, line_up, up_grad_out),
                (lambda el: part_down.at[el], sums_down, line_down, down_grad_out),
            )
        )
    ]

    def all_scatters(step, el, *more):
        for scatter in scatters:
            getattr(scatter, step)(el, *more)

    pairs = HEADS // 2
    columns = [slice(3 * LANES * p, 3 * LANES * (p + 1)) for p in range(pairs)]
    columns += [slice(3 * width, 4 * width), slice(4 * width, 4 * width + LANES)]
    par_out, par_small = pairs, pairs + 1
    par = Scatter(place, part_up.at[0], sums_par, across_par, line_par, columns, par_send, par_recv)

    def shares(item):
        at = columns[item]
        out = []
        for k in range(1, xs):
            to, back = lax.rem(place.x + k, xs), xs - 1 - k
            out.append(
                pltpu.make_async_remote_copy(
                    src_ref=swap_ref.at[place.x, :, at], dst_ref=swap_ref.at[place.x, :, at],
                    send_sem=share_send.at[item, back], recv_sem=share_recv.at[item, back],
                    device_id=(to, place.me), device_id_type=MESH,
                )
            )
        return out

    def par_last(item):
        swap_ref[place.x, :, columns[item]] = par.line_step(item).astype(BF16)
        for copy in shares(item):
            copy.start()

    def returned(kind, el, k):
        e = place.peer * count + el
        if kind == 1:
            source, target = dots_sent_ref.at[el * sources + k], dots_ref.at[e]
        else:
            here, there = (grad_ref, grad_slots_ref) if kind == 0 else (rows_ref, back_ref)
            source, target = here.at[source_rows(el, k), :], there.at[slot_rows(e), :]
        return pltpu.make_async_remote_copy(
            src_ref=source, dst_ref=target,
            send_sem=return_send.at[kind, el], recv_sem=return_recv.at[kind, el],
            device_id=place.at_peer(place.other_peer(k)), device_id_type=MESH,
        )

    def give_back(kind, el, first=1, stop=sources):
        @pl.loop(first, stop)
        def _(k):
            returned(kind, el, k).start()

    def outputs(el, across, along):
        @pl.loop(1, sources)
        def _(k):
            if across and along:
                returned(2, el, k).start()
            else:
                pl.when((lax.rem(k, xs) == 0) == across)(returned(2, el, k).start)

    def return_wait(kind, el):
        all_of(kind, return_send.at[kind, el], return_recv.at[kind, el]).wait_recv()

    def expert(el):
        blocks = expert_rows // row_block
        block_sources = row_block // capacity
        order = list(range(blocks))
        if el > 0 and el == count - 1:
            order.reverse()
        each("core_wait", el)
        for turn, block in enumerate(order):
            first, stop = block * block_sources, (block + 1) * block_sources
            for kind in range(3):
                pl.loop(max(first, 1), stop)(functools.partial(swap_wait, kind, el))
            do("before", el, turn)
            here = pl.ds(el * expert_rows + block * row_block, row_block)
            float_ref[: 2 * row_block, :] = jnp.zeros((2 * row_block, width), F32)

            @pl.loop(first, stop)
            def _(k):
                gate = to_column(gate_ref[el * sources + k, 0:1, :], capacity)
                cots = grad_ref[source_rows(el, k), :].astype(F32)
                local = pl.ds(pl.multiple_of((k - first) * capacity, 16), capacity)
                gated_ref[local, :] = (gate * cots).astype(BF16)

            @pl.loop(0, chunks)
            def _(f):
                at = pl.ds(pl.multiple_of(f * FF_CHUNK, FF_CHUNK), FF_CHUNK)
                down_at = pl.ds(pl.multiple_of(el * hidden_width + f * FF_CHUNK, FF_CHUNK), FF_CHUNK)
                rows, grads = rows_ref[here, :], gated_ref[...]
                up_part, down_part = up_ref[el * width : (el + 1) * width, at], down_ref[down_at, :]
                hidden = dot(rows, up_part)
                spread = 0.5 * (1.0 + lax.erf(hidden * ROOT_HALF))
                active = (hidden * spread).astype(BF16)
                slope = spread + hidden * (DENSITY_SCALE * jnp.exp(-0.5 * hidden * hidden))
                float_ref[:row_block, :] += dot(active, down_part)
                grad_hidden = (dot_against(grads, down_part) * slope).astype(BF16)
                float_ref[row_block : 2 * row_block, :] += dot_against(grad_hidden, up_part)
                size = up_in.shape[1]
                up_sum = dot_rows(rows, grad_hidden).reshape(A, B, 2, size, FF_CHUNK)
                down_sum = dot_rows(active, grads)
                if turn > 0:
                    up_sum += part_up[el, :, :, :, :, at].astype(F32)
                    down_sum += part_down_ref[down_at, :].astype(F32)
                part_up[el, :, :, :, :, at] = up_sum.astype(BF16)
                part_down_ref[down_at, :] = down_sum.astype(BF16)
                for i in range(chunks):
                    pl.when(f == i)(functools.partial(do, "expert", el, turn * chunks + i))

            @pl.loop(first, stop)
            def _(k):
                at = source_rows(el, k)
                local = pl.ds(pl.multiple_of((k - first) * capacity, 16), capacity)
                back = float_ref[local, :].astype(BF16)
                rows_ref[at, :] = back
                dots = jnp.sum(back.astype(F32) * grad_ref[at, :].astype(F32), axis=1, keepdims=True)
                dots_sent_ref[el * sources + k, 0:1, :] = to_row(dots)
                local = pl.ds(pl.multiple_of(row_block + (k - first) * capacity, 16), capacity)
                grad_ref[at, :] = float_ref[local, :].astype(BF16)

            give_back(0, el, max(first, 1), stop)
            give_back(1, el, max(first, 1), stop)

        all_scatters("start", el)
        own, e = source_rows(el, 0), place.peer * count + el
        back_ref[slot_rows(e), :] = rows_ref[own, :]
        grad_slots_ref[slot_rows(e), :] = grad_ref[own, :]
        dots_ref[e] = dots_sent_ref[el * sources]

    for el in range(count):
        expert(el)
        do("after_expert", el)

    def late_loads():
        out = [copy_in(weights_save, up_ref.at[pl.ds(0, rows_pad), :], late_sem.at[0])]
        for i, array in enumerate((act_one_save, attended_save, act_two_save)):
            out.append(copy_in(array, down_ref.at[pl.ds(i * rows_pad, rows_pad), :], late_sem.at[1 + i]))
        for i in range(2):
            out.append(copy_in(mid_save, float_ref.at[pl.ds(i * rows_pad, rows_pad), :], late_sem.at[4 + i]))
        return out

    for el in range(count):
        each("finish", el)
    for copy in late_loads():
        copy.start()
    spread(cot_raw, down_ref.at[pl.ds(3 * rows_pad, rows_pad), :])
    act_one, attended, act_two, cot_ref = (down_ref.at[pl.ds(i * rows_pad, rows_pad), :] for i in range(4))
    weights_ref = up_ref
    input_grad_ref = float_ref
    all_scatters("core_step", count - 1)
    if count > 1:
        all_scatters("relay_step", count - 2, 2)
    for copy in late_loads():
        copy.wait()
    for kind in range(2):
        for el in range(count):
            return_wait(kind, el)
    for el in range(count):
        do("returned", el)
    all_scatters("relay_step", count - 1, 0)
    for el in range(count):
        for kind in range(3):
            all_of(kind, swap_send.at[kind, el], return_recv.at[kind, el]).wait_send()

    grad_attended_ref = sent_ref.at[pl.ds(0, rows_pad), :]
    branch_ref = cot_sent_ref.at[pl.ds(0, rows_pad), :]
    gain_one = small_rows[NORM_LANE : NORM_LANE + 1]
    gain_two = small_rows[NORM_LANE + 2 : NORM_LANE + 3]
    column_ref[...] = jnp.zeros_like(column_ref)
    flat = jnp.zeros((8, places), F32)
    for e in range(experts):
        row = dots_ref[e]
        row = jnp.concatenate([row, jnp.zeros((8, places - row.shape[1]), F32)], axis=1)
        flat += pltpu.roll(row, e * capacity, 1) if e else row
    dot_row_ref[...] = flat

    def last_sums(g):
        with jax.named_scope("last_sums_%d" % g):
            last = count - 1
            if g == 3:
                pl.when(jnp.logical_not(inner))(lambda: all_scatters("relay_step", last, 1))
                if count > 1:
                    all_scatters("line_step", last - 1)
            if g == 4:
                pl.when(inner)(lambda: all_scatters("relay_step", last, 1))
            if g == 5:
                pl.when(jnp.logical_not(inner))(lambda: all_scatters("relay_step", last, 2))
            if g == 7:
                pl.when(inner)(lambda: all_scatters("relay_step", last, 2))

    def store(i, rows):
        here, there = ((cot_ref, out_out), (input_grad_ref, input_grad_out))[i]
        return copy_in(here.at[rows, :], there.at[rows, :], store_sem.at[i])

    @pl.loop(0, groups)
    def _(g):
        rows = rows_of(g)
        meta = meta_ref[rows, :]
        probs = probs_ref[rows, :]
        lane = iota((BLOCK, LANES), 1)
        grad_first = jnp.zeros((BLOCK, LANES), F32)
        grad_second = jnp.zeros((BLOCK, LANES), F32)
        for c in range(places // LANES):
            at = c * LANES
            in_first = lane == meta[:, 0:1] - at
            in_second = lane == meta[:, 1:2] - at
            place_ref[:, at : at + LANES] = jnp.where(jnp.logical_or(in_first, in_second), 1.0, 0.0).astype(BF16)
            dots = dot_row_ref[0:1, at : at + LANES]
            grad_first += jnp.where(in_first, dots, 0.0)
            grad_second += jnp.where(in_second, dots, 0.0)
        grad_first = jnp.sum(grad_first, axis=1, keepdims=True)
        grad_second = jnp.sum(grad_second, axis=1, keepdims=True)
        mid = input_grad_ref[rows, :]
        grad_probs = jnp.where(lane == meta[:, 2:3], grad_first, 0.0) + jnp.where(lane == meta[:, 3:4], grad_second, 0.0)
        grad_logits = (probs * (grad_probs - jnp.sum(grad_probs * probs, axis=-1, keepdims=True))).astype(BF16)
        logit_grad_ref[rows, :] = grad_logits
        grad_act = dot(place_ref[...], grad_slots_ref[...]) + dot_against(grad_logits, small)
        normed, inverse = normalize(mid)
        column_ref[NORM_LANE + 2 : NORM_LANE + 3, :] += jnp.sum(grad_act * normed, axis=0, keepdims=True)
        column_ref[NORM_LANE + 3 : NORM_LANE + 4, :] += jnp.sum(grad_act, axis=0, keepdims=True)
        grad_mid = cot_ref[rows, :].astype(F32) + denormalize(grad_act, normed, inverse, gain_two)
        input_grad_ref[rows, :] = grad_mid
        branch_ref[rows, :] = grad_mid.astype(BF16)
        grad_attended = dot_against(branch_ref[rows, :], params_ref[:, 3 * width : 4 * width])
        grad_attended_ref[rows, :] = grad_attended.astype(BF16)
        for i in range(groups):
            pl.when(g == i)(functools.partial(last_sums, i))

    split = (A, B, 2, up_in.shape[1])

    def put(item, value):
        at = columns[item]
        part_up[0, :, :, :, :, at] = value.astype(BF16).reshape(*split, at.stop - at.start)
        par.start(item)

    put(par_out, dot_rows(attended[...], branch_ref[...]))

    def attention_backward(pair, g):
        rows = rows_of(g)
        at = pair * LANES
        low = iota((BLOCK, LANES), 1) < HEAD_DIM
        q = triple_ref[rows, at : at + LANES] * HEAD_DIM ** (-0.5)
        k = triple_ref[rows, width + at : width + at + LANES]
        v = triple_ref[rows, 2 * width + at : 2 * width + at + LANES]
        upstream = grad_attended_ref[rows, at : at + LANES]
        grad_q = grad_k = grad_v = jnp.zeros((BLOCK, LANES), F32)
        for half in range(2):
            mask = low if half == 0 else jnp.logical_not(low)
            upstream_half = jnp.where(mask, upstream, 0.0).astype(BF16)
            head = (2 * pair + half) * BLOCK
            weights = weights_ref[rows, head : head + BLOCK]
            kept = weights.astype(F32)
            grad_weights = dot_against(upstream_half, v)
            inner = jnp.sum(grad_weights * kept, axis=-1, keepdims=True)
            grad_scores = (kept * (grad_weights - inner)).astype(BF16)
            grad_q += dot(grad_scores, jnp.where(mask, k, 0.0).astype(BF16))
            grad_k += dot_rows(grad_scores, jnp.where(mask, q, 0.0).astype(BF16))
            grad_v += dot_rows(weights, upstream_half)
        triple_ref[rows, at : at + LANES] = (grad_q * HEAD_DIM ** (-0.5)).astype(BF16)
        triple_ref[rows, width + at : width + at + LANES] = grad_k.astype(BF16)
        triple_ref[rows, 2 * width + at : 2 * width + at + LANES] = grad_v.astype(BF16)

    def par_steps(*steps):
        for name, item in steps:
            with jax.named_scope("%s_%d" % (name, item)):
                par_last(item) if name == "last" else getattr(par, name + "_step")(item)

    for pair in range(pairs):
        pl.loop(0, groups)(functools.partial(attention_backward, pair))
        if pair == 0:
            par_steps(("core", par_out))
        elif pair == 1:
            par_steps(("core", 0))
        else:
            par_steps(("across", par_out if pair == 2 else pair - 3), ("core", pair - 1))
        last_sums(groups + pair)
        kinds = [triple_ref[:, kind * width + pair * LANES : kind * width + (pair + 1) * LANES] for kind in range(3)]
        put(pair, dot_rows(act_one[...], jnp.concatenate(kinds, axis=1)))

    @pl.loop(0, groups)
    def _(g):
        rows = rows_of(g)
        grad_act = dot_against(triple_ref[rows, :], params_ref[:, : 3 * width])
        normed, inverse = normalize(x_ref[rows, :].astype(F32))
        column_ref[NORM_LANE : NORM_LANE + 1, :] += jnp.sum(grad_act * normed, axis=0, keepdims=True)
        column_ref[NORM_LANE + 1 : NORM_LANE + 2, :] += jnp.sum(grad_act, axis=0, keepdims=True)
        input_grad_ref[rows, :] += denormalize(grad_act, normed, inverse, gain_one)
        store(1, rows).start()

        @pl.when(g == 0)
        def _():
            par_steps(("core", pairs - 1), ("across", pairs - 3))

        @pl.when(g == 2)
        def _():
            par_steps(("across", pairs - 2))

    put(par_small, dot_rows(act_two[...], logit_grad_ref[...]) + jnp.transpose(column_ref[...]))
    for el in range(count):
        return_wait(2, el)

    def combine(g):
        rows = rows_of(g)
        meta = meta_ref[rows, :]
        gate_first, gate_second = gates_of(probs_ref[rows, :], meta)
        lane = iota((BLOCK, LANES), 1)
        for c in range(places // LANES):
            at = c * LANES
            in_first = lane == meta[:, 0:1] - at
            in_second = lane == meta[:, 1:2] - at
            place_ref[:, at : at + LANES] = jnp.where(in_first, gate_first, jnp.where(in_second, gate_second, 0.0)).astype(BF16)
        mid = float_ref[pl.ds(pl.multiple_of(rows_pad + g * BLOCK, BLOCK), BLOCK), :]
        cot_ref[rows, :] = (mid + dot(place_ref[...], back_ref[...])).astype(BF16)
        store(0, rows).start()

    steps = (
        [("across", pairs - 1), ("core", par_small)], [("across", par_small)], [], [("last", item) for item in (par_out, *range(pairs), par_small)],
    )

    @pl.loop(0, groups)
    def _(g):
        combine(g)
        pl.when(g == 2)(lambda: all_scatters("line_step", count - 1))
        for i in range(groups):
            pl.when(g == i)(functools.partial(par_steps, *steps[i]))

    for i in range(2):
        store(i, pl.ds(0, rows_pad)).wait()

    params.finish_send()
    for el in range(count):
        for kind in range(3):
            all_of(kind, return_send.at[kind, el], return_recv.at[kind, el]).wait_send()
        all_scatters("finish", el)
    for item in range(len(columns)):
        par.finish(item)
    for item in range(len(columns)):
        for copy in shares(item):
            copy.wait()
    total = swap_ref[0].astype(F32)
    for i in range(1, xs):
        total += swap_ref[i].astype(F32)
    share_out[...] = total


def finish_kernel(
    experts, out_pad, input_grad_pad, share, up_half, down_half,
    out, input_grad, qkv, out_weight, router, gain_one, shift_one, gain_two, shift_two, up, down,
):
    width = out.shape[1]
    for g in range(out_pad.shape[0] // BLOCK):
        here, there = slice(g * BLOCK, g * BLOCK + GROUP_ROWS), slice(g * GROUP_ROWS, (g + 1) * GROUP_ROWS)
        out[there, :] = out_pad[here, :]
        input_grad[there, :] = input_grad_pad[here, :]
    for pair in range(HEADS // 2):
        for kind in range(3):
            here, there = (3 * pair + kind) * LANES, kind * width + pair * LANES
            qkv[:, there : there + LANES] = share[:, here : here + LANES]
    out_weight[...] = share[:, 3 * width : 4 * width]
    small = jnp.transpose(share[:, 4 * width :])
    router[...] = small[:experts, :]
    for i, vector in enumerate((gain_one, shift_one, gain_two, shift_two)):
        vector[...] = small[NORM_LANE + i : NORM_LANE + i + 1, :].reshape(vector.shape)
    up[...] = up_half[...].astype(F32)
    down[...] = down_half[...].astype(F32)


def on_device(
    inputs, cotangent, routes, slots, qkv_weight, out_weight, router_weight,
    norm1_gain, norm1_shift, norm2_gain, norm2_shift, expert_up, expert_down,
):
    rows_dev, width = inputs.shape
    groups = rows_dev // GROUP_ROWS
    rows_pad = groups * BLOCK
    fsdp = lax.axis_size("fsdp")
    peers = lax.axis_size("expert")
    held = expert_up.shape[0]
    experts = held * peers
    capacity = (42 * rows_dev + 20 * experts - 1) // (20 * experts)
    capacity = -(-capacity // 16) * 16
    places = experts * capacity

    vmem = pl.BlockSpec(memory_space=pltpu.VMEM)
    hbm = pl.BlockSpec(memory_space=pl.ANY)
    shape = jax.ShapeDtypeStruct
    dma = pltpu.SemaphoreType.DMA
    A, B = 4, fsdp // 8
    count = held // B
    sources = peers * B
    up_rows, down_rows = expert_up.shape[1], expert_down.shape[1]
    hidden_width = expert_up.shape[2]
    packed_width = 4 * width + LANES
    items = HEADS // 2 + 2
    expert_rows = sources * capacity
    row_block = max(n for n in range(capacity, MAX_ROWS + 1, capacity) if expert_rows % n == 0)
    routes_of = 3 + B - 1
    lanes_of = -(-capacity // LANES) * LANES

    def buffer(*dims, dtype=BF16):
        return pltpu.VMEM(dims, dtype)

    out, input_grad, share, up_grad, down_grad, *_ = pl.pallas_call(
        functools.partial(block_kernel, experts, fsdp, peers, count),
        out_shape=(
            shape((rows_pad, width), BF16),
            shape((rows_pad, width), F32),
            shape((up_rows, packed_width), F32),
            shape(expert_up.shape, BF16),
            shape(expert_down.shape, BF16),
            shape((rows_pad, width), BF16),
            shape((rows_pad, HEADS * BLOCK), BF16),
            shape((rows_pad, width), BF16),
            shape((rows_pad, width), F32),
            shape((rows_pad, width), BF16),
        ),
        in_specs=[hbm] * 2 + [vmem] * 9 + [hbm] * 2,
        out_specs=[hbm] * 2 + [vmem] + [hbm] * 7,
        scratch_shapes=[
            buffer(rows_dev, width), buffer(rows_dev, width), buffer(up_rows, packed_width),
            buffer(8, rows_pad, dtype=jnp.int32), buffer(rows_pad, 8, dtype=jnp.int32),
            buffer(rows_pad, width), buffer(fsdp * up_rows, packed_width), buffer(rows_pad, 3 * width),
            buffer(rows_pad, LANES, dtype=F32),
            buffer(places, width), buffer(places, width), buffer(experts, 8, lanes_of, dtype=F32),
            buffer(places, width), buffer(places, width), buffer(experts, 8, lanes_of, dtype=F32),
            buffer(places, width), buffer(places, width),
            buffer(experts, 8, lanes_of, dtype=F32), buffer(experts, 8, lanes_of, dtype=F32),
            buffer(max(count * width, rows_pad), hidden_width), buffer(max(count * hidden_width, 4 * rows_pad), width),
            buffer(max(count * width, rows_pad), packed_width), buffer(max(count * hidden_width, 4 * rows_pad), width),
            buffer(max(2 * row_block, 2 * rows_pad), width, dtype=F32),
            buffer(count, A, B, up_rows, hidden_width), buffer(count, A, B, down_rows, width),
            buffer(count, 2, A - 1, B, up_rows, hidden_width), buffer(count, 2, A - 1, B, down_rows, width),
            buffer(A, B, up_rows, packed_width), buffer(B - 1, A, up_rows, packed_width),
            buffer(A - 1, up_rows, packed_width), buffer(peers, up_rows, packed_width),
            buffer(BLOCK, BLOCK, dtype=F32), buffer(8, rows_pad, dtype=F32), buffer(8, places, dtype=F32),
            buffer(BLOCK, places), buffer(row_block, width), buffer(rows_pad, LANES), buffer(LANES, width, dtype=F32),
            dma((2,)), dma((5,)), dma((6,)), dma((2,)), dma((routes_of,)), dma((A * B + 1,)), dma,
            dma((2, count, routes_of)), dma((2, count, A * B + 1)), dma((2, count)),
            dma((3, count)), dma((3, count, sources)), dma((3, count)), dma((3, count)),
            dma((2, count, 3 + B - 1)), dma((2, count, 2 * A + B - 2)), dma((2, count)),
            dma((items, 2)), dma((items, 3)), dma((items, peers - 1)), dma((items, peers - 1)),
        ],
        compiler_params=pltpu.CompilerParams(vmem_limit_bytes=VMEM_LIMIT, collective_id=0, has_side_effects=True),
        name="encoder_block",
    )(
        inputs, cotangent, routes.T, slots.T, qkv_weight, out_weight, router_weight.T,
        norm1_gain, norm1_shift, norm2_gain, norm2_shift, expert_up, expert_down,
    )
    vector = shape((up_rows,), F32)
    results = pl.pallas_call(
        functools.partial(finish_kernel, experts),
        out_shape=(
            shape((rows_dev, width), BF16),
            shape((rows_dev, width), F32),
            shape((up_rows, 3 * width), F32),
            shape((up_rows, width), F32),
            shape((experts, up_rows), F32),
            *[vector] * 4,
            shape(expert_up.shape, F32),
            shape(expert_down.shape, F32),
        ),
        in_specs=[vmem] * 5,
        out_specs=[vmem] * 11,
        compiler_params=pltpu.CompilerParams(vmem_limit_bytes=VMEM_LIMIT),
        name="results",
    )(out, input_grad, share, up_grad, down_grad)
    return (*results[:4], results[4].T, *results[5:])


def solution(mesh):
    tokens = P(("expert", "fsdp"), None)
    rows, vector, expert = P("fsdp", None), P("fsdp"), P("expert", "fsdp", None)
    return jax.shard_map(
        on_device,
        mesh=mesh,
        in_specs=(tokens,) * 4 + (rows,) * 3 + (vector,) * 4 + (expert,) * 2,
        out_specs=(tokens,) * 2 + (rows,) * 3 + (vector,) * 4 + (expert,) * 2,
        check_vma=False,
    )
```

```python
import functools

import jax
import jax.numpy as jnp
from jax import lax
from jax.experimental import pallas as pl
from jax.experimental.pallas import tpu as pltpu
from jax.sharding import PartitionSpec as P

HEADS = 8
HEAD_DIM = 64
PATCHES = 49
EPS = 1e-06
ROOT_HALF = 0.7071067811865476
DENSITY_SCALE = 0.3989422804014327

BLOCK = 256
GROUP_IMAGES = BLOCK // PATCHES
GROUP_ROWS = GROUP_IMAGES * PATCHES
LANES = 128
NORM_LANE = 64
FF_CHUNK = 512
MAX_ROWS = 640
VMEM_LIMIT = 63 * 1024 * 1024

MESH = pl.DeviceIdType.MESH
PLAN = {
    ("start", 0): [("across", 0)],
    ("start", 1): [("own", 0)],
    ("start", 3): [("passed", 0)],
    ("after", 3): [("relay", 0, 1, True)],
    ("after", 1): [("cots", 0, "x"), ("cots", 1, "x")],
    ("begin", 0): [("cots", 0, "y", "far")],
    ("end", 0): [("relay", 0, 1, False)],
    ("middle", 1): [("relay", 0, 2, True)],
    ("end", 1): [("across", 1)],
    ("end", 2): [("relay", 0, 2, False), ("cots", 1, "y")],
    ("dispatch", 7): [("own", 1), ("passed", 1), ("ends", 0)],
    ("expert", 0, 0): [("relay", 1, 1, True)],
    ("expert", 0, 1): [("relay", 1, 1, False)],
    ("expert", 0, 2): [("rows", 1)],
    ("expert", 0, 3): [("cots", 1, "far"), ("relay", 1, 2, True)],
    ("expert", 0, 4): [("relay", 1, 2, False)],
    ("after_expert", 0): [("sums", 0), ("sum_relay", 0, 0), ("ends", 1)],
    ("expert", 1, 2): [("sum_relay", 0, 1)],
    ("expert", 1, 7): [("sum_relay", 0, 2)],
    ("after_expert", 1): [("outputs", 0, "y")],
    ("returned", 0): [("outputs", 0, "x", "far")],
    ("returned", 1): [("outputs", 1, "x", "y", "far")],
}
F32 = jnp.float32
BF16 = jnp.bfloat16


def dot(left, right):
    return lax.dot_general(left, right, (((1,), (0,)), ((), ())), preferred_element_type=F32)


def dot_rows(left, right):
    return lax.dot_general(left, right, (((0,), (0,)), ((), ())), preferred_element_type=F32)


def dot_against(left, right):
    return lax.dot_general(left, right, (((1,), (1,)), ((), ())), preferred_element_type=F32)


def iota(shape, dim):
    return lax.broadcasted_iota(jnp.int32, shape, dim)


def normalize(values):
    center = jnp.mean(values, axis=-1, keepdims=True)
    offset = values - center
    spread = jnp.mean(offset * offset, axis=-1, keepdims=True)
    inverse = lax.rsqrt(spread + EPS)
    return offset * inverse, inverse


def denormalize(upstream, normed, inverse, gain):
    scaled = upstream * gain
    return inverse * (
        scaled
        - jnp.mean(scaled, axis=-1, keepdims=True)
        - normed * jnp.mean(scaled * normed, axis=-1, keepdims=True)
    )


def to_row(column):
    n = column.shape[0]
    parts = []
    for at in range(0, n, LANES):
        size = min(LANES, n - at)
        eye = iota((size, LANES), 0) == iota((size, LANES), 1)
        parts.append(jnp.sum(jnp.where(eye, column[at : at + size], 0.0), axis=0, keepdims=True))
    return parts[0] if len(parts) == 1 else jnp.concatenate(parts, axis=1)


def to_column(row, n):
    eye = iota((n, row.shape[1]), 0) == iota((n, row.shape[1]), 1)
    return jnp.sum(jnp.where(eye, row, 0.0), axis=1, keepdims=True)


def rows_of(g):
    return pl.ds(pl.multiple_of(g * BLOCK, BLOCK), BLOCK)


def gates_of(probs, meta):
    lane = iota(probs.shape, 1)
    first = jnp.sum(jnp.where(lane == meta[:, 2:3], probs, 0.0), axis=1, keepdims=True)
    second = jnp.sum(jnp.where(lane == meta[:, 3:4], probs, 0.0), axis=1, keepdims=True)
    return first, second


class Place:
    def __init__(self, fsdp, xs):
        self.A, self.B = 4, fsdp // 8
        self.x = lax.axis_index("expert")
        self.me = lax.axis_index("fsdp")
        self.c = lax.rem(self.me, 2)
        line = lax.div(self.me, 2)
        self.b = lax.rem(line, self.B)
        self.a = lax.div(line, self.B)
        self.xs, self.peers = xs, xs * self.B
        self.peer = self.x * self.B + self.b

    def index(self, a, b, c):
        return (a * self.B + b) * 2 + c

    def other_b(self, j):
        return lax.rem(self.b + 1 + j, self.B)

    def at(self, a, b, c):
        return (self.x, self.index(a, b, c))

    def at_peer(self, peer):
        return (lax.div(peer, self.B), self.index(self.a, lax.rem(peer, self.B), self.c))

    def other_peer(self, k):
        x, b = lax.rem(self.x + lax.rem(k, self.xs), self.xs), lax.rem(self.b + lax.div(k, self.xs), self.B)
        return x * self.B + b

    def seen_from(self, k):
        x, b = lax.rem(self.xs - lax.rem(k, self.xs), self.xs), lax.rem(self.B - lax.div(k, self.xs), self.B)
        return b * self.xs + x


def greet(place, meanwhile):
    barrier = pltpu.get_barrier_semaphore()

    def signal(device):
        pl.semaphore_signal(barrier, inc=1, device_id=device, device_id_type=MESH)

    for k in range(1, place.A):
        signal(place.at(lax.rem(place.a + k, place.A), place.b, place.c))
    for k in range(1, place.peers):
        signal(place.at_peer(place.other_peer(k)))
    signal(place.at(place.a, place.b, 1 - place.c))
    meanwhile()
    pl.semaphore_wait(barrier, place.A - 1 + place.peers - 1 + 1)


class Gather:
    RIGHT, LEFT, CORE, ACROSS = 0, 1, 2, 3

    def __init__(self, place, own, full, block, send_sem, recv_sem, local_sem):
        self.place, self.own, self.full, self.block = place, own, full, block
        self.send_sem, self.recv_sem, self.local_sem = send_sem, recv_sem, local_sem

    def copy(self, shard, route, source, a, b, c):
        return pltpu.make_async_remote_copy(
            src_ref=source, dst_ref=self.block(self.full, shard),
            send_sem=self.send_sem.at[route], recv_sem=self.recv_sem.at[self.arrival(shard, route)],
            device_id=self.place.at(a, b, c), device_id_type=MESH,
        )

    def arrival(self, shard, route):
        return self.place.A * self.place.B if route == self.CORE else lax.div(shard, 2)

    def some(self, route, blocks):
        size = self.own.shape[0]
        ref = self.full.at[pl.ds(0, blocks * size), :]
        p = self.place
        return pltpu.make_async_remote_copy(
            src_ref=ref, dst_ref=ref, send_sem=self.send_sem.at[route], recv_sem=self.recv_sem.at[p.A * p.B],
            device_id=p.at(p.a, p.b, 1 - p.c), device_id_type=MESH,
        )

    def onward(self, shard, source, right, left, across, act):
        p = self.place
        if right is not None:
            pl.when(right)(lambda: act(self.copy(shard, self.RIGHT, source, p.a + 1, p.b, p.c)))
        if left is not None:
            pl.when(left)(lambda: act(self.copy(shard, self.LEFT, source, p.a - 1, p.b, p.c)))
        if across:
            for j in range(p.B - 1):
                act(self.copy(shard, self.ACROSS + j, source, p.a, p.other_b(j), p.c))
        act(self.copy(shard, self.CORE, source, p.a, p.b, 1 - p.c))

    def local(self):
        return pltpu.make_async_copy(self.own, self.block(self.full, self.place.me), self.local_sem)

    def start(self):
        p = self.place
        self.local().start()
        self.onward(p.me, self.own, p.a < p.A - 1, p.a > 0, True, lambda copy: copy.start())

    def arrived(self, shard):
        p = self.place
        self.copy(shard, self.RIGHT, self.block(self.full, shard), p.a, p.b, 1 - p.c).wait_recv()

    def line_step(self, k):
        p = self.place

        def from_left():
            shard = p.index(p.a - k, p.b, p.c)
            self.arrived(shard)
            self.onward(shard, self.block(self.full, shard), p.a < p.A - 1, None, True, lambda copy: copy.start())

        def from_right():
            shard = p.index(p.a + k, p.b, p.c)
            self.arrived(shard)
            self.onward(shard, self.block(self.full, shard), None, p.a > 0, True, lambda copy: copy.start())

        pl.when(p.a - k >= 0)(from_left)
        pl.when(p.a + k < p.A)(from_right)

    def across_step(self, k):
        p = self.place

        def row(a):
            for j in range(p.B - 1):
                shard = p.index(a, p.other_b(j), p.c)
                self.arrived(shard)
                self.onward(shard, self.block(self.full, shard), None, None, False, lambda copy: copy.start())

        if k == 0:
            row(p.a)
        else:
            pl.when(p.a - k >= 0)(lambda: row(p.a - k))
            pl.when(p.a + k < p.A)(lambda: row(p.a + k))

    def finish_recv(self):
        p = self.place
        self.local().wait()
        self.some(self.CORE, p.A * p.B).wait_recv()

    def finish_send(self):
        p = self.place
        for a in range(p.A - 1):
            pl.when(p.a == a)(self.some(self.RIGHT, a + 1).wait_send)
            pl.when(p.a == a + 1)(self.some(self.LEFT, p.A - 1 - a).wait_send)
        for j in range(p.B - 1):
            self.some(self.ACROSS + j, p.A).wait_send()
        self.some(self.CORE, p.A * p.B).wait_send()


class ExpertGather:
    RIGHT, LEFT, CORE, ACROSS = 0, 1, 2, 3

    def __init__(self, place, own, full, count, send_sem, recv_sem, local_sem):
        self.place, self.own, self.full, self.count = place, own, full, count
        self.send_sem, self.recv_sem, self.local_sem = send_sem, recv_sem, local_sem
        self.size = own.shape[1]
        self.depth = self.size * place.A * place.B * 2

    def block(self, el, shard):
        return self.full.at[pl.ds(pl.multiple_of(el * self.depth + shard * self.size, self.size), self.size), :]

    def mine(self, el):
        return self.own.at[self.place.b * self.count + el]

    def copy(self, el, shard, route, source, a, b, c):
        return pltpu.make_async_remote_copy(
            src_ref=source, dst_ref=self.block(el, shard),
            send_sem=self.send_sem.at[el, route], recv_sem=self.recv_sem.at[el, self.arrival(shard, route)],
            device_id=self.place.at(a, b, c), device_id_type=MESH,
        )

    def arrival(self, shard, route):
        return self.place.A * self.place.B if route == self.CORE else lax.div(shard, 2)

    def some(self, el, route, blocks):
        ref = self.full.at[pl.ds(el * self.depth, blocks * self.size), :]
        p = self.place
        return pltpu.make_async_remote_copy(
            src_ref=ref, dst_ref=ref, send_sem=self.send_sem.at[el, route], recv_sem=self.recv_sem.at[el, p.A * p.B],
            device_id=p.at(p.a, p.b, 1 - p.c), device_id_type=MESH,
        )

    def across(self, el):
        p = self.place
        out = []
        for j in range(p.B - 1):
            to = p.other_b(j)
            out.append(self.copy(el, p.me, self.ACROSS + j, self.own.at[to * self.count + el], p.a, to, p.c))
        return out

    def local(self, el):
        return pltpu.make_async_copy(self.mine(el), self.block(el, self.place.me), self.local_sem.at[el])

    def onward(self, el, shard, source, right, left, act):
        p = self.place
        if right:
            pl.when(p.a < p.A - 1)(lambda: act(self.copy(el, shard, self.RIGHT, source, p.a + 1, p.b, p.c)))
        if left:
            pl.when(p.a > 0)(lambda: act(self.copy(el, shard, self.LEFT, source, p.a - 1, p.b, p.c)))
        act(self.copy(el, shard, self.CORE, source, p.a, p.b, 1 - p.c))

    def arrived(self, el, shard):
        p = self.place
        self.copy(el, shard, self.RIGHT, self.block(el, shard), p.a, p.b, 1 - p.c).wait_recv()

    def start_across(self, el):
        for copy in self.across(el):
            copy.start()

    def start_own(self, el):
        self.local(el).start()
        self.onward(el, self.place.me, self.mine(el), True, True, lambda copy: copy.start())

    def across_step(self, el):
        p = self.place
        for j in range(p.B - 1):
            shard = p.index(p.a, p.other_b(j), p.c)
            self.arrived(el, shard)
            self.onward(el, shard, self.block(el, shard), True, True, lambda copy: copy.start())

    def line_step(self, el, k, own):
        p = self.place

        def row(a, right, left):
            for b in [p.b] if own else [p.other_b(j) for j in range(p.B - 1)]:
                shard = p.index(a, b, p.c)
                self.arrived(el, shard)
                self.onward(el, shard, self.block(el, shard), right, left, lambda copy: copy.start())

        pl.when(p.a - k >= 0)(lambda: row(p.a - k, True, False))
        pl.when(p.a + k < p.A)(lambda: row(p.a + k, False, True))

    def core_wait(self, el):
        p = self.place
        self.local(el).wait()
        self.some(el, self.CORE, p.A * p.B).wait_recv()

    def finish(self, el):
        p = self.place
        for copy in self.across(el):
            copy.wait_send()
        for a in range(p.A - 1):
            pl.when(p.a == a)(self.some(el, self.RIGHT, (a + 1) * p.B).wait_send)
            pl.when(p.a == a + 1)(self.some(el, self.LEFT, (p.A - 1 - a) * p.B).wait_send)
        self.some(el, self.CORE, p.A * p.B).wait_send()


class ExpertScatter:
    def __init__(self, place, part, sums, line, out, count, send, recv, local_sem):
        self.place, self.part, self.sums, self.line, self.out, self.count = place, part, sums, line, out, count
        self.send, self.recv, self.local_sem = send, recv, local_sem

    CORE, RIGHT, LEFT, LAST = 0, 1, 2, 3

    def remote(self, source, target, el, route, arrival, a, b, c):
        return pltpu.make_async_remote_copy(
            src_ref=source, dst_ref=target, send_sem=self.send.at[el, route], recv_sem=self.recv.at[el, arrival],
            device_id=self.place.at(a, b, c), device_id_type=MESH,
        )

    def core_copy(self, el):
        p = self.place
        return self.remote(self.part(el).at[:, :, 1 - p.c], self.sums.at[el], el, self.CORE, 0, p.a, p.b, 1 - p.c)

    def right_copy(self, el, target):
        p = self.place
        return self.remote(
            self.sums.at[el, target], self.line.at[el, 0, target - 1], el, self.RIGHT, target, p.a + 1, p.b, p.c
        )

    def left_copy(self, el, target):
        p = self.place
        return self.remote(
            self.sums.at[el, target], self.line.at[el, 1, target], el, self.LEFT, p.A + target, p.a - 1, p.b, p.c
        )

    def add(self, el, target, way, slot):
        @pl.loop(0, self.place.B)
        def _(b):
            total = self.sums[el, target, b].astype(F32) + self.line[el, way, slot, b].astype(F32)
            self.sums[el, target, b] = total.astype(BF16)

    def relay_step(self, el, step):
        p = self.place

        @pl.when(p.a <= step)
        def _():
            target = p.a + p.A - 1 - step

            @pl.when(p.a > 0)
            def _():
                self.right_copy(el, target).wait_recv()
                self.add(el, target, 0, target - 1)

            self.right_copy(el, target).start()

        @pl.when(p.a >= p.A - 1 - step)
        def _():
            target = p.a - (p.A - 1 - step)

            @pl.when(p.a < p.A - 1)
            def _():
                self.left_copy(el, target).wait_recv()
                self.add(el, target, 1, target)

            self.left_copy(el, target).start()

    def last_copies(self, el):
        p = self.place
        out = []
        for j in range(p.B - 1):
            to, back = p.other_b(j), p.B - 2 - j
            target = self.out.at[p.b * self.count + el]
            out.append(self.remote(self.sums.at[el, p.a, to], target, el, self.LAST + j, 2 * p.A - 1 + back, p.a, to, p.c))
        return out

    def local(self, el):
        p = self.place
        return pltpu.make_async_copy(self.sums.at[el, p.a, p.b], self.out.at[p.b * self.count + el], self.local_sem.at[el])

    def start(self, el):
        self.core_copy(el).start()

    def core_step(self, el):
        p = self.place
        self.core_copy(el).wait()
        part = self.part(el)

        @pl.loop(0, p.A * p.B)
        def _(i):
            a, b = lax.div(i, p.B), lax.rem(i, p.B)
            total = self.sums[el, a, b].astype(F32) + part[a, b, p.c].astype(F32)
            self.sums[el, a, b] = total.astype(BF16)

    def line_step(self, el):
        p = self.place

        @pl.when(p.a > 0)
        def _():
            self.right_copy(el, p.a).wait_recv()
            self.add(el, p.a, 0, p.a - 1)

        @pl.when(p.a < p.A - 1)
        def _():
            self.left_copy(el, p.a).wait_recv()
            self.add(el, p.a, 1, p.a)

        for copy in self.last_copies(el) + [self.local(el)]:
            copy.start()

    def finish(self, el):
        p = self.place
        for a in range(p.A - 1):
            for route, at, count in ((self.RIGHT, a, p.A - 1 - a), (self.LEFT, a + 1, a + 1)):
                some = self.sums.at[el, pl.ds(0, count)]
                pl.when(p.a == at)(self.remote(some, some, el, route, 0, p.a, p.b, 1 - p.c).wait_send)
        for copy in self.last_copies(el) + [self.local(el)]:
            copy.wait()


class Scatter:
    def __init__(self, place, part, sums, across, line, columns, send, recv):
        self.place, self.part, self.sums, self.across, self.line = place, part, sums, across, line
        self.columns, self.send, self.recv = columns, send, recv

    CORE, ACROSS, LINE = 0, 1, 2

    def remote(self, source, target, item, route, a, b, c):
        return pltpu.make_async_remote_copy(
            src_ref=source, dst_ref=target,
            send_sem=self.send.at[item, min(route, 1)], recv_sem=self.recv.at[item, route],
            device_id=self.place.at(a, b, c), device_id_type=MESH,
        )

    def all_of(self, ref, item, route):
        p = self.place
        return self.remote(ref, ref, item, route, p.a, p.b, 1 - p.c)

    def core_copy(self, item):
        p, at = self.place, self.columns[item]
        return self.remote(self.part.at[:, :, 1 - p.c, :, at], self.sums.at[:, :, :, at], item, self.CORE, p.a, p.b, 1 - p.c)

    def across_copies(self, item):
        p, at = self.place, self.columns[item]
        out = []
        for j in range(p.B - 1):
            to, back = p.other_b(j), p.B - 2 - j
            copy = self.remote(self.sums.at[:, to, :, at], self.across.at[back, :, :, at], item, self.ACROSS, p.a, to, p.c)
            out.append(copy)
        return out

    def line_copies(self, item):
        p, at = self.place, self.columns[item]
        out = []
        for k in range(1, p.A):
            to, back = lax.rem(p.a + k, p.A), p.A - 1 - k
            copy = self.remote(self.sums.at[to, p.b, :, at], self.line.at[back, :, at], item, self.LINE, to, p.b, p.c)
            out.append(copy)
        return out

    def start(self, item):
        self.core_copy(item).start()

    def core_step(self, item):
        p, at = self.place, self.columns[item]
        self.core_copy(item).wait()

        @pl.loop(0, p.A * p.B)
        def _(i):
            a, b = lax.div(i, p.B), lax.rem(i, p.B)
            total = self.sums[a, b, :, at].astype(F32) + self.part[a, b, p.c, :, at].astype(F32)
            self.sums[a, b, :, at] = total.astype(BF16)

        for copy in self.across_copies(item):
            copy.start()

    def across_step(self, item):
        p, at = self.place, self.columns[item]
        self.all_of(self.across.at[:, :, :, at], item, self.ACROSS).wait_recv()

        @pl.loop(0, p.A)
        def _(a):
            total = self.sums[a, p.b, :, at].astype(F32)
            for j in range(p.B - 1):
                total += self.across[j, a, :, at].astype(F32)
            self.sums[a, p.b, :, at] = total.astype(BF16)

        for copy in self.line_copies(item):
            copy.start()

    def line_step(self, item):
        p, at = self.place, self.columns[item]
        self.all_of(self.line.at[:, :, at], item, self.LINE).wait_recv()
        total = self.sums[p.a, p.b, :, at].astype(F32)
        for k in range(p.A - 1):
            total += self.line[k, :, at].astype(F32)
        return total

    def finish(self, item):
        p, at = self.place, self.columns[item]
        blocks = self.sums.reshape(p.A * p.B, *self.sums.shape[2:])
        self.all_of(blocks.at[pl.ds(0, (p.B - 1) * p.A + p.A - 1), :, at], item, self.LINE).wait_send()


def block_kernel(
    experts, fsdp, xs, count,
    x_in, cot_in, routes_ref, slots_ref, qkv_ref, out_ref, router_ref, gain_one_ref, shift_one_ref, gain_two_ref, shift_two_ref,
    up_in, down_in,
    out_out, input_grad_out, share_out, up_grad_out, down_grad_out,
    act_one_save, weights_save, attended_save, mid_save, act_two_save,
    x_raw, cot_raw, shard_ref, meta_row_ref, meta_ref, x_ref, params_ref, triple_ref, probs_ref,
    sent_ref, cot_sent_ref, gate_sent_ref, rows_ref, grad_ref, gate_ref, back_ref, grad_slots_ref, dots_sent_ref, dots_ref,
    up_ref, down_ref, part_up_ref, part_down_ref, float_ref,
    sums_up, sums_down, line_up, line_down, sums_par, across_par, line_par, swap_ref,
    bias_ref, gate_rows_ref, dot_row_ref, place_ref, gated_ref, logit_grad_ref, column_ref,
    load_sem, save_sem, late_sem, store_sem, par_gather_send, par_gather_recv, par_gather_local,
    gather_send, gather_recv, gather_local, swap_send, swap_recv, return_send, return_recv,
    scatter_send, scatter_recv, scatter_local, par_send, par_recv, share_send, share_recv,
):
    rows_pad, width = x_ref.shape
    groups = rows_pad // BLOCK
    places = sent_ref.shape[0]
    capacity = places // experts
    hidden_width = up_ref.shape[1]
    chunks = hidden_width // FF_CHUNK
    held = up_in.shape[0]
    place = Place(fsdp, xs)
    A, B, sources = place.A, place.B, place.peers
    expert_rows = sources * capacity
    row_block = gated_ref.shape[0]
    copy_in = pltpu.make_async_copy

    weights_ref = part_up_ref
    act_one, attended, act_two, cot_ref = (part_down_ref.at[pl.ds(i * rows_pad, rows_pad), :] for i in range(4))
    mid_ref = float_ref

    loads = [copy_in(x_in, x_raw, load_sem.at[0]), copy_in(cot_in, cot_raw, load_sem.at[1])]
    for copy in loads:
        copy.start()

    def spread(raw, there):
        for g in range(groups):
            there[g * BLOCK : g * BLOCK + GROUP_ROWS, :] = raw[g * GROUP_ROWS : (g + 1) * GROUP_ROWS, :]
            there[g * BLOCK + GROUP_ROWS : (g + 1) * BLOCK, :] = jnp.zeros((BLOCK - GROUP_ROWS, width), BF16)

    def prepare():
        shard_ref[:, : 3 * width] = qkv_ref[...]
        shard_ref[:, 3 * width : 4 * width] = out_ref[...]
        size = shard_ref.shape[0]
        eye = iota((size, size), 0) == iota((size, size), 1)
        lane = iota((size, LANES), 1)
        small = jnp.zeros((size, LANES), F32)
        for i, norm_ref in enumerate((gain_one_ref, shift_one_ref, gain_two_ref, shift_two_ref)):
            row = norm_ref[...].astype(F32).reshape(1, size)
            column = jnp.sum(jnp.where(eye, row, 0.0), axis=1, keepdims=True)
            small = jnp.where(lane == NORM_LANE + i, column, small)
        shard_ref[:, 4 * width :] = small.astype(BF16)
        shard_ref[:, 4 * width : 4 * width + experts] = jnp.transpose(router_ref[...].astype(F32)).astype(BF16)

    greet(place, prepare)

    def rows_block(ref, shard):
        size = shard_ref.shape[0]
        return ref.at[pl.ds(pl.multiple_of(shard * size, size), size), :]

    params = Gather(place, shard_ref, params_ref, rows_block, par_gather_send, par_gather_recv, par_gather_local)
    weights_in = [
        ExpertGather(place, own, full, count, gather_send.at[i], gather_recv.at[i], gather_local.at[i])
        for i, (own, full) in enumerate(((up_in, up_ref), (down_in, down_ref)))
    ]

    def each(step, el, *more):
        if el < count:
            for gather in weights_in:
                getattr(gather, step)(el, *more)

    def do(*point):
        for name, el, *more in PLAN.get(point, ()):
            if el < count:
                with jax.named_scope("_".join(map(str, (name, el, *more)))):
                    actions[name](el, *more)

    inner = jnp.logical_and(place.a > 0, place.a < A - 1)

    def ends(el):
        for k in range(1, A):
            for own in (True, False):
                each("line_step", el, k, own)

    actions = {
        "across": lambda el: each("start_across", el),
        "own": lambda el: each("start_own", el),
        "passed": lambda el: each("across_step", el),
        "relay": lambda el, k, own: pl.when(inner)(lambda: each("line_step", el, k, own)),
        "ends": lambda el: pl.when(jnp.logical_not(inner))(lambda: ends(el)),
        "cots": lambda el, *which: cot_swaps(el, *which),
        "rows": lambda el: row_swaps(el),
        "sums": lambda el: all_scatters("core_step", el),
        "outputs": lambda el, *which: outputs(el, *which),
        "sum_relay": lambda el, step: all_scatters("relay_step", el, step),
    }
    params.start()
    do("start", 0)
    targets = jnp.where(slots_ref[...] >= 0, routes_ref[...] * capacity + slots_ref[...], -1)
    meta_row_ref[...] = jnp.full(meta_row_ref.shape, -1, jnp.int32)
    for g in range(groups):
        at = slice(g * BLOCK, g * BLOCK + GROUP_ROWS)
        meta_row_ref[0:2, at] = targets[:, g * GROUP_ROWS : (g + 1) * GROUP_ROWS]
        meta_row_ref[2:4, at] = routes_ref[:, g * GROUP_ROWS : (g + 1) * GROUP_ROWS]
    image_row = iota((BLOCK, BLOCK), 0) // PATCHES
    image_col = iota((BLOCK, BLOCK), 1) // PATCHES
    bias_ref[...] = jnp.where(image_row == image_col, 0.0, -1e30)

    def slot_rows(e):
        return pl.ds(pl.multiple_of(e * capacity, 16), capacity)

    def source_rows(el, source):
        return pl.ds(pl.multiple_of(el * expert_rows + source * capacity, 16), capacity)

    def find(e):
        slot = iota((capacity, rows_pad), 0) + e * capacity
        in_first = slot == meta_row_ref[0:1, :]
        in_second = slot == meta_row_ref[1:2, :]
        return in_first, in_second, jnp.where(jnp.logical_or(in_first, in_second), 1.0, 0.0).astype(BF16)

    def swap(kind, el, k):
        peer, back = place.other_peer(k), place.seen_from(k)
        e = peer * count + el
        if kind == 1:
            source, target = gate_sent_ref.at[e], gate_ref.at[el * sources + back]
        else:
            here, there = (sent_ref, rows_ref) if kind == 0 else (cot_sent_ref, grad_ref)
            source, target = here.at[slot_rows(e), :], there.at[source_rows(el, back), :]
        return pltpu.make_async_remote_copy(
            src_ref=source, dst_ref=target, send_sem=swap_send.at[kind, el], recv_sem=swap_recv.at[kind, el, back],
            device_id=place.at_peer(peer), device_id_type=MESH,
        )

    def swap_wait(kind, el, k):
        if kind == 1:
            target = gate_ref.at[el * sources + k]
        else:
            target = (rows_ref if kind == 0 else grad_ref).at[source_rows(el, k), :]
        pltpu.make_async_remote_copy(
            src_ref=target, dst_ref=target, send_sem=swap_send.at[kind, el], recv_sem=swap_recv.at[kind, el, k],
            device_id=place.at_peer(place.other_peer(k)), device_id_type=MESH,
        ).wait_recv()

    def all_of(kind, send, recv):
        some = gate_ref.at[pl.ds(0, sources - 1)] if kind == 1 else rows_ref.at[pl.ds(0, (sources - 1) * capacity), :]
        return pltpu.make_async_remote_copy(
            src_ref=some, dst_ref=some, send_sem=send, recv_sem=recv,
            device_id=place.at(place.a, place.b, 1 - place.c), device_id_type=MESH,
        )

    def peers_where(which, act):
        @pl.loop(1, sources)
        def _(k):
            for name, same in (("x", lax.div(k, xs) == 0), ("y", lax.rem(k, xs) == 0)):
                if which == name:
                    pl.when(same)(lambda: act(k))
            if which == "far":
                pl.when(jnp.logical_and(lax.div(k, xs) > 0, lax.rem(k, xs) > 0))(lambda: act(k))

    def cot_swaps(el, *which):
        for peers in which:
            peers_where(peers, lambda k: swap(2, el, k).start())

    def cot_own(el):
        grad_ref[source_rows(el, 0), :] = cot_sent_ref[slot_rows(place.peer * count + el), :]

    def row_swaps(el):
        @pl.loop(1, sources)
        def _(k):
            swap(0, el, k).start()
            swap(1, el, k).start()

    for copy in loads:
        copy.wait()
    spread(cot_raw, cot_ref)
    for k in range(1, A):
        params.line_step(k)
        do("start", k)

        @pl.loop((k - 1) * experts // (A - 1), k * experts // (A - 1))
        def _(i):
            e = place.other_peer(lax.rem(lax.div(i, count) + 1, sources)) * count + lax.rem(i, count)
            _, _, picks = find(e)
            cot_sent_ref[slot_rows(e), :] = dot(picks, cot_ref[...]).astype(BF16)

        if k == 1:
            spread(x_raw, x_ref)
            meta_ref[...] = jnp.transpose(meta_row_ref[...])
        do("after", k)
        params.across_step(k - 1)

    params.across_step(A - 1)
    params.finish_recv()
    for el in range(count):
        cot_own(el)
    do("begin", 0)

    small = params_ref[:, 4 * width :]
    small_rows = jnp.transpose(small.astype(F32))

    def saves(rows):
        pairs = (
            (act_one, act_one_save), (weights_ref.at[:, pl.ds(0, HEADS * BLOCK)], weights_save), (attended, attended_save),
            (mid_ref, mid_save), (act_two, act_two_save),
        )
        return [copy_in(here.at[rows, :], there.at[rows, :], save_sem.at[i]) for i, (here, there) in enumerate(pairs)]

    @pl.loop(0, groups)
    def _(g):
        rows = rows_of(g)
        x = x_ref[rows, :].astype(F32)
        normed, _ = normalize(x)
        act = (normed * small_rows[NORM_LANE : NORM_LANE + 1] + small_rows[NORM_LANE + 1 : NORM_LANE + 2]).astype(BF16)
        act_one[rows, :] = act
        triple_ref[rows, :] = dot(act, params_ref[:, : 3 * width]).astype(BF16)
        low = iota((BLOCK, LANES), 1) < HEAD_DIM
        for pair in range(HEADS // 2):
            at = pair * LANES
            q = triple_ref[rows, at : at + LANES] * HEAD_DIM ** (-0.5)
            k = triple_ref[rows, width + at : width + at + LANES]
            v = triple_ref[rows, 2 * width + at : 2 * width + at + LANES]
            total = None
            for half in range(2):
                mask = low if half == 0 else jnp.logical_not(low)
                scores = dot_against(jnp.where(mask, q, 0.0).astype(BF16), k) + bias_ref[...]
                top = jnp.max(scores, axis=-1, keepdims=True)
                raised = jnp.exp(scores - top)
                probs = raised / jnp.sum(raised, axis=-1, keepdims=True)
                probs = probs.astype(BF16)
                head = (2 * pair + half) * BLOCK
                weights_ref[rows, head : head + BLOCK] = probs
                part = dot(probs, jnp.where(mask, v, 0.0).astype(BF16))
                total = part if total is None else total + part
            attended[rows, at : at + LANES] = total.astype(BF16)

        for i in range(groups):
            pl.when(g == i)(functools.partial(do, "middle", i))

        mid = x + dot(attended[rows, :], params_ref[:, 3 * width : 4 * width])
        mid_ref[rows, :] = mid
        normed, _ = normalize(mid)
        act = (normed * small_rows[NORM_LANE + 2 : NORM_LANE + 3] + small_rows[NORM_LANE + 3 : NORM_LANE + 4]).astype(BF16)
        act_two[rows, :] = act
        logits = jnp.where(iota((BLOCK, LANES), 1) < experts, dot(act, small), -1e30)
        raised = jnp.exp(logits - jnp.max(logits, axis=-1, keepdims=True))
        probs = raised / jnp.sum(raised, axis=-1, keepdims=True)
        probs_ref[rows, :] = probs
        first, second = gates_of(probs, meta_ref[rows, :])
        gate_rows_ref[0:1, rows] = to_row(first)
        gate_rows_ref[1:2, rows] = to_row(second)
        for copy in saves(rows):
            copy.start()

        for i in range(groups):
            pl.when(g == i)(functools.partial(do, "end", i))

    @pl.loop(0, experts)
    def _(i):
        el, k = lax.div(i, sources), lax.rem(lax.rem(i, sources) + 1, sources)
        e = place.other_peer(k) * count + el
        in_first, in_second, picks = find(e)
        gate = jnp.sum(
            jnp.where(in_first, gate_rows_ref[0:1, :], jnp.where(in_second, gate_rows_ref[1:2, :], 0.0)),
            axis=1, keepdims=True,
        )
        sent_ref[slot_rows(e), :] = dot(picks, act_two[...]).astype(BF16)
        gate_sent_ref[e, 0:1, :] = to_row(gate)

        @pl.when(jnp.logical_and(el == 0, k > 0))
        def _():
            swap(0, el, k).start()
            swap(1, el, k).start()

        @pl.when(k == 0)
        def _():
            rows_ref[source_rows(el, 0), :] = sent_ref[slot_rows(e), :]
            gate_ref[el * sources] = gate_sent_ref[e]

        for at in range(8):
            pl.when(i == at)(functools.partial(do, "dispatch", at))

    for copy in saves(pl.ds(0, rows_pad)):
        copy.wait()

    part_up = part_up_ref.at[pl.ds(0, count * width), :].reshape(count, A, B, 2, up_in.shape[1], part_up_ref.shape[1])
    part_down = part_down_ref.at[pl.ds(0, count * hidden_width), :].reshape(count, A, B, 2, down_in.shape[1], width)
    scatters = [
        ExpertScatter(place, part, sums, line, out, count, scatter_send.at[i], scatter_recv.at[i], scatter_local.at[i])
        for i, (part, sums, line, out) in enumerate(
            (
                (lambda el: part_up.at[el, :, :, :, :, pl.ds(0, hidden_width)], sums_up, line_up, up_grad_out),
                (lambda el: part_down.at[el], sums_down, line_down, down_grad_out),
            )
        )
    ]

    def all_scatters(step, el, *more):
        for scatter in scatters:
            getattr(scatter, step)(el, *more)

    pairs = HEADS // 2
    columns = [slice(3 * LANES * p, 3 * LANES * (p + 1)) for p in range(pairs)]
    columns += [slice(3 * width, 4 * width), slice(4 * width, 4 * width + LANES)]
    par_out, par_small = pairs, pairs + 1
    par = Scatter(place, part_up.at[0], sums_par, across_par, line_par, columns, par_send, par_recv)

    def shares(item):
        at = columns[item]
        out = []
        for k in range(1, xs):
            to, back = lax.rem(place.x + k, xs), xs - 1 - k
            out.append(
                pltpu.make_async_remote_copy(
                    src_ref=swap_ref.at[place.x, :, at], dst_ref=swap_ref.at[place.x, :, at],
                    send_sem=share_send.at[item, back], recv_sem=share_recv.at[item, back],
                    device_id=(to, place.me), device_id_type=MESH,
                )
            )
        return out

    def par_last(item):
        swap_ref[place.x, :, columns[item]] = par.line_step(item).astype(BF16)
        for copy in shares(item):
            copy.start()

    def returned(kind, el, k):
        e = place.peer * count + el
        if kind == 1:
            source, target = dots_sent_ref.at[el * sources + k], dots_ref.at[e]
        else:
            here, there = (grad_ref, grad_slots_ref) if kind == 0 else (rows_ref, back_ref)
            source, target = here.at[source_rows(el, k), :], there.at[slot_rows(e), :]
        return pltpu.make_async_remote_copy(
            src_ref=source, dst_ref=target,
            send_sem=return_send.at[kind, el], recv_sem=return_recv.at[kind, el],
            device_id=place.at_peer(place.other_peer(k)), device_id_type=MESH,
        )

    def give_back(kind, el, first=1, stop=sources):
        @pl.loop(first, stop)
        def _(k):
            returned(kind, el, k).start()

    def outputs(el, *which):
        for peers in which:
            peers_where(peers, lambda k: returned(2, el, k).start())

    def return_wait(kind, el):
        all_of(kind, return_send.at[kind, el], return_recv.at[kind, el]).wait_recv()

    def expert(el):
        blocks = expert_rows // row_block
        block_sources = row_block // capacity
        order = list(range(blocks))
        if el > 0 and el == count - 1:
            order.reverse()
        each("core_wait", el)
        for turn, block in enumerate(order):
            first, stop = block * block_sources, (block + 1) * block_sources
            for kind in range(3):
                pl.loop(max(first, 1), stop)(functools.partial(swap_wait, kind, el))
            do("before", el, turn)
            here = pl.ds(el * expert_rows + block * row_block, row_block)
            float_ref[: 2 * row_block, :] = jnp.zeros((2 * row_block, width), F32)

            @pl.loop(first, stop)
            def _(k):
                gate = to_column(gate_ref[el * sources + k, 0:1, :], capacity)
                cots = grad_ref[source_rows(el, k), :].astype(F32)
                local = pl.ds(pl.multiple_of((k - first) * capacity, 16), capacity)
                gated_ref[local, :] = (gate * cots).astype(BF16)

            @pl.loop(0, chunks)
            def _(f):
                at = pl.ds(pl.multiple_of(f * FF_CHUNK, FF_CHUNK), FF_CHUNK)
                down_at = pl.ds(pl.multiple_of(el * hidden_width + f * FF_CHUNK, FF_CHUNK), FF_CHUNK)
                rows, grads = rows_ref[here, :], gated_ref[...]
                up_part, down_part = up_ref[el * width : (el + 1) * width, at], down_ref[down_at, :]
                hidden = dot(rows, up_part)
                spread = 0.5 * (1.0 + lax.erf(hidden * ROOT_HALF))
                active = (hidden * spread).astype(BF16)
                slope = spread + hidden * (DENSITY_SCALE * jnp.exp(-0.5 * hidden * hidden))
                grad_active = dot_against(grads, down_part)
                float_ref[:row_block, :] += dot(active, down_part)
                grad_hidden = (grad_active * slope).astype(BF16)
                float_ref[row_block : 2 * row_block, :] += dot_against(grad_hidden, up_part)
                size = up_in.shape[1]
                up_sum = dot_rows(rows, grad_hidden).reshape(A, B, 2, size, FF_CHUNK)
                down_sum = dot_rows(active, grads)
                if turn > 0:
                    up_sum += part_up[el, :, :, :, :, at].astype(F32)
                    down_sum += part_down_ref[down_at, :].astype(F32)
                part_up[el, :, :, :, :, at] = up_sum.astype(BF16)
                part_down_ref[down_at, :] = down_sum.astype(BF16)
                for i in range(chunks):
                    pl.when(f == i)(functools.partial(do, "expert", el, turn * chunks + i))

            @pl.loop(first, stop)
            def _(k):
                at = source_rows(el, k)
                local = pl.ds(pl.multiple_of((k - first) * capacity, 16), capacity)
                back = float_ref[local, :].astype(BF16)
                rows_ref[at, :] = back
                dots = jnp.sum(back.astype(F32) * grad_ref[at, :].astype(F32), axis=1, keepdims=True)
                dots_sent_ref[el * sources + k, 0:1, :] = to_row(dots)
                local = pl.ds(pl.multiple_of(row_block + (k - first) * capacity, 16), capacity)
                grad_ref[at, :] = float_ref[local, :].astype(BF16)

            give_back(0, el, max(first, 1), stop)
            give_back(1, el, max(first, 1), stop)

        all_scatters("start", el)
        own, e = source_rows(el, 0), place.peer * count + el
        back_ref[slot_rows(e), :] = rows_ref[own, :]
        grad_slots_ref[slot_rows(e), :] = grad_ref[own, :]
        dots_ref[e] = dots_sent_ref[el * sources]

    for el in range(count):
        expert(el)
        do("after_expert", el)

    def late_loads():
        out = [copy_in(weights_save, up_ref.at[pl.ds(0, rows_pad), :], late_sem.at[0])]
        for i, array in enumerate((act_one_save, attended_save, act_two_save)):
            out.append(copy_in(array, down_ref.at[pl.ds(i * rows_pad, rows_pad), :], late_sem.at[1 + i]))
        for i in range(2):
            out.append(copy_in(mid_save, float_ref.at[pl.ds(i * rows_pad, rows_pad), :], late_sem.at[4 + i]))
        return out

    for el in range(count):
        each("finish", el)
    for copy in late_loads():
        copy.start()
    spread(cot_raw, down_ref.at[pl.ds(3 * rows_pad, rows_pad), :])
    act_one, attended, act_two, cot_ref = (down_ref.at[pl.ds(i * rows_pad, rows_pad), :] for i in range(4))
    weights_ref = up_ref
    input_grad_ref = float_ref
    all_scatters("core_step", count - 1)
    all_scatters("relay_step", count - 1, 0)
    for copy in late_loads():
        copy.wait()
    for kind in range(2):
        for el in range(count):
            return_wait(kind, el)
    for el in range(count):
        do("returned", el)
    for el in range(count):
        for kind in range(3):
            all_of(kind, swap_send.at[kind, el], return_recv.at[kind, el]).wait_send()

    grad_attended_ref = sent_ref.at[pl.ds(0, rows_pad), :]
    branch_ref = cot_sent_ref.at[pl.ds(0, rows_pad), :]
    gain_one = small_rows[NORM_LANE : NORM_LANE + 1]
    gain_two = small_rows[NORM_LANE + 2 : NORM_LANE + 3]
    column_ref[...] = jnp.zeros_like(column_ref)
    flat = jnp.zeros((8, places), F32)
    for e in range(experts):
        row = dots_ref[e]
        row = jnp.concatenate([row, jnp.zeros((8, places - row.shape[1]), F32)], axis=1)
        flat += pltpu.roll(row, e * capacity, 1) if e else row
    dot_row_ref[...] = flat

    def last_sums(g):
        with jax.named_scope("last_sums_%d" % g):
            last = count - 1
            if g == 3:
                pl.when(jnp.logical_not(inner))(lambda: all_scatters("relay_step", last, 1))
                if count > 1:
                    all_scatters("line_step", last - 1)
            if g == 4:
                pl.when(inner)(lambda: all_scatters("relay_step", last, 1))
            if g == 6:
                pl.when(jnp.logical_not(inner))(lambda: all_scatters("relay_step", last, 2))
            if g == 7:
                pl.when(inner)(lambda: all_scatters("relay_step", last, 2))

    def store(i, rows):
        here, there = ((cot_ref, out_out), (input_grad_ref, input_grad_out))[i]
        return copy_in(here.at[rows, :], there.at[rows, :], store_sem.at[i])

    @pl.loop(0, groups)
    def _(g):
        rows = rows_of(g)
        meta = meta_ref[rows, :]
        probs = probs_ref[rows, :]
        lane = iota((BLOCK, LANES), 1)
        grad_first = jnp.zeros((BLOCK, LANES), F32)
        grad_second = jnp.zeros((BLOCK, LANES), F32)
        for c in range(places // LANES):
            at = c * LANES
            in_first = lane == meta[:, 0:1] - at
            in_second = lane == meta[:, 1:2] - at
            place_ref[:, at : at + LANES] = jnp.where(jnp.logical_or(in_first, in_second), 1.0, 0.0).astype(BF16)
            dots = dot_row_ref[0:1, at : at + LANES]
            grad_first += jnp.where(in_first, dots, 0.0)
            grad_second += jnp.where(in_second, dots, 0.0)
        grad_first = jnp.sum(grad_first, axis=1, keepdims=True)
        grad_second = jnp.sum(grad_second, axis=1, keepdims=True)
        mid = input_grad_ref[rows, :]
        grad_probs = jnp.where(lane == meta[:, 2:3], grad_first, 0.0) + jnp.where(lane == meta[:, 3:4], grad_second, 0.0)
        grad_logits = (probs * (grad_probs - jnp.sum(grad_probs * probs, axis=-1, keepdims=True))).astype(BF16)
        logit_grad_ref[rows, :] = grad_logits
        grad_act = dot(place_ref[...], grad_slots_ref[...]) + dot_against(grad_logits, small)
        normed, inverse = normalize(mid)
        column_ref[NORM_LANE + 2 : NORM_LANE + 3, :] += jnp.sum(grad_act * normed, axis=0, keepdims=True)
        column_ref[NORM_LANE + 3 : NORM_LANE + 4, :] += jnp.sum(grad_act, axis=0, keepdims=True)
        grad_mid = cot_ref[rows, :].astype(F32) + denormalize(grad_act, normed, inverse, gain_two)
        input_grad_ref[rows, :] = grad_mid
        branch_ref[rows, :] = grad_mid.astype(BF16)
        grad_attended = dot_against(branch_ref[rows, :], params_ref[:, 3 * width : 4 * width])
        grad_attended_ref[rows, :] = grad_attended.astype(BF16)
        for i in range(groups):
            pl.when(g == i)(functools.partial(last_sums, i))

    split = (A, B, 2, up_in.shape[1])

    def put(item, value):
        at = columns[item]
        part_up[0, :, :, :, :, at] = value.astype(BF16).reshape(*split, at.stop - at.start)
        par.start(item)

    put(par_out, dot_rows(attended[...], branch_ref[...]))

    def attention_backward(pair, g):
        rows = rows_of(g)
        at = pair * LANES
        low = iota((BLOCK, LANES), 1) < HEAD_DIM
        q = triple_ref[rows, at : at + LANES] * HEAD_DIM ** (-0.5)
        k = triple_ref[rows, width + at : width + at + LANES]
        v = triple_ref[rows, 2 * width + at : 2 * width + at + LANES]
        upstream = grad_attended_ref[rows, at : at + LANES]
        grad_q = grad_k = grad_v = jnp.zeros((BLOCK, LANES), F32)
        for half in range(2):
            mask = low if half == 0 else jnp.logical_not(low)
            upstream_half = jnp.where(mask, upstream, 0.0).astype(BF16)
            head = (2 * pair + half) * BLOCK
            weights = weights_ref[rows, head : head + BLOCK]
            kept = weights.astype(F32)
            grad_weights = dot_against(upstream_half, v)
            inner = jnp.sum(grad_weights * kept, axis=-1, keepdims=True)
            grad_scores = (kept * (grad_weights - inner)).astype(BF16)
            grad_q += dot(grad_scores, jnp.where(mask, k, 0.0).astype(BF16))
            grad_k += dot_rows(grad_scores, jnp.where(mask, q, 0.0).astype(BF16))
            grad_v += dot_rows(weights, upstream_half)
        triple_ref[rows, at : at + LANES] = (grad_q * HEAD_DIM ** (-0.5)).astype(BF16)
        triple_ref[rows, width + at : width + at + LANES] = grad_k.astype(BF16)
        triple_ref[rows, 2 * width + at : 2 * width + at + LANES] = grad_v.astype(BF16)

    def par_steps(*steps):
        for name, item in steps:
            with jax.named_scope("%s_%d" % (name, item)):
                par_last(item) if name == "last" else getattr(par, name + "_step")(item)

    for pair in range(pairs):
        pl.loop(0, groups)(functools.partial(attention_backward, pair))
        if pair == 0:
            par_steps(("core", par_out))
        else:
            par_steps(("core", pair - 1))
        last_sums(groups + pair)
        kinds = [triple_ref[:, kind * width + pair * LANES : kind * width + (pair + 1) * LANES] for kind in range(3)]
        put(pair, dot_rows(act_one[...], jnp.concatenate(kinds, axis=1)))

    @pl.loop(0, groups)
    def _(g):
        rows = rows_of(g)
        grad_act = dot_against(triple_ref[rows, :], params_ref[:, : 3 * width])
        normed, inverse = normalize(x_ref[rows, :].astype(F32))
        column_ref[NORM_LANE : NORM_LANE + 1, :] += jnp.sum(grad_act * normed, axis=0, keepdims=True)
        column_ref[NORM_LANE + 1 : NORM_LANE + 2, :] += jnp.sum(grad_act, axis=0, keepdims=True)
        input_grad_ref[rows, :] += denormalize(grad_act, normed, inverse, gain_one)
        store(1, rows).start()

        @pl.when(g == 0)
        def _():
            par_steps(("core", pairs - 1), ("across", par_out), *[("across", pair) for pair in range(pairs - 2)])

        @pl.when(g == 2)
        def _():
            par_steps(("across", pairs - 2))

    put(par_small, dot_rows(act_two[...], logit_grad_ref[...]) + jnp.transpose(column_ref[...]))
    for el in range(count):
        return_wait(2, el)

    def combine(g):
        rows = rows_of(g)
        meta = meta_ref[rows, :]
        gate_first, gate_second = gates_of(probs_ref[rows, :], meta)
        lane = iota((BLOCK, LANES), 1)
        for c in range(places // LANES):
            at = c * LANES
            in_first = lane == meta[:, 0:1] - at
            in_second = lane == meta[:, 1:2] - at
            place_ref[:, at : at + LANES] = jnp.where(in_first, gate_first, jnp.where(in_second, gate_second, 0.0)).astype(BF16)
        mid = float_ref[pl.ds(pl.multiple_of(rows_pad + g * BLOCK, BLOCK), BLOCK), :]
        cot_ref[rows, :] = (mid + dot(place_ref[...], back_ref[...])).astype(BF16)
        store(0, rows).start()

    steps = (
        [("across", pairs - 1), ("core", par_small)], [("across", par_small)], [], [("last", item) for item in (par_out, *range(pairs), par_small)],
    )

    @pl.loop(0, groups)
    def _(g):
        combine(g)
        pl.when(g == 2)(lambda: all_scatters("line_step", count - 1))
        for i in range(groups):
            pl.when(g == i)(functools.partial(par_steps, *steps[i]))

    for i in range(2):
        store(i, pl.ds(0, rows_pad)).wait()

    params.finish_send()
    for el in range(count):
        for kind in range(3):
            all_of(kind, return_send.at[kind, el], return_recv.at[kind, el]).wait_send()
        all_scatters("finish", el)
    for item in range(len(columns)):
        par.finish(item)
    for item in range(len(columns)):
        for copy in shares(item):
            copy.wait()
    total = swap_ref[0].astype(F32)
    for i in range(1, xs):
        total += swap_ref[i].astype(F32)
    share_out[...] = total


def finish_kernel(
    experts, out_pad, input_grad_pad, share, up_half, down_half,
    out, input_grad, qkv, out_weight, router, gain_one, shift_one, gain_two, shift_two, up, down,
):
    width = out.shape[1]
    for g in range(out_pad.shape[0] // BLOCK):
        here, there = slice(g * BLOCK, g * BLOCK + GROUP_ROWS), slice(g * GROUP_ROWS, (g + 1) * GROUP_ROWS)
        out[there, :] = out_pad[here, :]
        input_grad[there, :] = input_grad_pad[here, :]
    for pair in range(HEADS // 2):
        for kind in range(3):
            here, there = (3 * pair + kind) * LANES, kind * width + pair * LANES
            qkv[:, there : there + LANES] = share[:, here : here + LANES]
    out_weight[...] = share[:, 3 * width : 4 * width]
    small = jnp.transpose(share[:, 4 * width :])
    router[...] = small[:experts, :]
    for i, vector in enumerate((gain_one, shift_one, gain_two, shift_two)):
        vector[...] = small[NORM_LANE + i : NORM_LANE + i + 1, :].reshape(vector.shape)
    up[...] = up_half[...].astype(F32)
    down[...] = down_half[...].astype(F32)


def on_device(
    inputs, cotangent, routes, slots, qkv_weight, out_weight, router_weight,
    norm1_gain, norm1_shift, norm2_gain, norm2_shift, expert_up, expert_down,
):
    rows_dev, width = inputs.shape
    groups = rows_dev // GROUP_ROWS
    rows_pad = groups * BLOCK
    fsdp = lax.axis_size("fsdp")
    peers = lax.axis_size("expert")
    held = expert_up.shape[0]
    experts = held * peers
    capacity = (42 * rows_dev + 20 * experts - 1) // (20 * experts)
    capacity = -(-capacity // 16) * 16
    places = experts * capacity

    vmem = pl.BlockSpec(memory_space=pltpu.VMEM)
    hbm = pl.BlockSpec(memory_space=pl.ANY)
    shape = jax.ShapeDtypeStruct
    dma = pltpu.SemaphoreType.DMA
    A, B = 4, fsdp // 8
    count = held // B
    sources = peers * B
    up_rows, down_rows = expert_up.shape[1], expert_down.shape[1]
    hidden_width = expert_up.shape[2]
    packed_width = 4 * width + LANES
    items = HEADS // 2 + 2
    expert_rows = sources * capacity
    row_block = max(n for n in range(capacity, MAX_ROWS + 1, capacity) if expert_rows % n == 0)
    routes_of = 3 + B - 1
    lanes_of = -(-capacity // LANES) * LANES

    def buffer(*dims, dtype=BF16):
        return pltpu.VMEM(dims, dtype)

    out, input_grad, share, up_grad, down_grad, *_ = pl.pallas_call(
        functools.partial(block_kernel, experts, fsdp, peers, count),
        out_shape=(
            shape((rows_pad, width), BF16),
            shape((rows_pad, width), F32),
            shape((up_rows, packed_width), F32),
            shape(expert_up.shape, BF16),
            shape(expert_down.shape, BF16),
            shape((rows_pad, width), BF16),
            shape((rows_pad, HEADS * BLOCK), BF16),
            shape((rows_pad, width), BF16),
            shape((rows_pad, width), F32),
            shape((rows_pad, width), BF16),
        ),
        in_specs=[hbm] * 2 + [vmem] * 9 + [hbm] * 2,
        out_specs=[hbm] * 2 + [vmem] + [hbm] * 7,
        scratch_shapes=[
            buffer(rows_dev, width), buffer(rows_dev, width), buffer(up_rows, packed_width),
            buffer(8, rows_pad, dtype=jnp.int32), buffer(rows_pad, 8, dtype=jnp.int32),
            buffer(rows_pad, width), buffer(fsdp * up_rows, packed_width), buffer(rows_pad, 3 * width),
            buffer(rows_pad, LANES, dtype=F32),
            buffer(places, width), buffer(places, width), buffer(experts, 8, lanes_of, dtype=F32),
            buffer(places, width), buffer(places, width), buffer(experts, 8, lanes_of, dtype=F32),
            buffer(places, width), buffer(places, width),
            buffer(experts, 8, lanes_of, dtype=F32), buffer(experts, 8, lanes_of, dtype=F32),
            buffer(max(count * width, rows_pad), hidden_width), buffer(max(count * hidden_width, 4 * rows_pad), width),
            buffer(max(count * width, rows_pad), packed_width), buffer(max(count * hidden_width, 4 * rows_pad), width),
            buffer(max(2 * row_block, 2 * rows_pad), width, dtype=F32),
            buffer(count, A, B, up_rows, hidden_width), buffer(count, A, B, down_rows, width),
            buffer(count, 2, A - 1, B, up_rows, hidden_width), buffer(count, 2, A - 1, B, down_rows, width),
            buffer(A, B, up_rows, packed_width), buffer(B - 1, A, up_rows, packed_width),
            buffer(A - 1, up_rows, packed_width), buffer(peers, up_rows, packed_width),
            buffer(BLOCK, BLOCK, dtype=F32), buffer(8, rows_pad, dtype=F32), buffer(8, places, dtype=F32),
            buffer(BLOCK, places), buffer(row_block, width), buffer(rows_pad, LANES), buffer(LANES, width, dtype=F32),
            dma((2,)), dma((5,)), dma((6,)), dma((2,)), dma((routes_of,)), dma((A * B + 1,)), dma,
            dma((2, count, routes_of)), dma((2, count, A * B + 1)), dma((2, count)),
            dma((3, count)), dma((3, count, sources)), dma((3, count)), dma((3, count)),
            dma((2, count, 3 + B - 1)), dma((2, count, 2 * A + B - 2)), dma((2, count)),
            dma((items, 2)), dma((items, 3)), dma((items, peers - 1)), dma((items, peers - 1)),
        ],
        compiler_params=pltpu.CompilerParams(vmem_limit_bytes=VMEM_LIMIT, collective_id=0, has_side_effects=True),
        name="encoder_block",
    )(
        inputs, cotangent, routes.T, slots.T, qkv_weight, out_weight, router_weight.T,
        norm1_gain, norm1_shift, norm2_gain, norm2_shift, expert_up, expert_down,
    )
    vector = shape((up_rows,), F32)
    results = pl.pallas_call(
        functools.partial(finish_kernel, experts),
        out_shape=(
            shape((rows_dev, width), BF16),
            shape((rows_dev, width), F32),
            shape((up_rows, 3 * width), F32),
            shape((up_rows, width), F32),
            shape((experts, up_rows), F32),
            *[vector] * 4,
            shape(expert_up.shape, F32),
            shape(expert_down.shape, F32),
        ),
        in_specs=[vmem] * 5,
        out_specs=[vmem] * 11,
        compiler_params=pltpu.CompilerParams(vmem_limit_bytes=VMEM_LIMIT),
        name="results",
    )(out, input_grad, share, up_grad, down_grad)
    return (*results[:4], results[4].T, *results[5:])


def solution(mesh):
    tokens = P(("expert", "fsdp"), None)
    rows, vector, expert = P("fsdp", None), P("fsdp"), P("expert", "fsdp", None)
    return jax.shard_map(
        on_device,
        mesh=mesh,
        in_specs=(tokens,) * 4 + (rows,) * 3 + (vector,) * 4 + (expert,) * 2,
        out_specs=(tokens,) * 2 + (rows,) * 3 + (vector,) * 4 + (expert,) * 2,
        check_vma=False,
    )
```

```python
import functools

import jax
import jax.numpy as jnp
from jax import lax
from jax.experimental import pallas as pl
from jax.experimental.pallas import tpu as pltpu
from jax.sharding import PartitionSpec as P

HEADS = 8
HEAD_DIM = 64
PATCHES = 49
EPS = 1e-06
ROOT_HALF = 0.7071067811865476
DENSITY_SCALE = 0.3989422804014327

BLOCK = 256
GROUP_IMAGES = BLOCK // PATCHES
GROUP_ROWS = GROUP_IMAGES * PATCHES
LANES = 128
NORM_LANE = 64
FF_CHUNK = 512
MAX_ROWS = 640
VMEM_LIMIT = 63 * 1024 * 1024

MESH = pl.DeviceIdType.MESH
PLAN = {
    ("start", 0): [("across", 0)],
    ("start", 1): [("own", 0)],
    ("start", 3): [("passed", 0)],
    ("after", 3): [("relay", 0, 1, True)],
    ("after", 1): [("cots", 0, "x"), ("cots", 1, "x")],
    ("begin", 0): [("cots", 0, "y", "far")],
    ("end", 0): [("relay", 0, 1, False)],
    ("middle", 1): [("relay", 0, 2, True)],
    ("end", 1): [("across", 1)],
    ("end", 2): [("relay", 0, 2, False), ("cots", 1, "y")],
    ("dispatch", 7): [("own", 1), ("passed", 1), ("ends", 0)],
    ("expert", 0, 0): [("relay", 1, 1, True)],
    ("expert", 0, 1): [("relay", 1, 1, False)],
    ("expert", 0, 2): [("rows", 1)],
    ("expert", 0, 3): [("cots", 1, "far"), ("relay", 1, 2, True)],
    ("expert", 0, 4): [("relay", 1, 2, False)],
    ("after_expert", 0): [("sums", 0), ("sum_relay", 0, 0), ("ends", 1)],
    ("expert", 1, 2): [("sum_relay", 0, 1)],
    ("expert", 1, 7): [("sum_relay", 0, 2)],
    ("after_expert", 1): [("outputs", 0, "y")],
    ("returned", 0): [("outputs", 0, "x", "far")],
    ("returned", 1): [("outputs", 1, "x", "y", "far")],
}
F32 = jnp.float32
BF16 = jnp.bfloat16


def dot(left, right):
    return lax.dot_general(left, right, (((1,), (0,)), ((), ())), preferred_element_type=F32)


def dot_rows(left, right):
    return lax.dot_general(left, right, (((0,), (0,)), ((), ())), preferred_element_type=F32)


def dot_against(left, right):
    return lax.dot_general(left, right, (((1,), (1,)), ((), ())), preferred_element_type=F32)


def iota(shape, dim):
    return lax.broadcasted_iota(jnp.int32, shape, dim)


def normalize(values):
    center = jnp.mean(values, axis=-1, keepdims=True)
    offset = values - center
    spread = jnp.mean(offset * offset, axis=-1, keepdims=True)
    inverse = lax.rsqrt(spread + EPS)
    return offset * inverse, inverse


def denormalize(upstream, normed, inverse, gain):
    scaled = upstream * gain
    return inverse * (
        scaled
        - jnp.mean(scaled, axis=-1, keepdims=True)
        - normed * jnp.mean(scaled * normed, axis=-1, keepdims=True)
    )


def to_row(column):
    n = column.shape[0]
    parts = []
    for at in range(0, n, LANES):
        size = min(LANES, n - at)
        eye = iota((size, LANES), 0) == iota((size, LANES), 1)
        parts.append(jnp.sum(jnp.where(eye, column[at : at + size], 0.0), axis=0, keepdims=True))
    return parts[0] if len(parts) == 1 else jnp.concatenate(parts, axis=1)


def to_column(row, n):
    eye = iota((n, row.shape[1]), 0) == iota((n, row.shape[1]), 1)
    return jnp.sum(jnp.where(eye, row, 0.0), axis=1, keepdims=True)


def rows_of(g):
    return pl.ds(pl.multiple_of(g * BLOCK, BLOCK), BLOCK)


def gates_of(probs, meta):
    lane = iota(probs.shape, 1)
    first = jnp.sum(jnp.where(lane == meta[:, 2:3], probs, 0.0), axis=1, keepdims=True)
    second = jnp.sum(jnp.where(lane == meta[:, 3:4], probs, 0.0), axis=1, keepdims=True)
    return first, second


class Place:
    def __init__(self, fsdp, xs):
        self.A, self.B = 4, fsdp // 8
        self.x = lax.axis_index("expert")
        self.me = lax.axis_index("fsdp")
        self.c = lax.rem(self.me, 2)
        line = lax.div(self.me, 2)
        self.b = lax.rem(line, self.B)
        self.a = lax.div(line, self.B)
        self.xs, self.peers = xs, xs * self.B
        self.peer = self.x * self.B + self.b

    def index(self, a, b, c):
        return (a * self.B + b) * 2 + c

    def other_b(self, j):
        return lax.rem(self.b + 1 + j, self.B)

    def at(self, a, b, c):
        return (self.x, self.index(a, b, c))

    def at_peer(self, peer):
        return (lax.div(peer, self.B), self.index(self.a, lax.rem(peer, self.B), self.c))

    def other_peer(self, k):
        x, b = lax.rem(self.x + lax.rem(k, self.xs), self.xs), lax.rem(self.b + lax.div(k, self.xs), self.B)
        return x * self.B + b

    def seen_from(self, k):
        x, b = lax.rem(self.xs - lax.rem(k, self.xs), self.xs), lax.rem(self.B - lax.div(k, self.xs), self.B)
        return b * self.xs + x


def greet(place, meanwhile):
    barrier = pltpu.get_barrier_semaphore()

    def signal(device):
        pl.semaphore_signal(barrier, inc=1, device_id=device, device_id_type=MESH)

    for k in range(1, place.A):
        signal(place.at(lax.rem(place.a + k, place.A), place.b, place.c))
    for k in range(1, place.peers):
        signal(place.at_peer(place.other_peer(k)))
    signal(place.at(place.a, place.b, 1 - place.c))
    meanwhile()
    pl.semaphore_wait(barrier, place.A - 1 + place.peers - 1 + 1)


class Gather:
    RIGHT, LEFT, CORE, ACROSS = 0, 1, 2, 3

    def __init__(self, place, own, full, block, send_sem, recv_sem, local_sem):
        self.place, self.own, self.full, self.block = place, own, full, block
        self.send_sem, self.recv_sem, self.local_sem = send_sem, recv_sem, local_sem

    def copy(self, shard, route, source, a, b, c):
        return pltpu.make_async_remote_copy(
            src_ref=source, dst_ref=self.block(self.full, shard),
            send_sem=self.send_sem.at[route], recv_sem=self.recv_sem.at[self.arrival(shard, route)],
            device_id=self.place.at(a, b, c), device_id_type=MESH,
        )

    def arrival(self, shard, route):
        return self.place.A * self.place.B if route == self.CORE else lax.div(shard, 2)

    def some(self, route, blocks):
        size = self.own.shape[0]
        ref = self.full.at[pl.ds(0, blocks * size), :]
        p = self.place
        return pltpu.make_async_remote_copy(
            src_ref=ref, dst_ref=ref, send_sem=self.send_sem.at[route], recv_sem=self.recv_sem.at[p.A * p.B],
            device_id=p.at(p.a, p.b, 1 - p.c), device_id_type=MESH,
        )

    def onward(self, shard, source, right, left, across, act):
        p = self.place
        if right is not None:
            pl.when(right)(lambda: act(self.copy(shard, self.RIGHT, source, p.a + 1, p.b, p.c)))
        if left is not None:
            pl.when(left)(lambda: act(self.copy(shard, self.LEFT, source, p.a - 1, p.b, p.c)))
        if across:
            for j in range(p.B - 1):
                act(self.copy(shard, self.ACROSS + j, source, p.a, p.other_b(j), p.c))
        act(self.copy(shard, self.CORE, source, p.a, p.b, 1 - p.c))

    def local(self):
        return pltpu.make_async_copy(self.own, self.block(self.full, self.place.me), self.local_sem)

    def start(self):
        p = self.place
        self.local().start()
        self.onward(p.me, self.own, p.a < p.A - 1, p.a > 0, True, lambda copy: copy.start())

    def arrived(self, shard):
        p = self.place
        self.copy(shard, self.RIGHT, self.block(self.full, shard), p.a, p.b, 1 - p.c).wait_recv()

    def line_step(self, k):
        p = self.place

        def from_left():
            shard = p.index(p.a - k, p.b, p.c)
            self.arrived(shard)
            self.onward(shard, self.block(self.full, shard), p.a < p.A - 1, None, True, lambda copy: copy.start())

        def from_right():
            shard = p.index(p.a + k, p.b, p.c)
            self.arrived(shard)
            self.onward(shard, self.block(self.full, shard), None, p.a > 0, True, lambda copy: copy.start())

        pl.when(p.a - k >= 0)(from_left)
        pl.when(p.a + k < p.A)(from_right)

    def across_step(self, k):
        p = self.place

        def row(a):
            for j in range(p.B - 1):
                shard = p.index(a, p.other_b(j), p.c)
                self.arrived(shard)
                self.onward(shard, self.block(self.full, shard), None, None, False, lambda copy: copy.start())

        if k == 0:
            row(p.a)
        else:
            pl.when(p.a - k >= 0)(lambda: row(p.a - k))
            pl.when(p.a + k < p.A)(lambda: row(p.a + k))

    def finish_recv(self):
        p = self.place
        self.local().wait()
        self.some(self.CORE, p.A * p.B).wait_recv()

    def finish_send(self):
        p = self.place
        for a in range(p.A - 1):
            pl.when(p.a == a)(self.some(self.RIGHT, a + 1).wait_send)
            pl.when(p.a == a + 1)(self.some(self.LEFT, p.A - 1 - a).wait_send)
        for j in range(p.B - 1):
            self.some(self.ACROSS + j, p.A).wait_send()
        self.some(self.CORE, p.A * p.B).wait_send()


class ExpertGather:
    RIGHT, LEFT, CORE, ACROSS = 0, 1, 2, 3

    def __init__(self, place, own, full, count, send_sem, recv_sem, local_sem):
        self.place, self.own, self.full, self.count = place, own, full, count
        self.send_sem, self.recv_sem, self.local_sem = send_sem, recv_sem, local_sem
        self.size = own.shape[1]
        self.depth = self.size * place.A * place.B * 2

    def block(self, el, shard):
        return self.full.at[pl.ds(pl.multiple_of(el * self.depth + shard * self.size, self.size), self.size), :]

    def mine(self, el):
        return self.own.at[self.place.b * self.count + el]

    def copy(self, el, shard, route, source, a, b, c):
        return pltpu.make_async_remote_copy(
            src_ref=source, dst_ref=self.block(el, shard),
            send_sem=self.send_sem.at[el, route], recv_sem=self.recv_sem.at[el, self.arrival(shard, route)],
            device_id=self.place.at(a, b, c), device_id_type=MESH,
        )

    def arrival(self, shard, route):
        return self.place.A * self.place.B if route == self.CORE else lax.div(shard, 2)

    def some(self, el, route, blocks):
        ref = self.full.at[pl.ds(el * self.depth, blocks * self.size), :]
        p = self.place
        return pltpu.make_async_remote_copy(
            src_ref=ref, dst_ref=ref, send_sem=self.send_sem.at[el, route], recv_sem=self.recv_sem.at[el, p.A * p.B],
            device_id=p.at(p.a, p.b, 1 - p.c), device_id_type=MESH,
        )

    def across(self, el):
        p = self.place
        out = []
        for j in range(p.B - 1):
            to = p.other_b(j)
            out.append(self.copy(el, p.me, self.ACROSS + j, self.own.at[to * self.count + el], p.a, to, p.c))
        return out

    def local(self, el):
        return pltpu.make_async_copy(self.mine(el), self.block(el, self.place.me), self.local_sem.at[el])

    def onward(self, el, shard, source, right, left, act):
        p = self.place
        if right:
            pl.when(p.a < p.A - 1)(lambda: act(self.copy(el, shard, self.RIGHT, source, p.a + 1, p.b, p.c)))
        if left:
            pl.when(p.a > 0)(lambda: act(self.copy(el, shard, self.LEFT, source, p.a - 1, p.b, p.c)))
        act(self.copy(el, shard, self.CORE, source, p.a, p.b, 1 - p.c))

    def arrived(self, el, shard):
        p = self.place
        self.copy(el, shard, self.RIGHT, self.block(el, shard), p.a, p.b, 1 - p.c).wait_recv()

    def start_across(self, el):
        for copy in self.across(el):
            copy.start()

    def start_own(self, el):
        self.local(el).start()
        self.onward(el, self.place.me, self.mine(el), True, True, lambda copy: copy.start())

    def across_step(self, el):
        p = self.place
        for j in range(p.B - 1):
            shard = p.index(p.a, p.other_b(j), p.c)
            self.arrived(el, shard)
            self.onward(el, shard, self.block(el, shard), True, True, lambda copy: copy.start())

    def line_step(self, el, k, own):
        p = self.place

        def row(a, right, left):
            for b in [p.b] if own else [p.other_b(j) for j in range(p.B - 1)]:
                shard = p.index(a, b, p.c)
                self.arrived(el, shard)
                self.onward(el, shard, self.block(el, shard), right, left, lambda copy: copy.start())

        pl.when(p.a - k >= 0)(lambda: row(p.a - k, True, False))
        pl.when(p.a + k < p.A)(lambda: row(p.a + k, False, True))

    def core_wait(self, el):
        p = self.place
        self.local(el).wait()
        self.some(el, self.CORE, p.A * p.B).wait_recv()

    def finish(self, el):
        p = self.place
        for copy in self.across(el):
            copy.wait_send()
        for a in range(p.A - 1):
            pl.when(p.a == a)(self.some(el, self.RIGHT, (a + 1) * p.B).wait_send)
            pl.when(p.a == a + 1)(self.some(el, self.LEFT, (p.A - 1 - a) * p.B).wait_send)
        self.some(el, self.CORE, p.A * p.B).wait_send()


class ExpertScatter:
    def __init__(self, place, part, sums, line, out, count, send, recv, local_sem):
        self.place, self.part, self.sums, self.line, self.out, self.count = place, part, sums, line, out, count
        self.send, self.recv, self.local_sem = send, recv, local_sem

    CORE, RIGHT, LEFT, LAST = 0, 1, 2, 3

    def remote(self, source, target, el, route, arrival, a, b, c):
        return pltpu.make_async_remote_copy(
            src_ref=source, dst_ref=target, send_sem=self.send.at[el, route], recv_sem=self.recv.at[el, arrival],
            device_id=self.place.at(a, b, c), device_id_type=MESH,
        )

    def core_copy(self, el):
        p = self.place
        return self.remote(self.part(el).at[:, :, 1 - p.c], self.sums.at[el], el, self.CORE, 0, p.a, p.b, 1 - p.c)

    def right_copy(self, el, target):
        p = self.place
        return self.remote(
            self.sums.at[el, target], self.line.at[el, 0, target - 1], el, self.RIGHT, target, p.a + 1, p.b, p.c
        )

    def left_copy(self, el, target):
        p = self.place
        return self.remote(
            self.sums.at[el, target], self.line.at[el, 1, target], el, self.LEFT, p.A + target, p.a - 1, p.b, p.c
        )

    def add(self, el, target, way, slot):
        @pl.loop(0, self.place.B)
        def _(b):
            total = self.sums[el, target, b].astype(F32) + self.line[el, way, slot, b].astype(F32)
            self.sums[el, target, b] = total.astype(BF16)

    def relay_step(self, el, step):
        p = self.place

        @pl.when(p.a <= step)
        def _():
            target = p.a + p.A - 1 - step

            @pl.when(p.a > 0)
            def _():
                self.right_copy(el, target).wait_recv()
                self.add(el, target, 0, target - 1)

            self.right_copy(el, target).start()

        @pl.when(p.a >= p.A - 1 - step)
        def _():
            target = p.a - (p.A - 1 - step)

            @pl.when(p.a < p.A - 1)
            def _():
                self.left_copy(el, target).wait_recv()
                self.add(el, target, 1, target)

            self.left_copy(el, target).start()

    def last_copies(self, el):
        p = self.place
        out = []
        for j in range(p.B - 1):
            to, back = p.other_b(j), p.B - 2 - j
            target = self.out.at[p.b * self.count + el]
            out.append(self.remote(self.sums.at[el, p.a, to], target, el, self.LAST + j, 2 * p.A - 1 + back, p.a, to, p.c))
        return out

    def local(self, el):
        p = self.place
        return pltpu.make_async_copy(self.sums.at[el, p.a, p.b], self.out.at[p.b * self.count + el], self.local_sem.at[el])

    def start(self, el):
        self.core_copy(el).start()

    def core_step(self, el):
        p = self.place
        self.core_copy(el).wait()
        part = self.part(el)

        @pl.loop(0, p.A * p.B)
        def _(i):
            a, b = lax.div(i, p.B), lax.rem(i, p.B)
            total = self.sums[el, a, b].astype(F32) + part[a, b, p.c].astype(F32)
            self.sums[el, a, b] = total.astype(BF16)

    def line_step(self, el):
        p = self.place

        @pl.when(p.a > 0)
        def _():
            self.right_copy(el, p.a).wait_recv()
            self.add(el, p.a, 0, p.a - 1)

        @pl.when(p.a < p.A - 1)
        def _():
            self.left_copy(el, p.a).wait_recv()
            self.add(el, p.a, 1, p.a)

        for copy in self.last_copies(el) + [self.local(el)]:
            copy.start()

    def finish(self, el):
        p = self.place
        for a in range(p.A - 1):
            for route, at, count in ((self.RIGHT, a, p.A - 1 - a), (self.LEFT, a + 1, a + 1)):
                some = self.sums.at[el, pl.ds(0, count)]
                pl.when(p.a == at)(self.remote(some, some, el, route, 0, p.a, p.b, 1 - p.c).wait_send)
        for copy in self.last_copies(el) + [self.local(el)]:
            copy.wait()


class Scatter:
    def __init__(self, place, part, sums, across, line, columns, send, recv):
        self.place, self.part, self.sums, self.across, self.line = place, part, sums, across, line
        self.columns, self.send, self.recv = columns, send, recv

    CORE, ACROSS, LINE = 0, 1, 2

    def remote(self, source, target, item, route, a, b, c):
        return pltpu.make_async_remote_copy(
            src_ref=source, dst_ref=target,
            send_sem=self.send.at[item, min(route, 1)], recv_sem=self.recv.at[item, route],
            device_id=self.place.at(a, b, c), device_id_type=MESH,
        )

    def all_of(self, ref, item, route):
        p = self.place
        return self.remote(ref, ref, item, route, p.a, p.b, 1 - p.c)

    def core_copy(self, item):
        p, at = self.place, self.columns[item]
        return self.remote(self.part.at[:, :, 1 - p.c, :, at], self.sums.at[:, :, :, at], item, self.CORE, p.a, p.b, 1 - p.c)

    def across_copies(self, item):
        p, at = self.place, self.columns[item]
        out = []
        for j in range(p.B - 1):
            to, back = p.other_b(j), p.B - 2 - j
            copy = self.remote(self.sums.at[:, to, :, at], self.across.at[back, :, :, at], item, self.ACROSS, p.a, to, p.c)
            out.append(copy)
        return out

    def line_copies(self, item):
        p, at = self.place, self.columns[item]
        out = []
        for k in range(1, p.A):
            to, back = lax.rem(p.a + k, p.A), p.A - 1 - k
            copy = self.remote(self.sums.at[to, p.b, :, at], self.line.at[back, :, at], item, self.LINE, to, p.b, p.c)
            out.append(copy)
        return out

    def start(self, item):
        self.core_copy(item).start()

    def core_step(self, item):
        p, at = self.place, self.columns[item]
        self.core_copy(item).wait()

        @pl.loop(0, p.A * p.B)
        def _(i):
            a, b = lax.div(i, p.B), lax.rem(i, p.B)
            total = self.sums[a, b, :, at].astype(F32) + self.part[a, b, p.c, :, at].astype(F32)
            self.sums[a, b, :, at] = total.astype(BF16)

        for copy in self.across_copies(item):
            copy.start()

    def across_step(self, item):
        p, at = self.place, self.columns[item]
        self.all_of(self.across.at[:, :, :, at], item, self.ACROSS).wait_recv()

        @pl.loop(0, p.A)
        def _(a):
            total = self.sums[a, p.b, :, at].astype(F32)
            for j in range(p.B - 1):
                total += self.across[j, a, :, at].astype(F32)
            self.sums[a, p.b, :, at] = total.astype(BF16)

        for copy in self.line_copies(item):
            copy.start()

    def line_step(self, item):
        p, at = self.place, self.columns[item]
        self.all_of(self.line.at[:, :, at], item, self.LINE).wait_recv()
        total = self.sums[p.a, p.b, :, at].astype(F32)
        for k in range(p.A - 1):
            total += self.line[k, :, at].astype(F32)
        return total

    def finish(self, item):
        p, at = self.place, self.columns[item]
        blocks = self.sums.reshape(p.A * p.B, *self.sums.shape[2:])
        self.all_of(blocks.at[pl.ds(0, (p.B - 1) * p.A + p.A - 1), :, at], item, self.LINE).wait_send()


def block_kernel(
    experts, fsdp, xs, count,
    x_raw, cot_raw, routes_ref, slots_ref, qkv_ref, out_ref, router_ref, gain_one_ref, shift_one_ref, gain_two_ref, shift_two_ref,
    up_in, down_in,
    out_out, input_grad_out, share_out, up_grad_out, down_grad_out,
    act_one_save, weights_save, attended_save, mid_save, act_two_save,
    shard_ref, meta_row_ref, meta_ref, x_ref, params_ref, triple_ref, probs_ref,
    sent_ref, cot_sent_ref, gate_sent_ref, rows_ref, grad_ref, gate_ref, back_ref, grad_slots_ref, dots_sent_ref, dots_ref,
    up_ref, down_ref, part_up_ref, part_down_ref, float_ref,
    sums_up, sums_down, line_up, line_down, sums_par, across_par, line_par, swap_ref,
    bias_ref, gate_rows_ref, dot_row_ref, place_ref, gated_ref, logit_grad_ref, column_ref,
    save_sem, late_sem, store_sem, par_gather_send, par_gather_recv, par_gather_local,
    gather_send, gather_recv, gather_local, swap_send, swap_recv, return_send, return_recv,
    scatter_send, scatter_recv, scatter_local, par_send, par_recv, share_send, share_recv,
):
    rows_pad, width = x_ref.shape
    groups = rows_pad // BLOCK
    places = sent_ref.shape[0]
    capacity = places // experts
    hidden_width = up_ref.shape[1]
    chunks = hidden_width // FF_CHUNK
    held = up_in.shape[0]
    place = Place(fsdp, xs)
    A, B, sources = place.A, place.B, place.peers
    expert_rows = sources * capacity
    row_block = gated_ref.shape[0]
    copy_in = pltpu.make_async_copy

    weights_ref = part_up_ref
    act_one, attended, act_two, cot_ref = (part_down_ref.at[pl.ds(i * rows_pad, rows_pad), :] for i in range(4))
    mid_ref = float_ref

    def spread(raw, there):
        for g in range(groups):
            there[g * BLOCK : g * BLOCK + GROUP_ROWS, :] = raw[g * GROUP_ROWS : (g + 1) * GROUP_ROWS, :]
            there[g * BLOCK + GROUP_ROWS : (g + 1) * BLOCK, :] = jnp.zeros((BLOCK - GROUP_ROWS, width), BF16)

    def prepare():
        shard_ref[:, : 3 * width] = qkv_ref[...]
        shard_ref[:, 3 * width : 4 * width] = out_ref[...]
        size = shard_ref.shape[0]
        eye = iota((size, size), 0) == iota((size, size), 1)
        lane = iota((size, LANES), 1)
        small = jnp.zeros((size, LANES), F32)
        for i, norm_ref in enumerate((gain_one_ref, shift_one_ref, gain_two_ref, shift_two_ref)):
            row = norm_ref[...].astype(F32).reshape(1, size)
            column = jnp.sum(jnp.where(eye, row, 0.0), axis=1, keepdims=True)
            small = jnp.where(lane == NORM_LANE + i, column, small)
        shard_ref[:, 4 * width :] = small.astype(BF16)
        shard_ref[:, 4 * width : 4 * width + experts] = jnp.transpose(router_ref[...].astype(F32)).astype(BF16)

    greet(place, prepare)

    def rows_block(ref, shard):
        size = shard_ref.shape[0]
        return ref.at[pl.ds(pl.multiple_of(shard * size, size), size), :]

    params = Gather(place, shard_ref, params_ref, rows_block, par_gather_send, par_gather_recv, par_gather_local)
    weights_in = [
        ExpertGather(place, own, full, count, gather_send.at[i], gather_recv.at[i], gather_local.at[i])
        for i, (own, full) in enumerate(((up_in, up_ref), (down_in, down_ref)))
    ]

    def each(step, el, *more):
        if el < count:
            for gather in weights_in:
                getattr(gather, step)(el, *more)

    def do(*point):
        for name, el, *more in PLAN.get(point, ()):
            if el < count:
                with jax.named_scope("_".join(map(str, (name, el, *more)))):
                    actions[name](el, *more)

    inner = jnp.logical_and(place.a > 0, place.a < A - 1)

    def ends(el):
        for k in range(1, A):
            for own in (True, False):
                each("line_step", el, k, own)

    actions = {
        "across": lambda el: each("start_across", el),
        "own": lambda el: each("start_own", el),
        "passed": lambda el: each("across_step", el),
        "relay": lambda el, k, own: pl.when(inner)(lambda: each("line_step", el, k, own)),
        "ends": lambda el: pl.when(jnp.logical_not(inner))(lambda: ends(el)),
        "cots": lambda el, *which: cot_swaps(el, *which),
        "rows": lambda el: row_swaps(el),
        "sums": lambda el: all_scatters("core_step", el),
        "outputs": lambda el, *which: outputs(el, *which),
        "sum_relay": lambda el, step: all_scatters("relay_step", el, step),
    }
    params.start()
    do("start", 0)
    targets = jnp.where(slots_ref[...] >= 0, routes_ref[...] * capacity + slots_ref[...], -1)
    meta_row_ref[...] = jnp.full(meta_row_ref.shape, -1, jnp.int32)
    for g in range(groups):
        at = slice(g * BLOCK, g * BLOCK + GROUP_ROWS)
        meta_row_ref[0:2, at] = targets[:, g * GROUP_ROWS : (g + 1) * GROUP_ROWS]
        meta_row_ref[2:4, at] = routes_ref[:, g * GROUP_ROWS : (g + 1) * GROUP_ROWS]
    image_row = iota((BLOCK, BLOCK), 0) // PATCHES
    image_col = iota((BLOCK, BLOCK), 1) // PATCHES
    bias_ref[...] = jnp.where(image_row == image_col, 0.0, -1e30)

    def slot_rows(e):
        return pl.ds(pl.multiple_of(e * capacity, 16), capacity)

    def source_rows(el, source):
        return pl.ds(pl.multiple_of(el * expert_rows + source * capacity, 16), capacity)

    def find(e):
        slot = iota((capacity, rows_pad), 0) + e * capacity
        in_first = slot == meta_row_ref[0:1, :]
        in_second = slot == meta_row_ref[1:2, :]
        return in_first, in_second, jnp.where(jnp.logical_or(in_first, in_second), 1.0, 0.0).astype(BF16)

    def swap(kind, el, k):
        peer, back = place.other_peer(k), place.seen_from(k)
        e = peer * count + el
        if kind == 1:
            source, target = gate_sent_ref.at[e], gate_ref.at[el * sources + back]
        else:
            here, there = (sent_ref, rows_ref) if kind == 0 else (cot_sent_ref, grad_ref)
            source, target = here.at[slot_rows(e), :], there.at[source_rows(el, back), :]
        return pltpu.make_async_remote_copy(
            src_ref=source, dst_ref=target, send_sem=swap_send.at[kind, el], recv_sem=swap_recv.at[kind, el, back],
            device_id=place.at_peer(peer), device_id_type=MESH,
        )

    def swap_wait(kind, el, k):
        if kind == 1:
            target = gate_ref.at[el * sources + k]
        else:
            target = (rows_ref if kind == 0 else grad_ref).at[source_rows(el, k), :]
        pltpu.make_async_remote_copy(
            src_ref=target, dst_ref=target, send_sem=swap_send.at[kind, el], recv_sem=swap_recv.at[kind, el, k],
            device_id=place.at_peer(place.other_peer(k)), device_id_type=MESH,
        ).wait_recv()

    def all_of(kind, send, recv):
        some = gate_ref.at[pl.ds(0, sources - 1)] if kind == 1 else rows_ref.at[pl.ds(0, (sources - 1) * capacity), :]
        return pltpu.make_async_remote_copy(
            src_ref=some, dst_ref=some, send_sem=send, recv_sem=recv,
            device_id=place.at(place.a, place.b, 1 - place.c), device_id_type=MESH,
        )

    def peers_where(which, act):
        @pl.loop(1, sources)
        def _(k):
            for name, same in (("x", lax.div(k, xs) == 0), ("y", lax.rem(k, xs) == 0)):
                if which == name:
                    pl.when(same)(lambda: act(k))
            if which == "far":
                pl.when(jnp.logical_and(lax.div(k, xs) > 0, lax.rem(k, xs) > 0))(lambda: act(k))

    def cot_swaps(el, *which):
        for peers in which:
            peers_where(peers, lambda k: swap(2, el, k).start())

    def cot_own(el):
        grad_ref[source_rows(el, 0), :] = cot_sent_ref[slot_rows(place.peer * count + el), :]

    def row_swaps(el):
        @pl.loop(1, sources)
        def _(k):
            swap(0, el, k).start()
            swap(1, el, k).start()

    spread(cot_raw, cot_ref)
    for k in range(1, A):
        params.line_step(k)
        do("start", k)

        @pl.loop((k - 1) * experts // (A - 1), k * experts // (A - 1))
        def _(i):
            e = place.other_peer(lax.rem(lax.div(i, count) + 1, sources)) * count + lax.rem(i, count)
            _, _, picks = find(e)
            cot_sent_ref[slot_rows(e), :] = dot(picks, cot_ref[...]).astype(BF16)

        if k == 1:
            spread(x_raw, x_ref)
            meta_ref[...] = jnp.transpose(meta_row_ref[...])
        do("after", k)
        params.across_step(k - 1)

    params.across_step(A - 1)
    params.finish_recv()
    for el in range(count):
        cot_own(el)
    do("begin", 0)

    small = params_ref[:, 4 * width :]
    small_rows = jnp.transpose(small.astype(F32))

    def saves(rows):
        pairs = (
            (act_one, act_one_save), (weights_ref.at[:, pl.ds(0, HEADS * BLOCK)], weights_save), (attended, attended_save),
            (mid_ref, mid_save), (act_two, act_two_save),
        )
        return [copy_in(here.at[rows, :], there.at[rows, :], save_sem.at[i]) for i, (here, there) in enumerate(pairs)]

    @pl.loop(0, groups)
    def _(g):
        rows = rows_of(g)
        x = x_ref[rows, :].astype(F32)
        normed, _ = normalize(x)
        act = (normed * small_rows[NORM_LANE : NORM_LANE + 1] + small_rows[NORM_LANE + 1 : NORM_LANE + 2]).astype(BF16)
        act_one[rows, :] = act
        triple_ref[rows, :] = dot(act, params_ref[:, : 3 * width]).astype(BF16)
        low = iota((BLOCK, LANES), 1) < HEAD_DIM
        for pair in range(HEADS // 2):
            at = pair * LANES
            q = triple_ref[rows, at : at + LANES] * HEAD_DIM ** (-0.5)
            k = triple_ref[rows, width + at : width + at + LANES]
            v = triple_ref[rows, 2 * width + at : 2 * width + at + LANES]
            total = None
            for half in range(2):
                mask = low if half == 0 else jnp.logical_not(low)
                scores = dot_against(jnp.where(mask, q, 0.0).astype(BF16), k) + bias_ref[...]
                top = jnp.max(scores, axis=-1, keepdims=True)
                raised = jnp.exp(scores - top)
                probs = raised / jnp.sum(raised, axis=-1, keepdims=True)
                probs = probs.astype(BF16)
                head = (2 * pair + half) * BLOCK
                weights_ref[rows, head : head + BLOCK] = probs
                part = dot(probs, jnp.where(mask, v, 0.0).astype(BF16))
                total = part if total is None else total + part
            attended[rows, at : at + LANES] = total.astype(BF16)

        for i in range(groups):
            pl.when(g == i)(functools.partial(do, "middle", i))

        mid = x + dot(attended[rows, :], params_ref[:, 3 * width : 4 * width])
        mid_ref[rows, :] = mid
        normed, _ = normalize(mid)
        act = (normed * small_rows[NORM_LANE + 2 : NORM_LANE + 3] + small_rows[NORM_LANE + 3 : NORM_LANE + 4]).astype(BF16)
        act_two[rows, :] = act
        logits = jnp.where(iota((BLOCK, LANES), 1) < experts, dot(act, small), -1e30)
        raised = jnp.exp(logits - jnp.max(logits, axis=-1, keepdims=True))
        probs = raised / jnp.sum(raised, axis=-1, keepdims=True)
        probs_ref[rows, :] = probs
        first, second = gates_of(probs, meta_ref[rows, :])
        gate_rows_ref[0:1, rows] = to_row(first)
        gate_rows_ref[1:2, rows] = to_row(second)
        for copy in saves(rows):
            copy.start()

        for i in range(groups):
            pl.when(g == i)(functools.partial(do, "end", i))

    @pl.loop(0, experts)
    def _(i):
        el, k = lax.div(i, sources), lax.rem(lax.rem(i, sources) + 1, sources)
        e = place.other_peer(k) * count + el
        in_first, in_second, picks = find(e)
        gate = jnp.sum(
            jnp.where(in_first, gate_rows_ref[0:1, :], jnp.where(in_second, gate_rows_ref[1:2, :], 0.0)),
            axis=1, keepdims=True,
        )
        sent_ref[slot_rows(e), :] = dot(picks, act_two[...]).astype(BF16)
        gate_sent_ref[e, 0:1, :] = to_row(gate)

        @pl.when(jnp.logical_and(el == 0, k > 0))
        def _():
            swap(0, el, k).start()
            swap(1, el, k).start()

        @pl.when(k == 0)
        def _():
            rows_ref[source_rows(el, 0), :] = sent_ref[slot_rows(e), :]
            gate_ref[el * sources] = gate_sent_ref[e]

        for at in range(8):
            pl.when(i == at)(functools.partial(do, "dispatch", at))

    for copy in saves(pl.ds(0, rows_pad)):
        copy.wait()

    part_up = part_up_ref.at[pl.ds(0, count * width), :].reshape(count, A, B, 2, up_in.shape[1], part_up_ref.shape[1])
    part_down = part_down_ref.at[pl.ds(0, count * hidden_width), :].reshape(count, A, B, 2, down_in.shape[1], width)
    scatters = [
        ExpertScatter(place, part, sums, line, out, count, scatter_send.at[i], scatter_recv.at[i], scatter_local.at[i])
        for i, (part, sums, line, out) in enumerate(
            (
                (lambda el: part_up.at[el, :, :, :, :, pl.ds(0, hidden_width)], sums_up, line_up, up_grad_out),
                (lambda el: part_down.at[el], sums_down, line_down, down_grad_out),
            )
        )
    ]

    def all_scatters(step, el, *more):
        for scatter in scatters:
            getattr(scatter, step)(el, *more)

    pairs = HEADS // 2
    columns = [slice(3 * LANES * p, 3 * LANES * (p + 1)) for p in range(pairs)]
    columns += [slice(3 * width, 4 * width), slice(4 * width, 4 * width + LANES)]
    par_out, par_small = pairs, pairs + 1
    par = Scatter(place, part_up.at[0], sums_par, across_par, line_par, columns, par_send, par_recv)

    def shares(item):
        at = columns[item]
        out = []
        for k in range(1, xs):
            to, back = lax.rem(place.x + k, xs), xs - 1 - k
            out.append(
                pltpu.make_async_remote_copy(
                    src_ref=swap_ref.at[place.x, :, at], dst_ref=swap_ref.at[place.x, :, at],
                    send_sem=share_send.at[item, back], recv_sem=share_recv.at[item, back],
                    device_id=(to, place.me), device_id_type=MESH,
                )
            )
        return out

    def par_last(item):
        swap_ref[place.x, :, columns[item]] = par.line_step(item).astype(BF16)
        for copy in shares(item):
            copy.start()

    def returned(kind, el, k):
        e = place.peer * count + el
        if kind == 1:
            source, target = dots_sent_ref.at[el * sources + k], dots_ref.at[e]
        else:
            here, there = (grad_ref, grad_slots_ref) if kind == 0 else (rows_ref, back_ref)
            source, target = here.at[source_rows(el, k), :], there.at[slot_rows(e), :]
        return pltpu.make_async_remote_copy(
            src_ref=source, dst_ref=target,
            send_sem=return_send.at[kind, el], recv_sem=return_recv.at[kind, el],
            device_id=place.at_peer(place.other_peer(k)), device_id_type=MESH,
        )

    def give_back(kind, el, first=1, stop=sources):
        @pl.loop(first, stop)
        def _(k):
            returned(kind, el, k).start()

    def outputs(el, *which):
        for peers in which:
            peers_where(peers, lambda k: returned(2, el, k).start())

    def return_wait(kind, el):
        all_of(kind, return_send.at[kind, el], return_recv.at[kind, el]).wait_recv()

    def expert(el):
        blocks = expert_rows // row_block
        block_sources = row_block // capacity
        order = list(range(blocks))
        if el > 0 and el == count - 1:
            order.reverse()
        each("core_wait", el)
        for turn, block in enumerate(order):
            first, stop = block * block_sources, (block + 1) * block_sources
            for kind in range(3):
                pl.loop(max(first, 1), stop)(functools.partial(swap_wait, kind, el))
            do("before", el, turn)
            here = pl.ds(el * expert_rows + block * row_block, row_block)
            float_ref[: 2 * row_block, :] = jnp.zeros((2 * row_block, width), F32)

            @pl.loop(first, stop)
            def _(k):
                gate = to_column(gate_ref[el * sources + k, 0:1, :], capacity)
                cots = grad_ref[source_rows(el, k), :].astype(F32)
                local = pl.ds(pl.multiple_of((k - first) * capacity, 16), capacity)
                gated_ref[local, :] = (gate * cots).astype(BF16)

            @pl.loop(0, chunks)
            def _(f):
                at = pl.ds(pl.multiple_of(f * FF_CHUNK, FF_CHUNK), FF_CHUNK)
                down_at = pl.ds(pl.multiple_of(el * hidden_width + f * FF_CHUNK, FF_CHUNK), FF_CHUNK)
                rows, grads = rows_ref[here, :], gated_ref[...]
                up_part, down_part = up_ref[el * width : (el + 1) * width, at], down_ref[down_at, :]
                hidden = dot(rows, up_part)
                spread = 0.5 * (1.0 + lax.erf(hidden * ROOT_HALF))
                active = (hidden * spread).astype(BF16)
                slope = spread + hidden * (DENSITY_SCALE * jnp.exp(-0.5 * hidden * hidden))
                grad_active = dot_against(grads, down_part)
                float_ref[:row_block, :] += dot(active, down_part)
                grad_hidden = (grad_active * slope).astype(BF16)
                float_ref[row_block : 2 * row_block, :] += dot_against(grad_hidden, up_part)
                size = up_in.shape[1]
                up_sum = dot_rows(rows, grad_hidden).reshape(A, B, 2, size, FF_CHUNK)
                down_sum = dot_rows(active, grads)
                if turn > 0:
                    up_sum += part_up[el, :, :, :, :, at].astype(F32)
                    down_sum += part_down_ref[down_at, :].astype(F32)
                part_up[el, :, :, :, :, at] = up_sum.astype(BF16)
                part_down_ref[down_at, :] = down_sum.astype(BF16)
                for i in range(chunks):
                    pl.when(f == i)(functools.partial(do, "expert", el, turn * chunks + i))

            @pl.loop(first, stop)
            def _(k):
                at = source_rows(el, k)
                local = pl.ds(pl.multiple_of((k - first) * capacity, 16), capacity)
                back = float_ref[local, :].astype(BF16)
                rows_ref[at, :] = back
                dots = jnp.sum(back.astype(F32) * grad_ref[at, :].astype(F32), axis=1, keepdims=True)
                dots_sent_ref[el * sources + k, 0:1, :] = to_row(dots)
                local = pl.ds(pl.multiple_of(row_block + (k - first) * capacity, 16), capacity)
                grad_ref[at, :] = float_ref[local, :].astype(BF16)

            give_back(0, el, max(first, 1), stop)
            give_back(1, el, max(first, 1), stop)

        all_scatters("start", el)
        own, e = source_rows(el, 0), place.peer * count + el
        back_ref[slot_rows(e), :] = rows_ref[own, :]
        grad_slots_ref[slot_rows(e), :] = grad_ref[own, :]
        dots_ref[e] = dots_sent_ref[el * sources]

    for el in range(count):
        expert(el)
        do("after_expert", el)

    def late_loads():
        out = [copy_in(weights_save, up_ref.at[pl.ds(0, rows_pad), :], late_sem.at[0])]
        for i, array in enumerate((act_one_save, attended_save, act_two_save)):
            out.append(copy_in(array, down_ref.at[pl.ds(i * rows_pad, rows_pad), :], late_sem.at[1 + i]))
        for i in range(2):
            out.append(copy_in(mid_save, float_ref.at[pl.ds(i * rows_pad, rows_pad), :], late_sem.at[4 + i]))
        return out

    for el in range(count):
        each("finish", el)
    for copy in late_loads():
        copy.start()
    spread(cot_raw, down_ref.at[pl.ds(3 * rows_pad, rows_pad), :])
    act_one, attended, act_two, cot_ref = (down_ref.at[pl.ds(i * rows_pad, rows_pad), :] for i in range(4))
    weights_ref = up_ref
    input_grad_ref = float_ref
    all_scatters("core_step", count - 1)
    all_scatters("relay_step", count - 1, 0)
    for copy in late_loads():
        copy.wait()
    for kind in range(2):
        for el in range(count):
            return_wait(kind, el)
    for el in range(count):
        do("returned", el)
    for el in range(count):
        for kind in range(3):
            all_of(kind, swap_send.at[kind, el], return_recv.at[kind, el]).wait_send()

    grad_attended_ref = sent_ref.at[pl.ds(0, rows_pad), :]
    branch_ref = cot_sent_ref.at[pl.ds(0, rows_pad), :]
    gain_one = small_rows[NORM_LANE : NORM_LANE + 1]
    gain_two = small_rows[NORM_LANE + 2 : NORM_LANE + 3]
    column_ref[...] = jnp.zeros_like(column_ref)
    flat = jnp.zeros((8, places), F32)
    for e in range(experts):
        row = dots_ref[e]
        row = jnp.concatenate([row, jnp.zeros((8, places - row.shape[1]), F32)], axis=1)
        flat += pltpu.roll(row, e * capacity, 1) if e else row
    dot_row_ref[...] = flat

    def last_sums(g):
        with jax.named_scope("last_sums_%d" % g):
            last = count - 1
            if g == 2:
                pl.when(jnp.logical_not(inner))(lambda: all_scatters("relay_step", last, 1))
            if g == 3:
                pl.when(inner)(lambda: all_scatters("relay_step", last, 1))
                if count > 1:
                    all_scatters("line_step", last - 1)
            if g == 4:
                pl.when(jnp.logical_not(inner))(lambda: all_scatters("relay_step", last, 2))
            if g == 6:
                pl.when(inner)(lambda: all_scatters("relay_step", last, 2))

    def store(i, rows):
        here, there = ((cot_ref, out_out), (input_grad_ref, input_grad_out))[i]
        return copy_in(here.at[rows, :], there.at[rows, :], store_sem.at[i])

    @pl.loop(0, groups)
    def _(g):
        rows = rows_of(g)
        meta = meta_ref[rows, :]
        probs = probs_ref[rows, :]
        lane = iota((BLOCK, LANES), 1)
        grad_first = jnp.zeros((BLOCK, LANES), F32)
        grad_second = jnp.zeros((BLOCK, LANES), F32)
        for c in range(places // LANES):
            at = c * LANES
            in_first = lane == meta[:, 0:1] - at
            in_second = lane == meta[:, 1:2] - at
            place_ref[:, at : at + LANES] = jnp.where(jnp.logical_or(in_first, in_second), 1.0, 0.0).astype(BF16)
            dots = dot_row_ref[0:1, at : at + LANES]
            grad_first += jnp.where(in_first, dots, 0.0)
            grad_second += jnp.where(in_second, dots, 0.0)
        grad_first = jnp.sum(grad_first, axis=1, keepdims=True)
        grad_second = jnp.sum(grad_second, axis=1, keepdims=True)
        mid = input_grad_ref[rows, :]
        grad_probs = jnp.where(lane == meta[:, 2:3], grad_first, 0.0) + jnp.where(lane == meta[:, 3:4], grad_second, 0.0)
        grad_logits = (probs * (grad_probs - jnp.sum(grad_probs * probs, axis=-1, keepdims=True))).astype(BF16)
        logit_grad_ref[rows, :] = grad_logits
        grad_act = dot(place_ref[...], grad_slots_ref[...]) + dot_against(grad_logits, small)
        normed, inverse = normalize(mid)
        column_ref[NORM_LANE + 2 : NORM_LANE + 3, :] += jnp.sum(grad_act * normed, axis=0, keepdims=True)
        column_ref[NORM_LANE + 3 : NORM_LANE + 4, :] += jnp.sum(grad_act, axis=0, keepdims=True)
        grad_mid = cot_ref[rows, :].astype(F32) + denormalize(grad_act, normed, inverse, gain_two)
        input_grad_ref[rows, :] = grad_mid
        branch_ref[rows, :] = grad_mid.astype(BF16)
        grad_attended = dot_against(branch_ref[rows, :], params_ref[:, 3 * width : 4 * width])
        grad_attended_ref[rows, :] = grad_attended.astype(BF16)
        for i in range(groups):
            pl.when(g == i)(functools.partial(last_sums, i))

    split = (A, B, 2, up_in.shape[1])

    def put(item, value):
        at = columns[item]
        part_up[0, :, :, :, :, at] = value.astype(BF16).reshape(*split, at.stop - at.start)
        par.start(item)

    put(par_out, dot_rows(attended[...], branch_ref[...]))

    def attention_backward(pair, g):
        rows = rows_of(g)
        at = pair * LANES
        low = iota((BLOCK, LANES), 1) < HEAD_DIM
        q = triple_ref[rows, at : at + LANES] * HEAD_DIM ** (-0.5)
        k = triple_ref[rows, width + at : width + at + LANES]
        v = triple_ref[rows, 2 * width + at : 2 * width + at + LANES]
        upstream = grad_attended_ref[rows, at : at + LANES]
        grad_q = grad_k = grad_v = jnp.zeros((BLOCK, LANES), F32)
        for half in range(2):
            mask = low if half == 0 else jnp.logical_not(low)
            upstream_half = jnp.where(mask, upstream, 0.0).astype(BF16)
            head = (2 * pair + half) * BLOCK
            weights = weights_ref[rows, head : head + BLOCK]
            kept = weights.astype(F32)
            grad_weights = dot_against(upstream_half, v)
            inner = jnp.sum(grad_weights * kept, axis=-1, keepdims=True)
            grad_scores = (kept * (grad_weights - inner)).astype(BF16)
            grad_q += dot(grad_scores, jnp.where(mask, k, 0.0).astype(BF16))
            grad_k += dot_rows(grad_scores, jnp.where(mask, q, 0.0).astype(BF16))
            grad_v += dot_rows(weights, upstream_half)
        triple_ref[rows, at : at + LANES] = (grad_q * HEAD_DIM ** (-0.5)).astype(BF16)
        triple_ref[rows, width + at : width + at + LANES] = grad_k.astype(BF16)
        triple_ref[rows, 2 * width + at : 2 * width + at + LANES] = grad_v.astype(BF16)

    def par_steps(*steps):
        for name, item in steps:
            with jax.named_scope("%s_%d" % (name, item)):
                par_last(item) if name == "last" else getattr(par, name + "_step")(item)

    for pair in range(pairs):
        pl.loop(0, groups)(functools.partial(attention_backward, pair))
        if pair == 0:
            par_steps(("core", par_out))
        else:
            par_steps(("core", pair - 1))
        last_sums(groups + pair)
        kinds = [triple_ref[:, kind * width + pair * LANES : kind * width + (pair + 1) * LANES] for kind in range(3)]
        put(pair, dot_rows(act_one[...], jnp.concatenate(kinds, axis=1)))

    @pl.loop(0, groups)
    def _(g):
        rows = rows_of(g)
        grad_act = dot_against(triple_ref[rows, :], params_ref[:, : 3 * width])
        normed, inverse = normalize(x_ref[rows, :].astype(F32))
        column_ref[NORM_LANE : NORM_LANE + 1, :] += jnp.sum(grad_act * normed, axis=0, keepdims=True)
        column_ref[NORM_LANE + 1 : NORM_LANE + 2, :] += jnp.sum(grad_act, axis=0, keepdims=True)
        input_grad_ref[rows, :] += denormalize(grad_act, normed, inverse, gain_one)
        store(1, rows).start()

        @pl.when(g == 0)
        def _():
            par_steps(("core", pairs - 1), ("across", par_out), *[("across", pair) for pair in range(pairs - 2)])

        @pl.when(g == 2)
        def _():
            par_steps(("across", pairs - 2))

    put(par_small, dot_rows(act_two[...], logit_grad_ref[...]) + jnp.transpose(column_ref[...]))
    for el in range(count):
        return_wait(2, el)

    def combine(g):
        rows = rows_of(g)
        meta = meta_ref[rows, :]
        gate_first, gate_second = gates_of(probs_ref[rows, :], meta)
        lane = iota((BLOCK, LANES), 1)
        for c in range(places // LANES):
            at = c * LANES
            in_first = lane == meta[:, 0:1] - at
            in_second = lane == meta[:, 1:2] - at
            place_ref[:, at : at + LANES] = jnp.where(in_first, gate_first, jnp.where(in_second, gate_second, 0.0)).astype(BF16)
        mid = float_ref[pl.ds(pl.multiple_of(rows_pad + g * BLOCK, BLOCK), BLOCK), :]
        cot_ref[rows, :] = (mid + dot(place_ref[...], back_ref[...])).astype(BF16)
        store(0, rows).start()

    steps = (
        [("across", pairs - 1), ("core", par_small)], [("across", par_small)], [], [("last", item) for item in (par_out, *range(pairs), par_small)],
    )

    @pl.loop(0, groups)
    def _(g):
        combine(g)
        pl.when(g == 1)(lambda: all_scatters("line_step", count - 1))
        for i in range(groups):
            pl.when(g == i)(functools.partial(par_steps, *steps[i]))

    for i in range(2):
        store(i, pl.ds(0, rows_pad)).wait()

    params.finish_send()
    for el in range(count):
        for kind in range(3):
            all_of(kind, return_send.at[kind, el], return_recv.at[kind, el]).wait_send()
        all_scatters("finish", el)
    for item in range(len(columns)):
        par.finish(item)
    for item in range(len(columns)):
        for copy in shares(item):
            copy.wait()
    total = swap_ref[0].astype(F32)
    for i in range(1, xs):
        total += swap_ref[i].astype(F32)
    share_out[...] = total


def finish_kernel(
    experts, out_pad, input_grad_pad, share, up_half, down_half,
    out, input_grad, qkv, out_weight, router, gain_one, shift_one, gain_two, shift_two, up, down,
):
    width = out.shape[1]
    for g in range(out_pad.shape[0] // BLOCK):
        here, there = slice(g * BLOCK, g * BLOCK + GROUP_ROWS), slice(g * GROUP_ROWS, (g + 1) * GROUP_ROWS)
        out[there, :] = out_pad[here, :]
        input_grad[there, :] = input_grad_pad[here, :]
    for pair in range(HEADS // 2):
        for kind in range(3):
            here, there = (3 * pair + kind) * LANES, kind * width + pair * LANES
            qkv[:, there : there + LANES] = share[:, here : here + LANES]
    out_weight[...] = share[:, 3 * width : 4 * width]
    small = jnp.transpose(share[:, 4 * width :])
    router[...] = small[:experts, :]
    for i, vector in enumerate((gain_one, shift_one, gain_two, shift_two)):
        vector[...] = small[NORM_LANE + i : NORM_LANE + i + 1, :].reshape(vector.shape)
    up[...] = up_half[...].astype(F32)
    down[...] = down_half[...].astype(F32)


def on_device(
    inputs, cotangent, routes, slots, qkv_weight, out_weight, router_weight,
    norm1_gain, norm1_shift, norm2_gain, norm2_shift, expert_up, expert_down,
):
    rows_dev, width = inputs.shape
    groups = rows_dev // GROUP_ROWS
    rows_pad = groups * BLOCK
    fsdp = lax.axis_size("fsdp")
    peers = lax.axis_size("expert")
    held = expert_up.shape[0]
    experts = held * peers
    capacity = (42 * rows_dev + 20 * experts - 1) // (20 * experts)
    capacity = -(-capacity // 16) * 16
    places = experts * capacity

    vmem = pl.BlockSpec(memory_space=pltpu.VMEM)
    hbm = pl.BlockSpec(memory_space=pl.ANY)
    shape = jax.ShapeDtypeStruct
    dma = pltpu.SemaphoreType.DMA
    A, B = 4, fsdp // 8
    count = held // B
    sources = peers * B
    up_rows, down_rows = expert_up.shape[1], expert_down.shape[1]
    hidden_width = expert_up.shape[2]
    packed_width = 4 * width + LANES
    items = HEADS // 2 + 2
    expert_rows = sources * capacity
    row_block = max(n for n in range(capacity, MAX_ROWS + 1, capacity) if expert_rows % n == 0)
    routes_of = 3 + B - 1
    lanes_of = -(-capacity // LANES) * LANES

    def buffer(*dims, dtype=BF16):
        return pltpu.VMEM(dims, dtype)

    out, input_grad, share, up_grad, down_grad, *_ = pl.pallas_call(
        functools.partial(block_kernel, experts, fsdp, peers, count),
        out_shape=(
            shape((rows_pad, width), BF16),
            shape((rows_pad, width), F32),
            shape((up_rows, packed_width), F32),
            shape(expert_up.shape, BF16),
            shape(expert_down.shape, BF16),
            shape((rows_pad, width), BF16),
            shape((rows_pad, HEADS * BLOCK), BF16),
            shape((rows_pad, width), BF16),
            shape((rows_pad, width), F32),
            shape((rows_pad, width), BF16),
        ),
        in_specs=[vmem] * 11 + [hbm] * 2,
        out_specs=[hbm] * 2 + [vmem] + [hbm] * 7,
        scratch_shapes=[
            buffer(up_rows, packed_width),
            buffer(8, rows_pad, dtype=jnp.int32), buffer(rows_pad, 8, dtype=jnp.int32),
            buffer(rows_pad, width), buffer(fsdp * up_rows, packed_width), buffer(rows_pad, 3 * width),
            buffer(rows_pad, LANES, dtype=F32),
            buffer(places, width), buffer(places, width), buffer(experts, 8, lanes_of, dtype=F32),
            buffer(places, width), buffer(places, width), buffer(experts, 8, lanes_of, dtype=F32),
            buffer(places, width), buffer(places, width),
            buffer(experts, 8, lanes_of, dtype=F32), buffer(experts, 8, lanes_of, dtype=F32),
            buffer(max(count * width, rows_pad), hidden_width), buffer(max(count * hidden_width, 4 * rows_pad), width),
            buffer(max(count * width, rows_pad), packed_width), buffer(max(count * hidden_width, 4 * rows_pad), width),
            buffer(max(2 * row_block, 2 * rows_pad), width, dtype=F32),
            buffer(count, A, B, up_rows, hidden_width), buffer(count, A, B, down_rows, width),
            buffer(count, 2, A - 1, B, up_rows, hidden_width), buffer(count, 2, A - 1, B, down_rows, width),
            buffer(A, B, up_rows, packed_width), buffer(B - 1, A, up_rows, packed_width),
            buffer(A - 1, up_rows, packed_width), buffer(peers, up_rows, packed_width),
            buffer(BLOCK, BLOCK, dtype=F32), buffer(8, rows_pad, dtype=F32), buffer(8, places, dtype=F32),
            buffer(BLOCK, places), buffer(row_block, width), buffer(rows_pad, LANES), buffer(LANES, width, dtype=F32),
            dma((5,)), dma((6,)), dma((2,)), dma((routes_of,)), dma((A * B + 1,)), dma,
            dma((2, count, routes_of)), dma((2, count, A * B + 1)), dma((2, count)),
            dma((3, count)), dma((3, count, sources)), dma((3, count)), dma((3, count)),
            dma((2, count, 3 + B - 1)), dma((2, count, 2 * A + B - 2)), dma((2, count)),
            dma((items, 2)), dma((items, 3)), dma((items, peers - 1)), dma((items, peers - 1)),
        ],
        compiler_params=pltpu.CompilerParams(vmem_limit_bytes=VMEM_LIMIT, collective_id=0, has_side_effects=True),
        name="encoder_block",
    )(
        inputs, cotangent, routes.T, slots.T, qkv_weight, out_weight, router_weight.T,
        norm1_gain, norm1_shift, norm2_gain, norm2_shift, expert_up, expert_down,
    )
    vector = shape((up_rows,), F32)
    results = pl.pallas_call(
        functools.partial(finish_kernel, experts),
        out_shape=(
            shape((rows_dev, width), BF16),
            shape((rows_dev, width), F32),
            shape((up_rows, 3 * width), F32),
            shape((up_rows, width), F32),
            shape((experts, up_rows), F32),
            *[vector] * 4,
            shape(expert_up.shape, F32),
            shape(expert_down.shape, F32),
        ),
        in_specs=[vmem] * 5,
        out_specs=[vmem] * 11,
        compiler_params=pltpu.CompilerParams(vmem_limit_bytes=VMEM_LIMIT),
        name="results",
    )(out, input_grad, share, up_grad, down_grad)
    return (*results[:4], results[4].T, *results[5:])


def solution(mesh):
    tokens = P(("expert", "fsdp"), None)
    rows, vector, expert = P("fsdp", None), P("fsdp"), P("expert", "fsdp", None)
    return jax.shard_map(
        on_device,
        mesh=mesh,
        in_specs=(tokens,) * 4 + (rows,) * 3 + (vector,) * 4 + (expert,) * 2,
        out_specs=(tokens,) * 2 + (rows,) * 3 + (vector,) * 4 + (expert,) * 2,
        check_vma=False,
    )
```

```python
import functools

import jax
import jax.numpy as jnp
from jax import lax
from jax.experimental import pallas as pl
from jax.experimental.pallas import tpu as pltpu
from jax.sharding import PartitionSpec as P

HEADS = 8
HEAD_DIM = 64
PATCHES = 49
EPS = 1e-06
ROOT_HALF = 0.7071067811865476
DENSITY_SCALE = 0.3989422804014327

BLOCK = 256
GROUP_IMAGES = BLOCK // PATCHES
GROUP_ROWS = GROUP_IMAGES * PATCHES
LANES = 128
NORM_LANE = 64
FF_CHUNK = 512
MAX_ROWS = 640
VMEM_LIMIT = 63 * 1024 * 1024

MESH = pl.DeviceIdType.MESH
PLAN = {
    ("start", 0): [("across", 0)],
    ("start", 1): [("own", 0)],
    ("start", 3): [("passed", 0)],
    ("after", 3): [("relay", 0, 1, True)],
    ("after", 1): [("cots", 0, "x"), ("cots", 1, "x")],
    ("begin", 0): [("cots", 0, "y", "far")],
    ("end", 0): [("relay", 0, 1, False)],
    ("middle", 1): [("relay", 0, 2, True)],
    ("end", 1): [("across", 1)],
    ("end", 2): [("relay", 0, 2, False), ("cots", 1, "y")],
    ("dispatch", 7): [("own", 1), ("passed", 1), ("ends", 0)],
    ("expert", 0, 0): [("relay", 1, 1, True)],
    ("expert", 0, 1): [("relay", 1, 1, False)],
    ("expert", 0, 2): [("rows", 1)],
    ("expert", 0, 3): [("cots", 1, "far"), ("relay", 1, 2, True)],
    ("expert", 0, 4): [("relay", 1, 2, False)],
    ("after_expert", 0): [("sums", 0), ("sum_relay", 0, 0), ("ends", 1)],
    ("expert", 1, 2): [("sum_relay", 0, 1)],
    ("expert", 1, 7): [("sum_relay", 0, 2)],
    ("after_expert", 1): [("outputs", 0, "y")],
    ("returned", 0): [("outputs", 0, "x", "far")],
    ("returned", 1): [("outputs", 1, "x", "y", "far")],
}
F32 = jnp.float32
BF16 = jnp.bfloat16


def dot(left, right):
    return lax.dot_general(left, right, (((1,), (0,)), ((), ())), preferred_element_type=F32)


def dot_rows(left, right):
    return lax.dot_general(left, right, (((0,), (0,)), ((), ())), preferred_element_type=F32)


def dot_against(left, right):
    return lax.dot_general(left, right, (((1,), (1,)), ((), ())), preferred_element_type=F32)


def iota(shape, dim):
    return lax.broadcasted_iota(jnp.int32, shape, dim)


def normalize(values):
    center = jnp.mean(values, axis=-1, keepdims=True)
    offset = values - center
    spread = jnp.mean(offset * offset, axis=-1, keepdims=True)
    inverse = lax.rsqrt(spread + EPS)
    return offset * inverse, inverse


def denormalize(upstream, normed, inverse, gain):
    scaled = upstream * gain
    return inverse * (
        scaled
        - jnp.mean(scaled, axis=-1, keepdims=True)
        - normed * jnp.mean(scaled * normed, axis=-1, keepdims=True)
    )


def to_row(column):
    n = column.shape[0]
    parts = []
    for at in range(0, n, LANES):
        size = min(LANES, n - at)
        eye = iota((size, LANES), 0) == iota((size, LANES), 1)
        parts.append(jnp.sum(jnp.where(eye, column[at : at + size], 0.0), axis=0, keepdims=True))
    return parts[0] if len(parts) == 1 else jnp.concatenate(parts, axis=1)


def to_column(row, n):
    eye = iota((n, row.shape[1]), 0) == iota((n, row.shape[1]), 1)
    return jnp.sum(jnp.where(eye, row, 0.0), axis=1, keepdims=True)


def rows_of(g):
    return pl.ds(pl.multiple_of(g * BLOCK, BLOCK), BLOCK)


def gates_of(probs, meta):
    lane = iota(probs.shape, 1)
    first = jnp.sum(jnp.where(lane == meta[:, 2:3], probs, 0.0), axis=1, keepdims=True)
    second = jnp.sum(jnp.where(lane == meta[:, 3:4], probs, 0.0), axis=1, keepdims=True)
    return first, second


class Place:
    def __init__(self, fsdp, xs):
        self.A, self.B = 4, fsdp // 8
        self.x = lax.axis_index("expert")
        self.me = lax.axis_index("fsdp")
        self.c = lax.rem(self.me, 2)
        line = lax.div(self.me, 2)
        self.b = lax.rem(line, self.B)
        self.a = lax.div(line, self.B)
        self.xs, self.peers = xs, xs * self.B
        self.peer = self.x * self.B + self.b

    def index(self, a, b, c):
        return (a * self.B + b) * 2 + c

    def other_b(self, j):
        return lax.rem(self.b + 1 + j, self.B)

    def at(self, a, b, c):
        return (self.x, self.index(a, b, c))

    def at_peer(self, peer):
        return (lax.div(peer, self.B), self.index(self.a, lax.rem(peer, self.B), self.c))

    def other_peer(self, k):
        x, b = lax.rem(self.x + lax.rem(k, self.xs), self.xs), lax.rem(self.b + lax.div(k, self.xs), self.B)
        return x * self.B + b

    def seen_from(self, k):
        x, b = lax.rem(self.xs - lax.rem(k, self.xs), self.xs), lax.rem(self.B - lax.div(k, self.xs), self.B)
        return b * self.xs + x


def greet(place, meanwhile):
    barrier = pltpu.get_barrier_semaphore()

    def signal(device):
        pl.semaphore_signal(barrier, inc=1, device_id=device, device_id_type=MESH)

    for k in range(1, place.A):
        signal(place.at(lax.rem(place.a + k, place.A), place.b, place.c))
    for k in range(1, place.peers):
        signal(place.at_peer(place.other_peer(k)))
    signal(place.at(place.a, place.b, 1 - place.c))
    meanwhile()
    pl.semaphore_wait(barrier, place.A - 1 + place.peers - 1 + 1)


class Gather:
    RIGHT, LEFT, CORE, ACROSS = 0, 1, 2, 3

    def __init__(self, place, own, full, block, send_sem, recv_sem, local_sem):
        self.place, self.own, self.full, self.block = place, own, full, block
        self.send_sem, self.recv_sem, self.local_sem = send_sem, recv_sem, local_sem

    def copy(self, shard, route, source, a, b, c):
        return pltpu.make_async_remote_copy(
            src_ref=source, dst_ref=self.block(self.full, shard),
            send_sem=self.send_sem.at[route], recv_sem=self.recv_sem.at[self.arrival(shard, route)],
            device_id=self.place.at(a, b, c), device_id_type=MESH,
        )

    def arrival(self, shard, route):
        return self.place.A * self.place.B if route == self.CORE else lax.div(shard, 2)

    def some(self, route, blocks):
        size = self.own.shape[0]
        ref = self.full.at[pl.ds(0, blocks * size), :]
        p = self.place
        return pltpu.make_async_remote_copy(
            src_ref=ref, dst_ref=ref, send_sem=self.send_sem.at[route], recv_sem=self.recv_sem.at[p.A * p.B],
            device_id=p.at(p.a, p.b, 1 - p.c), device_id_type=MESH,
        )

    def onward(self, shard, source, right, left, across, act):
        p = self.place
        if right is not None:
            pl.when(right)(lambda: act(self.copy(shard, self.RIGHT, source, p.a + 1, p.b, p.c)))
        if left is not None:
            pl.when(left)(lambda: act(self.copy(shard, self.LEFT, source, p.a - 1, p.b, p.c)))
        if across:
            for j in range(p.B - 1):
                act(self.copy(shard, self.ACROSS + j, source, p.a, p.other_b(j), p.c))
        act(self.copy(shard, self.CORE, source, p.a, p.b, 1 - p.c))

    def local(self):
        return pltpu.make_async_copy(self.own, self.block(self.full, self.place.me), self.local_sem)

    def start(self):
        p = self.place
        self.local().start()
        self.onward(p.me, self.own, p.a < p.A - 1, p.a > 0, True, lambda copy: copy.start())

    def arrived(self, shard):
        p = self.place
        self.copy(shard, self.RIGHT, self.block(self.full, shard), p.a, p.b, 1 - p.c).wait_recv()

    def line_step(self, k):
        p = self.place

        def from_left():
            shard = p.index(p.a - k, p.b, p.c)
            self.arrived(shard)
            self.onward(shard, self.block(self.full, shard), p.a < p.A - 1, None, True, lambda copy: copy.start())

        def from_right():
            shard = p.index(p.a + k, p.b, p.c)
            self.arrived(shard)
            self.onward(shard, self.block(self.full, shard), None, p.a > 0, True, lambda copy: copy.start())

        pl.when(p.a - k >= 0)(from_left)
        pl.when(p.a + k < p.A)(from_right)

    def across_step(self, k):
        p = self.place

        def row(a):
            for j in range(p.B - 1):
                shard = p.index(a, p.other_b(j), p.c)
                self.arrived(shard)
                self.onward(shard, self.block(self.full, shard), None, None, False, lambda copy: copy.start())

        if k == 0:
            row(p.a)
        else:
            pl.when(p.a - k >= 0)(lambda: row(p.a - k))
            pl.when(p.a + k < p.A)(lambda: row(p.a + k))

    def finish_recv(self):
        p = self.place
        self.local().wait()
        self.some(self.CORE, p.A * p.B).wait_recv()

    def finish_send(self):
        p = self.place
        for a in range(p.A - 1):
            pl.when(p.a == a)(self.some(self.RIGHT, a + 1).wait_send)
            pl.when(p.a == a + 1)(self.some(self.LEFT, p.A - 1 - a).wait_send)
        for j in range(p.B - 1):
            self.some(self.ACROSS + j, p.A).wait_send()
        self.some(self.CORE, p.A * p.B).wait_send()


class ExpertGather:
    RIGHT, LEFT, CORE, ACROSS = 0, 1, 2, 3

    def __init__(self, place, own, full, count, send_sem, recv_sem, local_sem):
        self.place, self.own, self.full, self.count = place, own, full, count
        self.send_sem, self.recv_sem, self.local_sem = send_sem, recv_sem, local_sem
        self.size = own.shape[1]
        self.depth = self.size * place.A * place.B * 2

    def block(self, el, shard):
        return self.full.at[pl.ds(pl.multiple_of(el * self.depth + shard * self.size, self.size), self.size), :]

    def mine(self, el):
        return self.own.at[self.place.b * self.count + el]

    def copy(self, el, shard, route, source, a, b, c):
        return pltpu.make_async_remote_copy(
            src_ref=source, dst_ref=self.block(el, shard),
            send_sem=self.send_sem.at[el, route], recv_sem=self.recv_sem.at[el, self.arrival(shard, route)],
            device_id=self.place.at(a, b, c), device_id_type=MESH,
        )

    def arrival(self, shard, route):
        return self.place.A * self.place.B if route == self.CORE else lax.div(shard, 2)

    def some(self, el, route, blocks):
        ref = self.full.at[pl.ds(el * self.depth, blocks * self.size), :]
        p = self.place
        return pltpu.make_async_remote_copy(
            src_ref=ref, dst_ref=ref, send_sem=self.send_sem.at[el, route], recv_sem=self.recv_sem.at[el, p.A * p.B],
            device_id=p.at(p.a, p.b, 1 - p.c), device_id_type=MESH,
        )

    def across(self, el):
        p = self.place
        out = []
        for j in range(p.B - 1):
            to = p.other_b(j)
            out.append(self.copy(el, p.me, self.ACROSS + j, self.own.at[to * self.count + el], p.a, to, p.c))
        return out

    def local(self, el):
        return pltpu.make_async_copy(self.mine(el), self.block(el, self.place.me), self.local_sem.at[el])

    def onward(self, el, shard, source, right, left, act):
        p = self.place
        if right:
            pl.when(p.a < p.A - 1)(lambda: act(self.copy(el, shard, self.RIGHT, source, p.a + 1, p.b, p.c)))
        if left:
            pl.when(p.a > 0)(lambda: act(self.copy(el, shard, self.LEFT, source, p.a - 1, p.b, p.c)))
        act(self.copy(el, shard, self.CORE, source, p.a, p.b, 1 - p.c))

    def arrived(self, el, shard):
        p = self.place
        self.copy(el, shard, self.RIGHT, self.block(el, shard), p.a, p.b, 1 - p.c).wait_recv()

    def start_across(self, el):
        for copy in self.across(el):
            copy.start()

    def start_own(self, el):
        self.local(el).start()
        self.onward(el, self.place.me, self.mine(el), True, True, lambda copy: copy.start())

    def across_step(self, el):
        p = self.place
        for j in range(p.B - 1):
            shard = p.index(p.a, p.other_b(j), p.c)
            self.arrived(el, shard)
            self.onward(el, shard, self.block(el, shard), True, True, lambda copy: copy.start())

    def line_step(self, el, k, own):
        p = self.place

        def row(a, right, left):
            for b in [p.b] if own else [p.other_b(j) for j in range(p.B - 1)]:
                shard = p.index(a, b, p.c)
                self.arrived(el, shard)
                self.onward(el, shard, self.block(el, shard), right, left, lambda copy: copy.start())

        pl.when(p.a - k >= 0)(lambda: row(p.a - k, True, False))
        pl.when(p.a + k < p.A)(lambda: row(p.a + k, False, True))

    def core_wait(self, el):
        p = self.place
        self.local(el).wait()
        self.some(el, self.CORE, p.A * p.B).wait_recv()

    def finish(self, el):
        p = self.place
        for copy in self.across(el):
            copy.wait_send()
        for a in range(p.A - 1):
            pl.when(p.a == a)(self.some(el, self.RIGHT, (a + 1) * p.B).wait_send)
            pl.when(p.a == a + 1)(self.some(el, self.LEFT, (p.A - 1 - a) * p.B).wait_send)
        self.some(el, self.CORE, p.A * p.B).wait_send()


class ExpertScatter:
    def __init__(self, place, part, sums, line, out, count, send, recv, local_sem):
        self.place, self.part, self.sums, self.line, self.out, self.count = place, part, sums, line, out, count
        self.send, self.recv, self.local_sem = send, recv, local_sem

    CORE, RIGHT, LEFT, LAST = 0, 1, 2, 3

    def remote(self, source, target, el, route, arrival, a, b, c):
        return pltpu.make_async_remote_copy(
            src_ref=source, dst_ref=target, send_sem=self.send.at[el, route], recv_sem=self.recv.at[el, arrival],
            device_id=self.place.at(a, b, c), device_id_type=MESH,
        )

    def core_copy(self, el):
        p = self.place
        return self.remote(self.part(el).at[:, :, 1 - p.c], self.sums.at[el], el, self.CORE, 0, p.a, p.b, 1 - p.c)

    def right_copy(self, el, target):
        p = self.place
        return self.remote(
            self.sums.at[el, target], self.line.at[el, 0, target - 1], el, self.RIGHT, target, p.a + 1, p.b, p.c
        )

    def left_copy(self, el, target):
        p = self.place
        return self.remote(
            self.sums.at[el, target], self.line.at[el, 1, target], el, self.LEFT, p.A + target, p.a - 1, p.b, p.c
        )

    def add(self, el, target, way, slot):
        @pl.loop(0, self.place.B)
        def _(b):
            total = self.sums[el, target, b].astype(F32) + self.line[el, way, slot, b].astype(F32)
            self.sums[el, target, b] = total.astype(BF16)

    def relay_step(self, el, step):
        p = self.place

        @pl.when(p.a <= step)
        def _():
            target = p.a + p.A - 1 - step

            @pl.when(p.a > 0)
            def _():
                self.right_copy(el, target).wait_recv()
                self.add(el, target, 0, target - 1)

            self.right_copy(el, target).start()

        @pl.when(p.a >= p.A - 1 - step)
        def _():
            target = p.a - (p.A - 1 - step)

            @pl.when(p.a < p.A - 1)
            def _():
                self.left_copy(el, target).wait_recv()
                self.add(el, target, 1, target)

            self.left_copy(el, target).start()

    def last_copies(self, el):
        p = self.place
        out = []
        for j in range(p.B - 1):
            to, back = p.other_b(j), p.B - 2 - j
            target = self.out.at[p.b * self.count + el]
            out.append(self.remote(self.sums.at[el, p.a, to], target, el, self.LAST + j, 2 * p.A - 1 + back, p.a, to, p.c))
        return out

    def local(self, el):
        p = self.place
        return pltpu.make_async_copy(self.sums.at[el, p.a, p.b], self.out.at[p.b * self.count + el], self.local_sem.at[el])

    def start(self, el):
        self.core_copy(el).start()

    def core_step(self, el):
        p = self.place
        self.core_copy(el).wait()
        part = self.part(el)

        @pl.loop(0, p.A * p.B)
        def _(i):
            a, b = lax.div(i, p.B), lax.rem(i, p.B)
            total = self.sums[el, a, b].astype(F32) + part[a, b, p.c].astype(F32)
            self.sums[el, a, b] = total.astype(BF16)

    def line_step(self, el):
        p = self.place

        @pl.when(p.a > 0)
        def _():
            self.right_copy(el, p.a).wait_recv()
            self.add(el, p.a, 0, p.a - 1)

        @pl.when(p.a < p.A - 1)
        def _():
            self.left_copy(el, p.a).wait_recv()
            self.add(el, p.a, 1, p.a)

        for copy in self.last_copies(el) + [self.local(el)]:
            copy.start()

    def finish(self, el):
        p = self.place
        for a in range(p.A - 1):
            for route, at, count in ((self.RIGHT, a, p.A - 1 - a), (self.LEFT, a + 1, a + 1)):
                some = self.sums.at[el, pl.ds(0, count)]
                pl.when(p.a == at)(self.remote(some, some, el, route, 0, p.a, p.b, 1 - p.c).wait_send)
        for copy in self.last_copies(el) + [self.local(el)]:
            copy.wait()


class Scatter:
    def __init__(self, place, part, sums, across, line, columns, send, recv):
        self.place, self.part, self.sums, self.across, self.line = place, part, sums, across, line
        self.columns, self.send, self.recv = columns, send, recv

    CORE, ACROSS, LINE = 0, 1, 2

    def remote(self, source, target, item, route, a, b, c):
        return pltpu.make_async_remote_copy(
            src_ref=source, dst_ref=target,
            send_sem=self.send.at[item, min(route, 1)], recv_sem=self.recv.at[item, route],
            device_id=self.place.at(a, b, c), device_id_type=MESH,
        )

    def all_of(self, ref, item, route):
        p = self.place
        return self.remote(ref, ref, item, route, p.a, p.b, 1 - p.c)

    def core_copy(self, item):
        p, at = self.place, self.columns[item]
        return self.remote(self.part.at[:, :, 1 - p.c, :, at], self.sums.at[:, :, :, at], item, self.CORE, p.a, p.b, 1 - p.c)

    def across_copies(self, item):
        p, at = self.place, self.columns[item]
        out = []
        for j in range(p.B - 1):
            to, back = p.other_b(j), p.B - 2 - j
            copy = self.remote(self.sums.at[:, to, :, at], self.across.at[back, :, :, at], item, self.ACROSS, p.a, to, p.c)
            out.append(copy)
        return out

    def line_copies(self, item):
        p, at = self.place, self.columns[item]
        out = []
        for k in range(1, p.A):
            to, back = lax.rem(p.a + k, p.A), p.A - 1 - k
            copy = self.remote(self.sums.at[to, p.b, :, at], self.line.at[back, :, at], item, self.LINE, to, p.b, p.c)
            out.append(copy)
        return out

    def start(self, item):
        self.core_copy(item).start()

    def core_step(self, item):
        p, at = self.place, self.columns[item]
        self.core_copy(item).wait()

        @pl.loop(0, p.A * p.B)
        def _(i):
            a, b = lax.div(i, p.B), lax.rem(i, p.B)
            total = self.sums[a, b, :, at].astype(F32) + self.part[a, b, p.c, :, at].astype(F32)
            self.sums[a, b, :, at] = total.astype(BF16)

        for copy in self.across_copies(item):
            copy.start()

    def across_step(self, item):
        p, at = self.place, self.columns[item]
        self.all_of(self.across.at[:, :, :, at], item, self.ACROSS).wait_recv()

        @pl.loop(0, p.A)
        def _(a):
            total = self.sums[a, p.b, :, at].astype(F32)
            for j in range(p.B - 1):
                total += self.across[j, a, :, at].astype(F32)
            self.sums[a, p.b, :, at] = total.astype(BF16)

        for copy in self.line_copies(item):
            copy.start()

    def line_step(self, item):
        p, at = self.place, self.columns[item]
        self.all_of(self.line.at[:, :, at], item, self.LINE).wait_recv()
        total = self.sums[p.a, p.b, :, at].astype(F32)
        for k in range(p.A - 1):
            total += self.line[k, :, at].astype(F32)
        return total

    def finish(self, item):
        p, at = self.place, self.columns[item]
        blocks = self.sums.reshape(p.A * p.B, *self.sums.shape[2:])
        self.all_of(blocks.at[pl.ds(0, (p.B - 1) * p.A + p.A - 1), :, at], item, self.LINE).wait_send()


def block_kernel(
    experts, fsdp, xs, count,
    x_raw, cot_raw, routes_ref, slots_ref, qkv_ref, out_ref, router_ref, gain_one_ref, shift_one_ref, gain_two_ref, shift_two_ref,
    up_in, down_in,
    out_out, input_grad_out, share_out, up_grad_out, down_grad_out,
    act_one_save, weights_save, attended_save, mid_save, act_two_save,
    shard_ref, meta_row_ref, meta_ref, x_ref, params_ref, triple_ref, probs_ref,
    sent_ref, cot_sent_ref, gate_sent_ref, rows_ref, grad_ref, gate_ref, back_ref, grad_slots_ref, dots_sent_ref, dots_ref,
    up_ref, down_ref, part_up_ref, part_down_ref, float_ref,
    sums_up, sums_down, line_up, line_down, sums_par, across_par, line_par, swap_ref,
    bias_ref, gate_rows_ref, dot_row_ref, place_ref, gated_ref, logit_grad_ref, column_ref,
    save_sem, late_sem, store_sem, par_gather_send, par_gather_recv, par_gather_local,
    gather_send, gather_recv, gather_local, swap_send, swap_recv, return_send, return_recv,
    scatter_send, scatter_recv, scatter_local, par_send, par_recv, share_send, share_recv,
):
    rows_pad, width = x_ref.shape
    groups = rows_pad // BLOCK
    places = sent_ref.shape[0]
    capacity = places // experts
    hidden_width = up_ref.shape[1]
    chunks = hidden_width // FF_CHUNK
    held = up_in.shape[0]
    place = Place(fsdp, xs)
    A, B, sources = place.A, place.B, place.peers
    expert_rows = sources * capacity
    row_block = gated_ref.shape[0]
    copy_in = pltpu.make_async_copy

    weights_ref = part_up_ref
    act_one, attended, act_two, cot_ref = (part_down_ref.at[pl.ds(i * rows_pad, rows_pad), :] for i in range(4))
    mid_ref = float_ref

    def spread(raw, there):
        for g in range(groups):
            there[g * BLOCK : g * BLOCK + GROUP_ROWS, :] = raw[g * GROUP_ROWS : (g + 1) * GROUP_ROWS, :]
            there[g * BLOCK + GROUP_ROWS : (g + 1) * BLOCK, :] = jnp.zeros((BLOCK - GROUP_ROWS, width), BF16)

    def prepare():
        shard_ref[:, : 3 * width] = qkv_ref[...]
        shard_ref[:, 3 * width : 4 * width] = out_ref[...]
        size = shard_ref.shape[0]
        eye = iota((size, size), 0) == iota((size, size), 1)
        lane = iota((size, LANES), 1)
        small = jnp.zeros((size, LANES), F32)
        for i, norm_ref in enumerate((gain_one_ref, shift_one_ref, gain_two_ref, shift_two_ref)):
            row = norm_ref[...].astype(F32).reshape(1, size)
            column = jnp.sum(jnp.where(eye, row, 0.0), axis=1, keepdims=True)
            small = jnp.where(lane == NORM_LANE + i, column, small)
        shard_ref[:, 4 * width :] = small.astype(BF16)
        shard_ref[:, 4 * width : 4 * width + experts] = jnp.transpose(router_ref[...].astype(F32)).astype(BF16)

    greet(place, prepare)

    def rows_block(ref, shard):
        size = shard_ref.shape[0]
        return ref.at[pl.ds(pl.multiple_of(shard * size, size), size), :]

    params = Gather(place, shard_ref, params_ref, rows_block, par_gather_send, par_gather_recv, par_gather_local)
    weights_in = [
        ExpertGather(place, own, full, count, gather_send.at[i], gather_recv.at[i], gather_local.at[i])
        for i, (own, full) in enumerate(((up_in, up_ref), (down_in, down_ref)))
    ]

    def each(step, el, *more):
        if el < count:
            for gather in weights_in:
                getattr(gather, step)(el, *more)

    def do(*point):
        for name, el, *more in PLAN.get(point, ()):
            if el < count:
                with jax.named_scope("_".join(map(str, (name, el, *more)))):
                    actions[name](el, *more)

    inner = jnp.logical_and(place.a > 0, place.a < A - 1)

    def ends(el):
        for k in range(1, A):
            for own in (True, False):
                each("line_step", el, k, own)

    actions = {
        "across": lambda el: each("start_across", el),
        "own": lambda el: each("start_own", el),
        "passed": lambda el: each("across_step", el),
        "relay": lambda el, k, own: pl.when(inner)(lambda: each("line_step", el, k, own)),
        "ends": lambda el: pl.when(jnp.logical_not(inner))(lambda: ends(el)),
        "cots": lambda el, *which: cot_swaps(el, *which),
        "rows": lambda el: row_swaps(el),
        "sums": lambda el: all_scatters("core_step", el),
        "outputs": lambda el, *which: outputs(el, *which),
        "sum_relay": lambda el, step: all_scatters("relay_step", el, step),
    }
    params.start()
    do("start", 0)
    targets = jnp.where(slots_ref[...] >= 0, routes_ref[...] * capacity + slots_ref[...], -1)
    meta_row_ref[...] = jnp.full(meta_row_ref.shape, -1, jnp.int32)
    for g in range(groups):
        at = slice(g * BLOCK, g * BLOCK + GROUP_ROWS)
        meta_row_ref[0:2, at] = targets[:, g * GROUP_ROWS : (g + 1) * GROUP_ROWS]
        meta_row_ref[2:4, at] = routes_ref[:, g * GROUP_ROWS : (g + 1) * GROUP_ROWS]
    image_row = iota((BLOCK, BLOCK), 0) // PATCHES
    image_col = iota((BLOCK, BLOCK), 1) // PATCHES
    bias_ref[...] = jnp.where(image_row == image_col, 0.0, -1e30)

    def slot_rows(e):
        return pl.ds(pl.multiple_of(e * capacity, 16), capacity)

    def source_rows(el, source):
        return pl.ds(pl.multiple_of(el * expert_rows + source * capacity, 16), capacity)

    def find(e):
        slot = iota((capacity, rows_pad), 0) + e * capacity
        in_first = slot == meta_row_ref[0:1, :]
        in_second = slot == meta_row_ref[1:2, :]
        return in_first, in_second, jnp.where(jnp.logical_or(in_first, in_second), 1.0, 0.0).astype(BF16)

    def swap(kind, el, k):
        peer, back = place.other_peer(k), place.seen_from(k)
        e = peer * count + el
        if kind == 1:
            source, target = gate_sent_ref.at[e], gate_ref.at[el * sources + back]
        else:
            here, there = (sent_ref, rows_ref) if kind == 0 else (cot_sent_ref, grad_ref)
            source, target = here.at[slot_rows(e), :], there.at[source_rows(el, back), :]
        return pltpu.make_async_remote_copy(
            src_ref=source, dst_ref=target, send_sem=swap_send.at[kind, el], recv_sem=swap_recv.at[kind, el, back],
            device_id=place.at_peer(peer), device_id_type=MESH,
        )

    def swap_wait(kind, el, k):
        if kind == 1:
            target = gate_ref.at[el * sources + k]
        else:
            target = (rows_ref if kind == 0 else grad_ref).at[source_rows(el, k), :]
        pltpu.make_async_remote_copy(
            src_ref=target, dst_ref=target, send_sem=swap_send.at[kind, el], recv_sem=swap_recv.at[kind, el, k],
            device_id=place.at_peer(place.other_peer(k)), device_id_type=MESH,
        ).wait_recv()

    def all_of(kind, send, recv):
        some = gate_ref.at[pl.ds(0, sources - 1)] if kind == 1 else rows_ref.at[pl.ds(0, (sources - 1) * capacity), :]
        return pltpu.make_async_remote_copy(
            src_ref=some, dst_ref=some, send_sem=send, recv_sem=recv,
            device_id=place.at(place.a, place.b, 1 - place.c), device_id_type=MESH,
        )

    def peers_where(which, act):
        @pl.loop(1, sources)
        def _(k):
            for name, same in (("x", lax.div(k, xs) == 0), ("y", lax.rem(k, xs) == 0)):
                if which == name:
                    pl.when(same)(lambda: act(k))
            if which == "far":
                pl.when(jnp.logical_and(lax.div(k, xs) > 0, lax.rem(k, xs) > 0))(lambda: act(k))

    def cot_swaps(el, *which):
        for peers in which:
            peers_where(peers, lambda k: swap(2, el, k).start())

    def cot_own(el):
        grad_ref[source_rows(el, 0), :] = cot_sent_ref[slot_rows(place.peer * count + el), :]

    def row_swaps(el):
        @pl.loop(1, sources)
        def _(k):
            swap(0, el, k).start()
            swap(1, el, k).start()

    spread(cot_raw, cot_ref)
    for k in range(1, A):
        params.line_step(k)
        do("start", k)

        @pl.loop((k - 1) * experts // (A - 1), k * experts // (A - 1))
        def _(i):
            e = place.other_peer(lax.rem(lax.div(i, count) + 1, sources)) * count + lax.rem(i, count)
            _, _, picks = find(e)
            cot_sent_ref[slot_rows(e), :] = dot(picks, cot_ref[...]).astype(BF16)

        if k == 1:
            spread(x_raw, x_ref)
            meta_ref[...] = jnp.transpose(meta_row_ref[...])
        do("after", k)
        params.across_step(k - 1)

    params.across_step(A - 1)
    params.finish_recv()
    for el in range(count):
        cot_own(el)
    do("begin", 0)

    small = params_ref[:, 4 * width :]
    small_rows = jnp.transpose(small.astype(F32))

    def saves(rows):
        pairs = (
            (act_one, act_one_save), (weights_ref.at[:, pl.ds(0, HEADS * BLOCK)], weights_save), (attended, attended_save),
            (mid_ref, mid_save), (act_two, act_two_save),
        )
        return [copy_in(here.at[rows, :], there.at[rows, :], save_sem.at[i]) for i, (here, there) in enumerate(pairs)]

    @pl.loop(0, groups)
    def _(g):
        rows = rows_of(g)
        x = x_ref[rows, :].astype(F32)
        normed, _ = normalize(x)
        act = (normed * small_rows[NORM_LANE : NORM_LANE + 1] + small_rows[NORM_LANE + 1 : NORM_LANE + 2]).astype(BF16)
        act_one[rows, :] = act
        triple_ref[rows, :] = dot(act, params_ref[:, : 3 * width]).astype(BF16)
        low = iota((BLOCK, LANES), 1) < HEAD_DIM
        for pair in range(HEADS // 2):
            at = pair * LANES
            q = triple_ref[rows, at : at + LANES] * HEAD_DIM ** (-0.5)
            k = triple_ref[rows, width + at : width + at + LANES]
            v = triple_ref[rows, 2 * width + at : 2 * width + at + LANES]
            total = None
            for half in range(2):
                mask = low if half == 0 else jnp.logical_not(low)
                scores = dot_against(jnp.where(mask, q, 0.0).astype(BF16), k) + bias_ref[...]
                top = jnp.max(scores, axis=-1, keepdims=True)
                raised = jnp.exp(scores - top)
                probs = raised / jnp.sum(raised, axis=-1, keepdims=True)
                probs = probs.astype(BF16)
                head = (2 * pair + half) * BLOCK
                weights_ref[rows, head : head + BLOCK] = probs
                part = dot(probs, jnp.where(mask, v, 0.0).astype(BF16))
                total = part if total is None else total + part
            attended[rows, at : at + LANES] = total.astype(BF16)

        for i in range(groups):
            pl.when(g == i)(functools.partial(do, "middle", i))

        mid = x + dot(attended[rows, :], params_ref[:, 3 * width : 4 * width])
        mid_ref[rows, :] = mid
        normed, _ = normalize(mid)
        act = (normed * small_rows[NORM_LANE + 2 : NORM_LANE + 3] + small_rows[NORM_LANE + 3 : NORM_LANE + 4]).astype(BF16)
        act_two[rows, :] = act
        logits = jnp.where(iota((BLOCK, LANES), 1) < experts, dot(act, small), -1e30)
        raised = jnp.exp(logits - jnp.max(logits, axis=-1, keepdims=True))
        probs = raised / jnp.sum(raised, axis=-1, keepdims=True)
        probs_ref[rows, :] = probs
        first, second = gates_of(probs, meta_ref[rows, :])
        gate_rows_ref[0:1, rows] = to_row(first)
        gate_rows_ref[1:2, rows] = to_row(second)
        for copy in saves(rows):
            copy.start()

        for i in range(groups):
            pl.when(g == i)(functools.partial(do, "end", i))

    @pl.loop(0, experts)
    def _(i):
        el, k = lax.div(i, sources), lax.rem(lax.rem(i, sources) + 1, sources)
        e = place.other_peer(k) * count + el
        in_first, in_second, picks = find(e)
        gate = jnp.sum(
            jnp.where(in_first, gate_rows_ref[0:1, :], jnp.where(in_second, gate_rows_ref[1:2, :], 0.0)),
            axis=1, keepdims=True,
        )
        sent_ref[slot_rows(e), :] = dot(picks, act_two[...]).astype(BF16)
        gate_sent_ref[e, 0:1, :] = to_row(gate)

        @pl.when(jnp.logical_and(el == 0, k > 0))
        def _():
            swap(0, el, k).start()
            swap(1, el, k).start()

        @pl.when(k == 0)
        def _():
            rows_ref[source_rows(el, 0), :] = sent_ref[slot_rows(e), :]
            gate_ref[el * sources] = gate_sent_ref[e]

        for at in range(8):
            pl.when(i == at)(functools.partial(do, "dispatch", at))

    for copy in saves(pl.ds(0, rows_pad)):
        copy.wait()

    part_up = part_up_ref.at[pl.ds(0, count * width), :].reshape(count, A, B, 2, up_in.shape[1], part_up_ref.shape[1])
    part_down = part_down_ref.at[pl.ds(0, count * hidden_width), :].reshape(count, A, B, 2, down_in.shape[1], width)
    scatters = [
        ExpertScatter(place, part, sums, line, out, count, scatter_send.at[i], scatter_recv.at[i], scatter_local.at[i])
        for i, (part, sums, line, out) in enumerate(
            (
                (lambda el: part_up.at[el, :, :, :, :, pl.ds(0, hidden_width)], sums_up, line_up, up_grad_out),
                (lambda el: part_down.at[el], sums_down, line_down, down_grad_out),
            )
        )
    ]

    def all_scatters(step, el, *more):
        for scatter in scatters:
            getattr(scatter, step)(el, *more)

    pairs = HEADS // 2
    columns = [slice(3 * LANES * p, 3 * LANES * (p + 1)) for p in range(pairs)]
    columns += [slice(3 * width, 4 * width), slice(4 * width, 4 * width + LANES)]
    par_out, par_small = pairs, pairs + 1
    par = Scatter(place, part_up.at[0], sums_par, across_par, line_par, columns, par_send, par_recv)

    def shares(item):
        at = columns[item]
        out = []
        for k in range(1, xs):
            to, back = lax.rem(place.x + k, xs), xs - 1 - k
            out.append(
                pltpu.make_async_remote_copy(
                    src_ref=swap_ref.at[place.x, :, at], dst_ref=swap_ref.at[place.x, :, at],
                    send_sem=share_send.at[item, back], recv_sem=share_recv.at[item, back],
                    device_id=(to, place.me), device_id_type=MESH,
                )
            )
        return out

    def par_last(item):
        swap_ref[place.x, :, columns[item]] = par.line_step(item).astype(BF16)
        for copy in shares(item):
            copy.start()

    def returned(kind, el, k):
        e = place.peer * count + el
        if kind == 1:
            source, target = dots_sent_ref.at[el * sources + k], dots_ref.at[e]
        else:
            here, there = (grad_ref, grad_slots_ref) if kind == 0 else (rows_ref, back_ref)
            source, target = here.at[source_rows(el, k), :], there.at[slot_rows(e), :]
        return pltpu.make_async_remote_copy(
            src_ref=source, dst_ref=target,
            send_sem=return_send.at[kind, el], recv_sem=return_recv.at[kind, el],
            device_id=place.at_peer(place.other_peer(k)), device_id_type=MESH,
        )

    def give_back(kind, el, first=1, stop=sources):
        @pl.loop(first, stop)
        def _(k):
            returned(kind, el, k).start()

    def outputs(el, *which):
        for peers in which:
            peers_where(peers, lambda k: returned(2, el, k).start())

    def return_wait(kind, el):
        all_of(kind, return_send.at[kind, el], return_recv.at[kind, el]).wait_recv()

    def expert(el):
        blocks = expert_rows // row_block
        block_sources = row_block // capacity
        order = list(range(blocks))
        if el > 0 and el == count - 1:
            order.reverse()
        each("core_wait", el)
        for turn, block in enumerate(order):
            first, stop = block * block_sources, (block + 1) * block_sources
            for kind in range(3):
                pl.loop(max(first, 1), stop)(functools.partial(swap_wait, kind, el))
            do("before", el, turn)
            here = pl.ds(el * expert_rows + block * row_block, row_block)
            float_ref[: 2 * row_block, :] = jnp.zeros((2 * row_block, width), F32)

            @pl.loop(first, stop)
            def _(k):
                gate = to_column(gate_ref[el * sources + k, 0:1, :], capacity)
                cots = grad_ref[source_rows(el, k), :].astype(F32)
                local = pl.ds(pl.multiple_of((k - first) * capacity, 16), capacity)
                gated_ref[local, :] = (gate * cots).astype(BF16)

            @pl.loop(0, chunks)
            def _(f):
                at = pl.ds(pl.multiple_of(f * FF_CHUNK, FF_CHUNK), FF_CHUNK)
                down_at = pl.ds(pl.multiple_of(el * hidden_width + f * FF_CHUNK, FF_CHUNK), FF_CHUNK)
                rows, grads = rows_ref[here, :], gated_ref[...]
                up_part, down_part = up_ref[el * width : (el + 1) * width, at], down_ref[down_at, :]
                hidden = dot(rows, up_part)
                spread = 0.5 * (1.0 + lax.erf(hidden * ROOT_HALF))
                active = (hidden * spread).astype(BF16)
                slope = spread + hidden * (DENSITY_SCALE * jnp.exp(-0.5 * hidden * hidden))
                grad_active = dot_against(grads, down_part)
                float_ref[:row_block, :] += dot(active, down_part)
                grad_hidden = (grad_active * slope).astype(BF16)
                float_ref[row_block : 2 * row_block, :] += dot_against(grad_hidden, up_part)
                size = up_in.shape[1]
                up_sum = dot_rows(rows, grad_hidden).reshape(A, B, 2, size, FF_CHUNK)
                down_sum = dot_rows(active, grads)
                if turn > 0:
                    up_sum += part_up[el, :, :, :, :, at].astype(F32)
                    down_sum += part_down_ref[down_at, :].astype(F32)
                part_up[el, :, :, :, :, at] = up_sum.astype(BF16)
                part_down_ref[down_at, :] = down_sum.astype(BF16)
                for i in range(chunks):
                    pl.when(f == i)(functools.partial(do, "expert", el, turn * chunks + i))

            @pl.loop(first, stop)
            def _(k):
                at = source_rows(el, k)
                local = pl.ds(pl.multiple_of((k - first) * capacity, 16), capacity)
                back = float_ref[local, :].astype(BF16)
                rows_ref[at, :] = back
                dots = jnp.sum(back.astype(F32) * grad_ref[at, :].astype(F32), axis=1, keepdims=True)
                dots_sent_ref[el * sources + k, 0:1, :] = to_row(dots)
                local = pl.ds(pl.multiple_of(row_block + (k - first) * capacity, 16), capacity)
                grad_ref[at, :] = float_ref[local, :].astype(BF16)

            give_back(0, el, max(first, 1), stop)
            give_back(1, el, max(first, 1), stop)

        all_scatters("start", el)
        own, e = source_rows(el, 0), place.peer * count + el
        back_ref[slot_rows(e), :] = rows_ref[own, :]
        grad_slots_ref[slot_rows(e), :] = grad_ref[own, :]
        dots_ref[e] = dots_sent_ref[el * sources]

    for el in range(count):
        expert(el)
        do("after_expert", el)

    def late_loads():
        out = [copy_in(weights_save, up_ref.at[pl.ds(0, rows_pad), :], late_sem.at[0])]
        for i, array in enumerate((act_one_save, attended_save, act_two_save)):
            out.append(copy_in(array, down_ref.at[pl.ds(i * rows_pad, rows_pad), :], late_sem.at[1 + i]))
        for i in range(2):
            out.append(copy_in(mid_save, float_ref.at[pl.ds(i * rows_pad, rows_pad), :], late_sem.at[4 + i]))
        return out

    for el in range(count):
        each("finish", el)
    for copy in late_loads():
        copy.start()
    spread(cot_raw, down_ref.at[pl.ds(3 * rows_pad, rows_pad), :])
    act_one, attended, act_two, cot_ref = (down_ref.at[pl.ds(i * rows_pad, rows_pad), :] for i in range(4))
    weights_ref = up_ref
    input_grad_ref = float_ref
    all_scatters("core_step", count - 1)
    all_scatters("relay_step", count - 1, 0)
    for copy in late_loads():
        copy.wait()
    for kind in range(2):
        for el in range(count):
            return_wait(kind, el)
    for el in range(count):
        do("returned", el)
    for el in range(count):
        for kind in range(3):
            all_of(kind, swap_send.at[kind, el], return_recv.at[kind, el]).wait_send()

    grad_attended_ref = sent_ref.at[pl.ds(0, rows_pad), :]
    branch_ref = cot_sent_ref.at[pl.ds(0, rows_pad), :]
    gain_one = small_rows[NORM_LANE : NORM_LANE + 1]
    gain_two = small_rows[NORM_LANE + 2 : NORM_LANE + 3]
    column_ref[...] = jnp.zeros_like(column_ref)
    flat = jnp.zeros((8, places), F32)
    for e in range(experts):
        row = dots_ref[e]
        row = jnp.concatenate([row, jnp.zeros((8, places - row.shape[1]), F32)], axis=1)
        flat += pltpu.roll(row, e * capacity, 1) if e else row
    dot_row_ref[...] = flat

    def last_sums(g):
        with jax.named_scope("last_sums_%d" % g):
            last = count - 1
            if g == 2:
                pl.when(jnp.logical_not(inner))(lambda: all_scatters("relay_step", last, 1))
            if g == 3:
                pl.when(inner)(lambda: all_scatters("relay_step", last, 1))
                if count > 1:
                    all_scatters("line_step", last - 1)
            if g == 4:
                pl.when(jnp.logical_not(inner))(lambda: all_scatters("relay_step", last, 2))
            if g == 6:
                pl.when(inner)(lambda: all_scatters("relay_step", last, 2))

    def store(i, rows):
        here, there = ((cot_ref, out_out), (input_grad_ref, input_grad_out))[i]
        return copy_in(here.at[rows, :], there.at[rows, :], store_sem.at[i])

    @pl.loop(0, groups)
    def _(g):
        rows = rows_of(g)
        meta = meta_ref[rows, :]
        probs = probs_ref[rows, :]
        lane = iota((BLOCK, LANES), 1)
        grad_first = jnp.zeros((BLOCK, LANES), F32)
        grad_second = jnp.zeros((BLOCK, LANES), F32)
        first_slot = jnp.broadcast_to(meta[:, 0:1], (BLOCK, LANES))
        second_slot = jnp.broadcast_to(meta[:, 1:2], (BLOCK, LANES))
        for c in range(places // LANES):
            at = c * LANES
            in_first = lane + at == first_slot
            in_second = lane + at == second_slot
            place_ref[:, at : at + LANES] = jnp.where(jnp.logical_or(in_first, in_second), 1.0, 0.0).astype(BF16)
            dots = dot_row_ref[0:1, at : at + LANES]
            grad_first += jnp.where(in_first, dots, 0.0)
            grad_second += jnp.where(in_second, dots, 0.0)
        grad_first = jnp.sum(grad_first, axis=1, keepdims=True)
        grad_second = jnp.sum(grad_second, axis=1, keepdims=True)
        mid = input_grad_ref[rows, :]
        grad_probs = jnp.where(lane == meta[:, 2:3], grad_first, 0.0) + jnp.where(lane == meta[:, 3:4], grad_second, 0.0)
        grad_logits = (probs * (grad_probs - jnp.sum(grad_probs * probs, axis=-1, keepdims=True))).astype(BF16)
        logit_grad_ref[rows, :] = grad_logits
        grad_act = dot(place_ref[...], grad_slots_ref[...]) + dot_against(grad_logits, small)
        normed, inverse = normalize(mid)
        column_ref[NORM_LANE + 2 : NORM_LANE + 3, :] += jnp.sum(grad_act * normed, axis=0, keepdims=True)
        column_ref[NORM_LANE + 3 : NORM_LANE + 4, :] += jnp.sum(grad_act, axis=0, keepdims=True)
        grad_mid = cot_ref[rows, :].astype(F32) + denormalize(grad_act, normed, inverse, gain_two)
        input_grad_ref[rows, :] = grad_mid
        branch_ref[rows, :] = grad_mid.astype(BF16)
        grad_attended = dot_against(branch_ref[rows, :], params_ref[:, 3 * width : 4 * width])
        grad_attended_ref[rows, :] = grad_attended.astype(BF16)
        for i in range(groups):
            pl.when(g == i)(functools.partial(last_sums, i))

    split = (A, B, 2, up_in.shape[1])

    def put(item, value):
        at = columns[item]
        part_up[0, :, :, :, :, at] = value.astype(BF16).reshape(*split, at.stop - at.start)
        par.start(item)

    put(par_out, dot_rows(attended[...], branch_ref[...]))

    def attention_backward(pair, g):
        rows = rows_of(g)
        at = pair * LANES
        low = iota((BLOCK, LANES), 1) < HEAD_DIM
        q = triple_ref[rows, at : at + LANES] * HEAD_DIM ** (-0.5)
        k = triple_ref[rows, width + at : width + at + LANES]
        v = triple_ref[rows, 2 * width + at : 2 * width + at + LANES]
        upstream = grad_attended_ref[rows, at : at + LANES]
        grad_q = grad_k = grad_v = jnp.zeros((BLOCK, LANES), F32)
        for half in range(2):
            mask = low if half == 0 else jnp.logical_not(low)
            upstream_half = jnp.where(mask, upstream, 0.0).astype(BF16)
            head = (2 * pair + half) * BLOCK
            weights = weights_ref[rows, head : head + BLOCK]
            kept = weights.astype(F32)
            grad_weights = dot_against(upstream_half, v)
            inner = jnp.sum(grad_weights * kept, axis=-1, keepdims=True)
            grad_scores = (kept * (grad_weights - inner)).astype(BF16)
            grad_q += dot(grad_scores, jnp.where(mask, k, 0.0).astype(BF16))
            grad_k += dot_rows(grad_scores, jnp.where(mask, q, 0.0).astype(BF16))
            grad_v += dot_rows(weights, upstream_half)
        triple_ref[rows, at : at + LANES] = (grad_q * HEAD_DIM ** (-0.5)).astype(BF16)
        triple_ref[rows, width + at : width + at + LANES] = grad_k.astype(BF16)
        triple_ref[rows, 2 * width + at : 2 * width + at + LANES] = grad_v.astype(BF16)

    def par_steps(*steps):
        for name, item in steps:
            with jax.named_scope("%s_%d" % (name, item)):
                par_last(item) if name == "last" else getattr(par, name + "_step")(item)

    for pair in range(pairs):
        pl.loop(0, groups)(functools.partial(attention_backward, pair))
        if pair == 0:
            par_steps(("core", par_out))
        else:
            par_steps(("core", pair - 1))
        last_sums(groups + pair)
        kinds = [triple_ref[:, kind * width + pair * LANES : kind * width + (pair + 1) * LANES] for kind in range(3)]
        put(pair, dot_rows(act_one[...], jnp.concatenate(kinds, axis=1)))

    @pl.loop(0, groups)
    def _(g):
        rows = rows_of(g)
        grad_act = dot_against(triple_ref[rows, :], params_ref[:, : 3 * width])
        normed, inverse = normalize(x_ref[rows, :].astype(F32))
        column_ref[NORM_LANE : NORM_LANE + 1, :] += jnp.sum(grad_act * normed, axis=0, keepdims=True)
        column_ref[NORM_LANE + 1 : NORM_LANE + 2, :] += jnp.sum(grad_act, axis=0, keepdims=True)
        input_grad_ref[rows, :] += denormalize(grad_act, normed, inverse, gain_one)
        store(1, rows).start()

        @pl.when(g == 0)
        def _():
            par_steps(("core", pairs - 1), ("across", par_out), *[("across", pair) for pair in range(pairs - 2)])

        @pl.when(g == 2)
        def _():
            par_steps(("across", pairs - 2))

    put(par_small, dot_rows(act_two[...], logit_grad_ref[...]) + jnp.transpose(column_ref[...]))
    for el in range(count):
        return_wait(2, el)

    def combine(g):
        rows = rows_of(g)
        meta = meta_ref[rows, :]
        gate_first, gate_second = gates_of(probs_ref[rows, :], meta)
        lane = iota((BLOCK, LANES), 1)
        first_slot = jnp.broadcast_to(meta[:, 0:1], (BLOCK, LANES))
        second_slot = jnp.broadcast_to(meta[:, 1:2], (BLOCK, LANES))
        for c in range(places // LANES):
            at = c * LANES
            in_first = lane + at == first_slot
            in_second = lane + at == second_slot
            place_ref[:, at : at + LANES] = jnp.where(in_first, gate_first, jnp.where(in_second, gate_second, 0.0)).astype(BF16)
        mid = float_ref[pl.ds(pl.multiple_of(rows_pad + g * BLOCK, BLOCK), BLOCK), :]
        cot_ref[rows, :] = (mid + dot(place_ref[...], back_ref[...])).astype(BF16)
        store(0, rows).start()

    steps = (
        [("across", pairs - 1), ("core", par_small)], [("across", par_small)], [], [("last", item) for item in (par_out, *range(pairs), par_small)],
    )

    @pl.loop(0, groups)
    def _(g):
        combine(g)
        pl.when(g == 1)(lambda: all_scatters("line_step", count - 1))
        for i in range(groups):
            pl.when(g == i)(functools.partial(par_steps, *steps[i]))

    for i in range(2):
        store(i, pl.ds(0, rows_pad)).wait()

    params.finish_send()
    for el in range(count):
        for kind in range(3):
            all_of(kind, return_send.at[kind, el], return_recv.at[kind, el]).wait_send()
        all_scatters("finish", el)
    for item in range(len(columns)):
        par.finish(item)
    for item in range(len(columns)):
        for copy in shares(item):
            copy.wait()
    total = swap_ref[0].astype(F32)
    for i in range(1, xs):
        total += swap_ref[i].astype(F32)
    share_out[...] = total


def finish_kernel(
    experts, out_pad, input_grad_pad, share, up_half, down_half,
    out, input_grad, qkv, out_weight, router, gain_one, shift_one, gain_two, shift_two, up, down,
):
    width = out.shape[1]
    for g in range(out_pad.shape[0] // BLOCK):
        here, there = slice(g * BLOCK, g * BLOCK + GROUP_ROWS), slice(g * GROUP_ROWS, (g + 1) * GROUP_ROWS)
        out[there, :] = out_pad[here, :]
        input_grad[there, :] = input_grad_pad[here, :]
    for pair in range(HEADS // 2):
        for kind in range(3):
            here, there = (3 * pair + kind) * LANES, kind * width + pair * LANES
            qkv[:, there : there + LANES] = share[:, here : here + LANES]
    out_weight[...] = share[:, 3 * width : 4 * width]
    small = jnp.transpose(share[:, 4 * width :])
    router[...] = small[:experts, :]
    for i, vector in enumerate((gain_one, shift_one, gain_two, shift_two)):
        vector[...] = small[NORM_LANE + i : NORM_LANE + i + 1, :].reshape(vector.shape)
    up[...] = up_half[...].astype(F32)
    down[...] = down_half[...].astype(F32)


def on_device(
    inputs, cotangent, routes, slots, qkv_weight, out_weight, router_weight,
    norm1_gain, norm1_shift, norm2_gain, norm2_shift, expert_up, expert_down,
):
    rows_dev, width = inputs.shape
    groups = rows_dev // GROUP_ROWS
    rows_pad = groups * BLOCK
    fsdp = lax.axis_size("fsdp")
    peers = lax.axis_size("expert")
    held = expert_up.shape[0]
    experts = held * peers
    capacity = (42 * rows_dev + 20 * experts - 1) // (20 * experts)
    capacity = -(-capacity // 16) * 16
    places = experts * capacity

    vmem = pl.BlockSpec(memory_space=pltpu.VMEM)
    hbm = pl.BlockSpec(memory_space=pl.ANY)
    shape = jax.ShapeDtypeStruct
    dma = pltpu.SemaphoreType.DMA
    A, B = 4, fsdp // 8
    count = held // B
    sources = peers * B
    up_rows, down_rows = expert_up.shape[1], expert_down.shape[1]
    hidden_width = expert_up.shape[2]
    packed_width = 4 * width + LANES
    items = HEADS // 2 + 2
    expert_rows = sources * capacity
    row_block = max(n for n in range(capacity, MAX_ROWS + 1, capacity) if expert_rows % n == 0)
    routes_of = 3 + B - 1
    lanes_of = -(-capacity // LANES) * LANES

    def buffer(*dims, dtype=BF16):
        return pltpu.VMEM(dims, dtype)

    out, input_grad, share, up_grad, down_grad, *_ = pl.pallas_call(
        functools.partial(block_kernel, experts, fsdp, peers, count),
        out_shape=(
            shape((rows_pad, width), BF16),
            shape((rows_pad, width), F32),
            shape((up_rows, packed_width), F32),
            shape(expert_up.shape, BF16),
            shape(expert_down.shape, BF16),
            shape((rows_pad, width), BF16),
            shape((rows_pad, HEADS * BLOCK), BF16),
            shape((rows_pad, width), BF16),
            shape((rows_pad, width), F32),
            shape((rows_pad, width), BF16),
        ),
        in_specs=[vmem] * 11 + [hbm] * 2,
        out_specs=[hbm] * 2 + [vmem] + [hbm] * 7,
        scratch_shapes=[
            buffer(up_rows, packed_width),
            buffer(8, rows_pad, dtype=jnp.int32), buffer(rows_pad, 8, dtype=jnp.int32),
            buffer(rows_pad, width), buffer(fsdp * up_rows, packed_width), buffer(rows_pad, 3 * width),
            buffer(rows_pad, LANES, dtype=F32),
            buffer(places, width), buffer(places, width), buffer(experts, 8, lanes_of, dtype=F32),
            buffer(places, width), buffer(places, width), buffer(experts, 8, lanes_of, dtype=F32),
            buffer(places, width), buffer(places, width),
            buffer(experts, 8, lanes_of, dtype=F32), buffer(experts, 8, lanes_of, dtype=F32),
            buffer(max(count * width, rows_pad), hidden_width), buffer(max(count * hidden_width, 4 * rows_pad), width),
            buffer(max(count * width, rows_pad), packed_width), buffer(max(count * hidden_width, 4 * rows_pad), width),
            buffer(max(2 * row_block, 2 * rows_pad), width, dtype=F32),
            buffer(count, A, B, up_rows, hidden_width), buffer(count, A, B, down_rows, width),
            buffer(count, 2, A - 1, B, up_rows, hidden_width), buffer(count, 2, A - 1, B, down_rows, width),
            buffer(A, B, up_rows, packed_width), buffer(B - 1, A, up_rows, packed_width),
            buffer(A - 1, up_rows, packed_width), buffer(peers, up_rows, packed_width),
            buffer(BLOCK, BLOCK, dtype=F32), buffer(8, rows_pad, dtype=F32), buffer(8, places, dtype=F32),
            buffer(BLOCK, places), buffer(row_block, width), buffer(rows_pad, LANES), buffer(LANES, width, dtype=F32),
            dma((5,)), dma((6,)), dma((2,)), dma((routes_of,)), dma((A * B + 1,)), dma,
            dma((2, count, routes_of)), dma((2, count, A * B + 1)), dma((2, count)),
            dma((3, count)), dma((3, count, sources)), dma((3, count)), dma((3, count)),
            dma((2, count, 3 + B - 1)), dma((2, count, 2 * A + B - 2)), dma((2, count)),
            dma((items, 2)), dma((items, 3)), dma((items, peers - 1)), dma((items, peers - 1)),
        ],
        compiler_params=pltpu.CompilerParams(vmem_limit_bytes=VMEM_LIMIT, collective_id=0, has_side_effects=True),
        name="encoder_block",
    )(
        inputs, cotangent, routes.T, slots.T, qkv_weight, out_weight, router_weight.T,
        norm1_gain, norm1_shift, norm2_gain, norm2_shift, expert_up, expert_down,
    )
    vector = shape((up_rows,), F32)
    results = pl.pallas_call(
        functools.partial(finish_kernel, experts),
        out_shape=(
            shape((rows_dev, width), BF16),
            shape((rows_dev, width), F32),
            shape((up_rows, 3 * width), F32),
            shape((up_rows, width), F32),
            shape((experts, up_rows), F32),
            *[vector] * 4,
            shape(expert_up.shape, F32),
            shape(expert_down.shape, F32),
        ),
        in_specs=[vmem] * 5,
        out_specs=[vmem] * 11,
        compiler_params=pltpu.CompilerParams(vmem_limit_bytes=VMEM_LIMIT),
        name="results",
    )(out, input_grad, share, up_grad, down_grad)
    return (*results[:4], results[4].T, *results[5:])


def solution(mesh):
    tokens = P(("expert", "fsdp"), None)
    rows, vector, expert = P("fsdp", None), P("fsdp"), P("expert", "fsdp", None)
    return jax.shard_map(
        on_device,
        mesh=mesh,
        in_specs=(tokens,) * 4 + (rows,) * 3 + (vector,) * 4 + (expert,) * 2,
        out_specs=(tokens,) * 2 + (rows,) * 3 + (vector,) * 4 + (expert,) * 2,
        check_vma=False,
    )
```
